32 devices in a mesh: dp: 8 (over z, x), narrow: 4 (over y, core).
Axes of the slice: x: 2, y: 2, z: 4, core: 2. Of those that a mesh axis runs over, the one named last changes fastest.
Arguments:
- tokens: bfloat16 [64, 512, 768], P(('dp', 'narrow')), may hold values from -6 to 6
- doc_lengths: int32 [64, 4], P(('dp', 'narrow')), may hold values from 1 to 256, 512 in all within a row
- cotangent: bfloat16 [64, 512, 768], P(('dp', 'narrow')), may hold values from -6 to 6
- qkv_weight: float32 [12, 192, 192], P(None, 'narrow', 'dp'), may hold values from -0.4375 to 0.4375
- out_weight: float32 [1, 768, 768], P(None, 'narrow', 'dp'), may hold values from -1.25 to 1.25
- ffn_in_weight: float32 [4, 768, 192], P(None, 'narrow', 'dp'), may hold values from -0.4375 to 0.4375
- ffn_out_weight: float32 [4, 768, 192], P(None, 'narrow', 'dp'), may hold values from -0.21875 to 0.21875
- vectors: float32 [12, 768], replicated, may hold values from -1.2 to 1.4, as said below
- qkv_moment: float32 [12, 192, 192], P(None, 'narrow', 'dp'), may hold values from -320 to 320
- out_moment: float32 [1, 768, 768], P(None, 'narrow', 'dp'), may hold values from -320 to 320
- ffn_in_moment: float32 [4, 768, 192], P(None, 'narrow', 'dp'), may hold values from -320 to 320
- ffn_out_moment: float32 [4, 768, 192], P(None, 'narrow', 'dp'), may hold values from -320 to 320
- vec_moment1: float32 [12, 768], replicated, may hold values from -64 to 64
- vec_moment2: float32 [12, 768], replicated, may hold values from 9.8304 to 39.3216
Outputs:
- out_act: bfloat16 [64, 512, 768], P(('dp', 'narrow'))
- grad_tokens: bfloat16 [64, 512, 768], P(('dp', 'narrow'))
- qkv_moment_new: float32 [12, 192, 192], P(None, 'narrow', 'dp')
- out_moment_new: float32 [1, 768, 768], P(None, 'narrow', 'dp')
- ffn_in_moment_new: float32 [4, 768, 192], P(None, 'narrow', 'dp')
- ffn_out_moment_new: float32 [4, 768, 192], P(None, 'narrow', 'dp')
- qkv_weight_new: float32 [12, 192, 192], P(None, 'narrow', 'dp')
- out_weight_new: float32 [1, 768, 768], P(None, 'narrow', 'dp')
- ffn_in_weight_new: float32 [4, 768, 192], P(None, 'narrow', 'dp')
- ffn_out_weight_new: float32 [4, 768, 192], P(None, 'narrow', 'dp')
- vec_moment1_new: float32 [12, 768], replicated
- vec_moment2_new: float32 [12, 768], replicated
- vectors_new: float32 [12, 768], replicated
The draws below stay inside these ranges and needn't reach their ends.
Inputs may be any that keep to these rules, and one draw needn't show every extreme that they name: `vectors`: rows 0 and 2 lie near one, the other rows are spread around zero.
All inputs are finite; a program needn't handle non-finite values.
Results may differ from the reference program's by a relative error of at most 0.04.
Values may be sent and summed in bfloat16 or wider, within the bound.
A program may use at most 192 MiB of HBM per device.

```python
import math
import jax
import jax.numpy as jnp
import numpy as np
from jax import lax

D = 768
HEADS = 12
HEAD = 64
GROUPS = 4
FF = 3072
SEQ = 512
DOCS = 4
NS_STEPS = 5
STEP = 5
SLOTS = 64
VROWS = 12
N_NARROW = 4


def draw_vectors(key, part):
    key = jax.random.fold_in(key, 7)
    row_total = 8 + FF // D
    jitter = jnp.clip(jax.random.normal(key, (row_total, D), jnp.float32), -4.0, 4.0)
    row_index = jnp.arange(row_total)[:, None]
    gain_rows = jnp.logical_or(row_index == 0, row_index == 2)
    return jnp.where(gain_rows, 1.0 + 0.1 * jitter, 0.3 * jitter).astype(jnp.float32)


def level_of(stream_key, extent, shards, smallest, high):
    def one(axis_at, blocks):
        steps = jax.random.uniform(jax.random.fold_in(jax.random.fold_in(stream_key, 6), axis_at), (blocks,), jnp.float32, smallest / len(shards), high / len(shards))
        return jnp.repeat(jnp.exp(steps), extent[axis_at] // blocks).reshape((-1,) + (1,) * (len(extent) - axis_at - 1))

    level = one(*shards[0])
    for cut in shards[1:]:
        level = level * one(*cut)
    return level


def split_up(amount, total, bound, slope):
    weights = [(1 << 20) // math.isqrt(rank ** slope) + 1 for rank in range(2, amount + 1)]
    spare, holding = total - bound - (amount - 1), [1] * (amount - 1)
    while spare > 0:
        candidates = [i for i in range(amount - 1) if holding[i] < bound]
        whole, left = sum([weights[i] for i in candidates]), spare
        for i in candidates:
            extra = min(bound - holding[i], max(1, left * weights[i] // whole), spare)
            holding[i] = holding[i] + extra
            spare = spare - extra
    return np.array([bound] + holding)


def ragged(own_key, number_of, total, limit, slope):
    if number_of == 2:
        one = jax.random.randint(own_key, (), max(1, total - limit), min(limit, total - 1) + 1)
        return jnp.stack([one, total - one])
    sizes = jnp.asarray(split_up(number_of, total, limit, slope), jnp.int32)
    couples = (number_of - 1) // 2
    donor, sink = sizes[1:1 + 2 * couples:2], sizes[2:2 + 2 * couples:2]
    room = jnp.minimum(donor - 1, limit - sink)
    passed = jax.random.randint(jax.random.fold_in(own_key, 1), (couples,), 0, 1 << 20) % (room + 1)
    sizes = sizes.at[1:1 + 2 * couples:2].set(donor - passed).at[2:2 + 2 * couples:2].set(sink + passed)
    return sizes[jax.random.permutation(jax.random.fold_in(own_key, 2), number_of)]


def bell_draw(key, dims, width, most, cuts=(), kind=jnp.bfloat16):
    array = jax.random.normal(key, dims, jnp.float32) * width
    if len(cuts) > 0:
        array = level_of(key, dims, cuts, -0.22, 0.18) * array
    return jnp.clip(array, min=-most, max=most).astype(kind)


def setup_inputs(seed: int = 0) -> dict:
    key_of = jax.random.split(jax.random.key(seed), 15)
    tokens = bell_draw(key_of[0], (SLOTS, SEQ, D), 1.0, 6.0, ((0, 32),))
    doc_lengths = jax.vmap(lambda own: ragged(own, DOCS, SEQ, SEQ // 2, 2))(jax.random.split(key_of[1], SLOTS)).reshape((SLOTS, DOCS)).astype(jnp.int32)
    cotangent = bell_draw(key_of[2], (SLOTS, SEQ, D), 1.0, 6.0, ((0, 32),))
    qkv_weight = bell_draw(key_of[3], (3 * GROUPS, D // GROUPS, D // GROUPS), (D // GROUPS) ** -0.5, 0.4375, ((1, 4), (2, 8)), jnp.float32)
    out_weight = bell_draw(key_of[4], (1, D, D), (D // 32) ** -0.5, 1.25, ((1, 4), (2, 8)), jnp.float32)
    ffn_in_weight = bell_draw(key_of[5], (GROUPS, FF // GROUPS, D // GROUPS), (D // GROUPS) ** -0.5, 0.4375, ((1, 4), (2, 8)), jnp.float32)
    ffn_out_weight = bell_draw(key_of[6], (GROUPS, FF // GROUPS, D // GROUPS), (FF // GROUPS) ** -0.5, 0.21875, ((1, 4), (2, 8)), jnp.float32)
    vectors = draw_vectors(jax.random.fold_in(key_of[14], 71), 0)
    qkv_moment = bell_draw(key_of[8], (3 * GROUPS, D // GROUPS, D // GROUPS), (0.3 * (SLOTS * SEQ) ** 0.5), 320.0, ((1, 4), (2, 8)), jnp.float32)
    out_moment = bell_draw(key_of[9], (1, D, D), (0.3 * (SLOTS * SEQ) ** 0.5), 320.0, ((1, 4), (2, 8)), jnp.float32)
    ffn_in_moment = bell_draw(key_of[10], (GROUPS, FF // GROUPS, D // GROUPS), (0.3 * (SLOTS * SEQ) ** 0.5), 320.0, ((1, 4), (2, 8)), jnp.float32)
    ffn_out_moment = bell_draw(key_of[11], (GROUPS, FF // GROUPS, D // GROUPS), (0.3 * (SLOTS * SEQ) ** 0.5), 320.0, ((1, 4), (2, 8)), jnp.float32)
    vec_moment1 = bell_draw(key_of[12], (VROWS, D), (0.06 * (SLOTS * SEQ) ** 0.5), 64.0, (), jnp.float32)
    vec_moment2 = jnp.clip(jnp.exp(jax.random.uniform(key_of[13], (VROWS, D), jnp.float32, math.log(9.8304), math.log(39.3216))), 9.8304, 39.3216)
    return {"tokens": tokens, "doc_lengths": doc_lengths, "cotangent": cotangent, "qkv_weight": qkv_weight, "out_weight": out_weight, "ffn_in_weight": ffn_in_weight, "ffn_out_weight": ffn_out_weight, "vectors": vectors, "qkv_moment": qkv_moment, "out_moment": out_moment, "ffn_in_moment": ffn_in_moment, "ffn_out_moment": ffn_out_moment, "vec_moment1": vec_moment1, "vec_moment2": vec_moment2}


@jax.custom_vjp
def low(v):
    return lax.optimization_barrier(v.astype(jnp.bfloat16)).astype(jnp.float32)

@jax.custom_vjp
def low_back(v):
    return v

def low_keep(v):
    return (low(v), None)

def low_pass(kept, grad):
    return (grad,)

def back_keep(v):
    return (v, None)

def back_low(kept, grad):
    return (low(grad),)
low.defvjp(low_keep, low_pass)
low_back.defvjp(back_keep, back_low)
ns_first = 3.4445
ns_second = -4.775
ns_third = 2.0315
norm_eps = 1e-05
muon_rate = 0.5
muon_decay = 0.01
adam_rate = 0.4
highest = lax.Precision.HIGHEST

def layer_norm(values, gain_row, shift_row):
    centred = values - lax.optimization_barrier(jnp.mean(values, axis=-1, keepdims=True))
    inv_std = lax.rsqrt(lax.optimization_barrier(jnp.mean(centred * centred, axis=-1, keepdims=True)) + norm_eps)
    return centred * inv_std * gain_row + shift_row

def doc_ids(lengths):
    doc_ends = jnp.cumsum(lengths, axis=-1)
    position = jnp.arange(SEQ, dtype=jnp.int32)
    return lax.optimization_barrier(jnp.sum((position[None, :, None] >= doc_ends[:, None, :]).astype(jnp.int32), axis=-1))

def block_forward(tokens, doc_rows, qkv_full, out_full, in_full, back_full, vectors):
    slot_count = tokens.shape[0]
    row_count = slot_count * SEQ
    group_width = D // GROUPS
    grouped = tokens.reshape(row_count, GROUPS, group_width)
    projected = jnp.einsum('ngi,cgoi->cngo', grouped, qkv_full, precision=highest).reshape(3, row_count, D)
    query_part = low(low_back(projected[0] + vectors[4])).reshape(slot_count, SEQ, HEADS, HEAD)
    key_part = low(low_back(projected[1])).reshape(slot_count, SEQ, HEADS, HEAD)
    value_part = low(low_back(projected[2] + vectors[5])).reshape(slot_count, SEQ, HEADS, HEAD)
    scores = low_back(jnp.einsum('bqhd,bkhd->bhqk', query_part, key_part, precision=highest) * HEAD ** (-0.5))
    same_doc = doc_rows[:, :, None] == doc_rows[:, None, :]
    scores = jnp.where(same_doc[:, None], scores, -1e+30)
    attn_probs = low(jax.nn.softmax(scores, axis=-1))
    context = jnp.einsum('bhqk,bkhd->bqhd', attn_probs, value_part, precision=highest).reshape(row_count, D)
    context = low(low_back(context))
    attn_out = low_back(jnp.einsum('ni,oi->no', context, out_full, precision=highest) + vectors[6])
    first = layer_norm(tokens.reshape(row_count, D) + attn_out, vectors[0], vectors[1])
    first_low = low(first).reshape(row_count, GROUPS, group_width)
    inner = jnp.einsum('ngi,goi->ngo', first_low, in_full, precision=highest) + vectors[8:].reshape(GROUPS, -1)
    inner = low_back(inner)
    active = low(jax.nn.gelu(inner, approximate=False))
    branch = jnp.einsum('ngi,gio->ngo', active, back_full, precision=highest).reshape(row_count, D) + vectors[7]
    branch = low_back(branch)
    return layer_norm(first + branch, vectors[2], vectors[3]).reshape(slot_count, SEQ, D)

def forward(tokens, doc_rows, qkv_weight, out_weight, ffn_in_weight, ffn_out_weight, vectors):
    group_width = D // GROUPS
    qkv_full = low(qkv_weight).reshape(3, GROUPS, group_width, group_width)
    out_full = low(out_weight)[0]
    in_full = low(ffn_in_weight)
    back_full = low(ffn_out_weight)

    def scan_body(carry, operands):
        return (carry, block_forward(operands[0], operands[1], qkv_full, out_full, in_full, back_full, vectors))
    stacked_in = (tokens.reshape(-1, 8, SEQ, D), doc_rows.reshape(-1, 8, SEQ))
    _, results = lax.scan(jax.checkpoint(scan_body), None, stacked_in)
    return results.reshape(tokens.shape)

def gram(matrices):
    count = matrices.shape[0]
    blocks = matrices.reshape(count, N_NARROW, matrices.shape[1] // N_NARROW, matrices.shape[2])
    partial_sums = jnp.einsum('gbls,gblt->gbst', blocks, blocks, precision=highest)
    rounded = lax.optimization_barrier(partial_sums.astype(jnp.bfloat16)).astype(jnp.float32)
    return lax.optimization_barrier(jnp.sum(rounded, axis=1))

def muon(weight, moment, gradient):
    moment = 0.95 * moment + gradient
    grams = gram(moment)
    factor = 1.0 / (jnp.sqrt(jnp.trace(grams, axis1=1, axis2=2)) + 1e-07)
    matrices = moment * factor[:, None, None]
    grams = grams * (factor * factor)[:, None, None]
    for sweep in range(NS_STEPS):
        if sweep > 0:
            grams = gram(matrices)
        poly = ns_second * grams + ns_third * jnp.matmul(grams, grams, precision=highest)
        matrices = ns_first * matrices + jnp.matmul(matrices, poly, precision=highest)
    match_scale = 0.2 * math.sqrt(max(weight.shape[1], weight.shape[2]))
    return (moment, weight - muon_rate * (match_scale * matrices + muon_decay * weight))

def reference(tokens, doc_lengths, cotangent, qkv_weight, out_weight, ffn_in_weight, ffn_out_weight, vectors, qkv_moment, out_moment, ffn_in_moment, ffn_out_moment, vec_moment1, vec_moment2):
    doc_rows = doc_ids(doc_lengths)

    def run_layer(inputs, qkv_w, out_w, in_w, back_w, vec_w):
        return forward(inputs, doc_rows, qkv_w, out_w, in_w, back_w, vec_w)
    result, pull_back = jax.vjp(run_layer, tokens.astype(jnp.float32), qkv_weight, out_weight, ffn_in_weight, ffn_out_weight, vectors)
    grad_in, grad_qkv, grad_out, grad_ffn_in, grad_ffn_out, grad_vec = pull_back(cotangent.astype(jnp.float32))
    qkv_moment_new, qkv_weight_new = muon(qkv_weight, qkv_moment, grad_qkv)
    out_moment_new, out_weight_new = muon(out_weight, out_moment, grad_out)
    ffn_in_moment_new, ffn_in_weight_new = muon(ffn_in_weight, ffn_in_moment, grad_ffn_in)
    ffn_out_moment_new, ffn_out_weight_new = muon(ffn_out_weight, ffn_out_moment, grad_ffn_out)
    first_new = 0.9 * vec_moment1 + 0.1 * grad_vec
    second_new = 0.999 * vec_moment2 + 0.001 * grad_vec * grad_vec
    corr_first = 1.0 - 0.9 ** STEP
    corr_second = 1.0 - 0.999 ** STEP
    vectors_new = vectors - adam_rate * (first_new / corr_first) / (jnp.sqrt(second_new / corr_second) + 1e-08)
    return (result.astype(jnp.bfloat16), grad_in.astype(jnp.bfloat16), qkv_moment_new, out_moment_new, ffn_in_moment_new, ffn_out_moment_new, qkv_weight_new, out_weight_new, ffn_in_weight_new, ffn_out_weight_new, first_new, second_new, vectors_new)
```

```python
import functools
import math

import jax
import jax.numpy as jnp
from jax import lax
from jax.experimental import pallas as pl
from jax.experimental.pallas import tpu as pltpu
from jax.sharding import PartitionSpec as P

F32, BF16 = jnp.float32, jnp.bfloat16
MESH = pl.DeviceIdType.MESH
NORM_EPS = 1e-05
NS_STEPS = 5
STEP = 5
ns_first = 3.4445
ns_second = -4.775
ns_third = 2.0315
muon_rate = 0.5
muon_decay = 0.01
adam_rate = 0.4
VMEM = pl.BlockSpec(memory_space=pltpu.VMEM)


def nn(a, b):
    return lax.dot_general(a, b, (((1,), (0,)), ((), ())), preferred_element_type=F32)


def nt(a, b):
    return lax.dot_general(a, b, (((1,), (1,)), ((), ())), preferred_element_type=F32)


def window(g):
    return 128 * (3 * (g // 2) + g % 2)


def join(parts):
    out = []
    for p in range(2):
        a, b = parts[2 * p], parts[2 * p + 1]
        out += [a[:, :128], a[:, 128:] + b[:, :128], b[:, 128:]]
    return jnp.concatenate(out, axis=1)


def ids(len_ref, row, shape, dim):
    pos = lax.broadcasted_iota(jnp.int32, shape, dim)
    out = jnp.zeros(shape, jnp.int32)
    end = jnp.int32(0)
    for j in range(4):
        end = end + len_ref[row, j]
        out = out + (pos >= end).astype(jnp.int32)
    return out


def attn_fwd_kernel(len_ref, x_ref, w_ref, vec_ref, qt_ref, k_ref, kt_ref, v_ref, ct_ref, lse_ref, vt_s, bias_s, vcol_s):
    row = pl.program_id(0)
    seq = x_ref.shape[1]
    same = ids(len_ref, row, (seq, seq), 0) == ids(len_ref, row, (seq, seq), 1)
    bias_s[...] = jnp.where(same, 0.0, -1e30)
    vcol_s[...] = jnp.concatenate([vec_ref[0:8, :]] * 1, axis=0).T
    for g in range(4):
        lo = window(g)
        xw = x_ref[0, :, lo : lo + 256]
        off = 64 * (g % 2)
        r = pl.ds(192 * g, 192)
        q = nt(w_ref[0, g, off : off + 192, :], xw) + vcol_s[192 * g : 192 * g + 192, 4:5]
        qt_ref[0, r, :] = q.astype(BF16) * BF16(0.125)
        kt_ref[0, r, :] = nt(w_ref[1, g, off : off + 192, :], xw).astype(BF16)
        v = nt(w_ref[2, g, off : off + 192, :], xw) + vcol_s[192 * g : 192 * g + 192, 5:6]
        vt_s[r, :] = v.astype(BF16)
    k_ref[0] = join([nt(x_ref[0, :, window(g) : window(g) + 256], w_ref[1, g]) for g in range(4)]).astype(BF16)
    v_ref[0] = (join([nt(x_ref[0, :, window(g) : window(g) + 256], w_ref[2, g]) for g in range(4)]) + vec_ref[5:6, :]).astype(BF16)

    def pair(j, carry):
        base = pl.multiple_of(j * 128, 128)
        kp = k_ref[0, :, pl.ds(base, 128)]
        for e in range(2):
            mine = pl.multiple_of(base + 64 * e, 64)
            qh = qt_ref[0, pl.ds(mine, 64), :]
            z = jnp.zeros_like(qh)
            qz = jnp.concatenate([qh, z] if e == 0 else [z, qh], axis=0)
            s = nn(kp, qz) + bias_s[...]
            m = jnp.max(s, axis=0, keepdims=True)
            p = jnp.exp(s - m)
            tot = jnp.sum(p, axis=0, keepdims=True)
            c = nn(vt_s[pl.ds(mine, 64), :], p.astype(BF16))
            ct_ref[0, pl.ds(mine, 64), :] = (c * (1.0 / tot)).astype(BF16)
            lse_ref[0, pl.ds(2 * j + e, 1), :] = m + jnp.log(tot)
        return carry

    lax.fori_loop(0, 6, pair, 0)


def attn_fwd(tokens, lengths, wq, vec):
    n, seq, d = tokens.shape
    act = lambda a, b: pl.BlockSpec((1, a, b), lambda i: (i, 0, 0))
    return pl.pallas_call(
        attn_fwd_kernel,
        grid=(n,),
        out_shape=[
            jax.ShapeDtypeStruct((n, d, seq), BF16),
            jax.ShapeDtypeStruct((n, seq, d), BF16),
            jax.ShapeDtypeStruct((n, d, seq), BF16),
            jax.ShapeDtypeStruct((n, seq, d), BF16),
            jax.ShapeDtypeStruct((n, d, seq), BF16),
            jax.ShapeDtypeStruct((n, 16, seq), F32),
        ],
        in_specs=[
            pl.BlockSpec(memory_space=pltpu.SMEM),
            act(seq, d),
            pl.BlockSpec((3, 4, 256, 256), lambda i: (0, 0, 0, 0)),
            pl.BlockSpec((12, d), lambda i: (0, 0)),
        ],
        out_specs=[act(d, seq), act(seq, d), act(d, seq), act(seq, d), act(d, seq), act(16, seq)],
        scratch_shapes=[pltpu.VMEM((d, seq), BF16), pltpu.VMEM((seq, seq), F32), pltpu.VMEM((d, 8), F32)],
        compiler_params=pltpu.CompilerParams(vmem_limit_bytes=56 * 2**20),
    )(lengths, tokens, wq, vec)


def gelu_parts(v):
    u = jnp.abs(v) * 0.7071067811865476
    den = 1.0 + 0.3275911 * u
    t = pl.reciprocal(den, approx=True)
    t = t * (2.0 - den * t)
    ex = jnp.exp(-u * u)
    poly = t * (0.254829592 + t * (-0.284496736 + t * (1.421413741 + t * (-1.453152027 + t * 1.061405429))))
    half = 0.5 * poly * ex
    cdf = jnp.where(v >= 0, 1.0 - half, half)
    return v * cdf, cdf + v * ex * 0.3989422804014327


def norm(h):
    mu = jnp.mean(h, axis=-1, keepdims=True)
    c = h - mu
    inv = lax.rsqrt(jnp.mean(c * c, axis=-1, keepdims=True) + NORM_EPS)
    return c * inv, inv


def norm_back(up, n, inv, gain):
    w = up * gain
    return inv * (w - jnp.mean(w, axis=-1, keepdims=True) - n * jnp.mean(w * n, axis=-1, keepdims=True))


def col_sum(v):
    return jnp.sum(v, axis=0, keepdims=True)


def ffn_kernel(x_ref, cot_ref, ct_ref, w1_ref, w2_ref, wo_ref, vec_ref, out_ref, res_ref, dct_ref, g1_ref, g2_ref, go_ref, gv_ref,
               fl_s, act_s, slope_s, db_s):
    step = pl.program_id(0)
    T = x_ref.shape[1]
    vec = lambda i: vec_ref[i : i + 1, :]
    x = x_ref[0].astype(F32)
    ctx = ct_ref[0].T
    h1 = x + (nn(ctx, wo_ref[...]) + vec(6))
    n1, inv1 = norm(h1)
    first = n1 * vec(0) + vec(1)
    fl_s[...] = first.astype(BF16)
    branch = []
    for g in range(4):
        lo = window(g)
        inner = nn(fl_s[:, lo : lo + 256], w1_ref[g]) + vec(8 + g)
        a, sl = gelu_parts(inner)
        act_s[g] = a.astype(BF16)
        slope_s[g] = sl
        branch.append(nt(act_s[g], w2_ref[g]))
    h2 = first + (join(branch) + vec(7))
    n2, inv2 = norm(h2)
    out_ref[0] = (n2 * vec(2) + vec(3)).astype(BF16)
    dy = cot_ref[0].astype(F32)
    dh2 = norm_back(dy, n2, inv2, vec(2))
    dbl = dh2.astype(BF16)
    db_s[...] = dbl
    dbt = dbl.T
    flt = fl_s[...].T
    ones = jnp.ones((16, T), BF16)
    dfirst = []
    gb = []

    @pl.when(step == 0)
    def _():
        g1_ref[...] = jnp.zeros_like(g1_ref)
        g2_ref[...] = jnp.zeros_like(g2_ref)
        go_ref[...] = jnp.zeros_like(go_ref)
        gv_ref[...] = jnp.zeros_like(gv_ref)

    for g in range(4):
        lo = window(g)
        da = nn(db_s[:, lo : lo + 256], w2_ref[g])
        di = (da * slope_s[g]).astype(BF16)
        dfirst.append(nt(di, w1_ref[g]))
        g2_ref[g] += nn(dbt[192 * g : 192 * g + 192, :], act_s[g])
        ext = nn(jnp.concatenate([flt[192 * g : 192 * g + 192, :], ones], axis=0), di)
        g1_ref[g] += ext[:192]
        gb.append(ext[192:193])
    df = dh2 + join(dfirst)
    dh1 = norm_back(df, n1, inv1, vec(0))
    res_ref[0] = dh1
    dat = dh1.astype(BF16)
    go_ref[...] += nn(ct_ref[0], dat)
    dct_ref[0] = nt(wo_ref[...], dat).astype(BF16)
    z = jnp.zeros((1, x.shape[1]), F32)
    gv_ref[...] += jnp.concatenate(
        [col_sum(df * n1), col_sum(df), col_sum(dy * n2), col_sum(dy), z, z, col_sum(dat.astype(F32)), col_sum(dbl.astype(F32))] + gb, axis=0)


def ffn(tokens, cot, ct, w1, w2, wo, vec):
    n, seq, d = tokens.shape
    T = seq
    act = pl.BlockSpec((1, T, d), lambda i: (i, 0, 0))
    actt = pl.BlockSpec((1, d, T), lambda i: (i, 0, 0))
    full = lambda *s: pl.BlockSpec(s, lambda i: (0,) * len(s))
    return pl.pallas_call(
        ffn_kernel,
        grid=(n,),
        out_shape=[
            jax.ShapeDtypeStruct((n, seq, d), BF16),
            jax.ShapeDtypeStruct((n, seq, d), F32),
            jax.ShapeDtypeStruct((n, d, seq), BF16),
            jax.ShapeDtypeStruct((4, 192, 768), F32),
            jax.ShapeDtypeStruct((4, 192, 768), F32),
            jax.ShapeDtypeStruct((768, 768), F32),
            jax.ShapeDtypeStruct((12, 768), F32),
        ],
        in_specs=[act, act, actt, full(4, 256, 768), full(4, 256, 768), full(768, 768), full(12, 768)],
        out_specs=[act, act, actt, full(4, 192, 768), full(4, 192, 768), full(768, 768), full(12, 768)],
        scratch_shapes=[pltpu.VMEM((T, d), BF16), pltpu.VMEM((4, T, 768), BF16), pltpu.VMEM((4, T, 768), F32), pltpu.VMEM((T, d), BF16)],
        compiler_params=pltpu.CompilerParams(vmem_limit_bytes=60 * 2**20),
    )(tokens, cot, ct, w1, w2, wo, vec)


def attn_bwd_kernel(len_ref, x_ref, wt_ref, qt_ref, k_ref, kt_ref, v_ref, ct_ref, lse_ref, dct_ref, res_ref, gt_ref, gq_ref, gv_ref,
                    bias_s, dq_s, dk_s, dv_s):
    row = pl.program_id(0)
    seq = x_ref.shape[1]
    same = ids(len_ref, row, (seq, seq), 0) == ids(len_ref, row, (seq, seq), 1)
    bias_s[...] = jnp.where(same, 0.0, -1e30)

    def pair(j, carry):
        base = pl.multiple_of(j * 128, 128)
        kp = k_ref[0, :, pl.ds(base, 128)]
        vp = v_ref[0, :, pl.ds(base, 128)]
        for e in range(2):
            mine = pl.multiple_of(base + 64 * e, 64)
            at = pl.ds(mine, 64)
            qh = qt_ref[0, at, :]
            dc = dct_ref[0, at, :]
            z = jnp.zeros_like(qh)
            wide = lambda a: jnp.concatenate([a, z] if e == 0 else [z, a], axis=0)
            delta = jnp.sum(dc.astype(F32) * ct_ref[0, at, :].astype(F32), axis=0, keepdims=True)
            s = nn(kp, wide(qh)) + bias_s[...]
            p = jnp.exp(s - lse_ref[0, pl.ds(2 * j + e, 1), :])
            dp = nn(vp, wide(dc))
            ds = (p * (dp - delta)).astype(BF16)
            dv_s[at, :] = nt(dc, p.astype(BF16)).astype(BF16)
            dk_s[at, :] = nt(qh, ds).astype(BF16)
            dq_s[at, :] = (nn(kt_ref[0, at, :], ds) * 0.125).astype(BF16)
        return carry

    lax.fori_loop(0, 6, pair, 0)

    @pl.when(row == 0)
    def _():
        gq_ref[...] = jnp.zeros_like(gq_ref)
        gv_ref[...] = jnp.zeros_like(gv_ref)

    lane = lax.broadcasted_iota(jnp.int32, (192, 256), 1)
    dx = []
    for g in range(4):
        lo = window(g)
        r = slice(192 * g, 192 * g + 192)
        xw = x_ref[0, :, lo : lo + 256]
        cat = jnp.concatenate([dq_s[r, :], dk_s[r, :], dv_s[r, :]], axis=0)
        dx.append(nn(wt_ref[g], cat))
        gq = nn(cat, xw)
        keep = (lane < 192) if g % 2 == 0 else (lane >= 64)
        for c in range(3):
            part = jnp.where(keep, gq[192 * c : 192 * c + 192], 0.0)
            gq_ref[c, :, lo : lo + 256] += part
    gt_ref[0] = (res_ref[0] + jnp.concatenate(dx, axis=0).T).astype(BF16)
    ones = jnp.ones((16, seq), BF16)
    gv_ref[...] += jnp.concatenate([nt(ones, dq_s[...])[0:1], nt(ones, dv_s[...])[0:1]], axis=0)


def attn_bwd(lengths, tokens, wt, qt, k, kt, v, ct, lse, dct, res):
    n, seq, d = tokens.shape
    act = lambda a, b: pl.BlockSpec((1, a, b), lambda i: (i, 0, 0))
    full = lambda *s: pl.BlockSpec(s, lambda i: (0,) * len(s))
    return pl.pallas_call(
        attn_bwd_kernel,
        grid=(n,),
        out_shape=[
            jax.ShapeDtypeStruct((n, seq, d), BF16),
            jax.ShapeDtypeStruct((3, 192, 768), F32),
            jax.ShapeDtypeStruct((2, 768), F32),
        ],
        in_specs=[
            pl.BlockSpec(memory_space=pltpu.SMEM),
            act(seq, d), full(4, 192, 576), act(d, seq), act(seq, d), act(d, seq), act(seq, d), act(d, seq), act(16, seq), act(d, seq), act(seq, d),
        ],
        out_specs=[act(seq, d), full(3, 192, 768), full(2, 768)],
        scratch_shapes=[pltpu.VMEM((seq, seq), F32), pltpu.VMEM((d, seq), BF16), pltpu.VMEM((d, seq), BF16), pltpu.VMEM((d, seq), BF16)],
        compiler_params=pltpu.CompilerParams(vmem_limit_bytes=60 * 2**20),
    )(lengths, tokens, wt, qt, k, kt, v, ct, lse, dct, res)


class Place:
    def __init__(self, dp, narrow):
        self.X = 2 if dp % 2 == 0 else 1
        self.C = 2 if narrow % 2 == 0 else 1
        self.Z, self.Y = dp // self.X, narrow // self.C

    def locate(self):
        d, n = lax.axis_index("dp"), lax.axis_index("narrow")
        self.z, self.x = d // self.X, lax.rem(d, self.X)
        self.y, self.c = n // self.C, lax.rem(n, self.C)

    def count(self):
        return self.Z + self.X + self.Y + self.C - 4

    def at(self, axis, j):
        return lax.rem(getattr(self, axis) + j, getattr(self, axis.upper()))

    def device(self, axis, j):
        where = {a: getattr(self, a) for a in "zxyc"}
        where[axis] = self.at(axis, j)
        return (where["z"] * self.X + where["x"], where["y"] * self.C + where["c"])

    def barrier(self):
        sem = pltpu.get_barrier_semaphore()
        for axis in "zxyc":
            for j in range(1, getattr(self, axis.upper())):
                pl.semaphore_signal(sem, inc=1, device_id=self.device(axis, j), device_id_type=MESH)
        pl.semaphore_wait(sem, self.count())


class Wires:
    def __init__(self, place, send_sem, recv_sem):
        self.place, self.send_sem, self.recv_sem, self.used = place, send_sem, recv_sem, []

    def send(self, src, dst, axis, j):
        k = len(self.used)
        copy = pltpu.make_async_remote_copy(
            src_ref=src,
            dst_ref=dst,
            send_sem=self.send_sem.at[k],
            recv_sem=self.recv_sem.at[k],
            device_id=self.place.device(axis, j),
            device_id_type=MESH,
        )
        copy.start()
        self.used.append(copy)
        return copy

    def finish(self):
        for copy in self.used:
            copy.wait_send()


def gather_copies(p):
    return (p.Z - 1) + p.Z * ((p.X - 1) + (p.Y - 1) + 2 * (p.X - 1) * (p.Y - 1) + (p.C - 1))


def gather_steps(p, wires, buf, half):
    z, x, y, c = p.z, p.x, p.y, p.c
    along = {}
    for j in range(1, p.Z):
        along[j] = wires.send(buf.at[z, c, x, y], buf.at[z, c, x, y], "z", j)
    first, second, last = {}, {}, {}
    for k in range(p.Z + 2):
        if k < p.Z:
            zs = p.at("z", p.Z - k) if k else z
            if k:
                along[k].wait_recv()
            mine = buf.at[zs, c, x, y]
            first[k] = [("x", j, wires.send(mine, mine, "x", j)) for j in range(1, p.X)]
            first[k] += [("y", j, wires.send(mine, mine, "y", j)) for j in range(1, p.Y)]
            yield
        if 1 <= k <= p.Z:
            i = k - 1
            zs = p.at("z", p.Z - i) if i else z
            second[i] = []
            for axis, j, copy in first[i]:
                copy.wait_recv()
                if axis == "x":
                    part = buf.at[zs, c, p.at("x", p.X - j), y, pl.ds(0, half)]
                    second[i] += [wires.send(part, part, "y", q) for q in range(1, p.Y)]
                else:
                    part = buf.at[zs, c, x, p.at("y", p.Y - j), pl.ds(half, buf.shape[4] - half)]
                    second[i] += [wires.send(part, part, "x", q) for q in range(1, p.X)]
            yield
        if k >= 2:
            i = k - 2
            zs = p.at("z", p.Z - i) if i else z
            for copy in second[i]:
                copy.wait_recv()
            last[i] = [wires.send(buf.at[zs, c], buf.at[zs, c], "c", j) for j in range(1, p.C)]
            yield
    for i in last:
        for copy in last[i]:
            copy.wait_recv()
    yield


def gather_kernel(p, half, src_ref, out_ref, buf, send_sem, recv_sem, own_sem):
    p.locate()
    own = pltpu.make_async_copy(src_ref, buf.at[p.z, p.c, p.x, p.y], own_sem)
    own.start()
    own.wait()
    p.barrier()
    wires = Wires(p, send_sem, recv_sem)
    for _ in gather_steps(p, wires, buf, half):
        pass
    wires.finish()
    out_ref[...] = buf[...]


def gather(p, block, ident):
    rows = block.shape[0]
    full = (p.Z, p.C, p.X, p.Y, rows, 128)
    n = gather_copies(p)
    return pl.pallas_call(
        functools.partial(gather_kernel, p, rows // 32 * 16),
        out_shape=jax.ShapeDtypeStruct(full, BF16),
        in_specs=[VMEM],
        out_specs=VMEM,
        scratch_shapes=[
            pltpu.VMEM(full, BF16),
            pltpu.SemaphoreType.DMA((n,)),
            pltpu.SemaphoreType.DMA((n,)),
            pltpu.SemaphoreType.DMA,
        ],
        compiler_params=pltpu.CompilerParams(collective_id=ident, has_side_effects=True, vmem_limit_bytes=48 * 2**20),
    )(block)


class Shares:
    def __init__(self, p, rows):
        cells = p.X * p.Y * p.Z
        unit = 16 * cells * p.C
        units = -(-rows // unit)
        self.a, self.b = 16 * ((units + 1) // 2), 16 * max(units // 2, 1)
        self.per_core = cells * (self.a + self.b)
        self.rows = p.C * self.per_core
        self.cells = cells
        self.copies = 2 * ((p.C - 1) + 2 * ((p.X - 1) + (p.Y - 1)) + 2 * (p.Z - 1))

    def scratch(self, p):
        a, b = self.a, self.b
        kinds = [
            (self.per_core,),
            (p.C - 1, self.per_core),
            (p.X - 1, p.Y * p.Z * a),
            (p.Y - 1, p.X * p.Z * b),
            (p.Y - 1, p.Z * a),
            (p.X - 1, p.Z * b),
            (p.Z - 1, a),
            (p.Z - 1, b),
        ]
        return [pltpu.VMEM(k + (128,), BF16) for k in kinds] + [pltpu.SemaphoreType.DMA((self.copies,))] * 2


def spread(start, size):
    return pl.ds(pl.multiple_of(start, 16), size)


def add_into(dst, at, parts):
    total = dst[at, :].astype(F32)
    for part in parts:
        total = total + part.astype(F32)
    dst[at, :] = total.astype(BF16)


def sum_steps(p, s, src, out, scratch):
    held, from_c, a1, b1, a2, b2, a3, b3, send_sem, recv_sem = scratch
    wires = Wires(p, send_sem, recv_sem)
    a, b, per = s.a, s.b, s.per_core
    ax, by = p.Y * p.Z * a, p.X * p.Z * b
    in_a = lambda x, y=None, z=None: (x * p.Y + (0 if y is None else y)) * p.Z * a + (0 if z is None else z * a)
    in_b = lambda y, x=None, z=None: s.cells * a + (y * p.X + (0 if x is None else x)) * p.Z * b + (0 if z is None else z * b)
    x, y, z, c = p.x, p.y, p.z, p.c
    copies = [wires.send(src.at[spread(p.at("c", j) * per, per)], from_c.at[j - 1], "c", j) for j in range(1, p.C)]
    yield
    for copy in copies:
        copy.wait_recv()
    total = src[spread(c * per, per), :].astype(F32)
    for j in range(p.C - 1):
        total = total + from_c[j].astype(F32)
    held[...] = total.astype(BF16)
    copies = [wires.send(held.at[spread(in_a(p.at("x", j)), ax)], a1.at[j - 1], "x", j) for j in range(1, p.X)]
    copies += [wires.send(held.at[spread(in_b(p.at("y", j)), by)], b1.at[j - 1], "y", j) for j in range(1, p.Y)]
    yield
    for copy in copies:
        copy.wait_recv()
    add_into(held, spread(in_a(x), ax), [a1[j] for j in range(p.X - 1)])
    add_into(held, spread(in_b(y), by), [b1[j] for j in range(p.Y - 1)])
    copies = [wires.send(held.at[spread(in_a(x, p.at("y", j)), p.Z * a)], a2.at[j - 1], "y", j) for j in range(1, p.Y)]
    copies += [wires.send(held.at[spread(in_b(y, p.at("x", j)), p.Z * b)], b2.at[j - 1], "x", j) for j in range(1, p.X)]
    yield
    for copy in copies:
        copy.wait_recv()
    add_into(held, spread(in_a(x, y), p.Z * a), [a2[j] for j in range(p.Y - 1)])
    add_into(held, spread(in_b(y, x), p.Z * b), [b2[j] for j in range(p.X - 1)])
    copies = []
    for j in range(1, p.Z):
        copies.append(wires.send(held.at[spread(in_a(x, y, p.at("z", j)), a)], a3.at[j - 1], "z", j))
        copies.append(wires.send(held.at[spread(in_b(y, x, p.at("z", j)), b)], b3.at[j - 1], "z", j))
    yield
    for copy in copies:
        copy.wait_recv()
    base = c * per
    for at, size, parts in ((in_a(x, y, z), a, a3), (in_b(y, x, z), b, b3)):
        total = held[spread(at, size), :].astype(F32)
        for j in range(p.Z - 1):
            total = total + parts[j].astype(F32)
        out[spread(base + at, size), :] = total.astype(BF16)
    copies = []
    for j in range(1, p.Z):
        for at, size in ((in_a(x, y, z), a), (in_b(y, x, z), b)):
            part = out.at[spread(base + at, size)]
            copies.append(wires.send(part, part, "z", j))
    yield
    for copy in copies:
        copy.wait_recv()
    part_a = out.at[spread(base + in_a(x, y), p.Z * a)]
    part_b = out.at[spread(base + in_b(y, x), p.Z * b)]
    copies = [wires.send(part_a, part_a, "y", j) for j in range(1, p.Y)]
    copies += [wires.send(part_b, part_b, "x", j) for j in range(1, p.X)]
    yield
    for copy in copies:
        copy.wait_recv()
    part_a = out.at[spread(base + in_a(x), ax)]
    part_b = out.at[spread(base + in_b(y), by)]
    copies = [wires.send(part_a, part_a, "x", j) for j in range(1, p.X)]
    copies += [wires.send(part_b, part_b, "y", j) for j in range(1, p.Y)]
    yield
    for copy in copies:
        copy.wait_recv()
    part = out.at[spread(base, per)]
    copies = [wires.send(part, part, "c", j) for j in range(1, p.C)]
    yield
    for copy in copies:
        copy.wait_recv()
    wires.finish()
    yield


def run_all(steps):
    steps = list(steps)
    while steps:
        steps = [s for s in steps if next(s, "end") != "end"]


def hot(shape, row_at, col_at):
    rows = lax.broadcasted_iota(jnp.int32, shape, 0) + row_at
    cols = lax.broadcasted_iota(jnp.int32, shape, 1) + col_at
    return (rows == cols).astype(BF16)


def blocks_of(value):
    return jnp.concatenate([value[:, 128 * j : 128 * j + 128] for j in range(value.shape[1] // 128)], axis=0)


def sum_kernel(p, shares, dims, go_ref, g1_ref, g2_ref, gq_ref, gv_ref, gv2_ref, mq_ref, mo_ref, m1_ref, m2_ref,
               oo_ref, o1_ref, o2_ref, oq_ref, *scratch):
    p.locate()
    srcs, rest = scratch[:4], scratch[4:]
    d, n = lax.axis_index("dp"), lax.axis_index("narrow")
    wide = m1_ref.shape[1]
    cols = m1_ref.shape[2]
    sel_l = hot((wide, 768), n * wide, 0)
    sel_s = hot((192, cols), 0, d * cols)
    outs = (oo_ref, o1_ref, o2_ref, oq_ref)

    def put(dst, base, value):
        for j in range(value.shape[1] // 128):
            dst[base + 192 * j : base + 192 * j + 192, :] = value[:, 128 * j : 128 * j + 128].astype(BF16)

    big = mo_ref.shape[2]
    placed = nt(hot((768, big), 0, d * big), (0.95 * mo_ref[0]).astype(BF16)).astype(BF16)
    value = go_ref[...] + nn(placed, sel_l)
    for q in range(4):
        put(srcs[0], 1152 * q, value[192 * q : 192 * q + 192])
    for dst, g_ref, m_ref in ((srcs[1], g1_ref, m1_ref), (srcs[2], g2_ref, m2_ref)):
        for g in range(4):
            placed = nt(sel_s, (0.95 * m_ref[g]).astype(BF16)).astype(BF16)
            put(dst, 1152 * g, g_ref[g] + nn(placed, sel_l))
    tall, slim = mq_ref.shape[1:]
    up = hot((192, tall), 0, n * tall)
    for c in range(3):
        held = jnp.zeros((tall, 768), F32)
        for g in range(4):
            held = held + nn((0.95 * mq_ref[4 * c + g]).astype(BF16), hot((slim, 768), 192 * g + d * slim, 0))
        put(srcs[3], 1152 * c, gq_ref[c] + nn(up, held.astype(BF16)))
    gv = jnp.concatenate([gv_ref[0:4], gv2_ref[...], gv_ref[6:12]], axis=0)
    tail = srcs[3].shape[0] - 3456
    flat = jnp.concatenate([gv[:, 128 * j : 128 * j + 128] for j in range(6)] + [jnp.zeros((tail - 72, 128), F32)], axis=0)
    srcs[3][3456:, :] = flat.astype(BF16)
    for k in range(3):
        if srcs[k].shape[0] > 4608:
            srcs[k][4608:, :] = jnp.zeros((srcs[k].shape[0] - 4608, 128), BF16)
    p.barrier()
    run_all(sum_steps(p, s, srcs[k], outs[k], rest[10 * k : 10 * k + 10]) for k, s in enumerate(shares))


def sum_all(p, go, g1, g2, gq, gv, gv2, mq, mo, m1, m2, ident):
    shares = [Shares(p, r) for r in (4608, 4608, 4608, 3456 + 72)]
    scratch = [pltpu.VMEM((s.rows, 128), BF16) for s in shares]
    for s in shares:
        scratch += s.scratch(p)
    return pl.pallas_call(
        functools.partial(sum_kernel, p, shares, None),
        out_shape=[jax.ShapeDtypeStruct((s.rows, 128), BF16) for s in shares],
        in_specs=[VMEM] * 10,
        out_specs=[VMEM] * 4,
        scratch_shapes=scratch,
        compiler_params=pltpu.CompilerParams(collective_id=ident, has_side_effects=True, vmem_limit_bytes=60 * 2**20),
    )(go, g1, g2, gq, gv, gv2, mq, mo, m1, m2)


def newton(y):
    factor = 1.0 / (jnp.sqrt(jnp.sum(y * y)) + 1e-07)
    y = y * factor
    for _ in range(NS_STEPS):
        low = y.astype(BF16)
        gram = nt(low, low)
        gl = gram.astype(BF16)
        poly = ns_second * gram + ns_third * nn(gl, gl)
        y = ns_first * y + nn(poly.astype(BF16), low)
    return y


def muon_kernel(narrow, dp, oo_ref, o1_ref, o2_ref, oq_ref, wq_ref, wo_ref, w1_ref, w2_ref, vec_ref, vm1_ref, vm2_ref,
                mq_ref, mo_ref, m1_ref, m2_ref, nq_ref, no_ref, n1_ref, n2_ref, f_ref, s_ref, v_ref):
    d, n = lax.axis_index("dp"), lax.axis_index("narrow")
    wide, cols = w1_ref.shape[1:]
    sel_l = hot((wide, 768), n * wide, 0)
    sel_s = hot((cols, 192), d * cols, 0)

    def fresh(w, own, longest):
        return w - muon_rate * (0.2 * math.sqrt(longest) * own + muon_decay * w)

    def wide_rows(ref, base, count):
        return jnp.concatenate(
            [jnp.concatenate([ref[base + 1152 * q + 192 * j : base + 1152 * q + 192 * j + 192, :] for j in range(6)], axis=1) for q in range(count)],
            axis=0)

    for ref, m_ref, w_ref, n_ref in ((o1_ref, m1_ref, w1_ref, n1_ref), (o2_ref, m2_ref, w2_ref, n2_ref)):
        for g in range(4):
            low = wide_rows(ref, 1152 * g, 1)
            pick = lambda t: nt(sel_l, nn(sel_s, t).astype(BF16))
            m_ref[g] = pick(low)
            y = newton(low.astype(F32))
            n_ref[g] = fresh(w_ref[g], pick(y.astype(BF16)), 768)
    for c in range(3):
        rows = wide_rows(oq_ref, 1152 * c, 1)
        tall, slim = wq_ref.shape[1:]
        sel_o = hot((tall, 192), n * tall, 0)
        lane = lax.broadcasted_iota(jnp.int32, (192, 256), 1)
        mine = nn(sel_o, rows).astype(BF16)
        done = []
        for g in range(4):
            keep = (lane < 192) if g % 2 == 0 else (lane >= 64)
            y = newton(jnp.where(keep, rows[:, window(g) : window(g) + 256].astype(F32), 0.0))
            done.append(y)
        own = nn(sel_o, join(done).astype(BF16)).astype(BF16)
        for g in range(4):
            sel = hot((768, slim), 0, 192 * g + d * slim)
            mq_ref[4 * c + g] = nn(mine, sel)
            nq_ref[4 * c + g] = fresh(wq_ref[4 * c + g], nn(own, sel), 192)
    big = wo_ref.shape[2]
    sel_b = hot((big, 768), d * big, 0)
    low = wide_rows(oo_ref, 0, 4)
    pick = lambda t: nt(sel_l, nn(sel_b, t).astype(BF16))
    mo_ref[0] = pick(low)
    no_ref[0] = fresh(wo_ref[0], pick(newton(low.astype(F32)).astype(BF16)), 768)
    tail = oq_ref[3456 : 3456 + 72, :].astype(F32)
    grad = jnp.concatenate([tail[12 * j : 12 * j + 12] for j in range(6)], axis=1)
    first = 0.9 * vm1_ref[...] + 0.1 * grad
    second = 0.999 * vm2_ref[...] + 0.001 * grad * grad
    f_ref[...] = first
    s_ref[...] = second
    v_ref[...] = vec_ref[...] - adam_rate * (first * (1.0 / (1.0 - 0.9**STEP))) / (jnp.sqrt(second * (1.0 / (1.0 - 0.999**STEP))) + 1e-08)


def muon(dp, narrow, sums, weights, vectors, vm1, vm2):
    shape = lambda a: jax.ShapeDtypeStruct(a.shape, F32)
    outs = [shape(w) for w in weights] * 2 + [shape(vectors)] * 3
    return pl.pallas_call(
        functools.partial(muon_kernel, narrow, dp),
        out_shape=outs,
        in_specs=[VMEM] * 11,
        out_specs=[VMEM] * 11,
        compiler_params=pltpu.CompilerParams(vmem_limit_bytes=60 * 2**20),
    )(*sums, *weights, vectors, vm1, vm2)


def pack(weights):
    flat = jnp.concatenate([w.astype(BF16).reshape(-1) for w in weights])
    rows = -(-flat.shape[0] // 128)
    rows = -(-rows // 32) * 32
    return jnp.pad(flat, (0, rows * 128 - flat.shape[0])).reshape(rows, 128)


def unpack(p, full, weights):
    flat = full.reshape(p.Z, p.C, p.X, p.Y, -1)
    at = 0
    out = []
    for w in weights:
        m, r, s = w.shape
        part = flat[..., at : at + m * r * s].reshape(p.Z, p.C, p.X, p.Y, m, r, s)
        at += m * r * s
        out.append(part.transpose(4, 0, 2, 6, 3, 1, 5).reshape(m, p.Z * p.X * s, p.Y * p.C * r))
    return out


def local(tokens, doc_lengths, cotangent, qkv_weight, out_weight, ffn_in_weight, ffn_out_weight, vectors,
          qkv_moment, out_moment, ffn_in_moment, ffn_out_moment, vec_moment1, vec_moment2):
    dp, narrow = lax.axis_size("dp"), lax.axis_size("narrow")
    p = Place(dp, narrow)
    weights = (qkv_weight, out_weight, ffn_in_weight, ffn_out_weight)
    qt_full, ot_full, w1t, w2t = unpack(p, gather(p, pack(weights), 0), weights)
    pad = lambda w: jnp.stack([jnp.pad(w[g], ((64 * (g % 2), 64 - 64 * (g % 2)), (0, 0))) for g in range(4)])
    w1p, w2p = pad(w1t), pad(w2t)
    qn = qt_full.transpose(0, 2, 1).reshape(3, 4, 192, 192)
    wqp = jnp.stack([jnp.pad(qn[:, g], ((0, 0),) + ((64 * (g % 2), 64 - 64 * (g % 2)),) * 2) for g in range(4)], axis=1)
    wqt = qt_full.reshape(3, 4, 192, 192).transpose(1, 2, 0, 3).reshape(4, 192, 576)
    qt, k, kt, v, ct, lse = attn_fwd(tokens, doc_lengths, wqp, vectors)
    out_act, res, dct, g1, g2, go, gv = ffn(tokens, cotangent, ct, w1p, w2p, ot_full[0], vectors)
    grad_tokens, gq, gv2 = attn_bwd(doc_lengths, tokens, wqt, qt, k, kt, v, ct, lse, dct, res)
    sums = sum_all(p, go, g1, g2, gq, gv, gv2, qkv_moment, out_moment, ffn_in_moment, ffn_out_moment, 1)
    tail = muon(dp, narrow, sums, weights, vectors, vec_moment1, vec_moment2)
    return (out_act, grad_tokens) + tuple(tail)


def solution(mesh):
    rows = P(("dp", "narrow"), None, None)
    cut = P(None, "narrow", "dp")
    return jax.shard_map(
        local,
        mesh=mesh,
        in_specs=(rows, P(("dp", "narrow"), None), rows) + (cut,) * 4 + (P(),) + (cut,) * 4 + (P(), P()),
        out_specs=(rows, rows) + (cut,) * 8 + (P(),) * 3,
        check_vma=False,
    )
```

```python
import functools
import math

import jax
import jax.numpy as jnp
from jax import lax
from jax.experimental import pallas as pl
from jax.experimental.pallas import tpu as pltpu
from jax.sharding import PartitionSpec as P

F32, BF16 = jnp.float32, jnp.bfloat16
MESH = pl.DeviceIdType.MESH
NORM_EPS = 1e-05
NS_STEPS = 5
STEP = 5
ns_first = 3.4445
ns_second = -4.775
ns_third = 2.0315
muon_rate = 0.5
muon_decay = 0.01
adam_rate = 0.4
VMEM = pl.BlockSpec(memory_space=pltpu.VMEM)


def nn(a, b):
    return lax.dot_general(a, b, (((1,), (0,)), ((), ())), preferred_element_type=F32)


def nt(a, b):
    return lax.dot_general(a, b, (((1,), (1,)), ((), ())), preferred_element_type=F32)


def tn(a, b):
    return lax.dot_general(a, b, (((0,), (0,)), ((), ())), preferred_element_type=F32)


def window(g):
    return 128 * (3 * (g // 2) + g % 2)


def join(parts):
    out = []
    for p in range(2):
        a, b = parts[2 * p], parts[2 * p + 1]
        out += [a[:, :128], a[:, 128:] + b[:, :128], b[:, 128:]]
    return jnp.concatenate(out, axis=1)


def ids(len_ref, row, shape, dim):
    pos = lax.broadcasted_iota(jnp.int32, shape, dim)
    out = jnp.zeros(shape, jnp.int32)
    end = jnp.int32(0)
    for j in range(4):
        end = end + len_ref[row, j]
        out = out + (pos >= end).astype(jnp.int32)
    return out


def hot(shape, row_at, col_at):
    rows = lax.broadcasted_iota(jnp.int32, shape, 0) + row_at
    cols = lax.broadcasted_iota(jnp.int32, shape, 1) + col_at
    return (rows == cols).astype(BF16)


def put_blocks(dst, base, value):
    for j in range(value.shape[1] // 128):
        dst[base + 192 * j : base + 192 * j + 192, :] = value[:, 128 * j : 128 * j + 128].astype(BF16)


def wide_rows(ref, base, count):
    parts = []
    for q in range(count):
        at = base + 1152 * q
        parts.append(jnp.concatenate([ref[at + 192 * j : at + 192 * j + 192, :] for j in range(6)], axis=1))
    return parts[0] if count == 1 else jnp.concatenate(parts, axis=0)


def gelu_parts(v):
    u = jnp.abs(v) * 0.7071067811865476
    den = 1.0 + 0.3275911 * u
    t = pl.reciprocal(den, approx=True)
    t = t * (2.0 - den * t)
    ex = jnp.exp(-u * u)
    poly = t * (0.254829592 + t * (-0.284496736 + t * (1.421413741 + t * (-1.453152027 + t * 1.061405429))))
    half = 0.5 * poly * ex
    cdf = jnp.where(v >= 0, 1.0 - half, half)
    return v * cdf, cdf + v * ex * 0.3989422804014327


def norm(h):
    mu = jnp.mean(h, axis=-1, keepdims=True)
    c = h - mu
    inv = lax.rsqrt(jnp.mean(c * c, axis=-1, keepdims=True) + NORM_EPS)
    return c * inv, inv


def norm_back(up, n, inv, gain):
    w = up * gain
    return inv * (w - jnp.mean(w, axis=-1, keepdims=True) - n * jnp.mean(w * n, axis=-1, keepdims=True))


def col_sum(v):
    return jnp.sum(v, axis=0, keepdims=True)


def ffn_kernel(x_ref, cot_ref, ct_ref, w1_ref, w2_ref, wo_ref, vec_ref, mo_ref, m1_ref, m2_ref,
               out_ref, res_ref, dct_ref, so_ref, s1_ref, s2_ref, gv_ref,
               fl_s, act_s, slope_s, db_s, g1_ref, g2_ref, go_ref):
    step = pl.program_id(0)
    T = x_ref.shape[1]
    vec = lambda i: vec_ref[i : i + 1, :]
    x = x_ref[0].astype(F32)
    ctx = ct_ref[0].T
    h1 = x + (nn(ctx, wo_ref[...]) + vec(6))
    n1, inv1 = norm(h1)
    first = n1 * vec(0) + vec(1)
    fl_s[...] = first.astype(BF16)
    branch = []
    for g in range(4):
        lo = window(g)
        inner = nn(fl_s[:, lo : lo + 256], w1_ref[g]) + vec(8 + g)
        a, sl = gelu_parts(inner)
        act_s[g] = a.astype(BF16)
        slope_s[g] = sl
        branch.append(nt(act_s[g], w2_ref[g]))
    h2 = first + (join(branch) + vec(7))
    n2, inv2 = norm(h2)
    out_ref[0] = (n2 * vec(2) + vec(3)).astype(BF16)
    dy = cot_ref[0].astype(F32)
    dh2 = norm_back(dy, n2, inv2, vec(2))
    dbl = dh2.astype(BF16)
    db_s[...] = dbl
    dbt = dbl.T
    flt = fl_s[...].T
    ones = jnp.ones((16, T), BF16)
    dfirst = []
    gb = []

    @pl.when(step == 0)
    def _():
        g1_ref[...] = jnp.zeros_like(g1_ref)
        g2_ref[...] = jnp.zeros_like(g2_ref)
        go_ref[...] = jnp.zeros_like(go_ref)
        gv_ref[...] = jnp.zeros_like(gv_ref)

    for g in range(4):
        lo = window(g)
        da = nn(db_s[:, lo : lo + 256], w2_ref[g])
        di = (da * slope_s[g]).astype(BF16)
        dfirst.append(nt(di, w1_ref[g]))
        g2_ref[g] += nn(dbt[192 * g : 192 * g + 192, :], act_s[g])
        ext = nn(jnp.concatenate([flt[192 * g : 192 * g + 192, :], ones], axis=0), di)
        g1_ref[g] += ext[:192]
        gb.append(ext[192:193])
    df = dh2 + join(dfirst)
    dh1 = norm_back(df, n1, inv1, vec(0))
    res_ref[0] = dh1
    dat = dh1.astype(BF16)
    go_ref[...] += nn(ct_ref[0], dat)
    dct_ref[0] = nt(wo_ref[...], dat).astype(BF16)
    z = jnp.zeros((1, x.shape[1]), F32)
    gv_ref[...] += jnp.concatenate(
        [col_sum(df * n1), col_sum(df), col_sum(dy * n2), col_sum(dy), z, z, col_sum(dat.astype(F32)), col_sum(dbl.astype(F32))] + gb, axis=0)


    @pl.when(step == pl.num_programs(0) - 1)
    def _():
        d, n = lax.axis_index("dp"), lax.axis_index("narrow")
        slim, wide = m1_ref.shape[1:]
        big = mo_ref.shape[2]
        sel_l = hot((wide, 768), n * wide, 0)
        sel_s = hot((192, slim), 0, d * slim)
        placed = nt(hot((768, big), 0, d * big), (0.95 * mo_ref[0]).astype(BF16)).astype(BF16)
        value = go_ref[...] + nn(placed, sel_l)
        for q in range(4):
            put_blocks(so_ref, 1152 * q, value[192 * q : 192 * q + 192])
        for dst, g_ref, m_ref in ((s1_ref, g1_ref, m1_ref), (s2_ref, g2_ref, m2_ref)):
            for g in range(4):
                placed = nn(sel_s, (0.95 * m_ref[g]).astype(BF16)).astype(BF16)
                put_blocks(dst, 1152 * g, g_ref[g] + nn(placed, sel_l))
        for dst in (so_ref, s1_ref, s2_ref):
            if dst.shape[0] > 4608:
                dst[4608:, :] = jnp.zeros((dst.shape[0] - 4608, 128), BF16)


def ffn(tokens, cot, ct, w1, w2, wo, vec, mo, m1, m2, rows):
    n, seq, d = tokens.shape
    T = seq
    act = pl.BlockSpec((1, T, d), lambda i: (i, 0, 0))
    actt = pl.BlockSpec((1, d, T), lambda i: (i, 0, 0))
    full = lambda *s: pl.BlockSpec(s, lambda i: (0,) * len(s))
    return pl.pallas_call(
        ffn_kernel,
        grid=(n,),
        out_shape=[
            jax.ShapeDtypeStruct((n, seq, d), BF16),
            jax.ShapeDtypeStruct((n, seq, d), F32),
            jax.ShapeDtypeStruct((n, d, seq), BF16),
        ]
        + [jax.ShapeDtypeStruct((rows, 128), BF16)] * 3
        + [jax.ShapeDtypeStruct((12, 768), F32)],
        in_specs=[act, act, actt, full(4, 256, 768), full(4, 256, 768), full(768, 768), full(12, 768), full(*mo.shape), full(*m1.shape), full(*m2.shape)],
        out_specs=[act, act, actt] + [full(rows, 128)] * 3 + [full(12, 768)],
        scratch_shapes=[
            pltpu.VMEM((T, d), BF16), pltpu.VMEM((4, T, 768), BF16), pltpu.VMEM((4, T, 768), F32), pltpu.VMEM((T, d), BF16),
            pltpu.VMEM((4, 192, 768), F32), pltpu.VMEM((4, 192, 768), F32), pltpu.VMEM((768, 768), F32),
        ],
        compiler_params=pltpu.CompilerParams(vmem_limit_bytes=60 * 2**20),
    )(tokens, cot, ct, w1, w2, wo, vec, mo, m1, m2)


class Place:
    def __init__(self, dp, narrow):
        self.X = 2 if dp % 2 == 0 else 1
        self.C = 2 if narrow % 2 == 0 else 1
        self.Z, self.Y = dp // self.X, narrow // self.C

    def locate(self):
        d, n = lax.axis_index("dp"), lax.axis_index("narrow")
        self.z, self.x = d // self.X, lax.rem(d, self.X)
        self.y, self.c = n // self.C, lax.rem(n, self.C)

    def count(self):
        return self.Z + self.X + self.Y + self.C - 4

    def at(self, axis, j):
        return lax.rem(getattr(self, axis) + j, getattr(self, axis.upper()))

    def device(self, axis, j):
        where = {a: getattr(self, a) for a in "zxyc"}
        where[axis] = self.at(axis, j)
        return (where["z"] * self.X + where["x"], where["y"] * self.C + where["c"])

    def barrier(self):
        sem = pltpu.get_barrier_semaphore()
        for axis in "zxyc":
            for j in range(1, getattr(self, axis.upper())):
                pl.semaphore_signal(sem, inc=1, device_id=self.device(axis, j), device_id_type=MESH)
        pl.semaphore_wait(sem, self.count())


class Wires:
    def __init__(self, place, send_sem, recv_sem):
        self.place, self.send_sem, self.recv_sem, self.used = place, send_sem, recv_sem, []

    def send(self, src, dst, axis, j):
        k = len(self.used)
        copy = pltpu.make_async_remote_copy(
            src_ref=src,
            dst_ref=dst,
            send_sem=self.send_sem.at[k],
            recv_sem=self.recv_sem.at[k],
            device_id=self.place.device(axis, j),
            device_id_type=MESH,
        )
        copy.start()
        self.used.append(copy)
        return copy

    def finish(self):
        for copy in self.used:
            copy.wait_send()


def gather_copies(p):
    return (p.Z - 1) + p.Z * ((p.X - 1) + (p.Y - 1) + 2 * (p.X - 1) * (p.Y - 1) + (p.C - 1))


def gather_steps(p, wires, buf, half):
    z, x, y, c = p.z, p.x, p.y, p.c
    along = {}
    for j in range(1, p.Z):
        along[j] = wires.send(buf.at[z, c, x, y], buf.at[z, c, x, y], "z", j)
    first, second, last = {}, {}, {}
    for k in range(p.Z + 2):
        if k < p.Z:
            zs = p.at("z", p.Z - k) if k else z
            if k:
                along[k].wait_recv()
            mine = buf.at[zs, c, x, y]
            first[k] = [("x", j, wires.send(mine, mine, "x", j)) for j in range(1, p.X)]
            first[k] += [("y", j, wires.send(mine, mine, "y", j)) for j in range(1, p.Y)]
            yield
        if 1 <= k <= p.Z:
            i = k - 1
            zs = p.at("z", p.Z - i) if i else z
            second[i] = []
            for axis, j, copy in first[i]:
                copy.wait_recv()
                if axis == "x":
                    part = buf.at[zs, c, p.at("x", p.X - j), y, pl.ds(0, half)]
                    second[i] += [wires.send(part, part, "y", q) for q in range(1, p.Y)]
                else:
                    part = buf.at[zs, c, x, p.at("y", p.Y - j), pl.ds(half, buf.shape[4] - half)]
                    second[i] += [wires.send(part, part, "x", q) for q in range(1, p.X)]
            yield
        if k >= 2:
            i = k - 2
            zs = p.at("z", p.Z - i) if i else z
            for copy in second[i]:
                copy.wait_recv()
            last[i] = [wires.send(buf.at[zs, c], buf.at[zs, c], "c", j) for j in range(1, p.C)]
            yield
    for i in last:
        for copy in last[i]:
            copy.wait_recv()
    yield


class Shares:
    def __init__(self, p, rows):
        cells = p.X * p.Y * p.Z
        unit = 16 * cells * p.C
        units = -(-rows // unit)
        self.a, self.b = 16 * ((units + 1) // 2), 16 * max(units // 2, 1)
        self.per_core = cells * (self.a + self.b)
        self.rows = p.C * self.per_core
        self.cells = cells
        self.copies = 2 * ((p.C - 1) + 2 * ((p.X - 1) + (p.Y - 1)) + 2 * (p.Z - 1))

    def scratch(self, p):
        a, b = self.a, self.b
        kinds = [
            (self.per_core,),
            (p.C - 1, self.per_core),
            (p.X - 1, p.Y * p.Z * a),
            (p.Y - 1, p.X * p.Z * b),
            (p.Y - 1, p.Z * a),
            (p.X - 1, p.Z * b),
            (p.Z - 1, a),
            (p.Z - 1, b),
        ]
        return [pltpu.VMEM(k + (128,), BF16) for k in kinds] + [pltpu.SemaphoreType.DMA((self.copies,))] * 2


def spread(start, size):
    return pl.ds(pl.multiple_of(start, 16), size)


def add_into(dst, at, parts):
    total = dst[at, :].astype(F32)
    for part in parts:
        total = total + part.astype(F32)
    dst[at, :] = total.astype(BF16)


def sum_steps(p, s, src, out, scratch):
    held, from_c, a1, b1, a2, b2, a3, b3, send_sem, recv_sem = scratch
    wires = Wires(p, send_sem, recv_sem)
    a, b, per = s.a, s.b, s.per_core
    ax, by = p.Y * p.Z * a, p.X * p.Z * b
    in_a = lambda x, y=None, z=None: (x * p.Y + (0 if y is None else y)) * p.Z * a + (0 if z is None else z * a)
    in_b = lambda y, x=None, z=None: s.cells * a + (y * p.X + (0 if x is None else x)) * p.Z * b + (0 if z is None else z * b)
    x, y, z, c = p.x, p.y, p.z, p.c
    copies = [wires.send(src.at[spread(p.at("c", j) * per, per)], from_c.at[j - 1], "c", j) for j in range(1, p.C)]
    yield
    for copy in copies:
        copy.wait_recv()
    total = src[spread(c * per, per), :].astype(F32)
    for j in range(p.C - 1):
        total = total + from_c[j].astype(F32)
    held[...] = total.astype(BF16)
    copies = [wires.send(held.at[spread(in_a(p.at("x", j)), ax)], a1.at[j - 1], "x", j) for j in range(1, p.X)]
    copies += [wires.send(held.at[spread(in_b(p.at("y", j)), by)], b1.at[j - 1], "y", j) for j in range(1, p.Y)]
    yield
    for copy in copies:
        copy.wait_recv()
    add_into(held, spread(in_a(x), ax), [a1[j] for j in range(p.X - 1)])
    add_into(held, spread(in_b(y), by), [b1[j] for j in range(p.Y - 1)])
    copies = [wires.send(held.at[spread(in_a(x, p.at("y", j)), p.Z * a)], a2.at[j - 1], "y", j) for j in range(1, p.Y)]
    copies += [wires.send(held.at[spread(in_b(y, p.at("x", j)), p.Z * b)], b2.at[j - 1], "x", j) for j in range(1, p.X)]
    yield
    for copy in copies:
        copy.wait_recv()
    add_into(held, spread(in_a(x, y), p.Z * a), [a2[j] for j in range(p.Y - 1)])
    add_into(held, spread(in_b(y, x), p.Z * b), [b2[j] for j in range(p.X - 1)])
    copies = []
    for j in range(1, p.Z):
        copies.append(wires.send(held.at[spread(in_a(x, y, p.at("z", j)), a)], a3.at[j - 1], "z", j))
        copies.append(wires.send(held.at[spread(in_b(y, x, p.at("z", j)), b)], b3.at[j - 1], "z", j))
    yield
    for copy in copies:
        copy.wait_recv()
    base = c * per
    for at, size, parts in ((in_a(x, y, z), a, a3), (in_b(y, x, z), b, b3)):
        total = held[spread(at, size), :].astype(F32)
        for j in range(p.Z - 1):
            total = total + parts[j].astype(F32)
        out[spread(base + at, size), :] = total.astype(BF16)
    copies = []
    for j in range(1, p.Z):
        for at, size in ((in_a(x, y, z), a), (in_b(y, x, z), b)):
            part = out.at[spread(base + at, size)]
            copies.append(wires.send(part, part, "z", j))
    yield
    for copy in copies:
        copy.wait_recv()
    part_a = out.at[spread(base + in_a(x, y), p.Z * a)]
    part_b = out.at[spread(base + in_b(y, x), p.Z * b)]
    copies = [wires.send(part_a, part_a, "y", j) for j in range(1, p.Y)]
    copies += [wires.send(part_b, part_b, "x", j) for j in range(1, p.X)]
    yield
    for copy in copies:
        copy.wait_recv()
    part_a = out.at[spread(base + in_a(x), ax)]
    part_b = out.at[spread(base + in_b(y), by)]
    copies = [wires.send(part_a, part_a, "x", j) for j in range(1, p.X)]
    copies += [wires.send(part_b, part_b, "y", j) for j in range(1, p.Y)]
    yield
    for copy in copies:
        copy.wait_recv()
    part = out.at[spread(base, per)]
    copies = [wires.send(part, part, "c", j) for j in range(1, p.C)]
    yield
    for copy in copies:
        copy.wait_recv()
    wires.finish()
    yield


def run_all(steps):
    steps = list(steps)
    while steps:
        steps = [s for s in steps if next(s, "end") != "end"]


def fold(t, odd):
    rows, wide = t.shape
    if wide % 128 == 64:
        body = jnp.where(odd, t[:, 64:], t[:, : wide - 64])
        edge = jnp.where(odd, t[:, :64], t[:, wide - 64 :])
        a, b = edge[: rows // 2], edge[rows // 2 :]
        tiles = [body[:, 128 * j : 128 * j + 128] for j in range(wide // 128)]
        tiles.append(jnp.concatenate([jnp.where(odd, b, a), jnp.where(odd, a, b)], axis=1))
        return jnp.concatenate(tiles, axis=0)
    need = -(-wide // 128) * 128
    t = jnp.concatenate([t, jnp.zeros((rows, need - wide), t.dtype)], axis=1) if need > wide else t
    return jnp.concatenate([t[:, 128 * j : 128 * j + 128] for j in range(need // 128)], axis=0)


def fold_rows(rows, wide):
    return rows * (wide // 128) + rows // 2 if wide % 128 == 64 else rows * (-(-wide // 128))


def unfold(p, buf, base, rows, wide):
    out = []
    lane = lax.broadcasted_iota(jnp.int32, (rows // 2, 128), 1)
    size = fold_rows(rows, wide)
    for z in range(p.Z):
        for x in range(p.X):
            tiles = []
            for y in range(p.Y):
                got = [buf[z, c, x, y, base : base + size, :].astype(F32) for c in range(p.C)]
                if wide % 128 == 64:
                    k = wide // 128
                    even, odd = got
                    tiles += [even[rows * j : rows * j + rows] for j in range(k)]
                    e, o = even[rows * k :], odd[rows * k :]
                    top = jnp.where(lane < 64, e, o)
                    low = pltpu.roll(jnp.where(lane < 64, o, e), 64, 1)
                    tiles.append(jnp.concatenate([top, low], axis=0))
                    tiles += [odd[rows * j : rows * j + rows] for j in range(k)]
                else:
                    k = size // rows
                    for c in range(p.C):
                        t = jnp.concatenate([got[c][rows * j : rows * j + rows] for j in range(k)], axis=1).astype(BF16)
                        tiles.append(nn(t, hot((128 * k, 768), (y * p.C + c) * wide, 0)) if 128 * k == wide else nn(t, hot_cut((128 * k, 768), (y * p.C + c) * wide, wide)))
            if wide % 128 == 64:
                out.append(jnp.concatenate(tiles, axis=1))
            else:
                out.append(functools.reduce(lambda a, b: a + b, tiles))
    return out


def hot_cut(shape, at, limit):
    rows = lax.broadcasted_iota(jnp.int32, shape, 0)
    cols = lax.broadcasted_iota(jnp.int32, shape, 1)
    return jnp.logical_and(rows + at == cols, rows < limit).astype(BF16)


def open_kernel(p, len_ref, x_ref, wq_ref, wo_ref, w1_ref, w2_ref, vec_ref,
                qt_out, k_out, kt_out, v_out, ct_out, lse_ref, w1_out, w2_out, wo_out, wt_out,
                bufq, bufr, win_s, qt_s, k_s, kt_s, v_s, ct_s, vt_s, bias_s, vcol_s, send_q, recv_q, send_r, recv_r, out_sem):
    p.locate()
    n_rows, seq = x_ref.shape[:2]
    odd = lax.rem(lax.axis_index("narrow"), 2) == 1
    slim, tall = wq_ref.shape[1:]
    qrows = bufq.shape[4]
    for c in range(3):
        t = jnp.concatenate([wq_ref[4 * c + g] for g in range(4)], axis=0).T
        t = jnp.concatenate([t, jnp.zeros((tall, 128 - 4 * slim), F32)], axis=1)
        bufq[p.z, p.c, p.x, p.y, c * tall : c * tall + tall, :] = t.astype(BF16)
    if qrows > 3 * tall:
        bufq[p.z, p.c, p.x, p.y, 3 * tall :, :] = jnp.zeros((qrows - 3 * tall, 128), BF16)
    rows, wide = 4 * slim, 4 * tall
    size = fold_rows(rows, wide)
    big = wo_ref.shape[2]
    shards = [nt(hot((big, big), 0, 0), wo_ref[0].astype(BF16))]
    shards += [jnp.concatenate([r[g] for g in range(4)], axis=0) for r in (w1_ref, w2_ref)]
    folded = jnp.concatenate([fold(t, odd) for t in shards], axis=0)
    if bufr.shape[4] > 3 * size:
        folded = jnp.concatenate([folded, jnp.zeros((bufr.shape[4] - 3 * size, 128), F32)], axis=0)
    bufr[p.z, p.c, p.x, p.y] = folded.astype(BF16)
    p.barrier()
    wires_q = Wires(p, send_q, recv_q)
    for _ in gather_steps(p, wires_q, bufq, qrows // 32 * 16):
        pass
    wires_r = Wires(p, send_r, recv_r)
    steps_r = gather_steps(p, wires_r, bufr, bufr.shape[4] // 32 * 16)

    def tick(count=1):
        for _ in range(count):
            next(steps_r, None)

    tick(2)
    total = jnp.zeros((3 * 192, 1024), F32)
    dp = p.Z * p.X
    for pair in range(dp // 2):
        tiles = []
        for d in (2 * pair, 2 * pair + 1):
            z, x = d // p.X, d % p.X
            got = [bufq[z, c, x, y].astype(F32) for y in range(p.Y) for c in range(p.C)]
            tiles.append(jnp.concatenate([b[c * tall : c * tall + tall] for c in range(3) for b in got], axis=0))
        r = lax.broadcasted_iota(jnp.int32, (256, 1), 0)
        q = jnp.where(r < 128, r, r - 128)
        g = (q >= slim).astype(jnp.int32) + (q >= 2 * slim).astype(jnp.int32) + (q >= 3 * slim).astype(jnp.int32)
        col = 256 * g + jnp.where(jnp.logical_or(g == 1, g == 3), 64, 0) + jnp.where(r < 128, 2 * pair * slim, (2 * pair + 1) * slim) + q - g * slim
        col = jnp.where(q < 4 * slim, col, -1)
        place = (lax.broadcasted_iota(jnp.int32, (256, 1024), 1) == col).astype(BF16)
        total = total + nn(jnp.concatenate(tiles, axis=1).astype(BF16), place)
    tick()
    win_s[...] = jnp.zeros_like(win_s)
    for g in range(4):
        off = 64 * (g % 2)
        stack = total[:, 256 * g : 256 * g + 256].astype(BF16)
        for c in range(3):
            win_s[c, g, off : off + 192, :] = stack[192 * c : 192 * c + 192]
        wt_out[g] = nt(hot((192, 256), off, 0), stack).astype(BF16)
    vcol_s[...] = vec_ref[0:8, :].T
    copies = []
    for row in range(n_rows):
        same = ids(len_ref, row, (seq, seq), 0) == ids(len_ref, row, (seq, seq), 1)
        bias_s[...] = jnp.where(same, 0.0, -1e30)
        for g in range(4):
            lo = window(g)
            xw = x_ref[row, :, lo : lo + 256]
            off = 64 * (g % 2)
            r = slice(192 * g, 192 * g + 192)
            q = nt(win_s[0, g, off : off + 192, :], xw) + vcol_s[r, 4:5]
            qt_s[row, r, :] = q.astype(BF16) * BF16(0.125)
            kt_s[row, r, :] = nt(win_s[1, g, off : off + 192, :], xw).astype(BF16)
            v = nt(win_s[2, g, off : off + 192, :], xw) + vcol_s[r, 5:6]
            vt_s[r, :] = v.astype(BF16)
        wide_of = lambda c: join([nt(x_ref[row, :, window(g) : window(g) + 256], win_s[c, g]) for g in range(4)])
        k_s[row] = wide_of(1).astype(BF16)
        v_s[row] = (wide_of(2) + vec_ref[5:6, :]).astype(BF16)
        for i, (src, dst) in enumerate(((qt_s, qt_out), (k_s, k_out), (kt_s, kt_out), (v_s, v_out))):
            copies.append(pltpu.make_async_copy(src.at[row], dst.at[row], out_sem.at[row, i]))
            copies[-1].start()
        tick()
        for h in range(12):
            kp = k_s[row, :, 128 * (h // 2) : 128 * (h // 2) + 128]
            at = slice(64 * h, 64 * h + 64)
            qh = qt_s[row, at, :]
            none = jnp.zeros_like(qh)
            s = nn(kp, jnp.concatenate([qh, none] if h % 2 == 0 else [none, qh], axis=0)) + bias_s[...]
            m = jnp.max(s, axis=0, keepdims=True)
            e = jnp.exp(s - m)
            tot = jnp.sum(e, axis=0, keepdims=True)
            ctx = nn(vt_s[at, :], e.astype(BF16))
            ct_s[row, at, :] = (ctx * (1.0 / tot)).astype(BF16)
            lse_ref[row, h : h + 1, :] = m + jnp.log(tot)
            if h % 2:
                tick()
        copies.append(pltpu.make_async_copy(ct_s.at[row], ct_out.at[row], out_sem.at[row, 4]))
        copies[-1].start()
    for _ in steps_r:
        pass
    wires_q.finish()
    wires_r.finish()
    whole = unfold(p, bufr, 0, rows, wide)
    wo_out[...] = jnp.concatenate(whole, axis=0).astype(BF16)
    for i, dst in enumerate((w1_out, w2_out)):
        whole = unfold(p, bufr, (i + 1) * size, rows, wide)
        dst[...] = jnp.zeros_like(dst)
        for g in range(4):
            off = 64 * (g % 2)
            dst[g, off : off + 192, :] = jnp.concatenate([b[g * slim : g * slim + slim] for b in whole], axis=0).astype(BF16)
    for copy in copies:
        copy.wait()


def opening(p, lengths, tokens, wq, wo, w1, w2, vec, ident):
    n, seq, d = tokens.shape
    slim, tall = wq.shape[1:]
    up = lambda r, m: -(-r // m) * m
    qrows = up(3 * tall, 32)
    rrows = up(3 * fold_rows(4 * slim, 4 * tall), 32)
    count = gather_copies(p)
    hbm = pl.BlockSpec(memory_space=pl.ANY)
    act = lambda a, b: jax.ShapeDtypeStruct((n, a, b), BF16)
    return pl.pallas_call(
        functools.partial(open_kernel, p),
        out_shape=[act(d, seq), act(seq, d), act(d, seq), act(seq, d), act(d, seq), jax.ShapeDtypeStruct((n, 16, seq), F32)]
        + [jax.ShapeDtypeStruct((4, 256, 768), BF16)] * 2
        + [jax.ShapeDtypeStruct((768, 768), BF16), jax.ShapeDtypeStruct((4, 192, 576), BF16)],
        in_specs=[pl.BlockSpec(memory_space=pltpu.SMEM)] + [VMEM] * 6,
        out_specs=[hbm] * 5 + [VMEM] * 5,
        scratch_shapes=[
            pltpu.VMEM((p.Z, p.C, p.X, p.Y, qrows, 128), BF16),
            pltpu.VMEM((p.Z, p.C, p.X, p.Y, rrows, 128), BF16),
            pltpu.VMEM((3, 4, 256, 256), BF16),
            pltpu.VMEM((n, d, seq), BF16), pltpu.VMEM((n, seq, d), BF16), pltpu.VMEM((n, d, seq), BF16), pltpu.VMEM((n, seq, d), BF16), pltpu.VMEM((n, d, seq), BF16),
            pltpu.VMEM((d, seq), BF16), pltpu.VMEM((seq, seq), F32), pltpu.VMEM((d, 8), F32),
            pltpu.SemaphoreType.DMA((count,)), pltpu.SemaphoreType.DMA((count,)),
            pltpu.SemaphoreType.DMA((count,)), pltpu.SemaphoreType.DMA((count,)),
            pltpu.SemaphoreType.DMA((n, 5)),
        ],
        compiler_params=pltpu.CompilerParams(collective_id=ident, has_side_effects=True, vmem_limit_bytes=60 * 2**20),
    )(lengths, tokens, wq, wo, w1, w2, vec)


def on_diagonal(n):
    return lax.broadcasted_iota(jnp.int32, (n, n), 0) == lax.broadcasted_iota(jnp.int32, (n, n), 1)


def ns_start(values):
    return [y * (1.0 / (jnp.sqrt(jnp.sum(y * y)) + 1e-07)) for y in values]


def ns_poly(values):
    n = values[0].shape[0]
    diag = on_diagonal(n)
    lows = [y.astype(BF16) for y in values]
    grams = [nt(l, l) for l in lows]
    mids = [jnp.sum(jnp.where(diag, g, 0.0)) * (1.0 / n) for g in grams]
    rest = [jnp.where(diag, g - m, g) for g, m in zip(grams, mids)]
    lowr = [r.astype(BF16) for r in rest]
    squares = [nn(r, r) for r in lowr]
    return mids, [((ns_second + 2.0 * ns_third * m) * r + ns_third * s).astype(BF16) for m, r, s in zip(mids, rest, squares)]


def ns_step(values, mids, polys):
    moved = [nn(q, y.astype(BF16)) for q, y in zip(polys, values)]
    return [(ns_first + ns_second * m + ns_third * m * m) * y + t for m, y, t in zip(mids, values, moved)]


def close_kernel(p, shares, *refs):
    (len_ref, wt_ref, so_ref, s1_ref, s2_ref, gv_ref, gmq_ref, wq_ref, wo_ref, w1_ref, w2_ref, vec_ref, vm1_ref, vm2_ref,
     x_hbm, qt_hbm, k_hbm, kt_hbm, v_hbm, ct_hbm, lse_ref, dct_hbm, res_hbm,
     gt_ref, mq_ref, mo_ref, m1_ref, m2_ref, nq_ref, no_ref, n1_ref, n2_ref, f_ref, s_ref, v_ref,
     x_s, qt_s, k_s, kt_s, v_s, ct_s, dct_s, res_s, bias_s, dq_s, dk_s, dv_s, gq_s, gv2_s, sq_s, oo_s, o1_s, o2_s, oq_s,
     y_s, po_s, pf_s, mid_s, xo_s, xf_s, xq_s, xo_r, xf_r, xq_r, in_sem, x_send, x_recv) = refs[: 35 + 32]
    rest = refs[35 + 32 :]
    p.locate()
    d, n = lax.axis_index("dp"), lax.axis_index("narrow")
    n_rows, seq = x_s.shape[:2]
    loads = []
    for row in range(n_rows):
        mine = []
        for i, (src, dst) in enumerate(((qt_hbm, qt_s), (k_hbm, k_s), (dct_hbm, dct_s), (v_hbm, v_s), (ct_hbm, ct_s), (kt_hbm, kt_s), (x_hbm, x_s), (res_hbm, res_s))):
            mine.append(pltpu.make_async_copy(src.at[row], dst.at[row], in_sem.at[row, i]))
            mine[-1].start()
        loads.append(mine)
    p.barrier()
    sums = [sum_steps(p, s, src, out, rest[10 * i : 10 * i + 10])
            for i, (s, src, out) in enumerate(zip(shares, (so_ref, s1_ref, s2_ref, sq_s), (oo_s, o1_s, o2_s, oq_s)))]
    order = [i for _ in range(9) for i in range(3)]

    def tick(count=1):
        for _ in range(count):
            if order:
                next(sums[order.pop(0)], None)

    tick(3)
    gq_s[...] = jnp.zeros_like(gq_s)
    gv2_s[...] = jnp.zeros_like(gv2_s)
    lane = lax.broadcasted_iota(jnp.int32, (192, 256), 1)
    for row in range(n_rows):
        same = ids(len_ref, row, (seq, seq), 0) == ids(len_ref, row, (seq, seq), 1)
        bias_s[...] = jnp.where(same, 0.0, -1e30)
        for copy in loads[row]:
            copy.wait()
        for h in range(12):
            tile = slice(128 * (h // 2), 128 * (h // 2) + 128)
            at = slice(64 * h, 64 * h + 64)
            qh, dc = qt_s[row, at, :], dct_s[row, at, :]
            none = jnp.zeros_like(qh)
            wide = lambda a: jnp.concatenate([a, none] if h % 2 == 0 else [none, a], axis=0)
            delta = jnp.sum(dc.astype(F32) * ct_s[row, at, :].astype(F32), axis=0, keepdims=True)
            s = nn(k_s[row, :, tile], wide(qh)) + bias_s[...]
            e = jnp.exp(s - lse_ref[row, h : h + 1, :])
            de = nn(v_s[row, :, tile], wide(dc))
            ds = (e * (de - delta)).astype(BF16)
            dv_s[at, :] = nt(dc, e.astype(BF16)).astype(BF16)
            dk_s[at, :] = nt(qh, ds).astype(BF16)
            dq_s[at, :] = (nn(kt_s[row, at, :], ds) * 0.125).astype(BF16)
            tick()
        dx = []
        for g in range(4):
            lo = window(g)
            r = slice(192 * g, 192 * g + 192)
            cat = jnp.concatenate([dq_s[r, :], dk_s[r, :], dv_s[r, :]], axis=0)
            dx.append(nn(wt_ref[g], cat))
            gq = nn(cat, x_s[row, :, lo : lo + 256])
            keep = (lane < 192) if g % 2 == 0 else (lane >= 64)
            for c in range(3):
                gq_s[c, :, lo : lo + 256] += jnp.where(keep, gq[192 * c : 192 * c + 192], 0.0)
        gt_ref[row] = (res_s[row] + jnp.concatenate(dx, axis=0).T).astype(BF16)
        ones = jnp.ones((16, seq), BF16)
        gv2_s[0:1, :] += nt(ones, dq_s[...])[0:1]
        gv2_s[1:2, :] += nt(ones, dv_s[...])[0:1]
    slim, tall = gmq_ref.shape[1:]
    up = hot((192, tall), 0, n * tall)
    for c in range(3):
        held = jnp.zeros((tall, 768), F32)
        for g in range(4):
            held = held + tn((0.95 * gmq_ref[4 * c + g]).astype(BF16), hot((slim, 768), 192 * g + d * slim, 0))
        put_blocks(sq_s, 1152 * c, gq_s[c] + nn(up, held.astype(BF16)))
    gv = jnp.concatenate([gv_ref[0:4], gv2_s[0:2], gv_ref[6:12]], axis=0)
    tail = sq_s.shape[0] - 3456
    flat = jnp.concatenate([gv[:, 128 * j : 128 * j + 128] for j in range(6)] + [jnp.zeros((tail - 72, 128), F32)], axis=0)
    sq_s[3456:, :] = flat.astype(BF16)
    next(sums[3])
    for s in sums[:3]:
        run_all([s])
    next(sums[3])
    wide, cols = w1_ref.shape[2], w1_ref.shape[1]
    sel_l = hot((wide, 768), n * wide, 0)
    sel_s = hot((cols, 192), d * cols, 0)
    big = wo_ref.shape[2]
    sel_b = hot((big, 768), d * big, 0)
    core0, core1 = p.c == 0, p.c == 1
    eight = lambda: [y_s[192 * i : 192 * i + 192, :] for i in range(8)]

    @pl.when(core0)
    def _():
        y_s[0:768, :] = ns_start([wide_rows(oo_s, 0, 4).astype(F32)])[0]

    @pl.when(core1)
    def _():
        for i, y in enumerate(ns_start([wide_rows(r, 1152 * g, 1).astype(F32) for r in (o1_s, o2_s) for g in range(4)])):
            y_s[192 * i : 192 * i + 192, :] = y

    for sweep in range(NS_STEPS):
        @pl.when(core0)
        def _():
            mids, polys = ns_poly([y_s[0:768, :]])
            mid_s[0:1, :] = jnp.broadcast_to(mids[0], (1, 128))
            po_s[...] = polys[0]

        @pl.when(core1)
        def _():
            mids, polys = ns_poly(eight())
            for i in range(8):
                mid_s[i : i + 1, :] = jnp.broadcast_to(mids[i], (1, 128))
                pf_s[i] = polys[i]

        next(sums[3], None)

        @pl.when(core0)
        def _():
            y_s[0:768, :] = ns_step([y_s[0:768, :]], [mid_s[0:1, 0:1]], [po_s[...]])[0]

        @pl.when(core1)
        def _():
            for i, y in enumerate(ns_step(eight(), [mid_s[i : i + 1, 0:1] for i in range(8)], [pf_s[i] for i in range(8)])):
                y_s[192 * i : 192 * i + 192, :] = y

        next(sums[3], None)
    wires = Wires(p, x_send, x_recv)
    mo_ref[0] = nt(sel_l, nn(sel_b, wide_rows(oo_s, 0, 4)).astype(BF16))
    for ref, m_ref in ((o1_s, m1_ref), (o2_s, m2_ref)):
        for g in range(4):
            m_ref[g] = nt(nn(sel_s, wide_rows(ref, 1152 * g, 1)).astype(BF16), sel_l)

    @pl.when(core0)
    def _():
        xo_s[...] = nn(sel_b, y_s[0:768, :].astype(BF16)).astype(BF16)

    @pl.when(core1)
    def _():
        for i in range(8):
            xf_s[cols * i : cols * i + cols, :] = nn(sel_s, y_s[192 * i : 192 * i + 192, :].astype(BF16)).astype(BF16)

    run_all([sums[3]])
    rows = [wide_rows(oq_s, 1152 * c, 1) for c in range(3)]
    spot = lambda g: hot_cut((256, 128), 0, 0)

    def square(parity):
        keep = (lane < 192) if parity == 0 else (lane >= 64)
        which = [(c, g) for c in range(3) for g in (parity, parity + 2)]
        ys = ns_start([jnp.where(keep, rows[c][:, window(g) : window(g) + 256].astype(F32), 0.0) for c, g in which])
        for _ in range(NS_STEPS):
            ys = ns_step(ys, *ns_poly(ys))
        for c in range(3):
            part = jnp.zeros((192, 128), F32)
            for (cc, g), y in zip(which, ys):
                if cc == c:
                    at = 64 * (g % 2) + d * slim
                    r = lax.broadcasted_iota(jnp.int32, (256, 128), 0) - at
                    q = lax.broadcasted_iota(jnp.int32, (256, 128), 1) - g * slim
                    sel = jnp.logical_and(r == q, jnp.logical_and(q >= 0, q < slim)).astype(BF16)
                    part = part + nn(y.astype(BF16), sel)
            xq_s[192 * c : 192 * c + 192, :] = part.astype(BF16)

    @pl.when(core0)
    def _():
        square(0)

    @pl.when(core1)
    def _():
        square(1)

    copies = [wires.send(xq_s, xq_r, "c", 1), wires.send(xo_s, xo_r, "c", 1), wires.send(xf_s, xf_r, "c", 1)]
    sel_o = hot((tall, 192), n * tall, 0)
    for c in range(3):
        mine = nn(sel_o, rows[c]).astype(BF16)
        for g in range(4):
            mq_ref[4 * c + g] = nt(hot((slim, 768), 192 * g + d * slim, 0), mine)
    vt = oq_s[3456 : 3456 + 80, :].astype(F32)
    grad = jnp.concatenate([vt[12 * j : 12 * j + 12] for j in range(6)], axis=1)
    first = 0.9 * vm1_ref[...] + 0.1 * grad
    second = 0.999 * vm2_ref[...] + 0.001 * grad * grad
    f_ref[...] = first
    s_ref[...] = second
    v_ref[...] = vec_ref[...] - adam_rate * (first * (1.0 / (1.0 - 0.9**STEP))) / (jnp.sqrt(second * (1.0 / (1.0 - 0.999**STEP))) + 1e-08)

    def fresh(w, own, longest):
        return w - muon_rate * (0.2 * math.sqrt(longest) * own + muon_decay * w)

    for copy in copies:
        copy.wait_recv()
    for c in range(3):
        both = (xq_s[192 * c : 192 * c + 192, :].astype(F32) + xq_r[192 * c : 192 * c + 192, :].astype(F32)).astype(BF16)
        mine = nn(sel_o, both).astype(BF16)
        for g in range(4):
            nq_ref[4 * c + g] = fresh(wq_ref[4 * c + g], nt(hot((slim, 128), g * slim, 0), mine), 192)
    xo = jnp.where(core0, xo_s[...], xo_r[...])
    no_ref[0] = fresh(wo_ref[0], nt(sel_l, xo), 768)
    for i, (w_ref, n_ref) in enumerate(((w1_ref, n1_ref), (w2_ref, n2_ref))):
        for g in range(4):
            at = slice(cols * (4 * i + g), cols * (4 * i + g) + cols)
            n_ref[g] = fresh(w_ref[g], nt(jnp.where(core1, xf_s[at, :], xf_r[at, :]), sel_l), 768)
    wires.finish()


def closing(p, shares, lengths, wt, so, s1, s2, gv, mq, weights, vec, vm1, vm2, acts, ident):
    tokens, lse = acts[0], acts[6]
    n, seq, d = tokens.shape
    slim = mq.shape[1]
    shape = lambda a: jax.ShapeDtypeStruct(a.shape, F32)
    outs = [jax.ShapeDtypeStruct(tokens.shape, BF16)] + [shape(w) for w in weights] * 2 + [shape(vec)] * 3
    hbm = pl.BlockSpec(memory_space=pl.ANY)
    tm, mt = pltpu.VMEM((n, seq, d), BF16), pltpu.VMEM((n, d, seq), BF16)
    flat = lambda r: pltpu.VMEM((r, 128), BF16)
    scratch = [tm, mt, tm, mt, tm, mt, mt, pltpu.VMEM((n, seq, d), F32), pltpu.VMEM((seq, seq), F32)]
    scratch += [pltpu.VMEM((d, seq), BF16)] * 3 + [pltpu.VMEM((3, 192, 768), F32), pltpu.VMEM((8, 768), F32)]
    scratch += [flat(shares[3].rows)] + [flat(s.rows) for s in shares]
    scratch += [pltpu.VMEM((1536, 768), F32), pltpu.VMEM((768, 768), BF16), pltpu.VMEM((8, 192, 192), BF16), pltpu.VMEM((8, 128), F32)]
    scratch += [pltpu.VMEM((4 * slim, 768), BF16), pltpu.VMEM((8 * slim, 768), BF16), pltpu.VMEM((576, 128), BF16)] * 2
    scratch += [pltpu.SemaphoreType.DMA((n, 8)), pltpu.SemaphoreType.DMA((3,)), pltpu.SemaphoreType.DMA((3,))]
    for s in shares:
        scratch += s.scratch(p)
    return pl.pallas_call(
        functools.partial(close_kernel, p, shares),
        out_shape=outs,
        in_specs=[pl.BlockSpec(memory_space=pltpu.SMEM)] + [VMEM] * 13 + [hbm] * 6 + [VMEM] + [hbm] * 2,
        out_specs=[VMEM] * 12,
        scratch_shapes=scratch,
        compiler_params=pltpu.CompilerParams(collective_id=ident, has_side_effects=True, vmem_limit_bytes=62 * 2**20),
    )(lengths, wt, so, s1, s2, gv, mq, *weights, vec, vm1, vm2, *acts)


def hand_over_kernel(*refs):
    half = len(refs) // 2
    for src, dst in zip(refs[:half], refs[half:]):
        dst[...] = src[...]


def hand_over(values):
    return pl.pallas_call(
        hand_over_kernel,
        out_shape=[jax.ShapeDtypeStruct(a.shape, a.dtype) for a in values],
        in_specs=[VMEM] * len(values),
        out_specs=[VMEM] * len(values),
        compiler_params=pltpu.CompilerParams(vmem_limit_bytes=60 * 2**20),
    )(*values)


def local(tokens, doc_lengths, cotangent, qkv_weight, out_weight, ffn_in_weight, ffn_out_weight, vectors,
          qkv_moment, out_moment, ffn_in_moment, ffn_out_moment, vec_moment1, vec_moment2):
    p = Place(lax.axis_size("dp"), lax.axis_size("narrow"))
    flip = lambda a: a.transpose(0, 2, 1)
    wq, w1, w2, mq, m1, m2 = map(flip, (qkv_weight, ffn_in_weight, ffn_out_weight, qkv_moment, ffn_in_moment, ffn_out_moment))
    shares = [Shares(p, r) for r in (4608, 4608, 4608, 3456 + 72)]
    qt, k, kt, v, ct, lse, w1p, w2p, wot, wt = opening(p, doc_lengths, tokens, wq, out_weight, w1, w2, vectors, 0)
    out_act, res, dct, so, s1, s2, gv = ffn(tokens, cotangent, ct, w1p, w2p, wot, vectors, out_moment, m1, m2, shares[0].rows)
    acts = (tokens, qt, k, kt, v, ct, lse, dct, res)
    gt, gq, go, g1, g2, nq, no, n1, n2, f, s, vn = hand_over(closing(
        p, shares, doc_lengths, wt, so, s1, s2, gv, mq, (wq, out_weight, w1, w2), vectors, vec_moment1, vec_moment2, acts, 1))
    return (out_act, gt, flip(gq), go, flip(g1), flip(g2), flip(nq), no, flip(n1), flip(n2), f, s, vn)


def solution(mesh):
    rows = P(("dp", "narrow"), None, None)
    cut = P(None, "narrow", "dp")
    return jax.shard_map(
        local,
        mesh=mesh,
        in_specs=(rows, P(("dp", "narrow"), None), rows) + (cut,) * 4 + (P(),) + (cut,) * 4 + (P(), P()),
        out_specs=(rows, rows) + (cut,) * 8 + (P(),) * 3,
        check_vma=False,
    )
```

```python
import functools
import math

import jax
import jax.numpy as jnp
from jax import lax
from jax.experimental import pallas as pl
from jax.experimental.pallas import tpu as pltpu
from jax.sharding import PartitionSpec as P

F32, BF16 = jnp.float32, jnp.bfloat16
MESH = pl.DeviceIdType.MESH
NORM_EPS = 1e-05
NS_STEPS = 5
STEP = 5
ns_first = 3.4445
ns_second = -4.775
ns_third = 2.0315
muon_rate = 0.5
muon_decay = 0.01
adam_rate = 0.4
VMEM = pl.BlockSpec(memory_space=pltpu.VMEM)


def nn(a, b):
    return lax.dot_general(a, b, (((1,), (0,)), ((), ())), preferred_element_type=F32)


def nt(a, b):
    return lax.dot_general(a, b, (((1,), (1,)), ((), ())), preferred_element_type=F32)


def tn(a, b):
    return lax.dot_general(a, b, (((0,), (0,)), ((), ())), preferred_element_type=F32)


def window(g):
    return 128 * (3 * (g // 2) + g % 2)


def join(parts):
    out = []
    for p in range(2):
        a, b = parts[2 * p], parts[2 * p + 1]
        out += [a[:, :128], a[:, 128:] + b[:, :128], b[:, 128:]]
    return jnp.concatenate(out, axis=1)


def ids(len_ref, row, shape, dim):
    pos = lax.broadcasted_iota(jnp.int32, shape, dim)
    out = jnp.zeros(shape, jnp.int32)
    end = jnp.int32(0)
    for j in range(4):
        end = end + len_ref[row, j]
        out = out + (pos >= end).astype(jnp.int32)
    return out


def hot(shape, row_at, col_at):
    rows = lax.broadcasted_iota(jnp.int32, shape, 0) + row_at
    cols = lax.broadcasted_iota(jnp.int32, shape, 1) + col_at
    return (rows == cols).astype(BF16)


def put_blocks(dst, base, value):
    for j in range(value.shape[1] // 128):
        dst[base + 192 * j : base + 192 * j + 192, :] = value[:, 128 * j : 128 * j + 128].astype(BF16)


def wide_rows(ref, base, count):
    parts = []
    for q in range(count):
        at = base + 1152 * q
        parts.append(jnp.concatenate([ref[at + 192 * j : at + 192 * j + 192, :] for j in range(6)], axis=1))
    return parts[0] if count == 1 else jnp.concatenate(parts, axis=0)


def gelu_parts(v):
    u = jnp.abs(v) * 0.7071067811865476
    den = 1.0 + 0.3275911 * u
    t = pl.reciprocal(den, approx=True)
    t = t * (2.0 - den * t)
    ex = jnp.exp(-u * u)
    poly = t * (0.254829592 + t * (-0.284496736 + t * (1.421413741 + t * (-1.453152027 + t * 1.061405429))))
    half = 0.5 * poly * ex
    cdf = jnp.where(v >= 0, 1.0 - half, half)
    return v * cdf, cdf + v * ex * 0.3989422804014327


def norm(h):
    mu = jnp.mean(h, axis=-1, keepdims=True)
    c = h - mu
    inv = lax.rsqrt(jnp.mean(c * c, axis=-1, keepdims=True) + NORM_EPS)
    return c * inv, inv


def norm_back(up, n, inv, gain):
    w = up * gain
    return inv * (w - jnp.mean(w, axis=-1, keepdims=True) - n * jnp.mean(w * n, axis=-1, keepdims=True))


def col_sum(v):
    return jnp.sum(v, axis=0, keepdims=True)


def turned(g):
    return 2 * (g % 2) + g // 2


def ffn_kernel(owned, x_ref, cot_ref, ct_ref, w1_ref, w2_ref, wo_ref, vec_ref, mo_ref, m1_ref, m2_ref,
               out_ref, res_ref, dct_ref, so_ref, s1_ref, s2_ref, gv_ref,
               fl_s, act_s, slope_s, db_s, g1_ref, g2_ref, go_ref):
    step = pl.program_id(0)
    T = x_ref.shape[1]
    vec = lambda i: vec_ref[i : i + 1, :]
    x = x_ref[0].astype(F32)
    ctx = ct_ref[0].T
    h1 = x + (nn(ctx, wo_ref[...]) + vec(6))
    n1, inv1 = norm(h1)
    first = n1 * vec(0) + vec(1)
    fl_s[...] = first.astype(BF16)
    branch = []
    for g in range(4):
        lo = window(g)
        inner = nn(fl_s[:, lo : lo + 256], w1_ref[g]) + vec(8 + g)
        a, sl = gelu_parts(inner)
        act_s[g] = a.astype(BF16)
        slope_s[g] = sl
        branch.append(nt(act_s[g], w2_ref[g]))
    h2 = first + (join(branch) + vec(7))
    n2, inv2 = norm(h2)
    out_ref[0] = (n2 * vec(2) + vec(3)).astype(BF16)
    dy = cot_ref[0].astype(F32)
    dh2 = norm_back(dy, n2, inv2, vec(2))
    dbl = dh2.astype(BF16)
    db_s[...] = dbl
    dbt = dbl.T
    flt = fl_s[...].T
    ones = jnp.ones((16, T), BF16)
    dfirst = []
    gb = []

    @pl.when(step == 0)
    def _():
        g1_ref[...] = jnp.zeros_like(g1_ref)
        g2_ref[...] = jnp.zeros_like(g2_ref)
        go_ref[...] = jnp.zeros_like(go_ref)
        gv_ref[...] = jnp.zeros_like(gv_ref)

    for g in range(4):
        lo = window(g)
        da = nn(db_s[:, lo : lo + 256], w2_ref[g])
        di = (da * slope_s[g]).astype(BF16)
        dfirst.append(nt(di, w1_ref[g]))
        g2_ref[g] += nn(dbt[192 * g : 192 * g + 192, :], act_s[g])
        ext = nn(jnp.concatenate([flt[192 * g : 192 * g + 192, :], ones], axis=0), di)
        g1_ref[g] += ext[:192]
        gb.append(ext[192:193])
    df = dh2 + join(dfirst)
    dh1 = norm_back(df, n1, inv1, vec(0))
    res_ref[0] = dh1
    dat = dh1.astype(BF16)
    go_ref[...] += nn(ct_ref[0], dat)
    dct_ref[0] = nt(wo_ref[...], dat).astype(BF16)
    z = jnp.zeros((1, x.shape[1]), F32)
    gv_ref[...] += jnp.concatenate(
        [col_sum(df * n1), col_sum(df), col_sum(dy * n2), col_sum(dy), z, z, col_sum(dat.astype(F32)), col_sum(dbl.astype(F32))] + gb, axis=0)


    @pl.when(step == pl.num_programs(0) - 1)
    def _():
        d, n = lax.axis_index("dp"), lax.axis_index("narrow")
        slim, wide = m1_ref.shape[1:]
        big = mo_ref.shape[2]
        sel_l = hot((wide, 768), n * wide, 0)
        sel_s = hot((192, slim), 0, d * slim)
        placed = nt(hot((768, big), 0, d * big), (0.95 * mo_ref[0]).astype(BF16)).astype(BF16)
        value = go_ref[...] + nn(placed, sel_l)
        for q in range(4):
            put_blocks(so_ref, 1152 * q, value[192 * q : 192 * q + 192])
        for dst, g_ref, m_ref in ((s1_ref, g1_ref, m1_ref), (s2_ref, g2_ref, m2_ref)):
            for g in range(4):
                placed = nn(sel_s, (0.95 * m_ref[g]).astype(BF16)).astype(BF16)
                value = g_ref[g] + nn(placed, sel_l)
                if owned:
                    put_blocks(dst, 576 * g, value[:, :384])
                    put_blocks(dst, 2304 + 576 * turned(g), value[:, 384:])
                else:
                    put_blocks(dst, 1152 * g, value)
        for dst in (so_ref, s1_ref, s2_ref):
            if dst.shape[0] > 4608:
                dst[4608:, :] = jnp.zeros((dst.shape[0] - 4608, 128), BF16)


def ffn(tokens, cot, ct, w1, w2, wo, vec, mo, m1, m2, rows, owned):
    n, seq, d = tokens.shape
    T = seq
    act = pl.BlockSpec((1, T, d), lambda i: (i, 0, 0))
    actt = pl.BlockSpec((1, d, T), lambda i: (i, 0, 0))
    full = lambda *s: pl.BlockSpec(s, lambda i: (0,) * len(s))
    return pl.pallas_call(
        functools.partial(ffn_kernel, owned),
        grid=(n,),
        out_shape=[
            jax.ShapeDtypeStruct((n, seq, d), BF16),
            jax.ShapeDtypeStruct((n, seq, d), F32),
            jax.ShapeDtypeStruct((n, d, seq), BF16),
        ]
        + [jax.ShapeDtypeStruct((rows, 128), BF16)] * 3
        + [jax.ShapeDtypeStruct((12, 768), F32)],
        in_specs=[act, act, actt, full(4, 256, 768), full(4, 256, 768), full(768, 768), full(12, 768), full(*mo.shape), full(*m1.shape), full(*m2.shape)],
        out_specs=[act, act, actt] + [full(rows, 128)] * 3 + [full(12, 768)],
        scratch_shapes=[
            pltpu.VMEM((T, d), BF16), pltpu.VMEM((4, T, 768), BF16), pltpu.VMEM((4, T, 768), F32), pltpu.VMEM((T, d), BF16),
            pltpu.VMEM((4, 192, 768), F32), pltpu.VMEM((4, 192, 768), F32), pltpu.VMEM((768, 768), F32),
        ],
        compiler_params=pltpu.CompilerParams(vmem_limit_bytes=60 * 2**20),
    )(tokens, cot, ct, w1, w2, wo, vec, mo, m1, m2)


class Place:
    def __init__(self, dp, narrow):
        self.X = 2 if dp % 2 == 0 else 1
        self.C = 2 if narrow % 2 == 0 else 1
        self.Z, self.Y = dp // self.X, narrow // self.C

    def locate(self):
        d, n = lax.axis_index("dp"), lax.axis_index("narrow")
        self.z, self.x = d // self.X, lax.rem(d, self.X)
        self.y, self.c = n // self.C, lax.rem(n, self.C)

    def count(self):
        return self.Z + self.X + self.Y + self.C - 4

    def at(self, axis, j):
        return lax.rem(getattr(self, axis) + j, getattr(self, axis.upper()))

    def device(self, axis, j):
        where = {a: getattr(self, a) for a in "zxyc"}
        where[axis] = self.at(axis, j)
        return (where["z"] * self.X + where["x"], where["y"] * self.C + where["c"])

    def other(self, dx, dy):
        return (self.z * self.X + lax.rem(self.x + dx, self.X), lax.rem(self.y + dy, self.Y) * self.C + self.c)

    def barrier(self, corner=False):
        sem = pltpu.get_barrier_semaphore()
        if corner:
            pl.semaphore_signal(sem, inc=1, device_id=self.other(1, 1), device_id_type=MESH)
        for axis in "zxyc":
            for j in range(1, getattr(self, axis.upper())):
                pl.semaphore_signal(sem, inc=1, device_id=self.device(axis, j), device_id_type=MESH)
        pl.semaphore_wait(sem, self.count() + int(corner))


class Wires:
    def __init__(self, place, send_sem, recv_sem):
        self.place, self.send_sem, self.recv_sem, self.makers = place, send_sem, recv_sem, []

    def plan(self, src, dst, axis, j):
        return self.plan_to(src, dst, lambda: self.place.device(axis, j))

    def plan_to(self, src, dst, device):
        k = len(self.makers)
        self.makers.append(
            lambda: pltpu.make_async_remote_copy(
                src_ref=src(),
                dst_ref=dst(),
                send_sem=self.send_sem.at[k],
                recv_sem=self.recv_sem.at[k],
                device_id=device(),
                device_id_type=MESH,
            )
        )
        return k

    def start(self, copies):
        for k in copies:
            self.makers[k]().start()

    def arrive(self, copies):
        for k in copies:
            self.makers[k]().wait_recv()

    def leave(self, copies):
        for k in copies:
            self.makers[k]().wait_send()

    def finish(self, skip=()):
        self.leave([k for k in range(len(self.makers)) if k not in skip])


def gather_copies(p):
    return (p.Z - 1) + p.Z * ((p.X - 1) + (p.Y - 1) + 2 * (p.X - 1) * (p.Y - 1) + (p.C - 1))


def gather_steps(p, wires, buf, half):
    z, x, y, c = p.z, p.x, p.y, p.c
    rest = buf.shape[4] - half

    def same(at):
        return (lambda: buf.at[at()],) * 2

    along, first, second, last = {}, {}, {}, {}
    for j in range(1, p.Z):
        along[j] = wires.plan(*same(lambda: (z, c, x, y)), "z", j)
    for i in range(p.Z):
        from_z = lambda i=i: p.at("z", p.Z - i) if i else z
        mine = lambda f=from_z: (f(), c, x, y)
        first[i] = [wires.plan(*same(mine), "x", j) for j in range(1, p.X)] + [wires.plan(*same(mine), "y", j) for j in range(1, p.Y)]
        second[i] = []
        for j in range(1, p.X):
            part = lambda f=from_z, j=j: (f(), c, p.at("x", p.X - j), y, pl.ds(0, half))
            second[i] += [wires.plan(*same(part), "y", q) for q in range(1, p.Y)]
        for j in range(1, p.Y):
            part = lambda f=from_z, j=j: (f(), c, x, p.at("y", p.Y - j), pl.ds(half, rest))
            second[i] += [wires.plan(*same(part), "x", q) for q in range(1, p.X)]
        last[i] = [wires.plan(*same(lambda f=from_z: (f(), c)), "c", j) for j in range(1, p.C)]

    def step(t):
        if t == 0:
            wires.start(along.values())
        if t < p.Z:
            if t:
                wires.arrive([along[t]])
            wires.start(first[t])
        if 1 <= t <= p.Z:
            wires.arrive(first[t - 1])
            wires.start(second[t - 1])
        if 2 <= t <= p.Z + 1:
            wires.arrive(second[t - 2])
            wires.start(last[t - 2])
        if t == p.Z + 2:
            for i in last:
                wires.arrive(last[i])

    return [functools.partial(step, t) for t in range(p.Z + 3)]


class Shares:
    def __init__(self, p, rows):
        cells = p.X * p.Y * p.Z
        unit = 16 * cells * p.C
        units = -(-rows // unit)
        self.a, self.b = 16 * ((units + 1) // 2), 16 * max(units // 2, 1)
        self.per_core = cells * (self.a + self.b)
        self.rows = p.C * self.per_core
        self.cells = cells
        self.copies = 2 * ((p.C - 1) + 2 * ((p.X - 1) + (p.Y - 1)) + 2 * (p.Z - 1))

    def scratch(self, p):
        a, b = self.a, self.b
        kinds = [
            (self.per_core,),
            (p.C - 1, self.per_core),
            (p.X - 1, p.Y * p.Z * a),
            (p.Y - 1, p.X * p.Z * b),
            (p.Y - 1, p.Z * a),
            (p.X - 1, p.Z * b),
            (p.Z - 1, a),
            (p.Z - 1, b),
        ]
        return [pltpu.VMEM(k + (128,), BF16) for k in kinds] + [pltpu.SemaphoreType.DMA((self.copies,))] * 2


def spread(start, size):
    return pl.ds(pl.multiple_of(start, 16), size)


def add_into(dst, at, parts):
    total = dst[at, :].astype(F32)
    for part in parts:
        total = total + part.astype(F32)
    dst[at, :] = total.astype(BF16)


def sum_steps(p, s, src, out, scratch):
    held, from_c, a1, b1, a2, b2, a3, b3, send_sem, recv_sem = scratch
    wires = Wires(p, send_sem, recv_sem)
    a, b, per = s.a, s.b, s.per_core
    ax, by = p.Y * p.Z * a, p.X * p.Z * b
    in_a = lambda x, y=0, z=0: ((x * p.Y + y) * p.Z + z) * a
    in_b = lambda y, x=0, z=0: s.cells * a + ((y * p.X + x) * p.Z + z) * b
    x, y, z, c = p.x, p.y, p.z, p.c
    base = c * per

    def cut(ref, start, size):
        return lambda: ref.at[spread(start(), size)]

    def both(start, size):
        return (cut(out, start, size),) * 2

    def slot(ref, j):
        return lambda: ref.at[j - 1]

    sends = [[] for _ in range(8)]
    for j in range(1, p.C):
        sends[0].append(wires.plan(cut(src, lambda j=j: p.at("c", j) * per, per), slot(from_c, j), "c", j))
        sends[7].append(wires.plan(*both(lambda: base, per), "c", j))
    for j in range(1, p.X):
        sends[1].append(wires.plan(cut(held, lambda j=j: in_a(p.at("x", j)), ax), slot(a1, j), "x", j))
        sends[2].append(wires.plan(cut(held, lambda j=j: in_b(y, p.at("x", j)), p.Z * b), slot(b2, j), "x", j))
        sends[5].append(wires.plan(*both(lambda: base + in_b(y, x), p.Z * b), "x", j))
        sends[6].append(wires.plan(*both(lambda: base + in_a(x), ax), "x", j))
    for j in range(1, p.Y):
        sends[1].append(wires.plan(cut(held, lambda j=j: in_b(p.at("y", j)), by), slot(b1, j), "y", j))
        sends[2].append(wires.plan(cut(held, lambda j=j: in_a(x, p.at("y", j)), p.Z * a), slot(a2, j), "y", j))
        sends[5].append(wires.plan(*both(lambda: base + in_a(x, y), p.Z * a), "y", j))
        sends[6].append(wires.plan(*both(lambda: base + in_b(y), by), "y", j))
    for j in range(1, p.Z):
        sends[3].append(wires.plan(cut(held, lambda j=j: in_a(x, y, p.at("z", j)), a), slot(a3, j), "z", j))
        sends[3].append(wires.plan(cut(held, lambda j=j: in_b(y, x, p.at("z", j)), b), slot(b3, j), "z", j))
        sends[4].append(wires.plan(*both(lambda: base + in_a(x, y, z), a), "z", j))
        sends[4].append(wires.plan(*both(lambda: base + in_b(y, x, z), b), "z", j))

    def total(ref, at, size, parts, count):
        value = ref[spread(at, size), :].astype(F32)
        for j in range(count):
            value = value + parts[j].astype(F32)
        return value.astype(BF16)

    def step(t):
        if t:
            wires.arrive(sends[t - 1])
        if t == 1:
            held[...] = total(src, base, per, from_c, p.C - 1)
        if t == 2:
            held[spread(in_a(x), ax), :] = total(held, in_a(x), ax, a1, p.X - 1)
            held[spread(in_b(y), by), :] = total(held, in_b(y), by, b1, p.Y - 1)
        if t == 3:
            held[spread(in_a(x, y), p.Z * a), :] = total(held, in_a(x, y), p.Z * a, a2, p.Y - 1)
            held[spread(in_b(y, x), p.Z * b), :] = total(held, in_b(y, x), p.Z * b, b2, p.X - 1)
        if t == 4:
            out[spread(base + in_a(x, y, z), a), :] = total(held, in_a(x, y, z), a, a3, p.Z - 1)
            out[spread(base + in_b(y, x, z), b), :] = total(held, in_b(y, x, z), b, b3, p.Z - 1)
        if t < 8:
            wires.start(sends[t])
        else:
            wires.finish()

    return [functools.partial(step, t) for t in range(9)]


def at_turn(turn, steps):
    for i, todo in enumerate(steps):
        if todo:

            @pl.when(turn == i)
            def _():
                for step in todo:
                    step()


def dealt(steps, turns):
    return [steps[len(steps) * i // turns : len(steps) * (i + 1) // turns] for i in range(turns)]


def fold(t, odd):
    rows, wide = t.shape
    if wide % 128 == 64:
        body = jnp.where(odd, t[:, 64:], t[:, : wide - 64])
        edge = jnp.where(odd, t[:, :64], t[:, wide - 64 :])
        a, b = edge[: rows // 2], edge[rows // 2 :]
        tiles = [body[:, 128 * j : 128 * j + 128] for j in range(wide // 128)]
        tiles.append(jnp.concatenate([jnp.where(odd, b, a), jnp.where(odd, a, b)], axis=1))
        return jnp.concatenate(tiles, axis=0)
    need = -(-wide // 128) * 128
    t = jnp.concatenate([t, jnp.zeros((rows, need - wide), t.dtype)], axis=1) if need > wide else t
    return jnp.concatenate([t[:, 128 * j : 128 * j + 128] for j in range(need // 128)], axis=0)


def fold_rows(rows, wide):
    return rows * (wide // 128) + rows // 2 if wide % 128 == 64 else rows * (-(-wide // 128))


def unfold(p, buf, base, rows, wide):
    out = []
    lane = lax.broadcasted_iota(jnp.int32, (rows // 2, 128), 1)
    size = fold_rows(rows, wide)
    for z in range(p.Z):
        for x in range(p.X):
            tiles = []
            for y in range(p.Y):
                got = [buf[z, c, x, y, base : base + size, :].astype(F32) for c in range(p.C)]
                if wide % 128 == 64:
                    k = wide // 128
                    even, odd = got
                    tiles += [even[rows * j : rows * j + rows] for j in range(k)]
                    e, o = even[rows * k :], odd[rows * k :]
                    top = jnp.where(lane < 64, e, o)
                    low = pltpu.roll(jnp.where(lane < 64, o, e), 64, 1)
                    tiles.append(jnp.concatenate([top, low], axis=0))
                    tiles += [odd[rows * j : rows * j + rows] for j in range(k)]
                else:
                    k = size // rows
                    for c in range(p.C):
                        t = jnp.concatenate([got[c][rows * j : rows * j + rows] for j in range(k)], axis=1).astype(BF16)
                        tiles.append(nn(t, hot((128 * k, 768), (y * p.C + c) * wide, 0)) if 128 * k == wide else nn(t, hot_cut((128 * k, 768), (y * p.C + c) * wide, wide)))
            if wide % 128 == 64:
                out.append(jnp.concatenate(tiles, axis=1))
            else:
                out.append(functools.reduce(lambda a, b: a + b, tiles))
    return out


def hot_cut(shape, at, limit):
    rows = lax.broadcasted_iota(jnp.int32, shape, 0)
    cols = lax.broadcasted_iota(jnp.int32, shape, 1)
    return jnp.logical_and(rows + at == cols, rows < limit).astype(BF16)


def open_kernel(p, len_ref, x_ref, wq_ref, wo_ref, w1_ref, w2_ref, vec_ref,
                qt_out, k_out, kt_out, v_out, ct_out, lse_ref, w1_out, w2_out, wo_out, wt_out,
                bufq, bufr, win_s, qt_s, k_s, kt_s, v_s, ct_s, vt_s, bias_s, vcol_s, send_q, recv_q, send_r, recv_r, out_sem):
    p.locate()
    n_rows, seq = x_ref.shape[:2]
    odd = lax.rem(lax.axis_index("narrow"), 2) == 1
    slim, tall = wq_ref.shape[1:]
    qrows = bufq.shape[4]
    for c in range(3):
        t = jnp.concatenate([wq_ref[4 * c + g] for g in range(4)], axis=0).T
        t = jnp.concatenate([t, jnp.zeros((tall, 128 - 4 * slim), F32)], axis=1)
        bufq[p.z, p.c, p.x, p.y, c * tall : c * tall + tall, :] = t.astype(BF16)
    if qrows > 3 * tall:
        bufq[p.z, p.c, p.x, p.y, 3 * tall :, :] = jnp.zeros((qrows - 3 * tall, 128), BF16)
    rows, wide = 4 * slim, 4 * tall
    size = fold_rows(rows, wide)
    big = wo_ref.shape[2]
    shards = [nt(hot((big, big), 0, 0), wo_ref[0].astype(BF16))]
    shards += [jnp.concatenate([r[g] for g in range(4)], axis=0) for r in (w1_ref, w2_ref)]
    folded = jnp.concatenate([fold(t, odd) for t in shards], axis=0)
    if bufr.shape[4] > 3 * size:
        folded = jnp.concatenate([folded, jnp.zeros((bufr.shape[4] - 3 * size, 128), F32)], axis=0)
    bufr[p.z, p.c, p.x, p.y] = folded.astype(BF16)
    p.barrier()
    wires_q, wires_r = Wires(p, send_q, recv_q), Wires(p, send_r, recv_r)
    steps_q = gather_steps(p, wires_q, bufq, qrows // 32 * 16)
    steps_r = gather_steps(p, wires_r, bufr, bufr.shape[4] // 32 * 16)
    for i, step in enumerate(steps_q):
        step()
        if i == 2:
            steps_r[0]()
    total = jnp.zeros((3 * 192, 1024), F32)
    dp = p.Z * p.X
    for pair in range(dp // 2):
        tiles = []
        for d in (2 * pair, 2 * pair + 1):
            z, x = d // p.X, d % p.X
            got = [bufq[z, c, x, y].astype(F32) for y in range(p.Y) for c in range(p.C)]
            tiles.append(jnp.concatenate([b[c * tall : c * tall + tall] for c in range(3) for b in got], axis=0))
        r = lax.broadcasted_iota(jnp.int32, (256, 1), 0)
        q = jnp.where(r < 128, r, r - 128)
        g = (q >= slim).astype(jnp.int32) + (q >= 2 * slim).astype(jnp.int32) + (q >= 3 * slim).astype(jnp.int32)
        col = 256 * g + jnp.where(jnp.logical_or(g == 1, g == 3), 64, 0) + jnp.where(r < 128, 2 * pair * slim, (2 * pair + 1) * slim) + q - g * slim
        col = jnp.where(q < 4 * slim, col, -1)
        place = (lax.broadcasted_iota(jnp.int32, (256, 1024), 1) == col).astype(BF16)
        total = total + nn(jnp.concatenate(tiles, axis=1).astype(BF16), place)
    win_s[...] = jnp.zeros_like(win_s)
    for g in range(4):
        off = 64 * (g % 2)
        stack = total[:, 256 * g : 256 * g + 256].astype(BF16)
        for c in range(3):
            win_s[c, g, off : off + 192, :] = stack[192 * c : 192 * c + 192]
        wt_out[g] = nt(hot((192, 256), off, 0), stack).astype(BF16)
    vcol_s[...] = vec_ref[0:8, :].T
    turns = dealt(steps_r[1:], 6 * n_rows)

    def out_copies(row, which=range(5)):
        pairs = ((qt_s, qt_out), (k_s, k_out), (kt_s, kt_out), (v_s, v_out), (ct_s, ct_out))
        return [pltpu.make_async_copy(pairs[i][0].at[row], pairs[i][1].at[row], out_sem.at[row, i]) for i in which]

    def one_row(row, carry):
        same = ids(len_ref, row, (seq, seq), 0) == ids(len_ref, row, (seq, seq), 1)
        bias_s[...] = jnp.where(same, 0.0, -1e30)
        for g in range(4):
            lo = window(g)
            xw = x_ref[row, :, lo : lo + 256]
            off = 64 * (g % 2)
            r = slice(192 * g, 192 * g + 192)
            q = nt(win_s[0, g, off : off + 192, :], xw) + vcol_s[r, 4:5]
            qt_s[row, r, :] = q.astype(BF16) * BF16(0.125)
            kt_s[row, r, :] = nt(win_s[1, g, off : off + 192, :], xw).astype(BF16)
            v = nt(win_s[2, g, off : off + 192, :], xw) + vcol_s[r, 5:6]
            vt_s[r, :] = v.astype(BF16)
        wide_of = lambda c: join([nt(x_ref[row, :, window(g) : window(g) + 256], win_s[c, g]) for g in range(4)])
        k_s[row] = wide_of(1).astype(BF16)
        v_s[row] = (wide_of(2) + vec_ref[5:6, :]).astype(BF16)
        for copy in out_copies(row, range(4)):
            copy.start()

        def pair(j, carry):
            lo = pl.multiple_of(128 * j, 128)
            kp = k_s[row, :, pl.ds(lo, 128)]
            for e in range(2):
                at = pl.ds(pl.multiple_of(lo + 64 * e, 64), 64)
                qh = qt_s[row, at, :]
                none = jnp.zeros_like(qh)
                s = nn(kp, jnp.concatenate([none, qh] if e else [qh, none], axis=0)) + bias_s[...]
                m = jnp.max(s, axis=0, keepdims=True)
                ex = jnp.exp(s - m)
                tot = jnp.sum(ex, axis=0, keepdims=True)
                ctx = nn(vt_s[at, :], ex.astype(BF16))
                ct_s[row, at, :] = (ctx * (1.0 / tot)).astype(BF16)
                lse_ref[row, pl.ds(2 * j + e, 1), :] = m + jnp.log(tot)
            at_turn(row * 6 + j, turns)
            return carry

        lax.fori_loop(0, 6, pair, 0)
        out_copies(row, (4,))[0].start()
        return carry

    lax.fori_loop(0, n_rows, one_row, 0)
    wires_q.finish()
    wires_r.finish()
    whole = unfold(p, bufr, 0, rows, wide)
    wo_out[...] = jnp.concatenate(whole, axis=0).astype(BF16)
    for i, dst in enumerate((w1_out, w2_out)):
        whole = unfold(p, bufr, (i + 1) * size, rows, wide)
        dst[...] = jnp.zeros_like(dst)
        for g in range(4):
            off = 64 * (g % 2)
            dst[g, off : off + 192, :] = jnp.concatenate([b[g * slim : g * slim + slim] for b in whole], axis=0).astype(BF16)
    for row in range(n_rows):
        for copy in out_copies(row):
            copy.wait()


def opening(p, lengths, tokens, wq, wo, w1, w2, vec, ident):
    n, seq, d = tokens.shape
    slim, tall = wq.shape[1:]
    up = lambda r, m: -(-r // m) * m
    qrows = up(3 * tall, 32)
    rrows = up(3 * fold_rows(4 * slim, 4 * tall), 32)
    count = gather_copies(p)
    hbm = pl.BlockSpec(memory_space=pl.ANY)
    act = lambda a, b: jax.ShapeDtypeStruct((n, a, b), BF16)
    return pl.pallas_call(
        functools.partial(open_kernel, p),
        out_shape=[act(d, seq), act(seq, d), act(d, seq), act(seq, d), act(d, seq), jax.ShapeDtypeStruct((n, 16, seq), F32)]
        + [jax.ShapeDtypeStruct((4, 256, 768), BF16)] * 2
        + [jax.ShapeDtypeStruct((768, 768), BF16), jax.ShapeDtypeStruct((4, 192, 576), BF16)],
        in_specs=[pl.BlockSpec(memory_space=pltpu.SMEM)] + [VMEM] * 6,
        out_specs=[hbm] * 5 + [VMEM] * 5,
        scratch_shapes=[
            pltpu.VMEM((p.Z, p.C, p.X, p.Y, qrows, 128), BF16),
            pltpu.VMEM((p.Z, p.C, p.X, p.Y, rrows, 128), BF16),
            pltpu.VMEM((3, 4, 256, 256), BF16),
            pltpu.VMEM((n, d, seq), BF16), pltpu.VMEM((n, seq, d), BF16), pltpu.VMEM((n, d, seq), BF16), pltpu.VMEM((n, seq, d), BF16), pltpu.VMEM((n, d, seq), BF16),
            pltpu.VMEM((d, seq), BF16), pltpu.VMEM((seq, seq), F32), pltpu.VMEM((d, 8), F32),
            pltpu.SemaphoreType.DMA((count,)), pltpu.SemaphoreType.DMA((count,)),
            pltpu.SemaphoreType.DMA((count,)), pltpu.SemaphoreType.DMA((count,)),
            pltpu.SemaphoreType.DMA((n, 5)),
        ],
        compiler_params=pltpu.CompilerParams(collective_id=ident, has_side_effects=True, vmem_limit_bytes=60 * 2**20),
    )(lengths, tokens, wq, wo, w1, w2, vec)


def on_diagonal(n):
    return lax.broadcasted_iota(jnp.int32, (n, n), 0) == lax.broadcasted_iota(jnp.int32, (n, n), 1)


def ns_start(values):
    return [y * (1.0 / (jnp.sqrt(jnp.sum(y * y)) + 1e-07)) for y in values]


def ns_poly(values):
    n = values[0].shape[0]
    diag = on_diagonal(n)
    lows = [y.astype(BF16) for y in values]
    grams = [nt(l, l) for l in lows]
    mids = [jnp.sum(jnp.where(diag, g, 0.0)) * (1.0 / n) for g in grams]
    rest = [jnp.where(diag, g - m, g) for g, m in zip(grams, mids)]
    lowr = [r.astype(BF16) for r in rest]
    squares = [nn(r, r) for r in lowr]
    return mids, [((ns_second + 2.0 * ns_third * m) * r + ns_third * s).astype(BF16) for m, r, s in zip(mids, rest, squares)]


def ns_step(values, mids, polys):
    moved = [nn(q, y.astype(BF16)) for q, y in zip(polys, values)]
    return [(ns_first + ns_second * m + ns_third * m * m) * y + t for m, y, t in zip(mids, values, moved)]


def close_kernel(p, shares, *refs):
    (len_ref, wt_ref, so_ref, s1_ref, s2_ref, gv_ref, gmq_ref, wq_ref, wo_ref, w1_ref, w2_ref, vec_ref, vm1_ref, vm2_ref,
     x_hbm, qt_hbm, k_hbm, kt_hbm, v_hbm, ct_hbm, lse_ref, dct_hbm, res_hbm,
     gt_ref, mq_ref, mo_ref, m1_ref, m2_ref, nq_ref, no_ref, n1_ref, n2_ref, f_ref, s_ref, v_ref,
     x_s, qt_s, k_s, kt_s, v_s, ct_s, dct_s, res_s, bias_s, dq_s, dk_s, dv_s, gq_s, gv2_s, sq_s, oo_s, o1_s, o2_s, oq_s,
     y_s, po_s, pf_s, mid_s, xo_s, xf_s, xq_s, xo_r, xf_r, xq_r, in_sem, x_send, x_recv) = refs[: 35 + 32]
    rest = refs[35 + 32 :]
    p.locate()
    d, n = lax.axis_index("dp"), lax.axis_index("narrow")
    n_rows, seq = x_s.shape[:2]
    pairs = ((qt_hbm, qt_s), (k_hbm, k_s), (dct_hbm, dct_s), (v_hbm, v_s), (ct_hbm, ct_s), (kt_hbm, kt_s), (x_hbm, x_s), (res_hbm, res_s))

    def loads(row):
        return [pltpu.make_async_copy(src.at[row], dst.at[row], in_sem.at[row, i]) for i, (src, dst) in enumerate(pairs)]

    for row in range(n_rows):
        for copy in loads(row):
            copy.start()
    p.barrier()
    sums = [sum_steps(p, s, src, out, rest[10 * i : 10 * i + 10])
            for i, (s, src, out) in enumerate(zip(shares, (so_ref, s1_ref, s2_ref, sq_s), (oo_s, o1_s, o2_s, oq_s)))]
    o, f1, f2, q = sums
    for step in (o[0], f1[0], f2[0]):
        step()
    turns = dealt([o[1], f1[1], o[2], f2[1], o[3], f1[2], o[4], f2[2], o[5], f1[3], o[6], f2[3], o[7], f1[4], f2[4]], 6 * n_rows)
    gq_s[...] = jnp.zeros_like(gq_s)
    gv2_s[...] = jnp.zeros_like(gv2_s)
    lane = lax.broadcasted_iota(jnp.int32, (192, 256), 1)

    def one_row(row, carry):
        same = ids(len_ref, row, (seq, seq), 0) == ids(len_ref, row, (seq, seq), 1)
        bias_s[...] = jnp.where(same, 0.0, -1e30)
        for copy in loads(row):
            copy.wait()

        def pair(j, carry):
            lo = pl.multiple_of(128 * j, 128)
            kp, vp = k_s[row, :, pl.ds(lo, 128)], v_s[row, :, pl.ds(lo, 128)]
            for e in range(2):
                at = pl.ds(pl.multiple_of(lo + 64 * e, 64), 64)
                qh, dc = qt_s[row, at, :], dct_s[row, at, :]
                none = jnp.zeros_like(qh)
                wide = lambda a: jnp.concatenate([none, a] if e else [a, none], axis=0)
                delta = jnp.sum(dc.astype(F32) * ct_s[row, at, :].astype(F32), axis=0, keepdims=True)
                s = nn(kp, wide(qh)) + bias_s[...]
                ex = jnp.exp(s - lse_ref[row, pl.ds(2 * j + e, 1), :])
                de = nn(vp, wide(dc))
                ds = (ex * (de - delta)).astype(BF16)
                dv_s[at, :] = nt(dc, ex.astype(BF16)).astype(BF16)
                dk_s[at, :] = nt(qh, ds).astype(BF16)
                dq_s[at, :] = (nn(kt_s[row, at, :], ds) * 0.125).astype(BF16)
            at_turn(row * 6 + j, turns)
            return carry

        lax.fori_loop(0, 6, pair, 0)
        dx = []
        for g in range(4):
            lo = window(g)
            r = slice(192 * g, 192 * g + 192)
            cat = jnp.concatenate([dq_s[r, :], dk_s[r, :], dv_s[r, :]], axis=0)
            dx.append(nn(wt_ref[g], cat))
            gq = nn(cat, x_s[row, :, lo : lo + 256])
            keep = (lane < 192) if g % 2 == 0 else (lane >= 64)
            for c in range(3):
                gq_s[c, :, lo : lo + 256] += jnp.where(keep, gq[192 * c : 192 * c + 192], 0.0)
        gt_ref[row] = (res_s[row] + jnp.concatenate(dx, axis=0).T).astype(BF16)
        ones = jnp.ones((16, seq), BF16)
        gv2_s[0:1, :] += nt(ones, dq_s[...])[0:1]
        gv2_s[1:2, :] += nt(ones, dv_s[...])[0:1]
        return carry

    lax.fori_loop(0, n_rows, one_row, 0)
    slim, tall = gmq_ref.shape[1:]
    up = hot((192, tall), 0, n * tall)
    for c in range(3):
        held = jnp.zeros((tall, 768), F32)
        for g in range(4):
            held = held + tn((0.95 * gmq_ref[4 * c + g]).astype(BF16), hot((slim, 768), 192 * g + d * slim, 0))
        put_blocks(sq_s, 1152 * c, gq_s[c] + nn(up, held.astype(BF16)))
    gv = jnp.concatenate([gv_ref[0:4], gv2_s[0:2], gv_ref[6:12]], axis=0)
    tail = sq_s.shape[0] - 3456
    flat = jnp.concatenate([gv[:, 128 * j : 128 * j + 128] for j in range(6)] + [jnp.zeros((tail - 72, 128), F32)], axis=0)
    sq_s[3456:, :] = flat.astype(BF16)
    for step in (q[0], o[8], q[1]):
        step()
    wide, cols = w1_ref.shape[2], w1_ref.shape[1]
    sel_l = hot((wide, 768), n * wide, 0)
    sel_s = hot((cols, 192), d * cols, 0)
    big = wo_ref.shape[2]
    sel_b = hot((big, 768), d * big, 0)
    core0, core1 = p.c == 0, p.c == 1
    eight = lambda: [y_s[192 * i : 192 * i + 192, :] for i in range(8)]

    late = 3
    before = [[f1[5]], [f1[6]], [f1[7]], [q[5]], [q[7]]]
    between = [[q[2], f2[5]], [q[3], f2[6]], [q[4], f2[7], f1[8], f2[8]], [q[6]], [q[8]]]

    def sweep(t, carry):
        on0 = jnp.logical_and(core0, t < NS_STEPS)
        on1 = jnp.logical_and(core1, t >= late)

        @pl.when(jnp.logical_and(core0, t == 0))
        def _():
            y_s[0:768, :] = ns_start([wide_rows(oo_s, 0, 4).astype(F32)])[0]

        @pl.when(jnp.logical_and(core1, t == late))
        def _():
            for i, y in enumerate(ns_start([wide_rows(r, 1152 * g, 1).astype(F32) for r in (o1_s, o2_s) for g in range(4)])):
                y_s[192 * i : 192 * i + 192, :] = y

        @pl.when(on0)
        def _():
            mids, polys = ns_poly([y_s[0:768, :]])
            mid_s[0:1, :] = jnp.broadcast_to(mids[0], (1, 128))
            po_s[...] = polys[0]

        @pl.when(on1)
        def _():
            mids, polys = ns_poly(eight())
            for i in range(8):
                mid_s[i : i + 1, :] = jnp.broadcast_to(mids[i], (1, 128))
                pf_s[i] = polys[i]

        at_turn(t, before)

        @pl.when(on0)
        def _():
            y_s[0:768, :] = ns_step([y_s[0:768, :]], [mid_s[0:1, 0:1]], [po_s[...]])[0]

        @pl.when(on1)
        def _():
            for i, y in enumerate(ns_step(eight(), [mid_s[i : i + 1, 0:1] for i in range(8)], [pf_s[i] for i in range(8)])):
                y_s[192 * i : 192 * i + 192, :] = y

        at_turn(t, between)
        return carry

    lax.fori_loop(0, NS_STEPS + late, sweep, 0)
    wires = Wires(p, x_send, x_recv)
    mo_ref[0] = nt(sel_l, nn(sel_b, wide_rows(oo_s, 0, 4)).astype(BF16))
    for ref, m_ref in ((o1_s, m1_ref), (o2_s, m2_ref)):
        for g in range(4):
            m_ref[g] = nt(nn(sel_s, wide_rows(ref, 1152 * g, 1)).astype(BF16), sel_l)

    @pl.when(core0)
    def _():
        xo_s[...] = nn(sel_b, y_s[0:768, :].astype(BF16)).astype(BF16)

    @pl.when(core1)
    def _():
        for i in range(8):
            xf_s[cols * i : cols * i + cols, :] = nn(sel_s, y_s[192 * i : 192 * i + 192, :].astype(BF16)).astype(BF16)

    rows = [wide_rows(oq_s, 1152 * c, 1) for c in range(3)]
    spot = lambda g: hot_cut((256, 128), 0, 0)

    def square(parity):
        keep = (lane < 192) if parity == 0 else (lane >= 64)
        which = [(c, g) for c in range(3) for g in (parity, parity + 2)]
        ys = ns_start([jnp.where(keep, rows[c][:, window(g) : window(g) + 256].astype(F32), 0.0) for c, g in which])
        for i, y in enumerate(ys):
            y_s[192 * i : 192 * i + 192, :256] = y

        def turn(t, carry):
            ys = [y_s[192 * i : 192 * i + 192, :256] for i in range(6)]
            for i, y in enumerate(ns_step(ys, *ns_poly(ys))):
                y_s[192 * i : 192 * i + 192, :256] = y
            return carry

        lax.fori_loop(0, NS_STEPS, turn, 0)
        ys = [y_s[192 * i : 192 * i + 192, :256] for i in range(6)]
        for c in range(3):
            part = jnp.zeros((192, 128), F32)
            for (cc, g), y in zip(which, ys):
                if cc == c:
                    at = 64 * (g % 2) + d * slim
                    r = lax.broadcasted_iota(jnp.int32, (256, 128), 0) - at
                    q = lax.broadcasted_iota(jnp.int32, (256, 128), 1) - g * slim
                    sel = jnp.logical_and(r == q, jnp.logical_and(q >= 0, q < slim)).astype(BF16)
                    part = part + nn(y.astype(BF16), sel)
            xq_s[192 * c : 192 * c + 192, :] = part.astype(BF16)

    @pl.when(core0)
    def _():
        square(0)

    @pl.when(core1)
    def _():
        square(1)

    copies = [wires.plan(lambda a=a: a, lambda b=b: b, "c", 1) for a, b in ((xq_s, xq_r), (xo_s, xo_r), (xf_s, xf_r))]
    wires.start(copies)
    sel_o = hot((tall, 192), n * tall, 0)
    for c in range(3):
        mine = nn(sel_o, rows[c]).astype(BF16)
        for g in range(4):
            mq_ref[4 * c + g] = nt(hot((slim, 768), 192 * g + d * slim, 0), mine)
    vt = oq_s[3456 : 3456 + 80, :].astype(F32)
    grad = jnp.concatenate([vt[12 * j : 12 * j + 12] for j in range(6)], axis=1)
    first = 0.9 * vm1_ref[...] + 0.1 * grad
    second = 0.999 * vm2_ref[...] + 0.001 * grad * grad
    f_ref[...] = first
    s_ref[...] = second
    v_ref[...] = vec_ref[...] - adam_rate * (first * (1.0 / (1.0 - 0.9**STEP))) / (jnp.sqrt(second * (1.0 / (1.0 - 0.999**STEP))) + 1e-08)

    def fresh(w, own, longest):
        return w - muon_rate * (0.2 * math.sqrt(longest) * own + muon_decay * w)

    wires.arrive(copies)
    for c in range(3):
        both = (xq_s[192 * c : 192 * c + 192, :].astype(F32) + xq_r[192 * c : 192 * c + 192, :].astype(F32)).astype(BF16)
        mine = nn(sel_o, both).astype(BF16)
        for g in range(4):
            nq_ref[4 * c + g] = fresh(wq_ref[4 * c + g], nt(hot((slim, 128), g * slim, 0), mine), 192)
    xo = jnp.where(core0, xo_s[...], xo_r[...])
    no_ref[0] = fresh(wo_ref[0], nt(sel_l, xo), 768)
    for i, (w_ref, n_ref) in enumerate(((w1_ref, n1_ref), (w2_ref, n2_ref))):
        for g in range(4):
            at = slice(cols * (4 * i + g), cols * (4 * i + g) + cols)
            n_ref[g] = fresh(w_ref[g], nt(jnp.where(core1, xf_s[at, :], xf_r[at, :]), sel_l), 768)
    wires.finish()


def closing(p, shares, lengths, wt, so, s1, s2, gv, mq, weights, vec, vm1, vm2, acts, ident):
    tokens, lse = acts[0], acts[6]
    n, seq, d = tokens.shape
    slim = mq.shape[1]
    shape = lambda a: jax.ShapeDtypeStruct(a.shape, F32)
    outs = [jax.ShapeDtypeStruct(tokens.shape, BF16)] + [shape(w) for w in weights] * 2 + [shape(vec)] * 3
    hbm = pl.BlockSpec(memory_space=pl.ANY)
    tm, mt = pltpu.VMEM((n, seq, d), BF16), pltpu.VMEM((n, d, seq), BF16)
    flat = lambda r: pltpu.VMEM((r, 128), BF16)
    scratch = [tm, mt, tm, mt, tm, mt, mt, pltpu.VMEM((n, seq, d), F32), pltpu.VMEM((seq, seq), F32)]
    scratch += [pltpu.VMEM((d, seq), BF16)] * 3 + [pltpu.VMEM((3, 192, 768), F32), pltpu.VMEM((8, 768), F32)]
    scratch += [flat(shares[3].rows)] + [flat(s.rows) for s in shares]
    scratch += [pltpu.VMEM((1536, 768), F32), pltpu.VMEM((768, 768), BF16), pltpu.VMEM((8, 192, 192), BF16), pltpu.VMEM((8, 128), F32)]
    scratch += [pltpu.VMEM((4 * slim, 768), BF16), pltpu.VMEM((8 * slim, 768), BF16), pltpu.VMEM((576, 128), BF16)] * 2
    scratch += [pltpu.SemaphoreType.DMA((n, 8)), pltpu.SemaphoreType.DMA((3,)), pltpu.SemaphoreType.DMA((3,))]
    for s in shares:
        scratch += s.scratch(p)
    return pl.pallas_call(
        functools.partial(close_kernel, p, shares),
        out_shape=outs,
        in_specs=[pl.BlockSpec(memory_space=pltpu.SMEM)] + [VMEM] * 13 + [hbm] * 6 + [VMEM] + [hbm] * 2,
        out_specs=[VMEM] * 12,
        scratch_shapes=scratch,
        compiler_params=pltpu.CompilerParams(collective_id=ident, has_side_effects=True, vmem_limit_bytes=62 * 2**20),
    )(lengths, wt, so, s1, s2, gv, mq, *weights, vec, vm1, vm2, *acts)


class Owned:
    def __init__(self, p, half):
        self.half, self.rows, self.copies = half, 8 * half, 4 + 2 * (p.Z - 1)
        self.kinds = [4 * half, 4 * half, 2 * half, half, (p.Z - 1) * (half // p.Z), half, half]

    def scratch(self):
        return [pltpu.VMEM((k, 128), BF16) for k in self.kinds] + [pltpu.SemaphoreType.DMA((self.copies,))] * 2


def owned_steps(p, s, src, scratch):
    held, from_c, r1, r2, r3, mine, other, send_sem, recv_sem = scratch
    wires = Wires(p, send_sem, recv_sem)
    h, q, z, c = s.half, s.half // p.Z, p.z, p.c
    first = jnp.where(c == 0, p.x, p.y)
    second = jnp.where(c == 0, p.y, p.x)
    cut = lambda ref, start, size: lambda: ref.at[spread(start(), size)]

    def partner(turn):
        along_x = c == turn
        x, y = jnp.where(along_x, 1 - p.x, p.x), jnp.where(along_x, p.y, 1 - p.y)
        return (z * p.X + x, y * p.C + c)

    sibling = lambda: p.device("c", 1)
    spot = lambda: (2 * first + second) * h
    sends = [
        [wires.plan_to(cut(src, lambda: (1 - c) * 4 * h, 4 * h), lambda: from_c, sibling)],
        [wires.plan_to(cut(held, lambda: (1 - first) * 2 * h, 2 * h), lambda: r1, lambda: partner(0))],
        [wires.plan_to(cut(held, lambda: (2 * first + 1 - second) * h, h), lambda: r2, lambda: partner(1))],
        [],
        [],
        [wires.plan_to(lambda: mine, lambda: other, sibling)],
    ]
    for j in range(1, p.Z):
        sends[3].append(wires.plan(cut(held, lambda j=j: spot() + p.at("z", j) * q, q), lambda j=j: r3.at[pl.ds((j - 1) * q, q)], "z", j))
        sends[4].append(wires.plan(*(cut(mine, lambda: z * q, q),) * 2, "z", j))

    def add(dst, to, ref, start, size, parts):
        value = ref[spread(start, size), :].astype(F32)
        for part in parts:
            value = value + part().astype(F32)
        dst[spread(to, size), :] = value.astype(BF16)

    def step(t):
        if 1 <= t <= 5:
            wires.arrive(sends[t - 1])
        if t == 1:
            add(held, 0, src, c * 4 * h, 4 * h, [lambda: from_c[...]])
        if t == 2:
            add(held, first * 2 * h, held, first * 2 * h, 2 * h, [lambda: r1[...]])
        if t == 3:
            add(held, spot(), held, spot(), h, [lambda: r2[...]])
        if t == 4:
            add(mine, z * q, held, spot() + z * q, q, [lambda j=j: r3[(j - 1) * q : j * q, :] for j in range(1, p.Z)])
        if t < 5:
            wires.start(sends[t])
        if t == 5:

            @pl.when(c == 0)
            def _():
                wires.start(sends[5])

        if t == 6:
            wires.finish(skip=sends[5])

            @pl.when(c == 0)
            def _():
                wires.leave(sends[5])

            @pl.when(c == 1)
            def _():
                wires.arrive(sends[5])

    return [functools.partial(step, t) for t in range(7)]


def canon(odd, base):
    r = lax.broadcasted_iota(jnp.int32, (256, 128), 0)
    s = lax.broadcasted_iota(jnp.int32, (256, 128), 1)
    channel = jnp.where(odd, jnp.where(r < 128, r + 64, r - 128), r)
    return jnp.where(r < 192, channel - base, -1000), s


def owner_kernel(p, shares, *refs):
    (len_ref, wt_ref, so_ref, s1_ref, s2_ref, gv_ref, gmq_ref, wq_ref, wo_ref, w1_ref, w2_ref, vec_ref, vm1_ref, vm2_ref,
     x_hbm, qt_hbm, k_hbm, kt_hbm, v_hbm, ct_hbm, lse_ref, dct_hbm, res_hbm,
     gt_ref, mq_ref, mo_ref, m1_ref, m2_ref, nq_ref, no_ref, n1_ref, n2_ref, f_ref, s_ref, v_ref,
     x_s, qt_s, k_s, kt_s, v_s, ct_s, dct_s, res_s, bias_s, dq_s, dk_s, dv_s, gq_s, gv2_s, sq_s, oo_s,
     yo_s, po_s, yf_s, yq_s, mid_s, pf_s, xo_s, xo_r, tmf_s, txf_s, tmq_s, txq_s, tv_s, rmf_s, rxf_s, rmq_s, rxq_s, rv_s,
     in_sem, x_send, x_recv) = refs[: 35 + 37]
    rest = refs[35 + 37 :]
    p.locate()
    d, n = lax.axis_index("dp"), lax.axis_index("narrow")
    core0, core1 = p.c == 0, p.c == 1
    n_rows, seq = x_s.shape[:2]
    pairs = ((qt_hbm, qt_s), (k_hbm, k_s), (dct_hbm, dct_s), (v_hbm, v_s), (ct_hbm, ct_s), (kt_hbm, kt_s), (x_hbm, x_s), (res_hbm, res_s))

    def loads(row):
        return [pltpu.make_async_copy(src.at[row], dst.at[row], in_sem.at[row, i]) for i, (src, dst) in enumerate(pairs)]

    for row in range(n_rows):
        for copy in loads(row):
            copy.start()
    p.barrier(corner=True)
    o = sum_steps(p, shares[0], so_ref, oo_s, rest[:10])
    f1 = owned_steps(p, shares[1], s1_ref, rest[10:19])
    f2 = owned_steps(p, shares[2], s2_ref, rest[19:28])
    q = owned_steps(p, shares[3], sq_s, rest[28:37])
    f1_half, f1_other, f2_half, f2_other, q_half, q_other = rest[15], rest[16], rest[24], rest[25], rest[33], rest[34]
    for step in (o[0], f1[0], f2[0]):
        step()
    turns = dealt([o[1], f1[1], o[2], f2[1], o[3], f1[2], o[4], f2[2], f1[3], o[5], f2[3], o[6], f1[4], o[7], f2[4], f1[5], f2[5], o[8]], 6 * n_rows)
    gq_s[...] = jnp.zeros_like(gq_s)
    gv2_s[...] = jnp.zeros_like(gv2_s)
    lane = lax.broadcasted_iota(jnp.int32, (192, 256), 1)

    def one_row(row, carry):
        same = ids(len_ref, row, (seq, seq), 0) == ids(len_ref, row, (seq, seq), 1)
        bias_s[...] = jnp.where(same, 0.0, -1e30)
        for copy in loads(row):
            copy.wait()

        def pair(j, carry):
            lo = pl.multiple_of(128 * j, 128)
            kp, vp = k_s[row, :, pl.ds(lo, 128)], v_s[row, :, pl.ds(lo, 128)]
            for e in range(2):
                at = pl.ds(pl.multiple_of(lo + 64 * e, 64), 64)
                qh, dc = qt_s[row, at, :], dct_s[row, at, :]
                none = jnp.zeros_like(qh)
                wide = lambda a: jnp.concatenate([none, a] if e else [a, none], axis=0)
                delta = jnp.sum(dc.astype(F32) * ct_s[row, at, :].astype(F32), axis=0, keepdims=True)
                s = nn(kp, wide(qh)) + bias_s[...]
                ex = jnp.exp(s - lse_ref[row, pl.ds(2 * j + e, 1), :])
                de = nn(vp, wide(dc))
                ds = (ex * (de - delta)).astype(BF16)
                dv_s[at, :] = nt(dc, ex.astype(BF16)).astype(BF16)
                dk_s[at, :] = nt(qh, ds).astype(BF16)
                dq_s[at, :] = (nn(kt_s[row, at, :], ds) * 0.125).astype(BF16)
            at_turn(row * 6 + j, turns)
            return carry

        lax.fori_loop(0, 6, pair, 0)
        dx = []
        for g in range(4):
            lo = window(g)
            r = slice(192 * g, 192 * g + 192)
            cat = jnp.concatenate([dq_s[r, :], dk_s[r, :], dv_s[r, :]], axis=0)
            dx.append(nn(wt_ref[g], cat))
            gq = nn(cat, x_s[row, :, lo : lo + 256])
            keep = (lane < 192) if g % 2 == 0 else (lane >= 64)
            for c in range(3):
                gq_s[c, :, lo : lo + 256] += jnp.where(keep, gq[192 * c : 192 * c + 192], 0.0)
        gt_ref[row] = (res_s[row] + jnp.concatenate(dx, axis=0).T).astype(BF16)
        ones = jnp.ones((16, seq), BF16)
        gv2_s[0:1, :] += nt(ones, dq_s[...])[0:1]
        gv2_s[1:2, :] += nt(ones, dv_s[...])[0:1]
        return carry

    lax.fori_loop(0, n_rows, one_row, 0)
    slim, tall = gmq_ref.shape[1:]
    half = shares[3].half
    up = hot((192, tall), 0, n * tall)
    values = []
    for c in range(3):
        held = jnp.zeros((tall, 768), F32)
        for g in range(4):
            held = held + tn((0.95 * gmq_ref[4 * c + g]).astype(BF16), hot((slim, 768), 192 * g + d * slim, 0))
        values.append(gq_s[c] + nn(up, held.astype(BF16)))
    gv = jnp.concatenate([gv_ref[0:4], gv2_s[0:2], gv_ref[6:12]], axis=0)
    lane = lax.broadcasted_iota(jnp.int32, (192, 128), 1)
    for g in range(4):
        lo = window(g)
        tiles = []
        edges = []
        for c in range(3):
            a, b = values[c][:, lo : lo + 128], values[c][:, lo + 128 : lo + 256]
            whole, edge = (b, pltpu.roll(a, 64, 1)) if g % 2 else (a, b)
            tiles.append(whole)
            edges.append(jnp.where(lane < 64, edge, 0.0))
        tiles += [edges[0] + pltpu.roll(edges[1], 64, 1), edges[2]]
        vec = [gv[0:8, 192 * g : 192 * g + 128]]
        vec.append(jnp.concatenate([gv[0:8, 192 * g + 128 : 192 * g + 192], jnp.zeros((8, 64), F32)], axis=1))
        vec += [gv[8 + g : 9 + g, 128 * j : 128 * j + 128] for j in range(6)]
        vec.append(jnp.zeros((2 * half - 960 - 22, 128), F32))
        flat = jnp.concatenate(tiles + vec, axis=0).astype(BF16)
        sq_s[g * half : g * half + half, :] = flat[:half]
        sq_s[(4 + turned(g)) * half : (5 + turned(g)) * half, :] = flat[half:]
    for step in (q[0], f1[6], f2[6], q[1]):
        step()
    before = [[], [q[2]], [q[3]], [], []]
    between = [[], [], [], [q[4]], [q[5]]]

    def blocks(a_ref, b_ref):
        return jnp.concatenate([r[192 * j : 192 * j + 192, :] for r in (a_ref, b_ref) for j in range(3)], axis=1)

    def sweep(t, carry):
        @pl.when(jnp.logical_and(core0, t == 0))
        def _():
            yo_s[...] = ns_start([wide_rows(oo_s, 0, 4).astype(F32)])[0]

        @pl.when(jnp.logical_and(core1, t == 0))
        def _():
            for i, y in enumerate(ns_start([blocks(a, b).astype(F32) for a, b in ((f1_other, f1_half), (f2_other, f2_half))])):
                yf_s[i] = y

        @pl.when(core0)
        def _():
            mids, polys = ns_poly([yo_s[...]])
            mid_s[0:1, :] = jnp.broadcast_to(mids[0], (1, 128))
            po_s[...] = polys[0]

        @pl.when(core1)
        def _():
            mids, polys = ns_poly([yf_s[i] for i in range(2)])
            for i in range(2):
                mid_s[i : i + 1, :] = jnp.broadcast_to(mids[i], (1, 128))
                pf_s[i] = polys[i]

        at_turn(t, before)

        @pl.when(core0)
        def _():
            yo_s[...] = ns_step([yo_s[...]], [mid_s[0:1, 0:1]], [po_s[...]])[0]

        @pl.when(core1)
        def _():
            for i, y in enumerate(ns_step([yf_s[i] for i in range(2)], [mid_s[i : i + 1, 0:1] for i in range(2)], [pf_s[i] for i in range(2)])):
                yf_s[i] = y

        at_turn(t, between)
        return carry

    lax.fori_loop(0, NS_STEPS, sweep, 0)
    q[6]()
    wires = Wires(p, x_send, x_recv)
    me = 2 * p.x + p.y
    odd = lax.rem(me, 2) == 1
    around = ((1, 0), (0, 1), (1, 1))

    def scatter(src, dst):
        return [
            wires.plan_to(
                lambda dx=dx, dy=dy: src.at[lax.rem(p.x + dx, 2), lax.rem(p.y + dy, 2)], lambda: dst.at[me], lambda dx=dx, dy=dy: p.other(dx, dy)
            )
            for dx, dy in around
        ]

    early = [scatter(a, b) for a, b in ((tmf_s, rmf_s), (txf_s, rxf_s), (tmq_s, rmq_s), (tv_s, rv_s))]
    late = scatter(txq_s, rxq_s)
    sibling = lambda: p.device("c", 1)
    pass_early = [wires.plan_to(lambda a=a: a, lambda a=a: a, sibling) for a in (rmf_s, rxf_s, rmq_s, rv_s)]
    pass_late = [wires.plan_to(lambda: rxq_s, lambda: rxq_s, sibling)]
    pass_o = [wires.plan_to(lambda: xo_s, lambda: xo_r, sibling)]
    big = wo_ref.shape[2]
    sel_b = hot((big, 768), d * big, 0)
    wide, cols = w1_ref.shape[2], w1_ref.shape[1]

    def put_f(dst, pair):
        for x in range(2):
            sel = hot((cols, 192), (p.z * 2 + x) * cols, 0)
            part = jnp.concatenate([nn(sel, m) for m in pair], axis=0).astype(BF16)
            for y in range(2):
                dst[x, y] = part[:, 384 * y : 384 * y + 384]

    def put_q(dst, three):
        for x in range(2):
            part = jnp.zeros((192, 128), F32)
            for c, m in enumerate(three):
                at, s = canon(odd, (p.z * 2 + x) * slim)
                sel = jnp.logical_and(jnp.logical_and(at >= 0, at < slim), at + c * slim == s).astype(BF16)
                part = part + nn(m, sel)
            for y in range(2):
                dst[x, y] = part[96 * y : 96 * y + 96].astype(BF16)

    @pl.when(core0)
    def _():
        xo_s[...] = nn(sel_b, yo_s[...].astype(BF16)).astype(BF16)
        wires.start(pass_o)

    @pl.when(core1)
    def _():
        put_f(tmf_s, [blocks(f1_other, f1_half), blocks(f2_other, f2_half)])
        put_f(txf_s, [yf_s[i].astype(BF16) for i in range(2)])
        group = jnp.concatenate([q_other[...], q_half[...]], axis=0)
        tiles = [group[192 * j : 192 * j + 192] for j in range(5)]
        lane = lax.broadcasted_iota(jnp.int32, (192, 128), 1)
        pair = tiles[3].astype(F32)
        edges = [jnp.where(lane < 64, e, 0.0) for e in (pair, pltpu.roll(pair, 64, 1), tiles[4].astype(F32))]
        three = [jnp.concatenate([t.astype(F32), e], axis=1) for t, e in zip(tiles, edges)]
        put_q(tmq_s, [m.astype(BF16) for m in three])
        for x in range(2):
            for y in range(2):
                tv_s[x, y] = group[960:992]
        for copies in early:
            wires.start(copies)
        for a, b in ((tmf_s, rmf_s), (txf_s, rxf_s), (tmq_s, rmq_s), (tv_s, rv_s)):
            b[me] = a[p.x, p.y]
        for i, y in enumerate(ns_start(three)):
            yq_s[i] = y

        def turn(t, carry):
            ys = [yq_s[i] for i in range(3)]
            for i, y in enumerate(ns_step(ys, *ns_poly(ys))):
                yq_s[i] = y
            return carry

        lax.fori_loop(0, NS_STEPS, turn, 0)
        put_q(txq_s, [yq_s[i].astype(BF16) for i in range(3)])
        wires.start(late)
        rxq_s[me] = txq_s[p.x, p.y]
        for copies in early:
            wires.arrive(copies)
        wires.start(pass_early)
        wires.arrive(pass_o)

    @pl.when(core0)
    def _():
        wires.arrive(pass_early)

    def fresh(w, own, longest):
        return w - muon_rate * (0.2 * math.sqrt(longest) * own + muon_decay * w)

    sel_l = hot((wide, 768), n * wide, 0)
    sel_h = hot((wide, 384), p.c * wide, 0)
    sel_q = hot((tall, 96), p.c * tall, 0)
    mo_ref[0] = nt(sel_l, nn(sel_b, wide_rows(oo_s, 0, 4)).astype(BF16))
    no_ref[0] = fresh(wo_ref[0], nt(sel_l, jnp.where(core0, xo_s[...], xo_r[...])), 768)
    for g in range(4):
        for i, (w_ref, m_ref, n_ref) in enumerate(((w1_ref, m1_ref, n1_ref), (w2_ref, m2_ref, n2_ref))):
            at = slice(cols * i, cols * i + cols)
            m_ref[g] = nt(rmf_s[g, at, :], sel_h)
            n_ref[g] = fresh(w_ref[g], nt(rxf_s[g, at, :], sel_h), 768)
        own = nn(sel_q, rmq_s[g]).astype(BF16)
        for c in range(3):
            mq_ref[4 * c + g] = nt(hot((slim, 128), c * slim, 0), own)
    parts = [rv_s[g].astype(F32) for g in range(4)]
    top = jnp.concatenate([t for v in parts for t in (v[0:8], v[8:16, :64])], axis=1)
    low = [jnp.concatenate([v[16 + j : 17 + j] for j in range(6)], axis=1) for v in parts]
    grad = jnp.concatenate([top] + low, axis=0)
    first = 0.9 * vm1_ref[...] + 0.1 * grad
    second = 0.999 * vm2_ref[...] + 0.001 * grad * grad
    f_ref[...] = first
    s_ref[...] = second
    v_ref[...] = vec_ref[...] - adam_rate * (first * (1.0 / (1.0 - 0.9**STEP))) / (jnp.sqrt(second * (1.0 / (1.0 - 0.999**STEP))) + 1e-08)

    @pl.when(core1)
    def _():
        wires.arrive(late)
        wires.start(pass_late)

    @pl.when(core0)
    def _():
        wires.arrive(pass_late)

    for g in range(4):
        own = nn(sel_q, rxq_s[g]).astype(BF16)
        for c in range(3):
            nq_ref[4 * c + g] = fresh(wq_ref[4 * c + g], nt(hot((slim, 128), c * slim, 0), own), 192)

    @pl.when(core0)
    def _():
        wires.leave(pass_o)

    @pl.when(core1)
    def _():
        for copies in early + [late, pass_early, pass_late]:
            wires.leave(copies)


def closing_owned(p, shares, lengths, wt, so, s1, s2, gv, mq, weights, vec, vm1, vm2, acts, ident):
    tokens = acts[0]
    n, seq, d = tokens.shape
    slim = mq.shape[1]
    shape = lambda a: jax.ShapeDtypeStruct(a.shape, F32)
    outs = [jax.ShapeDtypeStruct(tokens.shape, BF16)] + [shape(w) for w in weights] * 2 + [shape(vec)] * 3
    hbm = pl.BlockSpec(memory_space=pl.ANY)
    tm, mt = pltpu.VMEM((n, seq, d), BF16), pltpu.VMEM((n, d, seq), BF16)
    scratch = [tm, mt, tm, mt, tm, mt, mt, pltpu.VMEM((n, seq, d), F32), pltpu.VMEM((seq, seq), F32)]
    scratch += [pltpu.VMEM((d, seq), BF16)] * 3 + [pltpu.VMEM((3, 192, 768), F32), pltpu.VMEM((8, 768), F32)]
    scratch += [pltpu.VMEM((shares[3].rows, 128), BF16), pltpu.VMEM((shares[0].rows, 128), BF16)]
    scratch += [pltpu.VMEM((768, 768), F32), pltpu.VMEM((768, 768), BF16), pltpu.VMEM((2, 192, 768), F32), pltpu.VMEM((3, 192, 256), F32)]
    scratch += [pltpu.VMEM((8, 128), F32), pltpu.VMEM((2, 192, 192), BF16)]
    scratch += [pltpu.VMEM((4 * slim, 768), BF16)] * 2
    to_f, to_q, to_v = (2 * slim, 384), (96, 128), (32, 128)
    scratch += [pltpu.VMEM((2, 2) + k, BF16) for k in (to_f, to_f, to_q, to_q, to_v)]
    scratch += [pltpu.VMEM((4,) + k, BF16) for k in (to_f, to_f, to_q, to_q, to_v)]
    scratch += [pltpu.SemaphoreType.DMA((n, 8)), pltpu.SemaphoreType.DMA((21,)), pltpu.SemaphoreType.DMA((21,))]
    scratch += shares[0].scratch(p)
    for s in shares[1:]:
        scratch += s.scratch()
    return pl.pallas_call(
        functools.partial(owner_kernel, p, shares),
        out_shape=outs,
        in_specs=[pl.BlockSpec(memory_space=pltpu.SMEM)] + [VMEM] * 13 + [hbm] * 6 + [VMEM] + [hbm] * 2,
        out_specs=[VMEM] * 12,
        scratch_shapes=scratch,
        compiler_params=pltpu.CompilerParams(collective_id=ident, has_side_effects=True, vmem_limit_bytes=62 * 2**20),
    )(lengths, wt, so, s1, s2, gv, mq, *weights, vec, vm1, vm2, *acts)


def hand_over_kernel(*refs):
    half = len(refs) // 2
    for src, dst in zip(refs[:half], refs[half:]):
        dst[...] = src[...]


def hand_over(values):
    return pl.pallas_call(
        hand_over_kernel,
        out_shape=[jax.ShapeDtypeStruct(a.shape, a.dtype) for a in values],
        in_specs=[VMEM] * len(values),
        out_specs=[VMEM] * len(values),
        compiler_params=pltpu.CompilerParams(vmem_limit_bytes=60 * 2**20),
    )(*values)


def local(tokens, doc_lengths, cotangent, qkv_weight, out_weight, ffn_in_weight, ffn_out_weight, vectors,
          qkv_moment, out_moment, ffn_in_moment, ffn_out_moment, vec_moment1, vec_moment2):
    p = Place(lax.axis_size("dp"), lax.axis_size("narrow"))
    flip = lambda a: a.transpose(0, 2, 1)
    wq, w1, w2, mq, m1, m2 = map(flip, (qkv_weight, ffn_in_weight, ffn_out_weight, qkv_moment, ffn_in_moment, ffn_out_moment))
    owned = p.X == 2 and p.Y == 2 and p.C == 2 and p.Z in (2, 4)
    if owned:
        shares = [Shares(p, 4608), Owned(p, 576), Owned(p, 576), Owned(p, 512)]
    else:
        shares = [Shares(p, r) for r in (4608, 4608, 4608, 3456 + 72)]
    qt, k, kt, v, ct, lse, w1p, w2p, wot, wt = opening(p, doc_lengths, tokens, wq, out_weight, w1, w2, vectors, 0)
    out_act, res, dct, so, s1, s2, gv = ffn(tokens, cotangent, ct, w1p, w2p, wot, vectors, out_moment, m1, m2, shares[0].rows, owned)
    acts = (tokens, qt, k, kt, v, ct, lse, dct, res)
    gt, gq, go, g1, g2, nq, no, n1, n2, f, s, vn = hand_over((closing_owned if owned else closing)(
        p, shares, doc_lengths, wt, so, s1, s2, gv, mq, (wq, out_weight, w1, w2), vectors, vec_moment1, vec_moment2, acts, 1))
    return (out_act, gt, flip(gq), go, flip(g1), flip(g2), flip(nq), no, flip(n1), flip(n2), f, s, vn)


def solution(mesh):
    rows = P(("dp", "narrow"), None, None)
    cut = P(None, "narrow", "dp")
    return jax.shard_map(
        local,
        mesh=mesh,
        in_specs=(rows, P(("dp", "narrow"), None), rows) + (cut,) * 4 + (P(),) + (cut,) * 4 + (P(), P()),
        out_specs=(rows, rows) + (cut,) * 8 + (P(),) * 3,
        check_vma=False,
    )
```

```python
import functools
import math

import jax
import jax.numpy as jnp
from jax import lax
from jax.experimental import pallas as pl
from jax.experimental.pallas import tpu as pltpu
from jax.sharding import PartitionSpec as P

F32, BF16 = jnp.float32, jnp.bfloat16
MESH = pl.DeviceIdType.MESH
NORM_EPS = 1e-05
NS_STEPS = 5
R_FIRST = 2
STEP = 5
ns_first = 3.4445
ns_second = -4.775
ns_third = 2.0315
muon_rate = 0.5
muon_decay = 0.01
adam_rate = 0.4
VMEM = pl.BlockSpec(memory_space=pltpu.VMEM)


def nn(a, b):
    return lax.dot_general(a, b, (((1,), (0,)), ((), ())), preferred_element_type=F32)


def nt(a, b):
    return lax.dot_general(a, b, (((1,), (1,)), ((), ())), preferred_element_type=F32)


def tn(a, b):
    return lax.dot_general(a, b, (((0,), (0,)), ((), ())), preferred_element_type=F32)


def window(g):
    return 128 * (3 * (g // 2) + g % 2)


def join(parts):
    out = []
    for p in range(2):
        a, b = parts[2 * p], parts[2 * p + 1]
        out += [a[:, :128], a[:, 128:] + b[:, :128], b[:, 128:]]
    return jnp.concatenate(out, axis=1)


def ids(len_ref, row, shape, dim):
    pos = lax.broadcasted_iota(jnp.int32, shape, dim)
    out = jnp.zeros(shape, jnp.int32)
    end = jnp.int32(0)
    for j in range(4):
        end = end + len_ref[row, j]
        out = out + (pos >= end).astype(jnp.int32)
    return out


def hot(shape, row_at, col_at):
    rows = lax.broadcasted_iota(jnp.int32, shape, 0) + row_at
    cols = lax.broadcasted_iota(jnp.int32, shape, 1) + col_at
    return (rows == cols).astype(BF16)


def put_blocks(dst, base, value):
    for j in range(value.shape[1] // 128):
        dst[base + 192 * j : base + 192 * j + 192, :] = value[:, 128 * j : 128 * j + 128].astype(BF16)


def wide_rows(ref, base, count):
    parts = []
    for q in range(count):
        at = base + 1152 * q
        parts.append(jnp.concatenate([ref[at + 192 * j : at + 192 * j + 192, :] for j in range(6)], axis=1))
    return parts[0] if count == 1 else jnp.concatenate(parts, axis=0)


def gelu_parts(v):
    t = pl.reciprocal(1.0 + (0.3275911 * 0.7071067811865476) * jnp.abs(v), approx=True)
    ex = jnp.exp2(v * v * (-0.5 * 1.4426950408889634))
    half = t * ex * (0.127414796 + t * (-0.142248368 + t * (0.7107068705 + t * (-0.7265760135 + t * 0.5307027145))))
    cdf = jnp.where(v >= 0, 1.0 - half, half)
    return v * cdf, cdf + (v * ex) * 0.3989422804014327


def norm(h):
    mu = jnp.mean(h, axis=-1, keepdims=True)
    c = h - mu
    inv = lax.rsqrt(jnp.mean(c * c, axis=-1, keepdims=True) + NORM_EPS)
    return c * inv, inv


def norm_back(up, n, inv, gain):
    w = up * gain
    return inv * (w - jnp.mean(w, axis=-1, keepdims=True) - n * jnp.mean(w * n, axis=-1, keepdims=True))


def col_sum(v):
    return jnp.sum(v, axis=0, keepdims=True)


def turned(g):
    return 2 * (g % 2) + g // 2


def ffn_kernel(owned, x_ref, cot_ref, ct_ref, w1_ref, w2_ref, wo_ref, vec_ref, mo_ref, m1_ref, m2_ref,
               out_ref, res_ref, dct_ref, so_ref, s1_ref, s2_ref, gv_ref, g1_ref, g2_ref, go_ref):
    step = pl.program_id(0)
    T = x_ref.shape[1]
    vec = lambda i: vec_ref[i : i + 1, :]

    @pl.when(step == 0)
    def _():
        g1_ref[...] = jnp.zeros_like(g1_ref)
        g2_ref[...] = jnp.zeros_like(g2_ref)
        go_ref[...] = jnp.zeros_like(go_ref)
        gv_ref[...] = jnp.zeros_like(gv_ref)

    h1 = x_ref[0].astype(F32) + (nn(ct_ref[0].T, wo_ref[...]) + vec(6))
    n1, inv1 = norm(h1)
    first = n1 * vec(0) + vec(1)
    fl = first.astype(BF16)
    inner = lambda g: nn(fl[:, window(g) : window(g) + 256], w1_ref[g]) + vec(8 + g)
    active, slope, branch = [], [], []
    ahead = inner(0)
    for g in range(4):
        now, ahead = ahead, (inner(g + 1) if g < 3 else None)
        a, sl = gelu_parts(now)
        active.append(a.astype(BF16))
        slope.append(sl)
        branch.append(nt(active[g], w2_ref[g]))
    h2 = first + (join(branch) + vec(7))
    n2, inv2 = norm(h2)
    out_ref[0] = (n2 * vec(2) + vec(3)).astype(BF16)
    dy = cot_ref[0].astype(F32)
    dh2 = norm_back(dy, n2, inv2, vec(2))
    dbl = dh2.astype(BF16)
    dbt = dbl.T
    flt = fl.T
    ones = jnp.ones((16, T), BF16)
    dfirst = []
    gb = []
    for g in range(4):
        da = nn(dbl[:, window(g) : window(g) + 256], w2_ref[g])
        di = (da * slope[g]).astype(BF16)
        dfirst.append(nt(di, w1_ref[g]))
        g2_ref[g] += nn(dbt[192 * g : 192 * g + 192, :], active[g])
        ext = nn(jnp.concatenate([flt[192 * g : 192 * g + 192, :], ones], axis=0), di)
        g1_ref[g] += ext[:192]
        gb.append(ext[192:193])
    df = dh2 + join(dfirst)
    dh1 = norm_back(df, n1, inv1, vec(0))
    dat = dh1.astype(BF16)
    res_ref[0] = dat
    go_ref[...] += nn(ct_ref[0], dat)
    dct_ref[0] = nt(wo_ref[...], dat).astype(BF16)
    z = jnp.zeros((1, dy.shape[1]), F32)
    gv_ref[...] += jnp.concatenate(
        [col_sum(df * n1), col_sum(df), col_sum(dy * n2), col_sum(dy), z, z, col_sum(dat.astype(F32)), col_sum(dbl.astype(F32))] + gb, axis=0)

    @pl.when(step == pl.num_programs(0) - 1)
    def _():
        d, n = lax.axis_index("dp"), lax.axis_index("narrow")
        slim, wide = m1_ref.shape[1:]
        big = mo_ref.shape[2]
        sel_l = hot((wide, 768), n * wide, 0)
        sel_s = hot((192, slim), 0, d * slim)
        placed = nt(hot((768, big), 0, d * big), (0.95 * mo_ref[0]).astype(BF16)).astype(BF16)
        value = go_ref[...] + nn(placed, sel_l)
        for q in range(4):
            put_blocks(so_ref, 1152 * q, value[192 * q : 192 * q + 192])
        for dst, g_ref, m_ref in ((s1_ref, g1_ref, m1_ref), (s2_ref, g2_ref, m2_ref)):
            for g in range(4):
                placed = nn(sel_s, (0.95 * m_ref[g]).astype(BF16)).astype(BF16)
                value = g_ref[g] + nn(placed, sel_l)
                if owned:
                    put_blocks(dst, 576 * g, value[:, :384])
                    put_blocks(dst, 2304 + 576 * turned(g), value[:, 384:])
                else:
                    put_blocks(dst, 1152 * g, value)
        for dst in (so_ref, s1_ref, s2_ref):
            if dst.shape[0] > 4608:
                dst[4608:, :] = jnp.zeros((dst.shape[0] - 4608, 128), BF16)


def ffn(tokens, cot, ct, w1, w2, wo, vec, mo, m1, m2, rows, owned):
    n, seq, d = tokens.shape
    T = seq
    act = pl.BlockSpec((1, T, d), lambda i: (i, 0, 0))
    actt = pl.BlockSpec((1, d, T), lambda i: (i, 0, 0))
    full = lambda *s: pl.BlockSpec(s, lambda i: (0,) * len(s))
    return pl.pallas_call(
        functools.partial(ffn_kernel, owned),
        grid=(n,),
        out_shape=[
            jax.ShapeDtypeStruct((n, seq, d), BF16),
            jax.ShapeDtypeStruct((n, seq, d), BF16),
            jax.ShapeDtypeStruct((n, d, seq), BF16),
        ]
        + [jax.ShapeDtypeStruct((rows, 128), BF16)] * 3
        + [jax.ShapeDtypeStruct((12, 768), F32)],
        in_specs=[act, act, actt, full(4, 256, 768), full(4, 256, 768), full(768, 768), full(12, 768), full(*mo.shape), full(*m1.shape), full(*m2.shape)],
        out_specs=[act, act, actt] + [full(rows, 128)] * 3 + [full(12, 768)],
        scratch_shapes=[
            pltpu.VMEM((4, 192, 768), F32), pltpu.VMEM((4, 192, 768), F32), pltpu.VMEM((768, 768), F32),
        ],
        compiler_params=pltpu.CompilerParams(vmem_limit_bytes=60 * 2**20),
    )(tokens, cot, ct, w1, w2, wo, vec, mo, m1, m2)


class Place:
    def __init__(self, dp, narrow):
        self.X = 2 if dp % 2 == 0 else 1
        self.C = 2 if narrow % 2 == 0 else 1
        self.Z, self.Y = dp // self.X, narrow // self.C

    def locate(self):
        d, n = lax.axis_index("dp"), lax.axis_index("narrow")
        self.z, self.x = d // self.X, lax.rem(d, self.X)
        self.y, self.c = n // self.C, lax.rem(n, self.C)

    def count(self):
        return self.Z + self.X + self.Y + self.C - 4

    def at(self, axis, j):
        return lax.rem(getattr(self, axis) + j, getattr(self, axis.upper()))

    def device(self, axis, j):
        where = {a: getattr(self, a) for a in "zxyc"}
        where[axis] = self.at(axis, j)
        return (where["z"] * self.X + where["x"], where["y"] * self.C + where["c"])

    def other(self, dx, dy, c):
        return (self.z * self.X + lax.rem(self.x + dx, self.X), lax.rem(self.y + dy, self.Y) * self.C + c)

    def barrier(self, corner=False):
        self.greet(corner)
        self.meet(corner)

    def greet(self, corner=False):
        sem = pltpu.get_barrier_semaphore()
        if corner:
            for c in range(self.C):
                pl.semaphore_signal(sem, inc=1, device_id=self.other(1, 1, c), device_id_type=MESH)
            for dx, dy in ((1, 0), (0, 1)):
                pl.semaphore_signal(sem, inc=1, device_id=self.other(dx, dy, 1 - self.c), device_id_type=MESH)
        for axis in "zxyc":
            for j in range(1, getattr(self, axis.upper())):
                pl.semaphore_signal(sem, inc=1, device_id=self.device(axis, j), device_id_type=MESH)

    def meet(self, corner=False):
        pl.semaphore_wait(pltpu.get_barrier_semaphore(), self.count() + 4 * int(corner))


class Wires:
    def __init__(self, place, send_sem, recv_sem):
        self.place, self.send_sem, self.recv_sem, self.makers = place, send_sem, recv_sem, []

    def plan(self, src, dst, axis, j):
        return self.plan_to(src, dst, lambda: self.place.device(axis, j))

    def plan_to(self, src, dst, device):
        k = len(self.makers)
        self.makers.append(
            lambda: pltpu.make_async_remote_copy(
                src_ref=src(),
                dst_ref=dst(),
                send_sem=self.send_sem.at[k],
                recv_sem=self.recv_sem.at[k],
                device_id=device(),
                device_id_type=MESH,
            )
        )
        return k

    def start(self, copies):
        for k in copies:
            self.makers[k]().start()

    def arrive(self, copies):
        for k in copies:
            self.makers[k]().wait_recv()

    def leave(self, copies):
        for k in copies:
            self.makers[k]().wait_send()

    def finish(self, skip=()):
        self.leave([k for k in range(len(self.makers)) if k not in skip])


def gather_copies(p):
    return (p.Z - 1) + p.Z * ((p.X - 1) + (p.Y - 1) + 2 * (p.X - 1) * (p.Y - 1) + (p.C - 1))


def gather_steps(p, wires, buf, half):
    z, x, y, c = p.z, p.x, p.y, p.c
    rest = buf.shape[4] - half

    def same(at):
        return (lambda: buf.at[at()],) * 2

    along, first, second, last = {}, {}, {}, {}
    for j in range(1, p.Z):
        along[j] = wires.plan(*same(lambda: (z, c, x, y)), "z", j)
    for i in range(p.Z):
        from_z = lambda i=i: p.at("z", p.Z - i) if i else z
        mine = lambda f=from_z: (f(), c, x, y)
        first[i] = [wires.plan(*same(mine), "x", j) for j in range(1, p.X)] + [wires.plan(*same(mine), "y", j) for j in range(1, p.Y)]
        second[i] = []
        for j in range(1, p.X):
            part = lambda f=from_z, j=j: (f(), c, p.at("x", p.X - j), y, pl.ds(0, half))
            second[i] += [wires.plan(*same(part), "y", q) for q in range(1, p.Y)]
        for j in range(1, p.Y):
            part = lambda f=from_z, j=j: (f(), c, x, p.at("y", p.Y - j), pl.ds(half, rest))
            second[i] += [wires.plan(*same(part), "x", q) for q in range(1, p.X)]
        last[i] = [wires.plan(*same(lambda f=from_z: (f(), c)), "c", j) for j in range(1, p.C)]

    def step(t):
        if t == 0:
            wires.start(along.values())
        if t < p.Z:
            if t:
                wires.arrive([along[t]])
            wires.start(first[t])
        if 1 <= t <= p.Z:
            wires.arrive(first[t - 1])
            wires.start(second[t - 1])
        if 2 <= t <= p.Z + 1:
            wires.arrive(second[t - 2])
            wires.start(last[t - 2])
        if t == p.Z + 2:
            for i in last:
                wires.arrive(last[i])

    return [functools.partial(step, t) for t in range(p.Z + 3)]


class Shares:
    def __init__(self, p, rows):
        cells = p.X * p.Y * p.Z
        unit = 16 * cells * p.C
        units = -(-rows // unit)
        self.a, self.b = 16 * ((units + 1) // 2), 16 * max(units // 2, 1)
        self.per_core = cells * (self.a + self.b)
        self.rows = p.C * self.per_core
        self.cells = cells
        self.copies = 2 * ((p.C - 1) + 2 * ((p.X - 1) + (p.Y - 1)) + 2 * (p.Z - 1))

    def scratch(self, p):
        a, b = self.a, self.b
        kinds = [
            (self.per_core,),
            (p.C - 1, self.per_core),
            (p.X - 1, p.Y * p.Z * a),
            (p.Y - 1, p.X * p.Z * b),
            (p.Y - 1, p.Z * a),
            (p.X - 1, p.Z * b),
            (p.Z - 1, a),
            (p.Z - 1, b),
        ]
        return [pltpu.VMEM(k + (128,), BF16) for k in kinds] + [pltpu.SemaphoreType.DMA((self.copies,))] * 2


def spread(start, size):
    return pl.ds(pl.multiple_of(start, 16), size)


def add_into(dst, at, parts):
    total = dst[at, :].astype(F32)
    for part in parts:
        total = total + part.astype(F32)
    dst[at, :] = total.astype(BF16)


def sum_steps(p, s, src, out, scratch):
    held, from_c, a1, b1, a2, b2, a3, b3, send_sem, recv_sem = scratch
    wires = Wires(p, send_sem, recv_sem)
    a, b, per = s.a, s.b, s.per_core
    ax, by = p.Y * p.Z * a, p.X * p.Z * b
    in_a = lambda x, y=0, z=0: ((x * p.Y + y) * p.Z + z) * a
    in_b = lambda y, x=0, z=0: s.cells * a + ((y * p.X + x) * p.Z + z) * b
    x, y, z, c = p.x, p.y, p.z, p.c
    base = c * per

    def cut(ref, start, size):
        return lambda: ref.at[spread(start(), size)]

    def both(start, size):
        return (cut(out, start, size),) * 2

    def slot(ref, j):
        return lambda: ref.at[j - 1]

    sends = [[] for _ in range(8)]
    for j in range(1, p.C):
        sends[0].append(wires.plan(cut(src, lambda j=j: p.at("c", j) * per, per), slot(from_c, j), "c", j))
        sends[7].append(wires.plan(*both(lambda: base, per), "c", j))
    for j in range(1, p.X):
        sends[1].append(wires.plan(cut(held, lambda j=j: in_a(p.at("x", j)), ax), slot(a1, j), "x", j))
        sends[2].append(wires.plan(cut(held, lambda j=j: in_b(y, p.at("x", j)), p.Z * b), slot(b2, j), "x", j))
        sends[5].append(wires.plan(*both(lambda: base + in_b(y, x), p.Z * b), "x", j))
        sends[6].append(wires.plan(*both(lambda: base + in_a(x), ax), "x", j))
    for j in range(1, p.Y):
        sends[1].append(wires.plan(cut(held, lambda j=j: in_b(p.at("y", j)), by), slot(b1, j), "y", j))
        sends[2].append(wires.plan(cut(held, lambda j=j: in_a(x, p.at("y", j)), p.Z * a), slot(a2, j), "y", j))
        sends[5].append(wires.plan(*both(lambda: base + in_a(x, y), p.Z * a), "y", j))
        sends[6].append(wires.plan(*both(lambda: base + in_b(y), by), "y", j))
    for j in range(1, p.Z):
        sends[3].append(wires.plan(cut(held, lambda j=j: in_a(x, y, p.at("z", j)), a), slot(a3, j), "z", j))
        sends[3].append(wires.plan(cut(held, lambda j=j: in_b(y, x, p.at("z", j)), b), slot(b3, j), "z", j))
        sends[4].append(wires.plan(*both(lambda: base + in_a(x, y, z), a), "z", j))
        sends[4].append(wires.plan(*both(lambda: base + in_b(y, x, z), b), "z", j))

    def total(ref, at, size, parts, count):
        value = ref[spread(at, size), :].astype(F32)
        for j in range(count):
            value = value + parts[j].astype(F32)
        return value.astype(BF16)

    def step(t):
        if t:
            wires.arrive(sends[t - 1])
        if t == 1:
            held[...] = total(src, base, per, from_c, p.C - 1)
        if t == 2:
            held[spread(in_a(x), ax), :] = total(held, in_a(x), ax, a1, p.X - 1)
            held[spread(in_b(y), by), :] = total(held, in_b(y), by, b1, p.Y - 1)
        if t == 3:
            held[spread(in_a(x, y), p.Z * a), :] = total(held, in_a(x, y), p.Z * a, a2, p.Y - 1)
            held[spread(in_b(y, x), p.Z * b), :] = total(held, in_b(y, x), p.Z * b, b2, p.X - 1)
        if t == 4:
            out[spread(base + in_a(x, y, z), a), :] = total(held, in_a(x, y, z), a, a3, p.Z - 1)
            out[spread(base + in_b(y, x, z), b), :] = total(held, in_b(y, x, z), b, b3, p.Z - 1)
        if t < 8:
            wires.start(sends[t])
        else:
            wires.finish()

    return [functools.partial(step, t) for t in range(9)]


def at_turn(turn, steps):
    for i, todo in enumerate(steps):
        if todo:

            @pl.when(turn == i)
            def _():
                for step in todo:
                    step()


def dealt(steps, turns):
    return [steps[len(steps) * i // turns : len(steps) * (i + 1) // turns] for i in range(turns)]


def fold(t, odd):
    rows, wide = t.shape
    if wide % 128 == 64:
        body = jnp.where(odd, t[:, 64:], t[:, : wide - 64])
        edge = jnp.where(odd, t[:, :64], t[:, wide - 64 :])
        a, b = edge[: rows // 2], edge[rows // 2 :]
        tiles = [body[:, 128 * j : 128 * j + 128] for j in range(wide // 128)]
        tiles.append(jnp.concatenate([jnp.where(odd, b, a), jnp.where(odd, a, b)], axis=1))
        return jnp.concatenate(tiles, axis=0)
    need = -(-wide // 128) * 128
    t = jnp.concatenate([t, jnp.zeros((rows, need - wide), t.dtype)], axis=1) if need > wide else t
    return jnp.concatenate([t[:, 128 * j : 128 * j + 128] for j in range(need // 128)], axis=0)


def fold_rows(rows, wide):
    return rows * (wide // 128) + rows // 2 if wide % 128 == 64 else rows * (-(-wide // 128))


def unfold(p, buf, base, rows, wide):
    out = []
    lane = lax.broadcasted_iota(jnp.int32, (rows // 2, 128), 1)
    size = fold_rows(rows, wide)
    for z in range(p.Z):
        for x in range(p.X):
            tiles = []
            for y in range(p.Y):
                got = [buf[z, c, x, y, base : base + size, :].astype(F32) for c in range(p.C)]
                if wide % 128 == 64:
                    k = wide // 128
                    even, odd = got
                    tiles += [even[rows * j : rows * j + rows] for j in range(k)]
                    e, o = even[rows * k :], odd[rows * k :]
                    top = jnp.where(lane < 64, e, o)
                    low = pltpu.roll(jnp.where(lane < 64, o, e), 64, 1)
                    tiles.append(jnp.concatenate([top, low], axis=0))
                    tiles += [odd[rows * j : rows * j + rows] for j in range(k)]
                else:
                    k = size // rows
                    for c in range(p.C):
                        t = jnp.concatenate([got[c][rows * j : rows * j + rows] for j in range(k)], axis=1).astype(BF16)
                        tiles.append(nn(t, hot((128 * k, 768), (y * p.C + c) * wide, 0)) if 128 * k == wide else nn(t, hot_cut((128 * k, 768), (y * p.C + c) * wide, wide)))
            if wide % 128 == 64:
                out.append(jnp.concatenate(tiles, axis=1))
            else:
                out.append(functools.reduce(lambda a, b: a + b, tiles))
    return out


def hot_cut(shape, at, limit):
    rows = lax.broadcasted_iota(jnp.int32, shape, 0)
    cols = lax.broadcasted_iota(jnp.int32, shape, 1)
    return jnp.logical_and(rows + at == cols, rows < limit).astype(BF16)


def open_kernel(p, len_ref, x_ref, wq_ref, wo_ref, w1_ref, w2_ref, vec_ref,
                qt_out, k_out, kt_out, v_out, ct_out, lse_ref, w1_out, w2_out, wo_out, wt_out,
                bufq, bufr, win_s, qt_s, k_s, kt_s, v_s, ct_s, vt_s, bias_s, vcol_s, send_q, recv_q, send_r, recv_r, out_sem):
    p.locate()
    p.greet()
    n_rows, seq = x_ref.shape[:2]
    odd = lax.rem(lax.axis_index("narrow"), 2) == 1
    slim, tall = wq_ref.shape[1:]
    qrows = bufq.shape[4]
    for c in range(3):
        t = jnp.concatenate([wq_ref[4 * c + g] for g in range(4)], axis=0).T
        t = jnp.concatenate([t, jnp.zeros((tall, 128 - 4 * slim), F32)], axis=1)
        bufq[p.z, p.c, p.x, p.y, c * tall : c * tall + tall, :] = t.astype(BF16)
    if qrows > 3 * tall:
        bufq[p.z, p.c, p.x, p.y, 3 * tall :, :] = jnp.zeros((qrows - 3 * tall, 128), BF16)
    rows, wide = 4 * slim, 4 * tall
    size = fold_rows(rows, wide)
    big = wo_ref.shape[2]
    shards = [nt(hot((big, big), 0, 0), wo_ref[0].astype(BF16))]
    shards += [jnp.concatenate([r[g] for g in range(4)], axis=0) for r in (w1_ref, w2_ref)]
    folded = jnp.concatenate([fold(t, odd) for t in shards], axis=0)
    if bufr.shape[4] > 3 * size:
        folded = jnp.concatenate([folded, jnp.zeros((bufr.shape[4] - 3 * size, 128), F32)], axis=0)
    bufr[p.z, p.c, p.x, p.y] = folded.astype(BF16)
    p.meet()
    wires_q, wires_r = Wires(p, send_q, recv_q), Wires(p, send_r, recv_r)
    steps_q = gather_steps(p, wires_q, bufq, qrows // 32 * 16)
    steps_r = gather_steps(p, wires_r, bufr, bufr.shape[4] // 32 * 16)
    for i, step in enumerate(steps_q):
        step()
        if i == R_FIRST:
            steps_r[0]()
    total = jnp.zeros((3 * 192, 1024), F32)
    dp = p.Z * p.X
    for pair in range(dp // 2):
        tiles = []
        for d in (2 * pair, 2 * pair + 1):
            z, x = d // p.X, d % p.X
            got = [bufq[z, c, x, y].astype(F32) for y in range(p.Y) for c in range(p.C)]
            tiles.append(jnp.concatenate([b[c * tall : c * tall + tall] for c in range(3) for b in got], axis=0))
        r = lax.broadcasted_iota(jnp.int32, (256, 1), 0)
        q = jnp.where(r < 128, r, r - 128)
        g = (q >= slim).astype(jnp.int32) + (q >= 2 * slim).astype(jnp.int32) + (q >= 3 * slim).astype(jnp.int32)
        col = 256 * g + jnp.where(jnp.logical_or(g == 1, g == 3), 64, 0) + jnp.where(r < 128, 2 * pair * slim, (2 * pair + 1) * slim) + q - g * slim
        col = jnp.where(q < 4 * slim, col, -1)
        place = (lax.broadcasted_iota(jnp.int32, (256, 1024), 1) == col).astype(BF16)
        total = total + nn(jnp.concatenate(tiles, axis=1).astype(BF16), place)
    win_s[...] = jnp.zeros_like(win_s)
    for g in range(4):
        off = 64 * (g % 2)
        stack = total[:, 256 * g : 256 * g + 256].astype(BF16)
        for c in range(3):
            win_s[c, g, off : off + 192, :] = stack[192 * c : 192 * c + 192]
        wt_out[g] = nt(hot((192, 256), off, 0), stack).astype(BF16)
    vcol_s[...] = vec_ref[0:8, :].T
    turns = dealt(steps_r[1:], 3 * n_rows)

    def out_copies(row, which=range(5)):
        pairs = ((qt_s, qt_out), (k_s, k_out), (kt_s, kt_out), (v_s, v_out), (ct_s, ct_out))
        return [pltpu.make_async_copy(pairs[i][0].at[row], pairs[i][1].at[row], out_sem.at[row, i]) for i in which]

    def one_row(row, carry):
        same = ids(len_ref, row, (seq, seq), 0) == ids(len_ref, row, (seq, seq), 1)
        bias_s[...] = jnp.where(same, 0.0, -1e30)
        for g in range(4):
            lo = window(g)
            xw = x_ref[row, :, lo : lo + 256]
            off = 64 * (g % 2)
            r = slice(192 * g, 192 * g + 192)
            q = nt(win_s[0, g, off : off + 192, :], xw) + vcol_s[r, 4:5]
            qt_s[row, r, :] = q.astype(BF16) * BF16(0.125)
            kt_s[row, r, :] = nt(win_s[1, g, off : off + 192, :], xw).astype(BF16)
            v = nt(win_s[2, g, off : off + 192, :], xw) + vcol_s[r, 5:6]
            vt_s[r, :] = v.astype(BF16)
        wide_of = lambda c: join([nt(x_ref[row, :, window(g) : window(g) + 256], win_s[c, g]) for g in range(4)])
        k_s[row] = wide_of(1).astype(BF16)
        v_s[row] = (wide_of(2) + vec_ref[5:6, :]).astype(BF16)
        for copy in out_copies(row, range(4)):
            copy.start()

        def four(j, carry):
            heads = [(pl.multiple_of(256 * j + 128 * u, 128), e) for u in range(2) for e in range(2)]
            spots = [pl.ds(pl.multiple_of(lo + 64 * e, 64), 64) for lo, e in heads]
            scores = []
            for (lo, e), at in zip(heads, spots):
                qh = qt_s[row, at, :]
                none = jnp.zeros_like(qh)
                scores.append(nn(k_s[row, :, pl.ds(lo, 128)], jnp.concatenate([none, qh] if e else [qh, none], axis=0)))
            soft = []
            for s in scores:
                s = s + bias_s[...]
                m = jnp.max(s, axis=0, keepdims=True)
                ex = jnp.exp(s - m)
                soft.append((m, ex.astype(BF16), jnp.sum(ex, axis=0, keepdims=True)))
            for i, (at, (m, ex, tot)) in enumerate(zip(spots, soft)):
                ct_s[row, at, :] = (nn(vt_s[at, :], ex) * (1.0 / tot)).astype(BF16)
                lse_ref[row, pl.ds(4 * j + i, 1), :] = m + jnp.log(tot)
            at_turn(row * 3 + j, turns)
            return carry

        lax.fori_loop(0, 3, four, 0)
        out_copies(row, (4,))[0].start()
        return carry

    lax.fori_loop(0, n_rows, one_row, 0)
    wires_q.finish()
    wires_r.finish()
    whole = unfold(p, bufr, 0, rows, wide)
    wo_out[...] = jnp.concatenate(whole, axis=0).astype(BF16)
    for i, dst in enumerate((w1_out, w2_out)):
        whole = unfold(p, bufr, (i + 1) * size, rows, wide)
        dst[...] = jnp.zeros_like(dst)
        for g in range(4):
            off = 64 * (g % 2)
            dst[g, off : off + 192, :] = jnp.concatenate([b[g * slim : g * slim + slim] for b in whole], axis=0).astype(BF16)
    for row in range(n_rows):
        for copy in out_copies(row):
            copy.wait()


def opening(p, lengths, tokens, wq, wo, w1, w2, vec, ident):
    n, seq, d = tokens.shape
    slim, tall = wq.shape[1:]
    up = lambda r, m: -(-r // m) * m
    qrows = up(3 * tall, 32)
    rrows = up(3 * fold_rows(4 * slim, 4 * tall), 32)
    count = gather_copies(p)
    hbm = pl.BlockSpec(memory_space=pl.ANY)
    act = lambda a, b: jax.ShapeDtypeStruct((n, a, b), BF16)
    return pl.pallas_call(
        functools.partial(open_kernel, p),
        out_shape=[act(d, seq), act(seq, d), act(d, seq), act(seq, d), act(d, seq), jax.ShapeDtypeStruct((n, 16, seq), F32)]
        + [jax.ShapeDtypeStruct((4, 256, 768), BF16)] * 2
        + [jax.ShapeDtypeStruct((768, 768), BF16), jax.ShapeDtypeStruct((4, 192, 576), BF16)],
        in_specs=[pl.BlockSpec(memory_space=pltpu.SMEM)] + [VMEM] * 6,
        out_specs=[hbm] * 5 + [VMEM] * 5,
        scratch_shapes=[
            pltpu.VMEM((p.Z, p.C, p.X, p.Y, qrows, 128), BF16),
            pltpu.VMEM((p.Z, p.C, p.X, p.Y, rrows, 128), BF16),
            pltpu.VMEM((3, 4, 256, 256), BF16),
            pltpu.VMEM((n, d, seq), BF16), pltpu.VMEM((n, seq, d), BF16), pltpu.VMEM((n, d, seq), BF16), pltpu.VMEM((n, seq, d), BF16), pltpu.VMEM((n, d, seq), BF16),
            pltpu.VMEM((d, seq), BF16), pltpu.VMEM((seq, seq), F32), pltpu.VMEM((d, 8), F32),
            pltpu.SemaphoreType.DMA((count,)), pltpu.SemaphoreType.DMA((count,)),
            pltpu.SemaphoreType.DMA((count,)), pltpu.SemaphoreType.DMA((count,)),
            pltpu.SemaphoreType.DMA((n, 5)),
        ],
        compiler_params=pltpu.CompilerParams(collective_id=ident, has_side_effects=True, vmem_limit_bytes=60 * 2**20),
    )(lengths, tokens, wq, wo, w1, w2, vec)


def on_diagonal(n):
    return lax.broadcasted_iota(jnp.int32, (n, n), 0) == lax.broadcasted_iota(jnp.int32, (n, n), 1)


def ns_start(values):
    return [y * (1.0 / (jnp.sqrt(jnp.sum(y * y)) + 1e-07)) for y in values]


def ns_poly(values):
    n = values[0].shape[0]
    diag = on_diagonal(n)
    lows = [y.astype(BF16) for y in values]
    grams = [nt(l, l) for l in lows]
    mids = [jnp.sum(jnp.where(diag, g, 0.0)) * (1.0 / n) for g in grams]
    rest = [jnp.where(diag, g - m, g) for g, m in zip(grams, mids)]
    lowr = [r.astype(BF16) for r in rest]
    squares = [nn(r, r) for r in lowr]
    return mids, [((ns_second + 2.0 * ns_third * m) * r + ns_third * s).astype(BF16) for m, r, s in zip(mids, rest, squares)]


def ns_step(values, mids, polys):
    moved = [nn(q, y.astype(BF16)) for q, y in zip(polys, values)]
    return [(ns_first + ns_second * m + ns_third * m * m) * y + t for m, y, t in zip(mids, values, moved)]


def close_kernel(p, shares, *refs):
    (len_ref, wt_ref, so_ref, s1_ref, s2_ref, gv_ref, gmq_ref, wq_ref, wo_ref, w1_ref, w2_ref, vec_ref, vm1_ref, vm2_ref,
     x_hbm, qt_hbm, k_hbm, kt_hbm, v_hbm, ct_hbm, lse_ref, dct_hbm, res_hbm,
     gt_ref, mq_ref, mo_ref, m1_ref, m2_ref, nq_ref, no_ref, n1_ref, n2_ref, f_ref, s_ref, v_ref,
     x_s, qt_s, k_s, kt_s, v_s, ct_s, dct_s, res_s, bias_s, dq_s, dk_s, dv_s, gq_s, gv2_s, sq_s, oo_s, o1_s, o2_s, oq_s,
     y_s, po_s, pf_s, mid_s, xo_s, xf_s, xq_s, xo_r, xf_r, xq_r, in_sem, x_send, x_recv) = refs[: 35 + 32]
    rest = refs[35 + 32 :]
    p.locate()
    d, n = lax.axis_index("dp"), lax.axis_index("narrow")
    n_rows, seq = x_s.shape[:2]
    pairs = ((qt_hbm, qt_s), (k_hbm, k_s), (dct_hbm, dct_s), (v_hbm, v_s), (ct_hbm, ct_s), (kt_hbm, kt_s), (x_hbm, x_s), (res_hbm, res_s))

    def loads(row):
        return [pltpu.make_async_copy(src.at[row], dst.at[row], in_sem.at[row, i]) for i, (src, dst) in enumerate(pairs)]

    for row in range(n_rows):
        for copy in loads(row):
            copy.start()
    p.barrier()
    sums = [sum_steps(p, s, src, out, rest[10 * i : 10 * i + 10])
            for i, (s, src, out) in enumerate(zip(shares, (so_ref, s1_ref, s2_ref, sq_s), (oo_s, o1_s, o2_s, oq_s)))]
    o, f1, f2, q = sums
    for step in (o[0], f1[0], f2[0]):
        step()
    turns = dealt([o[1], f1[1], o[2], f2[1], o[3], f1[2], o[4], f2[2], o[5], f1[3], o[6], f2[3], o[7], f1[4], f2[4]], 6 * n_rows)
    gq_s[...] = jnp.zeros_like(gq_s)
    gv2_s[...] = jnp.zeros_like(gv2_s)
    lane = lax.broadcasted_iota(jnp.int32, (192, 256), 1)

    def one_row(row, carry):
        same = ids(len_ref, row, (seq, seq), 0) == ids(len_ref, row, (seq, seq), 1)
        bias_s[...] = jnp.where(same, 0.0, -1e30)
        for copy in loads(row):
            copy.wait()

        def pair(j, carry):
            lo = pl.multiple_of(128 * j, 128)
            kp, vp = k_s[row, :, pl.ds(lo, 128)], v_s[row, :, pl.ds(lo, 128)]
            for e in range(2):
                at = pl.ds(pl.multiple_of(lo + 64 * e, 64), 64)
                qh, dc = qt_s[row, at, :], dct_s[row, at, :]
                none = jnp.zeros_like(qh)
                wide = lambda a: jnp.concatenate([none, a] if e else [a, none], axis=0)
                delta = jnp.sum(dc.astype(F32) * ct_s[row, at, :].astype(F32), axis=0, keepdims=True)
                s = nn(kp, wide(qh)) + bias_s[...]
                ex = jnp.exp(s - lse_ref[row, pl.ds(2 * j + e, 1), :])
                de = nn(vp, wide(dc))
                ds = (ex * (de - delta)).astype(BF16)
                dv_s[at, :] = nt(dc, ex.astype(BF16)).astype(BF16)
                dk_s[at, :] = nt(qh, ds).astype(BF16)
                dq_s[at, :] = (nn(kt_s[row, at, :], ds) * 0.125).astype(BF16)
            at_turn(row * 6 + j, turns)
            return carry

        lax.fori_loop(0, 6, pair, 0)
        dx = []
        for g in range(4):
            lo = window(g)
            r = slice(192 * g, 192 * g + 192)
            cat = jnp.concatenate([dq_s[r, :], dk_s[r, :], dv_s[r, :]], axis=0)
            dx.append(nn(wt_ref[g], cat))
            gq = nn(cat, x_s[row, :, lo : lo + 256])
            keep = (lane < 192) if g % 2 == 0 else (lane >= 64)
            for c in range(3):
                gq_s[c, :, lo : lo + 256] += jnp.where(keep, gq[192 * c : 192 * c + 192], 0.0)
        gt_ref[row] = (res_s[row] + jnp.concatenate(dx, axis=0).T).astype(BF16)
        ones = jnp.ones((16, seq), BF16)
        gv2_s[0:1, :] += nt(ones, dq_s[...])[0:1]
        gv2_s[1:2, :] += nt(ones, dv_s[...])[0:1]
        return carry

    lax.fori_loop(0, n_rows, one_row, 0)
    slim, tall = gmq_ref.shape[1:]
    up = hot((192, tall), 0, n * tall)
    for c in range(3):
        held = jnp.zeros((tall, 768), F32)
        for g in range(4):
            held = held + tn((0.95 * gmq_ref[4 * c + g]).astype(BF16), hot((slim, 768), 192 * g + d * slim, 0))
        put_blocks(sq_s, 1152 * c, gq_s[c] + nn(up, held.astype(BF16)))
    gv = jnp.concatenate([gv_ref[0:4], gv2_s[0:2], gv_ref[6:12]], axis=0)
    tail = sq_s.shape[0] - 3456
    flat = jnp.concatenate([gv[:, 128 * j : 128 * j + 128] for j in range(6)] + [jnp.zeros((tail - 72, 128), F32)], axis=0)
    sq_s[3456:, :] = flat.astype(BF16)
    for step in (q[0], o[8], q[1]):
        step()
    wide, cols = w1_ref.shape[2], w1_ref.shape[1]
    sel_l = hot((wide, 768), n * wide, 0)
    sel_s = hot((cols, 192), d * cols, 0)
    big = wo_ref.shape[2]
    sel_b = hot((big, 768), d * big, 0)
    core0, core1 = p.c == 0, p.c == 1
    eight = lambda: [y_s[192 * i : 192 * i + 192, :] for i in range(8)]

    late = 3
    before = [[f1[5]], [f1[6]], [f1[7]], [q[5]], [q[7]]]
    between = [[q[2], f2[5]], [q[3], f2[6]], [q[4], f2[7], f1[8], f2[8]], [q[6]], [q[8]]]

    def sweep(t, carry):
        on0 = jnp.logical_and(core0, t < NS_STEPS)
        on1 = jnp.logical_and(core1, t >= late)

        @pl.when(jnp.logical_and(core0, t == 0))
        def _():
            y_s[0:768, :] = ns_start([wide_rows(oo_s, 0, 4).astype(F32)])[0]

        @pl.when(jnp.logical_and(core1, t == late))
        def _():
            for i, y in enumerate(ns_start([wide_rows(r, 1152 * g, 1).astype(F32) for r in (o1_s, o2_s) for g in range(4)])):
                y_s[192 * i : 192 * i + 192, :] = y

        @pl.when(on0)
        def _():
            mids, polys = ns_poly([y_s[0:768, :]])
            mid_s[0:1, :] = jnp.broadcast_to(mids[0], (1, 128))
            po_s[...] = polys[0]

        @pl.when(on1)
        def _():
            mids, polys = ns_poly(eight())
            for i in range(8):
                mid_s[i : i + 1, :] = jnp.broadcast_to(mids[i], (1, 128))
                pf_s[i] = polys[i]

        at_turn(t, before)

        @pl.when(on0)
        def _():
            y_s[0:768, :] = ns_step([y_s[0:768, :]], [mid_s[0:1, 0:1]], [po_s[...]])[0]

        @pl.when(on1)
        def _():
            for i, y in enumerate(ns_step(eight(), [mid_s[i : i + 1, 0:1] for i in range(8)], [pf_s[i] for i in range(8)])):
                y_s[192 * i : 192 * i + 192, :] = y

        at_turn(t, between)
        return carry

    lax.fori_loop(0, NS_STEPS + late, sweep, 0)
    wires = Wires(p, x_send, x_recv)
    mo_ref[0] = nt(sel_l, nn(sel_b, wide_rows(oo_s, 0, 4)).astype(BF16))
    for ref, m_ref in ((o1_s, m1_ref), (o2_s, m2_ref)):
        for g in range(4):
            m_ref[g] = nt(nn(sel_s, wide_rows(ref, 1152 * g, 1)).astype(BF16), sel_l)

    @pl.when(core0)
    def _():
        xo_s[...] = nn(sel_b, y_s[0:768, :].astype(BF16)).astype(BF16)

    @pl.when(core1)
    def _():
        for i in range(8):
            xf_s[cols * i : cols * i + cols, :] = nn(sel_s, y_s[192 * i : 192 * i + 192, :].astype(BF16)).astype(BF16)

    rows = [wide_rows(oq_s, 1152 * c, 1) for c in range(3)]
    spot = lambda g: hot_cut((256, 128), 0, 0)

    def square(parity):
        keep = (lane < 192) if parity == 0 else (lane >= 64)
        which = [(c, g) for c in range(3) for g in (parity, parity + 2)]
        ys = ns_start([jnp.where(keep, rows[c][:, window(g) : window(g) + 256].astype(F32), 0.0) for c, g in which])
        for i, y in enumerate(ys):
            y_s[192 * i : 192 * i + 192, :256] = y

        def turn(t, carry):
            ys = [y_s[192 * i : 192 * i + 192, :256] for i in range(6)]
            for i, y in enumerate(ns_step(ys, *ns_poly(ys))):
                y_s[192 * i : 192 * i + 192, :256] = y
            return carry

        lax.fori_loop(0, NS_STEPS, turn, 0)
        ys = [y_s[192 * i : 192 * i + 192, :256] for i in range(6)]
        for c in range(3):
            part = jnp.zeros((192, 128), F32)
            for (cc, g), y in zip(which, ys):
                if cc == c:
                    at = 64 * (g % 2) + d * slim
                    r = lax.broadcasted_iota(jnp.int32, (256, 128), 0) - at
                    q = lax.broadcasted_iota(jnp.int32, (256, 128), 1) - g * slim
                    sel = jnp.logical_and(r == q, jnp.logical_and(q >= 0, q < slim)).astype(BF16)
                    part = part + nn(y.astype(BF16), sel)
            xq_s[192 * c : 192 * c + 192, :] = part.astype(BF16)

    @pl.when(core0)
    def _():
        square(0)

    @pl.when(core1)
    def _():
        square(1)

    copies = [wires.plan(lambda a=a: a, lambda b=b: b, "c", 1) for a, b in ((xq_s, xq_r), (xo_s, xo_r), (xf_s, xf_r))]
    wires.start(copies)
    sel_o = hot((tall, 192), n * tall, 0)
    for c in range(3):
        mine = nn(sel_o, rows[c]).astype(BF16)
        for g in range(4):
            mq_ref[4 * c + g] = nt(hot((slim, 768), 192 * g + d * slim, 0), mine)
    vt = oq_s[3456 : 3456 + 80, :].astype(F32)
    grad = jnp.concatenate([vt[12 * j : 12 * j + 12] for j in range(6)], axis=1)
    first = 0.9 * vm1_ref[...] + 0.1 * grad
    second = 0.999 * vm2_ref[...] + 0.001 * grad * grad
    f_ref[...] = first
    s_ref[...] = second
    v_ref[...] = vec_ref[...] - adam_rate * (first * (1.0 / (1.0 - 0.9**STEP))) / (jnp.sqrt(second * (1.0 / (1.0 - 0.999**STEP))) + 1e-08)

    def fresh(w, own, longest):
        return w - muon_rate * (0.2 * math.sqrt(longest) * own + muon_decay * w)

    wires.arrive(copies)
    for c in range(3):
        both = (xq_s[192 * c : 192 * c + 192, :].astype(F32) + xq_r[192 * c : 192 * c + 192, :].astype(F32)).astype(BF16)
        mine = nn(sel_o, both).astype(BF16)
        for g in range(4):
            nq_ref[4 * c + g] = fresh(wq_ref[4 * c + g], nt(hot((slim, 128), g * slim, 0), mine), 192)
    xo = jnp.where(core0, xo_s[...], xo_r[...])
    no_ref[0] = fresh(wo_ref[0], nt(sel_l, xo), 768)
    for i, (w_ref, n_ref) in enumerate(((w1_ref, n1_ref), (w2_ref, n2_ref))):
        for g in range(4):
            at = slice(cols * (4 * i + g), cols * (4 * i + g) + cols)
            n_ref[g] = fresh(w_ref[g], nt(jnp.where(core1, xf_s[at, :], xf_r[at, :]), sel_l), 768)
    wires.finish()


def closing(p, shares, lengths, wt, so, s1, s2, gv, mq, weights, vec, vm1, vm2, acts, ident):
    tokens, lse = acts[0], acts[6]
    n, seq, d = tokens.shape
    slim = mq.shape[1]
    shape = lambda a: jax.ShapeDtypeStruct(a.shape, F32)
    outs = [jax.ShapeDtypeStruct(tokens.shape, BF16)] + [shape(w) for w in weights] * 2 + [shape(vec)] * 3
    hbm = pl.BlockSpec(memory_space=pl.ANY)
    tm, mt = pltpu.VMEM((n, seq, d), BF16), pltpu.VMEM((n, d, seq), BF16)
    flat = lambda r: pltpu.VMEM((r, 128), BF16)
    scratch = [tm, mt, tm, mt, tm, mt, mt, pltpu.VMEM((n, seq, d), BF16), pltpu.VMEM((seq, seq), F32)]
    scratch += [pltpu.VMEM((d, seq), BF16)] * 3 + [pltpu.VMEM((3, 192, 768), F32), pltpu.VMEM((8, 768), F32)]
    scratch += [flat(shares[3].rows)] + [flat(s.rows) for s in shares]
    scratch += [pltpu.VMEM((1536, 768), F32), pltpu.VMEM((768, 768), BF16), pltpu.VMEM((8, 192, 192), BF16), pltpu.VMEM((8, 128), F32)]
    scratch += [pltpu.VMEM((4 * slim, 768), BF16), pltpu.VMEM((8 * slim, 768), BF16), pltpu.VMEM((576, 128), BF16)] * 2
    scratch += [pltpu.SemaphoreType.DMA((n, 8)), pltpu.SemaphoreType.DMA((3,)), pltpu.SemaphoreType.DMA((3,))]
    for s in shares:
        scratch += s.scratch(p)
    return pl.pallas_call(
        functools.partial(close_kernel, p, shares),
        out_shape=outs,
        in_specs=[pl.BlockSpec(memory_space=pltpu.SMEM)] + [VMEM] * 13 + [hbm] * 6 + [VMEM] + [hbm] * 2,
        out_specs=[VMEM] * 12,
        scratch_shapes=scratch,
        compiler_params=pltpu.CompilerParams(collective_id=ident, has_side_effects=True, vmem_limit_bytes=62 * 2**20),
    )(lengths, wt, so, s1, s2, gv, mq, *weights, vec, vm1, vm2, *acts)


class Owned:
    def __init__(self, p, half):
        self.half, self.rows, self.copies = half, 8 * half, 4 + 2 * (p.Z - 1)
        self.kinds = [4 * half, 4 * half, 2 * half, half, (p.Z - 1) * (half // p.Z), half, half]

    def scratch(self):
        return [pltpu.VMEM((k, 128), BF16) for k in self.kinds] + [pltpu.SemaphoreType.DMA((self.copies,))] * 2


def owned_steps(p, s, src, scratch):
    held, from_c, r1, r2, r3, mine, other, send_sem, recv_sem = scratch
    wires = Wires(p, send_sem, recv_sem)
    h, q, z, c = s.half, s.half // p.Z, p.z, p.c
    first = jnp.where(c == 0, p.x, p.y)
    second = jnp.where(c == 0, p.y, p.x)
    cut = lambda ref, start, size: lambda: ref.at[spread(start(), size)]

    def partner(turn):
        along_x = c == turn
        x, y = jnp.where(along_x, 1 - p.x, p.x), jnp.where(along_x, p.y, 1 - p.y)
        return (z * p.X + x, y * p.C + c)

    sibling = lambda: p.device("c", 1)
    spot = lambda: (2 * first + second) * h
    sends = [
        [wires.plan_to(cut(src, lambda: (1 - c) * 4 * h, 4 * h), lambda: from_c, sibling)],
        [wires.plan_to(cut(held, lambda: (1 - first) * 2 * h, 2 * h), lambda: r1, lambda: partner(0))],
        [wires.plan_to(cut(held, lambda: (2 * first + 1 - second) * h, h), lambda: r2, lambda: partner(1))],
        [],
        [],
        [wires.plan_to(lambda: mine, lambda: other, sibling)],
    ]
    for j in range(1, p.Z):
        sends[3].append(wires.plan(cut(held, lambda j=j: spot() + p.at("z", j) * q, q), lambda j=j: r3.at[pl.ds((j - 1) * q, q)], "z", j))
        sends[4].append(wires.plan(*(cut(mine, lambda: z * q, q),) * 2, "z", j))

    def add(dst, to, ref, start, size, parts):
        value = ref[spread(start, size), :].astype(F32)
        for part in parts:
            value = value + part().astype(F32)
        dst[spread(to, size), :] = value.astype(BF16)

    def step(t):
        if 1 <= t <= 5:
            wires.arrive(sends[t - 1])
        if t == 1:
            add(held, 0, src, c * 4 * h, 4 * h, [lambda: from_c[...]])
        if t == 2:
            add(held, first * 2 * h, held, first * 2 * h, 2 * h, [lambda: r1[...]])
        if t == 3:
            add(held, spot(), held, spot(), h, [lambda: r2[...]])
        if t == 4:
            add(mine, z * q, held, spot() + z * q, q, [lambda j=j: r3[(j - 1) * q : j * q, :] for j in range(1, p.Z)])
        if t < 5:
            wires.start(sends[t])
        if t == 5:

            @pl.when(c == 0)
            def _():
                wires.start(sends[5])

        if t == 6:
            wires.finish(skip=sends[5])

            @pl.when(c == 0)
            def _():
                wires.leave(sends[5])

            @pl.when(c == 1)
            def _():
                wires.arrive(sends[5])

    return [functools.partial(step, t) for t in range(7)]


class Solo:
    def __init__(self, p, half):
        self.half, self.rows, self.copies = half, 8 * half, 1 + 4 + 4 * (p.Z - 1)
        q = (p.Z - 1) * (half // p.Z)
        self.kinds = [8 * half, 8 * half] + [2 * half, half, q] * 2 + [2 * half]

    def scratch(self):
        return [pltpu.VMEM((k, 128), BF16) for k in self.kinds] + [pltpu.SemaphoreType.DMA((self.copies,))] * 2


def solo_steps(p, s, src, scratch):
    held, from_c, a1, a2, a3, b1, b2, b3, mine, send_sem, recv_sem = scratch
    wires = Wires(p, send_sem, recv_sem)
    h, q, z = s.half, s.half // p.Z, p.z
    cut = lambda ref, start, size: lambda: ref.at[spread(start(), size)]
    over = [wires.plan_to(lambda: src, lambda: from_c, lambda: p.device("c", 1))]
    sends = [[], [], [], []]
    ways = (("x", "y", p.x, p.y, 0, a1, a2, a3, 0), ("y", "x", p.y, p.x, 4 * h, b1, b2, b3, h))
    for one, two, first, second, base, r1, r2, r3, to in ways:
        sends[0].append(wires.plan(cut(held, lambda f=first, b=base: b + (1 - f) * 2 * h, 2 * h), lambda r=r1: r, one, 1))
        sends[1].append(wires.plan(cut(held, lambda f=first, e=second, b=base: b + (2 * f + 1 - e) * h, h), lambda r=r2: r, two, 1))
        for j in range(1, p.Z):
            part = lambda f=first, e=second, b=base, j=j: b + (2 * f + e) * h + p.at("z", j) * q
            sends[2].append(wires.plan(cut(held, part, q), lambda r=r3, j=j: r.at[pl.ds((j - 1) * q, q)], "z", j))
            sends[3].append(wires.plan(*(cut(mine, lambda t=to: t + z * q, q),) * 2, "z", j))

    def add(dst, to, ref, start, size, parts):
        value = ref[spread(start, size), :].astype(F32)
        for part in parts:
            value = value + part.astype(F32)
        dst[spread(to, size), :] = value.astype(BF16)

    def give():
        wires.start(over)

    def gave():
        wires.leave(over)

    def step(t):
        wires.arrive(over if t == 0 else sends[t - 1])
        if t == 0:
            held[...] = (src[...].astype(F32) + from_c[...].astype(F32)).astype(BF16)
        for one, two, first, second, base, r1, r2, r3, to in ways:
            spot = base + (2 * first + second) * h
            if t == 1:
                add(held, base + first * 2 * h, held, base + first * 2 * h, 2 * h, [r1[...]])
            if t == 2:
                add(held, spot, held, spot, h, [r2[...]])
            if t == 3:
                add(mine, to + z * q, held, spot + z * q, q, [r3[(j - 1) * q : j * q, :] for j in range(1, p.Z)])
        if t < 4:
            wires.start(sends[t])
        else:
            wires.finish(skip=over)

    return give, gave, [functools.partial(step, t) for t in range(5)]


def canon(odd, base):
    r = lax.broadcasted_iota(jnp.int32, (256, 128), 0)
    s = lax.broadcasted_iota(jnp.int32, (256, 128), 1)
    channel = jnp.where(odd, jnp.where(r < 128, r + 64, r - 128), r)
    return jnp.where(r < 192, channel - base, -1000), s


def owner_kernel(p, shares, *refs):
    (len_ref, wt_ref, so_ref, s1_ref, s2_ref, gv_ref, gmq_ref, wq_ref, wo_ref, w1_ref, w2_ref, vec_ref, vm1_ref, vm2_ref,
     x_hbm, qt_hbm, k_hbm, kt_hbm, v_hbm, ct_hbm, lse_ref, dct_hbm, res_hbm,
     gt_ref, mq_ref, mo_ref, m1_ref, m2_ref, nq_ref, no_ref, n1_ref, n2_ref, f_ref, s_ref, v_ref,
     x_s, qt_s, k_s, kt_s, v_s, ct_s, dct_s, res_s, bias_s, dq_s, dk_s, dv_s, gq_s, gv2_s, sq_s, oo_s,
     yo_s, yf_s, yq_s, xo_s, xo_r, tmf_s, txf_s, tmq_s, txq_s, tv_s, rmf_s, rxf_s, rmq_s, rxq_s, rv_s,
     in_sem, x_send, x_recv) = refs[: 35 + 34]
    rest = refs[35 + 34 :]
    p.locate()
    p.greet(corner=True)
    d, n = lax.axis_index("dp"), lax.axis_index("narrow")
    core0, core1 = p.c == 0, p.c == 1
    n_rows, seq = x_s.shape[:2]
    pairs = ((qt_hbm, qt_s), (k_hbm, k_s), (dct_hbm, dct_s), (v_hbm, v_s), (ct_hbm, ct_s), (kt_hbm, kt_s), (x_hbm, x_s), (res_hbm, res_s))

    def loads(row):
        return [pltpu.make_async_copy(src.at[row], dst.at[row], in_sem.at[row, i]) for i, (src, dst) in enumerate(pairs)]

    for row in range(n_rows):
        for copy in loads(row):
            copy.start()
    o = sum_steps(p, shares[0], so_ref, oo_s, rest[:10])
    f1 = owned_steps(p, shares[1], s1_ref, rest[10:19])
    f2 = owned_steps(p, shares[2], s2_ref, rest[19:28])
    q_give, q_gave, q = solo_steps(p, shares[3], sq_s, rest[28:39])
    q_all = rest[36]
    f1_half, f1_other, f2_half, f2_other = rest[15], rest[16], rest[24], rest[25]
    p.meet(corner=True)
    for step in (o[0], f1[0], f2[0]):
        step()
    turns = [[] for _ in range(12 * n_rows)]
    for i, step in ((0, f1[1]), (5, o[2]), (6, f2[1]), (9, f1[2]), (10, o[3]), (14, f2[2]), (14, f1[3]), (16, o[4]), (18, f2[3]), (22, f1[4]), (23, o[5])):
        turns[i * n_rows // 2].append(step)
    gq_s[...] = jnp.zeros_like(gq_s)
    gv2_s[...] = jnp.zeros_like(gv2_s)
    lane = lax.broadcasted_iota(jnp.int32, (192, 256), 1)

    def one_row(row, carry):
        same = ids(len_ref, row, (seq, seq), 0) == ids(len_ref, row, (seq, seq), 1)
        bias_s[...] = jnp.where(same, 0.0, -1e30)
        for copy in loads(row):
            copy.wait()

        @pl.when(row == 0)
        def _():
            o[1]()

        def pair(j, carry):
            lo = pl.multiple_of(128 * j, 128)
            kp, vp = k_s[row, :, pl.ds(lo, 128)], v_s[row, :, pl.ds(lo, 128)]
            for e in range(2):
                at = pl.ds(pl.multiple_of(lo + 64 * e, 64), 64)
                qh, dc = qt_s[row, at, :], dct_s[row, at, :]
                none = jnp.zeros_like(qh)
                wide = lambda a: jnp.concatenate([none, a] if e else [a, none], axis=0)
                delta = jnp.sum(dc.astype(F32) * ct_s[row, at, :].astype(F32), axis=0, keepdims=True)
                s = nn(kp, wide(qh)) + bias_s[...]
                ex = jnp.exp(s - lse_ref[row, pl.ds(2 * j + e, 1), :])
                de = nn(vp, wide(dc))
                ds = (ex * (de - delta)).astype(BF16)
                dv_s[row, at, :] = nt(dc, ex.astype(BF16)).astype(BF16)
                dk_s[row, at, :] = nt(qh, ds).astype(BF16)
                dq_s[row, at, :] = (nn(kt_s[row, at, :], ds) * 0.125).astype(BF16)
                at_turn(row * 12 + 2 * j + e, turns)
            return carry

        lax.fori_loop(0, 6, pair, 0)
        for g in range(4):
            lo = window(g)
            r = slice(192 * g, 192 * g + 192)
            gq = nn(jnp.concatenate([dq_s[row, r, :], dk_s[row, r, :], dv_s[row, r, :]], axis=0), x_s[row, :, lo : lo + 256])
            keep = (lane < 192) if g % 2 == 0 else (lane >= 64)
            for c in range(3):
                gq_s[c, :, lo : lo + 256] += jnp.where(keep, gq[192 * c : 192 * c + 192], 0.0)
        ones = jnp.ones((16, seq), BF16)
        gv2_s[0:1, :] += nt(ones, dq_s[row])[0:1]
        gv2_s[1:2, :] += nt(ones, dv_s[row])[0:1]
        return carry

    lax.fori_loop(0, n_rows, one_row, 0)
    slim, tall = gmq_ref.shape[1:]
    half = shares[3].half
    up = hot((192, tall), 0, n * tall)
    values = []
    for c in range(3):
        held = jnp.zeros((tall, 768), F32)
        for g in range(4):
            held = held + tn((0.95 * gmq_ref[4 * c + g]).astype(BF16), hot((slim, 768), 192 * g + d * slim, 0))
        values.append(gq_s[c] + nn(up, held.astype(BF16)))
    gv = jnp.concatenate([gv_ref[0:4], gv2_s[0:2], gv_ref[6:12]], axis=0)
    lane = lax.broadcasted_iota(jnp.int32, (192, 128), 1)
    for g in range(4):
        lo = window(g)
        tiles = []
        edges = []
        for c in range(3):
            a, b = values[c][:, lo : lo + 128], values[c][:, lo + 128 : lo + 256]
            whole, edge = (b, pltpu.roll(a, 64, 1)) if g % 2 else (a, b)
            tiles.append(whole)
            edges.append(jnp.where(lane < 64, edge, 0.0))
        tiles.append(edges[0] + pltpu.roll(edges[1], 64, 1))
        tiles.append(edges[2][:96] + pltpu.roll(edges[2][96:], 64, 1))
        vec = [gv[0:8, 192 * g : 192 * g + 128]]
        vec.append(jnp.concatenate([gv[0:8, 192 * g + 128 : 192 * g + 192], jnp.zeros((8, 64), F32)], axis=1))
        vec += [gv[8 + g : 9 + g, 128 * j : 128 * j + 128] for j in range(6)]
        vec.append(jnp.zeros((2 * half - 864 - 22, 128), F32))
        flat = jnp.concatenate(tiles + vec, axis=0).astype(BF16)
        sq_s[g * half : g * half + half, :] = flat[:half]
        sq_s[(4 + turned(g)) * half : (5 + turned(g)) * half, :] = flat[half:]
    def blocks(a_ref, b_ref):
        return jnp.concatenate([r[192 * j : 192 * j + 192, :] for r in (a_ref, b_ref) for j in range(3)], axis=1)

    def grad_in(row):
        dx = []
        for g in range(4):
            r = slice(192 * g, 192 * g + 192)
            dx.append(nn(wt_ref[g], jnp.concatenate([dq_s[row, r, :], dk_s[row, r, :], dv_s[row, r, :]], axis=0)))
        gt_ref[row] = (res_s[row].astype(F32) + jnp.concatenate(dx, axis=0).T).astype(BF16)

    wires = Wires(p, x_send, x_recv)
    me = 2 * p.x + p.y
    odd = lax.rem(me, 2) == 1
    around = ((1, 0), (0, 1), (1, 1))

    def scatter(src, dst, cores=(1,)):
        return [
            wires.plan_to(
                lambda dx=dx, dy=dy: src.at[lax.rem(p.x + dx, 2), lax.rem(p.y + dy, 2)], lambda: dst.at[me], lambda dx=dx, dy=dy, c=c: p.other(dx, dy, c)
            )
            for dx, dy in around
            for c in cores
        ]

    early = [scatter(a, b) for a, b in ((tmf_s, rmf_s), (txf_s, rxf_s), (tmq_s, rmq_s), (tv_s, rv_s))]
    late = scatter(txq_s, rxq_s, (0, 1))
    late += [wires.plan_to(lambda: txq_s.at[p.x, p.y], lambda: rxq_s.at[me], lambda: p.device("c", 1))]
    late_on = {0: [late[0], late[2], late[4], late[6]], 1: [late[1], late[3], late[5]]}
    sibling = lambda: p.device("c", 1)
    pass_early = [wires.plan_to(lambda a=a: a, lambda a=a: a, sibling) for a in (rmf_s, rxf_s, rmq_s, rv_s)]
    pass_o = [wires.plan_to(lambda: xo_s, lambda: xo_r, sibling)]
    big = wo_ref.shape[2]
    sel_b = hot((big, 768), d * big, 0)
    wide, cols = w1_ref.shape[2], w1_ref.shape[1]

    def put_f(dst, pair):
        for x in range(2):
            sel = hot((cols, 192), (p.z * 2 + x) * cols, 0)
            part = jnp.concatenate([nn(sel, m) for m in pair], axis=0).astype(BF16)
            for y in range(2):
                dst[x, y] = part[:, 384 * y : 384 * y + 384]

    def put_q(dst, three):
        for x in range(2):
            part = jnp.zeros((192, 128), F32)
            for c, m in enumerate(three):
                at, s = canon(odd, (p.z * 2 + x) * slim)
                sel = jnp.logical_and(jnp.logical_and(at >= 0, at < slim), at + c * slim == s).astype(BF16)
                part = part + nn(m, sel)
            for y in range(2):
                dst[x, y] = part[96 * y : 96 * y + 96].astype(BF16)

    @pl.when(core0)
    def _():
        q_give()
        for step in (lambda: grad_in(0), o[6], f2[4], lambda: grad_in(1), f1[5], f2[5], o[7], o[8], f1[6], f2[6]):
            step()
        yo_s[...] = ns_start([wide_rows(oo_s, 0, 4).astype(F32)])[0]

        def turn(t, carry):
            y = yo_s[...]
            yo_s[...] = ns_step([y], *ns_poly([y]))[0]
            return carry

        lax.fori_loop(0, NS_STEPS, turn, 0)
        xo_s[...] = nn(sel_b, yo_s[...].astype(BF16)).astype(BF16)
        wires.start(pass_o)
        q_gave()

    @pl.when(core1)
    def _():
        for step in (q[0], o[6], f2[4], lambda: grad_in(0), q[1], lambda: grad_in(1), f1[5], f2[5], o[7], o[8], q[2], f1[6], f2[6]):
            step()
        for i, y in enumerate(ns_start([blocks(a, b).astype(F32) for a, b in ((f1_other, f1_half), (f2_other, f2_half))])):
            yf_s[i] = y

        def f_turn(t, carry):
            ys = [yf_s[i] for i in range(2)]
            for i, y in enumerate(ns_step(ys, *ns_poly(ys))):
                yf_s[i] = y
            return carry

        lax.fori_loop(0, 3, f_turn, 0)
        q[3]()
        lax.fori_loop(3, NS_STEPS, f_turn, 0)
        put_f(tmf_s, [blocks(f1_other, f1_half), blocks(f2_other, f2_half)])
        put_f(txf_s, [yf_s[i].astype(BF16) for i in range(2)])
        for a, b, copies in zip((tmf_s, txf_s), (rmf_s, rxf_s), early[:2]):
            wires.start(copies)
            b[me] = a[p.x, p.y]
        q[4]()
        tiles = [q_all[192 * j : 192 * j + 192, :].astype(F32) for j in range(4)]
        lane = lax.broadcasted_iota(jnp.int32, (192, 128), 1)
        last = q_all[768:864, :].astype(F32)
        last = jnp.concatenate([last, pltpu.roll(last, 64, 1)], axis=0)
        edges = [jnp.where(lane < 64, e, 0.0) for e in (tiles[3], pltpu.roll(tiles[3], 64, 1), last)]
        three = [jnp.concatenate([t, e], axis=1) for t, e in zip(tiles, edges)]
        for i, y in enumerate(ns_start(three)):
            yq_s[i] = y

        def turn(t, carry):
            ys = [yq_s[i] for i in range(3)]
            for i, y in enumerate(ns_step(ys, *ns_poly(ys))):
                yq_s[i] = y
            return carry

        lax.fori_loop(0, NS_STEPS, turn, 0)
        put_q(txq_s, [yq_s[i].astype(BF16) for i in range(3)])
        wires.start(late)
        rxq_s[me] = txq_s[p.x, p.y]
        put_q(tmq_s, [m.astype(BF16) for m in three])
        for x in range(2):
            for y in range(2):
                tv_s[x, y] = q_all[864:896, :]
        for a, b, copies in zip((tmq_s, tv_s), (rmq_s, rv_s), early[2:]):
            wires.start(copies)
            b[me] = a[p.x, p.y]
        for copies in early[:2]:
            wires.arrive(copies)
        wires.start(pass_early[:2])
        wires.arrive(pass_o)

    @pl.when(core0)
    def _():
        wires.arrive(pass_early[:2])

    def fresh(w, own, longest):
        return w - muon_rate * (0.2 * math.sqrt(longest) * own + muon_decay * w)

    sel_l = hot((wide, 768), n * wide, 0)
    sel_h = hot((wide, 384), p.c * wide, 0)
    sel_q = hot((tall, 96), p.c * tall, 0)
    mo_ref[0] = nt(sel_l, nn(sel_b, wide_rows(oo_s, 0, 4)).astype(BF16))
    no_ref[0] = fresh(wo_ref[0], nt(sel_l, jnp.where(core0, xo_s[...], xo_r[...])), 768)
    for g in range(4):
        for i, (w_ref, m_ref, n_ref) in enumerate(((w1_ref, m1_ref, n1_ref), (w2_ref, m2_ref, n2_ref))):
            at = slice(cols * i, cols * i + cols)
            m_ref[g] = nt(rmf_s[g, at, :], sel_h)
            n_ref[g] = fresh(w_ref[g], nt(rxf_s[g, at, :], sel_h), 768)

    @pl.when(core1)
    def _():
        for copies in early[2:]:
            wires.arrive(copies)
        wires.start(pass_early[2:])
        wires.arrive(late_on[1])

    @pl.when(core0)
    def _():
        wires.arrive(late_on[0])

    for g in range(4):
        own = nn(sel_q, rxq_s[g]).astype(BF16)
        for c in range(3):
            nq_ref[4 * c + g] = fresh(wq_ref[4 * c + g], nt(hot((slim, 128), c * slim, 0), own), 192)

    @pl.when(core0)
    def _():
        wires.arrive(pass_early[2:])

    for g in range(4):
        own = nn(sel_q, rmq_s[g]).astype(BF16)
        for c in range(3):
            mq_ref[4 * c + g] = nt(hot((slim, 128), c * slim, 0), own)
    parts = [rv_s[g].astype(F32) for g in range(4)]
    top = jnp.concatenate([t for v in parts for t in (v[0:8], v[8:16, :64])], axis=1)
    low = [jnp.concatenate([v[16 + j : 17 + j] for j in range(6)], axis=1) for v in parts]
    grad = jnp.concatenate([top] + low, axis=0)
    first = 0.9 * vm1_ref[...] + 0.1 * grad
    second = 0.999 * vm2_ref[...] + 0.001 * grad * grad
    f_ref[...] = first
    s_ref[...] = second
    v_ref[...] = vec_ref[...] - adam_rate * (first * (1.0 / (1.0 - 0.9**STEP))) / (jnp.sqrt(second * (1.0 / (1.0 - 0.999**STEP))) + 1e-08)

    @pl.when(core0)
    def _():
        wires.leave(pass_o)

    @pl.when(core1)
    def _():
        for copies in early + [late, pass_early]:
            wires.leave(copies)


def closing_owned(p, shares, lengths, wt, so, s1, s2, gv, mq, weights, vec, vm1, vm2, acts, ident):
    tokens = acts[0]
    n, seq, d = tokens.shape
    slim = mq.shape[1]
    shape = lambda a: jax.ShapeDtypeStruct(a.shape, F32)
    outs = [jax.ShapeDtypeStruct(tokens.shape, BF16)] + [shape(w) for w in weights] * 2 + [shape(vec)] * 3
    hbm = pl.BlockSpec(memory_space=pl.ANY)
    tm, mt = pltpu.VMEM((n, seq, d), BF16), pltpu.VMEM((n, d, seq), BF16)
    scratch = [tm, mt, tm, mt, tm, mt, mt, pltpu.VMEM((n, seq, d), BF16), pltpu.VMEM((seq, seq), F32)]
    scratch += [mt] * 3 + [pltpu.VMEM((3, 192, 768), F32), pltpu.VMEM((8, 768), F32)]
    scratch += [pltpu.VMEM((shares[3].rows, 128), BF16), pltpu.VMEM((shares[0].rows, 128), BF16)]
    scratch += [pltpu.VMEM((768, 768), F32), pltpu.VMEM((2, 192, 768), F32), pltpu.VMEM((3, 192, 256), F32)]
    scratch += [pltpu.VMEM((4 * slim, 768), BF16)] * 2
    to_f, to_q, to_v = (2 * slim, 384), (96, 128), (32, 128)
    scratch += [pltpu.VMEM((2, 2) + k, BF16) for k in (to_f, to_f, to_q, to_q, to_v)]
    scratch += [pltpu.VMEM((4,) + k, BF16) for k in (to_f, to_f, to_q, to_q, to_v)]
    scratch += [pltpu.SemaphoreType.DMA((n, 8)), pltpu.SemaphoreType.DMA((24,)), pltpu.SemaphoreType.DMA((24,))]
    scratch += shares[0].scratch(p)
    for s in shares[1:]:
        scratch += s.scratch()
    return pl.pallas_call(
        functools.partial(owner_kernel, p, shares),
        out_shape=outs,
        in_specs=[pl.BlockSpec(memory_space=pltpu.SMEM)] + [VMEM] * 13 + [hbm] * 6 + [VMEM] + [hbm] * 2,
        out_specs=[VMEM] * 12,
        scratch_shapes=scratch,
        compiler_params=pltpu.CompilerParams(collective_id=ident, has_side_effects=True, vmem_limit_bytes=62 * 2**20),
    )(lengths, wt, so, s1, s2, gv, mq, *weights, vec, vm1, vm2, *acts)


def hand_over_kernel(*refs):
    half = len(refs) // 2
    for src, dst in zip(refs[:half], refs[half:]):
        dst[...] = src[...]


def hand_over(values):
    return pl.pallas_call(
        hand_over_kernel,
        out_shape=[jax.ShapeDtypeStruct(a.shape, a.dtype) for a in values],
        in_specs=[VMEM] * len(values),
        out_specs=[VMEM] * len(values),
        compiler_params=pltpu.CompilerParams(vmem_limit_bytes=60 * 2**20),
    )(*values)


def local(tokens, doc_lengths, cotangent, qkv_weight, out_weight, ffn_in_weight, ffn_out_weight, vectors,
          qkv_moment, out_moment, ffn_in_moment, ffn_out_moment, vec_moment1, vec_moment2):
    p = Place(lax.axis_size("dp"), lax.axis_size("narrow"))
    flip = lambda a: a.transpose(0, 2, 1)
    wq, w1, w2, mq, m1, m2 = map(flip, (qkv_weight, ffn_in_weight, ffn_out_weight, qkv_moment, ffn_in_moment, ffn_out_moment))
    owned = p.X == 2 and p.Y == 2 and p.C == 2 and p.Z in (2, 4)
    if owned:
        shares = [Shares(p, 4608), Owned(p, 576), Owned(p, 576), Solo(p, 448)]
    else:
        shares = [Shares(p, r) for r in (4608, 4608, 4608, 3456 + 72)]
    qt, k, kt, v, ct, lse, w1p, w2p, wot, wt = opening(p, doc_lengths, tokens, wq, out_weight, w1, w2, vectors, 0)
    out_act, res, dct, so, s1, s2, gv = ffn(tokens, cotangent, ct, w1p, w2p, wot, vectors, out_moment, m1, m2, shares[0].rows, owned)
    acts = (tokens, qt, k, kt, v, ct, lse, dct, res)
    gt, gq, go, g1, g2, nq, no, n1, n2, f, s, vn = hand_over((closing_owned if owned else closing)(
        p, shares, doc_lengths, wt, so, s1, s2, gv, mq, (wq, out_weight, w1, w2), vectors, vec_moment1, vec_moment2, acts, 1))
    return (out_act, gt, flip(gq), go, flip(g1), flip(g2), flip(nq), no, flip(n1), flip(n2), f, s, vn)


def solution(mesh):
    rows = P(("dp", "narrow"), None, None)
    cut = P(None, "narrow", "dp")
    return jax.shard_map(
        local,
        mesh=mesh,
        in_specs=(rows, P(("dp", "narrow"), None), rows) + (cut,) * 4 + (P(),) + (cut,) * 4 + (P(), P()),
        out_specs=(rows, rows) + (cut,) * 8 + (P(),) * 3,
        check_vma=False,
    )
```

```python
import functools
import math

import jax
import jax.numpy as jnp
from jax import lax
from jax.experimental import pallas as pl
from jax.experimental.pallas import tpu as pltpu
from jax.sharding import PartitionSpec as P

F32, BF16 = jnp.float32, jnp.bfloat16
MESH = pl.DeviceIdType.MESH
NORM_EPS = 1e-05
NS_STEPS = 5
STEP = 5
ns_first = 3.4445
ns_second = -4.775
ns_third = 2.0315
muon_rate = 0.5
muon_decay = 0.01
adam_rate = 0.4
VMEM = pl.BlockSpec(memory_space=pltpu.VMEM)


def nn(a, b):
    return lax.dot_general(a, b, (((1,), (0,)), ((), ())), preferred_element_type=F32)


def nt(a, b):
    return lax.dot_general(a, b, (((1,), (1,)), ((), ())), preferred_element_type=F32)


def tn(a, b):
    return lax.dot_general(a, b, (((0,), (0,)), ((), ())), preferred_element_type=F32)


def window(g):
    return 128 * (3 * (g // 2) + g % 2)


def join(parts):
    out = []
    for p in range(2):
        a, b = parts[2 * p], parts[2 * p + 1]
        out += [a[:, :128], a[:, 128:] + b[:, :128], b[:, 128:]]
    return jnp.concatenate(out, axis=1)


def ids(len_ref, row, shape, dim):
    pos = lax.broadcasted_iota(jnp.int32, shape, dim)
    out = jnp.zeros(shape, jnp.int32)
    end = jnp.int32(0)
    for j in range(4):
        end = end + len_ref[row, j]
        out = out + (pos >= end).astype(jnp.int32)
    return out


def hot(shape, row_at, col_at):
    rows = lax.broadcasted_iota(jnp.int32, shape, 0) + row_at
    cols = lax.broadcasted_iota(jnp.int32, shape, 1) + col_at
    return (rows == cols).astype(BF16)


def put_blocks(dst, base, value):
    for j in range(value.shape[1] // 128):
        dst[base + 192 * j : base + 192 * j + 192, :] = value[:, 128 * j : 128 * j + 128].astype(BF16)


def add_blocks(dst, base, value):
    for j in range(value.shape[1] // 128):
        at = slice(base + 192 * j, base + 192 * j + 192)
        dst[at, :] = (dst[at, :].astype(F32) + value[:, 128 * j : 128 * j + 128]).astype(BF16)


def group_rows(owned, g):
    return (576 * g, 2304 + 576 * turned(g)) if owned else (1152 * g, 1152 * g + 576)


def wide_rows(ref, base, count):
    parts = []
    for q in range(count):
        at = base + 1152 * q
        parts.append(jnp.concatenate([ref[at + 192 * j : at + 192 * j + 192, :] for j in range(6)], axis=1))
    return parts[0] if count == 1 else jnp.concatenate(parts, axis=0)


def gelu_parts(v):
    t = pl.reciprocal(1.0 + (0.3275911 * 0.7071067811865476) * jnp.abs(v), approx=True)
    ex = jnp.exp2(v * v * (-0.5 * 1.4426950408889634))
    half = t * ex * (0.127414796 + t * (-0.142248368 + t * (0.7107068705 + t * (-0.7265760135 + t * 0.5307027145))))
    cdf = jnp.where(v >= 0, 1.0 - half, half)
    return v * cdf, cdf + (v * ex) * 0.3989422804014327


def norm(h):
    mu = jnp.mean(h, axis=-1, keepdims=True)
    c = h - mu
    inv = lax.rsqrt(jnp.mean(c * c, axis=-1, keepdims=True) + NORM_EPS)
    return c * inv, inv


def norm_back(up, n, inv, gain):
    w = up * gain
    return inv * (w - jnp.mean(w, axis=-1, keepdims=True) - n * jnp.mean(w * n, axis=-1, keepdims=True))


def col_sum(v):
    return jnp.sum(v, axis=0, keepdims=True)


def turned(g):
    return 2 * (g % 2) + g // 2


class Place:
    def __init__(self, dp, narrow):
        self.X = 2 if dp % 2 == 0 else 1
        self.C = 2 if narrow % 2 == 0 else 1
        self.Z, self.Y = dp // self.X, narrow // self.C

    def locate(self):
        d, n = lax.axis_index("dp"), lax.axis_index("narrow")
        self.z, self.x = d // self.X, lax.rem(d, self.X)
        self.y, self.c = n // self.C, lax.rem(n, self.C)

    def count(self):
        return self.Z + self.X + self.Y + self.C - 4

    def at(self, axis, j):
        return lax.rem(getattr(self, axis) + j, getattr(self, axis.upper()))

    def device(self, axis, j):
        where = {a: getattr(self, a) for a in "zxyc"}
        where[axis] = self.at(axis, j)
        return (where["z"] * self.X + where["x"], where["y"] * self.C + where["c"])

    def other(self, dx, dy, c):
        return (self.z * self.X + lax.rem(self.x + dx, self.X), lax.rem(self.y + dy, self.Y) * self.C + c)

    def barrier(self, corner=False):
        self.greet(corner)
        self.meet(corner)

    def greet(self, corner=False):
        sem = pltpu.get_barrier_semaphore()
        if corner:
            for c in range(self.C):
                pl.semaphore_signal(sem, inc=1, device_id=self.other(1, 1, c), device_id_type=MESH)
            for dx, dy in ((1, 0), (0, 1)):
                pl.semaphore_signal(sem, inc=1, device_id=self.other(dx, dy, 1 - self.c), device_id_type=MESH)
        for axis in "zxyc":
            for j in range(1, getattr(self, axis.upper())):
                pl.semaphore_signal(sem, inc=1, device_id=self.device(axis, j), device_id_type=MESH)

    def meet(self, corner=False):
        pl.semaphore_wait(pltpu.get_barrier_semaphore(), self.count() + 4 * int(corner))


class Wires:
    def __init__(self, place, send_sem, recv_sem):
        self.place, self.send_sem, self.recv_sem, self.makers = place, send_sem, recv_sem, []

    def plan(self, src, dst, axis, j):
        return self.plan_to(src, dst, lambda: self.place.device(axis, j))

    def plan_to(self, src, dst, device):
        k = len(self.makers)
        self.makers.append(
            lambda: pltpu.make_async_remote_copy(
                src_ref=src(),
                dst_ref=dst(),
                send_sem=self.send_sem.at[k],
                recv_sem=self.recv_sem.at[k],
                device_id=device(),
                device_id_type=MESH,
            )
        )
        return k

    def start(self, copies):
        for k in copies:
            self.makers[k]().start()

    def arrive(self, copies):
        for k in copies:
            self.makers[k]().wait_recv()

    def leave(self, copies):
        for k in copies:
            self.makers[k]().wait_send()

    def finish(self, skip=()):
        self.leave([k for k in range(len(self.makers)) if k not in skip])


def gather_copies(p):
    return (p.Z - 1) + p.Z * ((p.X - 1) + (p.Y - 1) + 2 * (p.X - 1) * (p.Y - 1) + (p.C - 1))


def gather_steps(p, wires, buf, half, corner=False):
    z, x, y, c = p.z, p.x, p.y, p.c
    rest = buf.shape[4] - half

    def same(at):
        return (lambda: buf.at[at()],) * 2

    along, first, second, last = {}, {}, {}, {}
    for j in range(1, p.Z):
        along[j] = wires.plan(*same(lambda: (z, c, x, y)), "z", j)
    for i in range(p.Z):
        from_z = lambda i=i: p.at("z", p.Z - i) if i else z
        mine = lambda f=from_z: (f(), c, x, y)
        first[i] = [wires.plan(*same(mine), "x", j) for j in range(1, p.X)] + [wires.plan(*same(mine), "y", j) for j in range(1, p.Y)]
        second[i] = []
        if corner:
            first[i].append(wires.plan_to(*same(mine), lambda: p.other(1, 1, c)))
        for j in range(1, p.X if not corner else 1):
            part = lambda f=from_z, j=j: (f(), c, p.at("x", p.X - j), y, pl.ds(0, half))
            second[i] += [wires.plan(*same(part), "y", q) for q in range(1, p.Y)]
        for j in range(1, p.Y if not corner else 1):
            part = lambda f=from_z, j=j: (f(), c, x, p.at("y", p.Y - j), pl.ds(half, rest))
            second[i] += [wires.plan(*same(part), "x", q) for q in range(1, p.X)]
        last[i] = [wires.plan(*same(lambda f=from_z: (f(), c)), "c", j) for j in range(1, p.C)]

    def own(i):
        if i:
            wires.arrive([along[i]])
        wires.start(first[i])

    def onward(i):
        wires.arrive(first[i])
        wires.start(second[i])

    def over(i):
        wires.arrive(first[i] if corner else second[i])
        wires.start(last[i])

    def done():
        for i in last:
            wires.arrive(last[i])

    of = lambda f: [functools.partial(f, i) for i in range(p.Z)]
    return lambda: wires.start(along.values()), of(own), [] if corner else of(onward), of(over), done


class Shares:
    def __init__(self, p, rows):
        cells = p.X * p.Y * p.Z
        unit = 16 * cells * p.C
        units = -(-rows // unit)
        self.a, self.b = 16 * ((units + 1) // 2), 16 * max(units // 2, 1)
        self.per_core = cells * (self.a + self.b)
        self.rows = p.C * self.per_core
        self.cells = cells
        self.copies = 2 * ((p.C - 1) + 2 * ((p.X - 1) + (p.Y - 1)) + 2 * (p.Z - 1))

    def scratch(self, p):
        a, b = self.a, self.b
        kinds = [
            (self.per_core,),
            (p.C - 1, self.per_core),
            (p.X - 1, p.Y * p.Z * a),
            (p.Y - 1, p.X * p.Z * b),
            (p.Y - 1, p.Z * a),
            (p.X - 1, p.Z * b),
            (p.Z - 1, a),
            (p.Z - 1, b),
        ]
        return [pltpu.VMEM(k + (128,), BF16) for k in kinds] + [pltpu.SemaphoreType.DMA((self.copies,))] * 2


def spread(start, size):
    return pl.ds(pl.multiple_of(start, 16), size)


def add_into(dst, at, parts):
    total = dst[at, :].astype(F32)
    for part in parts:
        total = total + part.astype(F32)
    dst[at, :] = total.astype(BF16)


def sum_steps(p, s, src, out, scratch):
    held, from_c, a1, b1, a2, b2, a3, b3, send_sem, recv_sem = scratch
    wires = Wires(p, send_sem, recv_sem)
    a, b, per = s.a, s.b, s.per_core
    ax, by = p.Y * p.Z * a, p.X * p.Z * b
    in_a = lambda x, y=0, z=0: ((x * p.Y + y) * p.Z + z) * a
    in_b = lambda y, x=0, z=0: s.cells * a + ((y * p.X + x) * p.Z + z) * b
    x, y, z, c = p.x, p.y, p.z, p.c
    base = c * per

    def cut(ref, start, size):
        return lambda: ref.at[spread(start(), size)]

    def both(start, size):
        return (cut(out, start, size),) * 2

    def slot(ref, j):
        return lambda: ref.at[j - 1]

    sends = [[] for _ in range(8)]
    for j in range(1, p.C):
        sends[0].append(wires.plan(cut(src, lambda j=j: p.at("c", j) * per, per), slot(from_c, j), "c", j))
        sends[7].append(wires.plan(*both(lambda: base, per), "c", j))
    for j in range(1, p.X):
        sends[1].append(wires.plan(cut(held, lambda j=j: in_a(p.at("x", j)), ax), slot(a1, j), "x", j))
        sends[2].append(wires.plan(cut(held, lambda j=j: in_b(y, p.at("x", j)), p.Z * b), slot(b2, j), "x", j))
        sends[5].append(wires.plan(*both(lambda: base + in_b(y, x), p.Z * b), "x", j))
        sends[6].append(wires.plan(*both(lambda: base + in_a(x), ax), "x", j))
    for j in range(1, p.Y):
        sends[1].append(wires.plan(cut(held, lambda j=j: in_b(p.at("y", j)), by), slot(b1, j), "y", j))
        sends[2].append(wires.plan(cut(held, lambda j=j: in_a(x, p.at("y", j)), p.Z * a), slot(a2, j), "y", j))
        sends[5].append(wires.plan(*both(lambda: base + in_a(x, y), p.Z * a), "y", j))
        sends[6].append(wires.plan(*both(lambda: base + in_b(y), by), "y", j))
    for j in range(1, p.Z):
        sends[3].append(wires.plan(cut(held, lambda j=j: in_a(x, y, p.at("z", j)), a), slot(a3, j), "z", j))
        sends[3].append(wires.plan(cut(held, lambda j=j: in_b(y, x, p.at("z", j)), b), slot(b3, j), "z", j))
        sends[4].append(wires.plan(*both(lambda: base + in_a(x, y, z), a), "z", j))
        sends[4].append(wires.plan(*both(lambda: base + in_b(y, x, z), b), "z", j))

    def total(ref, at, size, parts, count):
        value = ref[spread(at, size), :].astype(F32)
        for j in range(count):
            value = value + parts[j].astype(F32)
        return value.astype(BF16)

    def step(t):
        if t:
            wires.arrive(sends[t - 1])
        if t == 1:
            held[...] = total(src, base, per, from_c, p.C - 1)
        if t == 2:
            held[spread(in_a(x), ax), :] = total(held, in_a(x), ax, a1, p.X - 1)
            held[spread(in_b(y), by), :] = total(held, in_b(y), by, b1, p.Y - 1)
        if t == 3:
            held[spread(in_a(x, y), p.Z * a), :] = total(held, in_a(x, y), p.Z * a, a2, p.Y - 1)
            held[spread(in_b(y, x), p.Z * b), :] = total(held, in_b(y, x), p.Z * b, b2, p.X - 1)
        if t == 4:
            out[spread(base + in_a(x, y, z), a), :] = total(held, in_a(x, y, z), a, a3, p.Z - 1)
            out[spread(base + in_b(y, x, z), b), :] = total(held, in_b(y, x, z), b, b3, p.Z - 1)
        if t < 8:
            wires.start(sends[t])
        else:
            wires.finish()

    return [functools.partial(step, t) for t in range(9)]


def at_turn(turn, steps):
    for i, todo in enumerate(steps):
        if todo:

            @pl.when(turn == i)
            def _():
                for step in todo:
                    step()


def dealt(steps, turns):
    return [steps[len(steps) * i // turns : len(steps) * (i + 1) // turns] for i in range(turns)]


def fold(t, odd):
    rows, wide = t.shape
    if wide % 128 == 64:
        body = jnp.where(odd, t[:, 64:], t[:, : wide - 64])
        edge = jnp.where(odd, t[:, :64], t[:, wide - 64 :])
        a, b = edge[: rows // 2], edge[rows // 2 :]
        tiles = [body[:, 128 * j : 128 * j + 128] for j in range(wide // 128)]
        tiles.append(jnp.concatenate([jnp.where(odd, b, a), jnp.where(odd, a, b)], axis=1))
        return jnp.concatenate(tiles, axis=0)
    need = -(-wide // 128) * 128
    t = jnp.concatenate([t, jnp.zeros((rows, need - wide), t.dtype)], axis=1) if need > wide else t
    return jnp.concatenate([t[:, 128 * j : 128 * j + 128] for j in range(need // 128)], axis=0)


def fold_rows(rows, wide):
    return rows * (wide // 128) + rows // 2 if wide % 128 == 64 else rows * (-(-wide // 128))


def unfold(p, buf, base, rows, wide):
    out = []
    lane = lax.broadcasted_iota(jnp.int32, (rows // 2, 128), 1)
    size = fold_rows(rows, wide)
    for z in range(p.Z):
        for x in range(p.X):
            tiles = []
            for y in range(p.Y):
                got = [buf[z, c, x, y, base : base + size, :].astype(F32) for c in range(p.C)]
                if wide % 128 == 64:
                    k = wide // 128
                    even, odd = got
                    tiles += [even[rows * j : rows * j + rows] for j in range(k)]
                    e, o = even[rows * k :], odd[rows * k :]
                    top = jnp.where(lane < 64, e, o)
                    low = pltpu.roll(jnp.where(lane < 64, o, e), 64, 1)
                    tiles.append(jnp.concatenate([top, low], axis=0))
                    tiles += [odd[rows * j : rows * j + rows] for j in range(k)]
                else:
                    k = size // rows
                    for c in range(p.C):
                        t = jnp.concatenate([got[c][rows * j : rows * j + rows] for j in range(k)], axis=1).astype(BF16)
                        tiles.append(nn(t, hot((128 * k, 768), (y * p.C + c) * wide, 0)) if 128 * k == wide else nn(t, hot_cut((128 * k, 768), (y * p.C + c) * wide, wide)))
            if wide % 128 == 64:
                out.append(jnp.concatenate(tiles, axis=1))
            else:
                out.append(functools.reduce(lambda a, b: a + b, tiles))
    return out


def hot_cut(shape, at, limit):
    rows = lax.broadcasted_iota(jnp.int32, shape, 0)
    cols = lax.broadcasted_iota(jnp.int32, shape, 1)
    return jnp.logical_and(rows + at == cols, rows < limit).astype(BF16)


def front_kernel(p, owned, len_ref, x_ref, cot_ref, wq_ref, wo_ref, w1_ref, w2_ref, vec_ref, mo_ref, m1_ref, m2_ref,
                 qt_out, k_out, kt_out, v_out, ct_out, out_out, res_out, dct_out, lse_ref, wt_out, so_ref, s1_ref, s2_ref, gv_ref,
                 bufq, bufr, place_s, win_s, qt_s, k_s, kt_s, v_s, ct_s, vt_s, bias_s, vcol_s, w1_s, w2_s, wo_s, out_s, res_s, dct_s,
                 send_q, recv_q, send_r, recv_r, out_sem):
    p.locate()
    p.greet(corner=owned)
    n_rows, seq = x_ref.shape[:2]
    odd = lax.rem(lax.axis_index("narrow"), 2) == 1
    slim, tall = wq_ref.shape[1:]
    qrows = bufq.shape[4]
    for c in range(3):
        t = jnp.concatenate([wq_ref[4 * c + g] for g in range(4)], axis=0).T
        t = jnp.concatenate([t, jnp.zeros((tall, 128 - 4 * slim), F32)], axis=1)
        bufq[p.z, p.c, p.x, p.y, c * tall : c * tall + tall, :] = t.astype(BF16)
    if qrows > 3 * tall:
        bufq[p.z, p.c, p.x, p.y, 3 * tall :, :] = jnp.zeros((qrows - 3 * tall, 128), BF16)
    p.meet(corner=owned)
    wires_q, wires_r = Wires(p, send_q, recv_q), Wires(p, send_r, recv_r)
    q_z, q_own, q_on, q_over, q_done = gather_steps(p, wires_q, bufq, qrows // 32 * 16, corner=owned)
    q_z()
    q_own[0]()
    rows, wide = 4 * slim, 4 * tall
    size = fold_rows(rows, wide)
    big = wo_ref.shape[2]
    shards = [nt(hot((big, big), 0, 0), wo_ref[0].astype(BF16))]
    shards += [jnp.concatenate([r[g] for g in range(4)], axis=0) for r in (w1_ref, w2_ref)]
    folded = jnp.concatenate([fold(t, odd) for t in shards], axis=0)
    if bufr.shape[4] > 3 * size:
        folded = jnp.concatenate([folded, jnp.zeros((bufr.shape[4] - 3 * size, 128), F32)], axis=0)
    bufr[p.z, p.c, p.x, p.y] = folded.astype(BF16)
    d, n = lax.axis_index("dp"), lax.axis_index("narrow")
    sel_l = hot((wide, 768), n * wide, 0)
    placed = nt(hot((768, big), 0, d * big), (0.95 * mo_ref[0]).astype(BF16)).astype(BF16)
    value = nn(placed, sel_l)
    for q in range(4):
        put_blocks(so_ref, 1152 * q, value[192 * q : 192 * q + 192])
    for dst, m_ref in ((s1_ref, m1_ref), (s2_ref, m2_ref)):
        for g in range(4):
            value = nn(nn(hot((192, slim), 0, d * slim), (0.95 * m_ref[g]).astype(BF16)).astype(BF16), sel_l)
            for half, base in enumerate(group_rows(owned, g)):
                put_blocks(dst, base, value[:, 384 * half : 384 * half + 384])
    for dst in (so_ref, s1_ref, s2_ref):
        if dst.shape[0] > 4608:
            dst[4608:, :] = jnp.zeros((dst.shape[0] - 4608, 128), BF16)
    gv_ref[...] = jnp.zeros_like(gv_ref)
    dp = p.Z * p.X
    for pair in range(dp // 2):
        r = lax.broadcasted_iota(jnp.int32, (256, 1), 0)
        q = jnp.where(r < 128, r, r - 128)
        g = (q >= slim).astype(jnp.int32) + (q >= 2 * slim).astype(jnp.int32) + (q >= 3 * slim).astype(jnp.int32)
        col = 256 * g + jnp.where(jnp.logical_or(g == 1, g == 3), 64, 0) + jnp.where(r < 128, 2 * pair * slim, (2 * pair + 1) * slim) + q - g * slim
        col = jnp.where(q < 4 * slim, col, -1)
        place_s[pair] = (lax.broadcasted_iota(jnp.int32, (256, 1024), 1) == col).astype(BF16)
    win_s[...] = jnp.zeros_like(win_s)
    vcol_s[...] = vec_ref[0:8, :].T
    r_z, r_own, r_on, r_over, r_done = gather_steps(p, wires_r, bufr, bufr.shape[4] // 32 * 16)
    for t in range(1, p.Z + 2):
        for steps, at in ((q_own, t), (q_on, t - 1), (q_over, t - (1 if owned else 2))):
            if 0 <= at < len(steps):
                steps[at]()
        if t == p.Z - 2:
            r_z()
    r_own[0]()
    q_done()
    total = jnp.zeros((3 * 192, 1024), F32)
    for pair in range(dp // 2):
        tiles = []
        for d in (2 * pair, 2 * pair + 1):
            z, x = d // p.X, d % p.X
            got = [bufq[z, c, x, y].astype(F32) for y in range(p.Y) for c in range(p.C)]
            tiles.append(jnp.concatenate([b[c * tall : c * tall + tall] for c in range(3) for b in got], axis=0))
        total = total + nn(jnp.concatenate(tiles, axis=1).astype(BF16), place_s[pair])
    for g in range(4):
        off = 64 * (g % 2)
        stack = total[:, 256 * g : 256 * g + 256].astype(BF16)
        for c in range(3):
            win_s[c, g, off : off + 192, :] = stack[192 * c : 192 * c + 192]
        wt_out[g] = nt(hot((192, 256), off, 0), stack).astype(BF16)
    turns = [[] for _ in range(3 * n_rows)]
    for i, step in enumerate(r_on):
        turns[min(i, 3, len(turns) - 1)].append(step)
    for i, step in enumerate(r_over):
        turns[min(min(i, 3) // 2 + 3, len(turns) - 1)].append(step)
    turns[-1].append(r_done)

    for step in r_own[1:]:
        step()

    def out_copies(row, which):
        pairs = ((qt_s, qt_out), (k_s, k_out), (kt_s, kt_out), (v_s, v_out), (ct_s.at[row], ct_out), (out_s, out_out), (res_s, res_out), (dct_s, dct_out))
        return [pltpu.make_async_copy(pairs[i][0], pairs[i][1].at[row], out_sem.at[i]) for i in which]

    def reuse(row, which):
        @pl.when(row > 0)
        def _():
            for copy in out_copies(row - 1, which):
                copy.wait()

    def one_row(row, carry):
        same = ids(len_ref, row, (seq, seq), 0) == ids(len_ref, row, (seq, seq), 1)
        bias_s[...] = jnp.where(same, 0.0, -1e30)
        reuse(row, range(5))
        for g in range(4):
            lo = window(g)
            xw = x_ref[row, :, lo : lo + 256]
            off = 64 * (g % 2)
            r = slice(192 * g, 192 * g + 192)
            q = nt(win_s[0, g, off : off + 192, :], xw) + vcol_s[r, 4:5]
            qt_s[r, :] = q.astype(BF16) * BF16(0.125)
            kt_s[r, :] = nt(win_s[1, g, off : off + 192, :], xw).astype(BF16)
            v = nt(win_s[2, g, off : off + 192, :], xw) + vcol_s[r, 5:6]
            vt_s[r, :] = v.astype(BF16)
        wide_of = lambda c: join([nt(x_ref[row, :, window(g) : window(g) + 256], win_s[c, g]) for g in range(4)])
        k_s[...] = wide_of(1).astype(BF16)
        v_s[...] = (wide_of(2) + vec_ref[5:6, :]).astype(BF16)
        for copy in out_copies(row, range(4)):
            copy.start()

        def four(j, carry):
            heads = [(pl.multiple_of(256 * j + 128 * u, 128), e) for u in range(2) for e in range(2)]
            spots = [pl.ds(pl.multiple_of(lo + 64 * e, 64), 64) for lo, e in heads]
            scores = []
            for (lo, e), at in zip(heads, spots):
                qh = qt_s[at, :]
                none = jnp.zeros_like(qh)
                scores.append(nn(k_s[:, pl.ds(lo, 128)], jnp.concatenate([none, qh] if e else [qh, none], axis=0)))
            soft = []
            for s in scores:
                s = s + bias_s[...]
                m = jnp.max(s, axis=0, keepdims=True)
                ex = jnp.exp(s - m)
                soft.append((m, ex.astype(BF16), jnp.sum(ex, axis=0, keepdims=True)))
            for i, (at, (m, ex, tot)) in enumerate(zip(spots, soft)):
                ct_s[row, at, :] = (nn(vt_s[at, :], ex) * (1.0 / tot)).astype(BF16)
                lse_ref[row, pl.ds(4 * j + i, 1), :] = m + jnp.log(tot)
            at_turn(row * 3 + j, turns)
            return carry

        lax.fori_loop(0, 3, four, 0)
        out_copies(row, (4,))[0].start()
        return carry

    lax.fori_loop(0, n_rows, one_row, 0)
    wires_q.finish()
    wires_r.finish()
    whole = unfold(p, bufr, 0, rows, wide)
    wo_s[...] = jnp.concatenate(whole, axis=0).astype(BF16)
    for i, dst in enumerate((w1_s, w2_s)):
        whole = unfold(p, bufr, (i + 1) * size, rows, wide)
        for g in range(4):
            off = 64 * (g % 2)
            dst[g, off : off + 192, :] = jnp.concatenate([b[g * slim : g * slim + slim] for b in whole], axis=0).astype(BF16)
            dst[g, 192 - 192 * (g % 2) : 256 - 192 * (g % 2), :] = jnp.zeros((64, 768), BF16)
    vec = lambda i: vec_ref[i : i + 1, :]

    def feed_forward(row, carry):
        h1 = x_ref[row].astype(F32) + (nn(ct_s[row].T, wo_s[...]) + vec(6))
        n1, inv1 = norm(h1)
        first = n1 * vec(0) + vec(1)
        fl = first.astype(BF16)
        inner = lambda g: nn(fl[:, window(g) : window(g) + 256], w1_s[g]) + vec(8 + g)
        active, slope, branch = [], [], []
        ahead = inner(0)
        for g in range(4):
            now, ahead = ahead, (inner(g + 1) if g < 3 else None)
            a, sl = gelu_parts(now)
            active.append(a.astype(BF16))
            slope.append(sl)
            branch.append(nt(active[g], w2_s[g]))
        h2 = first + (join(branch) + vec(7))
        n2, inv2 = norm(h2)
        reuse(row, (5, 6, 7))
        out_s[...] = (n2 * vec(2) + vec(3)).astype(BF16)
        out_copies(row, (5,))[0].start()
        dy = cot_ref[row].astype(F32)
        dh2 = norm_back(dy, n2, inv2, vec(2))
        dbl = dh2.astype(BF16)
        dbt = dbl.T
        flt = fl.T
        ones = jnp.ones((16, seq), BF16)
        dfirst = []
        gb = []
        for g in range(4):
            da = nn(dbl[:, window(g) : window(g) + 256], w2_s[g])
            di = (da * slope[g]).astype(BF16)
            dfirst.append(nt(di, w1_s[g]))
            g2 = nn(dbt[192 * g : 192 * g + 192, :], active[g])
            ext = nn(jnp.concatenate([flt[192 * g : 192 * g + 192, :], ones], axis=0), di)
            for half, base in enumerate(group_rows(owned, g)):
                add_blocks(s2_ref, base, g2[:, 384 * half : 384 * half + 384])
                add_blocks(s1_ref, base, ext[:192, 384 * half : 384 * half + 384])
            gb.append(ext[192:193])
        df = dh2 + join(dfirst)
        dh1 = norm_back(df, n1, inv1, vec(0))
        dat = dh1.astype(BF16)
        res_s[...] = dat
        out_copies(row, (6,))[0].start()
        go = nn(ct_s[row], dat)
        for q in range(4):
            add_blocks(so_ref, 1152 * q, go[192 * q : 192 * q + 192])
        dct_s[...] = nt(wo_s[...], dat).astype(BF16)
        out_copies(row, (7,))[0].start()
        z = jnp.zeros((1, dy.shape[1]), F32)
        gv_ref[...] += jnp.concatenate(
            [col_sum(df * n1), col_sum(df), col_sum(dy * n2), col_sum(dy), z, z, col_sum(dat.astype(F32)), col_sum(dbl.astype(F32))] + gb, axis=0)
        return carry

    lax.fori_loop(0, n_rows, feed_forward, 0)
    for copy in out_copies(n_rows - 1, range(8)):
        copy.wait()


def front(p, owned, sum_rows, lengths, tokens, cot, wq, wo, w1, w2, vec, mo, m1, m2, ident):
    n, seq, d = tokens.shape
    slim, tall = wq.shape[1:]
    up = lambda r, m: -(-r // m) * m
    qrows = up(3 * tall, 32)
    rrows = up(3 * fold_rows(4 * slim, 4 * tall), 16)
    count = gather_copies(p)
    hbm = pl.BlockSpec(memory_space=pl.ANY)
    act = lambda a, b: jax.ShapeDtypeStruct((n, a, b), BF16)
    tm, mt = pltpu.VMEM((seq, d), BF16), pltpu.VMEM((d, seq), BF16)
    return pl.pallas_call(
        functools.partial(front_kernel, p, owned),
        out_shape=[act(d, seq), act(seq, d), act(d, seq), act(seq, d), act(d, seq), act(seq, d), act(seq, d), act(d, seq)]
        + [jax.ShapeDtypeStruct((n, 16, seq), F32), jax.ShapeDtypeStruct((4, 192, 576), BF16)]
        + [jax.ShapeDtypeStruct((sum_rows, 128), BF16)] * 3
        + [jax.ShapeDtypeStruct((12, 768), F32)],
        in_specs=[pl.BlockSpec(memory_space=pltpu.SMEM)] + [VMEM] * 10,
        out_specs=[hbm] * 8 + [VMEM] * 6,
        scratch_shapes=[
            pltpu.VMEM((p.Z, p.C, p.X, p.Y, qrows, 128), BF16),
            pltpu.VMEM((p.Z, p.C, p.X, p.Y, rrows, 128), BF16),
            pltpu.VMEM((p.Z * p.X // 2, 256, 1024), BF16),
            pltpu.VMEM((3, 4, 256, 256), BF16),
            mt, tm, mt, tm, pltpu.VMEM((n, d, seq), BF16),
            mt, pltpu.VMEM((seq, seq), F32), pltpu.VMEM((d, 8), F32),
            pltpu.VMEM((4, 256, 768), BF16), pltpu.VMEM((4, 256, 768), BF16), pltpu.VMEM((768, 768), BF16),
            tm, tm, mt,
            pltpu.SemaphoreType.DMA((count,)), pltpu.SemaphoreType.DMA((count,)),
            pltpu.SemaphoreType.DMA((count,)), pltpu.SemaphoreType.DMA((count,)),
            pltpu.SemaphoreType.DMA((8,)),
        ],
        compiler_params=pltpu.CompilerParams(collective_id=ident, has_side_effects=True, vmem_limit_bytes=62 * 2**20),
    )(lengths, tokens, cot, wq, wo, w1, w2, vec, mo, m1, m2)


def on_diagonal(n):
    return lax.broadcasted_iota(jnp.int32, (n, n), 0) == lax.broadcasted_iota(jnp.int32, (n, n), 1)


def ns_start(values):
    return [y * (1.0 / (jnp.sqrt(jnp.sum(y * y)) + 1e-07)) for y in values]


def ns_poly(values):
    n = values[0].shape[0]
    diag = on_diagonal(n)
    lows = [y.astype(BF16) for y in values]
    grams = [nt(l, l) for l in lows]
    mids = [jnp.sum(jnp.where(diag, g, 0.0)) * (1.0 / n) for g in grams]
    rest = [jnp.where(diag, g - m, g) for g, m in zip(grams, mids)]
    lowr = [r.astype(BF16) for r in rest]
    squares = [nn(r, r) for r in lowr]
    return mids, [((ns_second + 2.0 * ns_third * m) * r + ns_third * s).astype(BF16) for m, r, s in zip(mids, rest, squares)]


def ns_step(values, mids, polys):
    moved = [nn(q, y.astype(BF16)) for q, y in zip(polys, values)]
    return [(ns_first + ns_second * m + ns_third * m * m) * y + t for m, y, t in zip(mids, values, moved)]


def close_kernel(p, shares, *refs):
    (len_ref, wt_ref, so_ref, s1_ref, s2_ref, gv_ref, gmq_ref, wq_ref, wo_ref, w1_ref, w2_ref, vec_ref, vm1_ref, vm2_ref,
     x_hbm, qt_hbm, k_hbm, kt_hbm, v_hbm, ct_hbm, lse_ref, dct_hbm, res_hbm,
     gt_ref, mq_ref, mo_ref, m1_ref, m2_ref, nq_ref, no_ref, n1_ref, n2_ref, f_ref, s_ref, v_ref,
     x_s, qt_s, k_s, kt_s, v_s, ct_s, dct_s, res_s, bias_s, dq_s, dk_s, dv_s, gq_s, gv2_s, sq_s, oo_s, o1_s, o2_s, oq_s,
     y_s, po_s, pf_s, mid_s, xo_s, xf_s, xq_s, xo_r, xf_r, xq_r, in_sem, x_send, x_recv) = refs[: 35 + 32]
    rest = refs[35 + 32 :]
    p.locate()
    d, n = lax.axis_index("dp"), lax.axis_index("narrow")
    n_rows, seq = x_s.shape[:2]
    pairs = ((qt_hbm, qt_s), (k_hbm, k_s), (dct_hbm, dct_s), (v_hbm, v_s), (ct_hbm, ct_s), (kt_hbm, kt_s), (x_hbm, x_s), (res_hbm, res_s))

    def loads(row):
        return [pltpu.make_async_copy(src.at[row], dst.at[row], in_sem.at[row, i]) for i, (src, dst) in enumerate(pairs)]

    for row in range(n_rows):
        for copy in loads(row):
            copy.start()
    p.barrier()
    sums = [sum_steps(p, s, src, out, rest[10 * i : 10 * i + 10])
            for i, (s, src, out) in enumerate(zip(shares, (so_ref, s1_ref, s2_ref, sq_s), (oo_s, o1_s, o2_s, oq_s)))]
    o, f1, f2, q = sums
    for step in (o[0], f1[0], f2[0]):
        step()
    turns = dealt([o[1], f1[1], o[2], f2[1], o[3], f1[2], o[4], f2[2], o[5], f1[3], o[6], f2[3], o[7], f1[4], f2[4]], 6 * n_rows)
    gq_s[...] = jnp.zeros_like(gq_s)
    gv2_s[...] = jnp.zeros_like(gv2_s)
    lane = lax.broadcasted_iota(jnp.int32, (192, 256), 1)

    def one_row(row, carry):
        same = ids(len_ref, row, (seq, seq), 0) == ids(len_ref, row, (seq, seq), 1)
        bias_s[...] = jnp.where(same, 0.0, -1e30)
        for copy in loads(row):
            copy.wait()

        def pair(j, carry):
            lo = pl.multiple_of(128 * j, 128)
            kp, vp = k_s[row, :, pl.ds(lo, 128)], v_s[row, :, pl.ds(lo, 128)]
            for e in range(2):
                at = pl.ds(pl.multiple_of(lo + 64 * e, 64), 64)
                qh, dc = qt_s[row, at, :], dct_s[row, at, :]
                none = jnp.zeros_like(qh)
                wide = lambda a: jnp.concatenate([none, a] if e else [a, none], axis=0)
                delta = jnp.sum(dc.astype(F32) * ct_s[row, at, :].astype(F32), axis=0, keepdims=True)
                s = nn(kp, wide(qh)) + bias_s[...]
                ex = jnp.exp(s - lse_ref[row, pl.ds(2 * j + e, 1), :])
                de = nn(vp, wide(dc))
                ds = (ex * (de - delta)).astype(BF16)
                dv_s[at, :] = nt(dc, ex.astype(BF16)).astype(BF16)
                dk_s[at, :] = nt(qh, ds).astype(BF16)
                dq_s[at, :] = (nn(kt_s[row, at, :], ds) * 0.125).astype(BF16)
            at_turn(row * 6 + j, turns)
            return carry

        lax.fori_loop(0, 6, pair, 0)
        dx = []
        for g in range(4):
            lo = window(g)
            r = slice(192 * g, 192 * g + 192)
            cat = jnp.concatenate([dq_s[r, :], dk_s[r, :], dv_s[r, :]], axis=0)
            dx.append(nn(wt_ref[g], cat))
            gq = nn(cat, x_s[row, :, lo : lo + 256])
            keep = (lane < 192) if g % 2 == 0 else (lane >= 64)
            for c in range(3):
                gq_s[c, :, lo : lo + 256] += jnp.where(keep, gq[192 * c : 192 * c + 192], 0.0)
        gt_ref[row] = (res_s[row] + jnp.concatenate(dx, axis=0).T).astype(BF16)
        ones = jnp.ones((16, seq), BF16)
        gv2_s[0:1, :] += nt(ones, dq_s[...])[0:1]
        gv2_s[1:2, :] += nt(ones, dv_s[...])[0:1]
        return carry

    lax.fori_loop(0, n_rows, one_row, 0)
    slim, tall = gmq_ref.shape[1:]
    up = hot((192, tall), 0, n * tall)
    for c in range(3):
        held = jnp.zeros((tall, 768), F32)
        for g in range(4):
            held = held + tn((0.95 * gmq_ref[4 * c + g]).astype(BF16), hot((slim, 768), 192 * g + d * slim, 0))
        put_blocks(sq_s, 1152 * c, gq_s[c] + nn(up, held.astype(BF16)))
    gv = jnp.concatenate([gv_ref[0:4], gv2_s[0:2], gv_ref[6:12]], axis=0)
    tail = sq_s.shape[0] - 3456
    flat = jnp.concatenate([gv[:, 128 * j : 128 * j + 128] for j in range(6)] + [jnp.zeros((tail - 72, 128), F32)], axis=0)
    sq_s[3456:, :] = flat.astype(BF16)
    for step in (q[0], o[8], q[1]):
        step()
    wide, cols = w1_ref.shape[2], w1_ref.shape[1]
    sel_l = hot((wide, 768), n * wide, 0)
    sel_s = hot((cols, 192), d * cols, 0)
    big = wo_ref.shape[2]
    sel_b = hot((big, 768), d * big, 0)
    core0, core1 = p.c == 0, p.c == 1
    eight = lambda: [y_s[192 * i : 192 * i + 192, :] for i in range(8)]

    late = 3
    before = [[f1[5]], [f1[6]], [f1[7]], [q[5]], [q[7]]]
    between = [[q[2], f2[5]], [q[3], f2[6]], [q[4], f2[7], f1[8], f2[8]], [q[6]], [q[8]]]

    def sweep(t, carry):
        on0 = jnp.logical_and(core0, t < NS_STEPS)
        on1 = jnp.logical_and(core1, t >= late)

        @pl.when(jnp.logical_and(core0, t == 0))
        def _():
            y_s[0:768, :] = ns_start([wide_rows(oo_s, 0, 4).astype(F32)])[0]

        @pl.when(jnp.logical_and(core1, t == late))
        def _():
            for i, y in enumerate(ns_start([wide_rows(r, 1152 * g, 1).astype(F32) for r in (o1_s, o2_s) for g in range(4)])):
                y_s[192 * i : 192 * i + 192, :] = y

        @pl.when(on0)
        def _():
            mids, polys = ns_poly([y_s[0:768, :]])
            mid_s[0:1, :] = jnp.broadcast_to(mids[0], (1, 128))
            po_s[...] = polys[0]

        @pl.when(on1)
        def _():
            mids, polys = ns_poly(eight())
            for i in range(8):
                mid_s[i : i + 1, :] = jnp.broadcast_to(mids[i], (1, 128))
                pf_s[i] = polys[i]

        at_turn(t, before)

        @pl.when(on0)
        def _():
            y_s[0:768, :] = ns_step([y_s[0:768, :]], [mid_s[0:1, 0:1]], [po_s[...]])[0]

        @pl.when(on1)
        def _():
            for i, y in enumerate(ns_step(eight(), [mid_s[i : i + 1, 0:1] for i in range(8)], [pf_s[i] for i in range(8)])):
                y_s[192 * i : 192 * i + 192, :] = y

        at_turn(t, between)
        return carry

    lax.fori_loop(0, NS_STEPS + late, sweep, 0)
    wires = Wires(p, x_send, x_recv)
    mo_ref[0] = nt(sel_l, nn(sel_b, wide_rows(oo_s, 0, 4)).astype(BF16))
    for ref, m_ref in ((o1_s, m1_ref), (o2_s, m2_ref)):
        for g in range(4):
            m_ref[g] = nt(nn(sel_s, wide_rows(ref, 1152 * g, 1)).astype(BF16), sel_l)

    @pl.when(core0)
    def _():
        xo_s[...] = nn(sel_b, y_s[0:768, :].astype(BF16)).astype(BF16)

    @pl.when(core1)
    def _():
        for i in range(8):
            xf_s[cols * i : cols * i + cols, :] = nn(sel_s, y_s[192 * i : 192 * i + 192, :].astype(BF16)).astype(BF16)

    rows = [wide_rows(oq_s, 1152 * c, 1) for c in range(3)]
    spot = lambda g: hot_cut((256, 128), 0, 0)

    def square(parity):
        keep = (lane < 192) if parity == 0 else (lane >= 64)
        which = [(c, g) for c in range(3) for g in (parity, parity + 2)]
        ys = ns_start([jnp.where(keep, rows[c][:, window(g) : window(g) + 256].astype(F32), 0.0) for c, g in which])
        for i, y in enumerate(ys):
            y_s[192 * i : 192 * i + 192, :256] = y

        def turn(t, carry):
            ys = [y_s[192 * i : 192 * i + 192, :256] for i in range(6)]
            for i, y in enumerate(ns_step(ys, *ns_poly(ys))):
                y_s[192 * i : 192 * i + 192, :256] = y
            return carry

        lax.fori_loop(0, NS_STEPS, turn, 0)
        ys = [y_s[192 * i : 192 * i + 192, :256] for i in range(6)]
        for c in range(3):
            part = jnp.zeros((192, 128), F32)
            for (cc, g), y in zip(which, ys):
                if cc == c:
                    at = 64 * (g % 2) + d * slim
                    r = lax.broadcasted_iota(jnp.int32, (256, 128), 0) - at
                    q = lax.broadcasted_iota(jnp.int32, (256, 128), 1) - g * slim
                    sel = jnp.logical_and(r == q, jnp.logical_and(q >= 0, q < slim)).astype(BF16)
                    part = part + nn(y.astype(BF16), sel)
            xq_s[192 * c : 192 * c + 192, :] = part.astype(BF16)

    @pl.when(core0)
    def _():
        square(0)

    @pl.when(core1)
    def _():
        square(1)

    copies = [wires.plan(lambda a=a: a, lambda b=b: b, "c", 1) for a, b in ((xq_s, xq_r), (xo_s, xo_r), (xf_s, xf_r))]
    wires.start(copies)
    sel_o = hot((tall, 192), n * tall, 0)
    for c in range(3):
        mine = nn(sel_o, rows[c]).astype(BF16)
        for g in range(4):
            mq_ref[4 * c + g] = nt(hot((slim, 768), 192 * g + d * slim, 0), mine)
    vt = oq_s[3456 : 3456 + 80, :].astype(F32)
    grad = jnp.concatenate([vt[12 * j : 12 * j + 12] for j in range(6)], axis=1)
    first = 0.9 * vm1_ref[...] + 0.1 * grad
    second = 0.999 * vm2_ref[...] + 0.001 * grad * grad
    f_ref[...] = first
    s_ref[...] = second
    v_ref[...] = vec_ref[...] - adam_rate * (first * (1.0 / (1.0 - 0.9**STEP))) / (jnp.sqrt(second * (1.0 / (1.0 - 0.999**STEP))) + 1e-08)

    def fresh(w, own, longest):
        return w - muon_rate * (0.2 * math.sqrt(longest) * own + muon_decay * w)

    wires.arrive(copies)
    for c in range(3):
        both = (xq_s[192 * c : 192 * c + 192, :].astype(F32) + xq_r[192 * c : 192 * c + 192, :].astype(F32)).astype(BF16)
        mine = nn(sel_o, both).astype(BF16)
        for g in range(4):
            nq_ref[4 * c + g] = fresh(wq_ref[4 * c + g], nt(hot((slim, 128), g * slim, 0), mine), 192)
    xo = jnp.where(core0, xo_s[...], xo_r[...])
    no_ref[0] = fresh(wo_ref[0], nt(sel_l, xo), 768)
    for i, (w_ref, n_ref) in enumerate(((w1_ref, n1_ref), (w2_ref, n2_ref))):
        for g in range(4):
            at = slice(cols * (4 * i + g), cols * (4 * i + g) + cols)
            n_ref[g] = fresh(w_ref[g], nt(jnp.where(core1, xf_s[at, :], xf_r[at, :]), sel_l), 768)
    wires.finish()


def closing(p, shares, lengths, wt, so, s1, s2, gv, mq, weights, vec, vm1, vm2, acts, ident):
    tokens, lse = acts[0], acts[6]
    n, seq, d = tokens.shape
    slim = mq.shape[1]
    shape = lambda a: jax.ShapeDtypeStruct(a.shape, F32)
    outs = [jax.ShapeDtypeStruct(tokens.shape, BF16)] + [shape(w) for w in weights] * 2 + [shape(vec)] * 3
    hbm = pl.BlockSpec(memory_space=pl.ANY)
    tm, mt = pltpu.VMEM((n, seq, d), BF16), pltpu.VMEM((n, d, seq), BF16)
    flat = lambda r: pltpu.VMEM((r, 128), BF16)
    scratch = [tm, mt, tm, mt, tm, mt, mt, pltpu.VMEM((n, seq, d), BF16), pltpu.VMEM((seq, seq), F32)]
    scratch += [pltpu.VMEM((d, seq), BF16)] * 3 + [pltpu.VMEM((3, 192, 768), F32), pltpu.VMEM((8, 768), F32)]
    scratch += [flat(shares[3].rows)] + [flat(s.rows) for s in shares]
    scratch += [pltpu.VMEM((1536, 768), F32), pltpu.VMEM((768, 768), BF16), pltpu.VMEM((8, 192, 192), BF16), pltpu.VMEM((8, 128), F32)]
    scratch += [pltpu.VMEM((4 * slim, 768), BF16), pltpu.VMEM((8 * slim, 768), BF16), pltpu.VMEM((576, 128), BF16)] * 2
    scratch += [pltpu.SemaphoreType.DMA((n, 8)), pltpu.SemaphoreType.DMA((3,)), pltpu.SemaphoreType.DMA((3,))]
    for s in shares:
        scratch += s.scratch(p)
    return pl.pallas_call(
        functools.partial(close_kernel, p, shares),
        out_shape=outs,
        in_specs=[pl.BlockSpec(memory_space=pltpu.SMEM)] + [VMEM] * 13 + [hbm] * 6 + [VMEM] + [hbm] * 2,
        out_specs=[VMEM] * 12,
        scratch_shapes=scratch,
        compiler_params=pltpu.CompilerParams(collective_id=ident, has_side_effects=True, vmem_limit_bytes=62 * 2**20),
    )(lengths, wt, so, s1, s2, gv, mq, *weights, vec, vm1, vm2, *acts)


class Owned:
    def __init__(self, p, half):
        self.half, self.rows, self.copies = half, 8 * half, 4 + 2 * (p.Z - 1)
        self.kinds = [4 * half, 4 * half, 2 * half, half, (p.Z - 1) * (half // p.Z), half, half]

    def scratch(self):
        return [pltpu.VMEM((k, 128), BF16) for k in self.kinds] + [pltpu.SemaphoreType.DMA((self.copies,))] * 2


def owned_steps(p, s, src, scratch):
    held, from_c, r1, r2, r3, mine, other, send_sem, recv_sem = scratch
    wires = Wires(p, send_sem, recv_sem)
    h, q, z, c = s.half, s.half // p.Z, p.z, p.c
    first = jnp.where(c == 0, p.x, p.y)
    second = jnp.where(c == 0, p.y, p.x)
    cut = lambda ref, start, size: lambda: ref.at[spread(start(), size)]

    def partner(turn):
        along_x = c == turn
        x, y = jnp.where(along_x, 1 - p.x, p.x), jnp.where(along_x, p.y, 1 - p.y)
        return (z * p.X + x, y * p.C + c)

    sibling = lambda: p.device("c", 1)
    spot = lambda: (2 * first + second) * h
    sends = [
        [wires.plan_to(cut(src, lambda: (1 - c) * 4 * h, 4 * h), lambda: from_c, sibling)],
        [wires.plan_to(cut(held, lambda: (1 - first) * 2 * h, 2 * h), lambda: r1, lambda: partner(0))],
        [wires.plan_to(cut(held, lambda: (2 * first + 1 - second) * h, h), lambda: r2, lambda: partner(1))],
        [],
        [],
        [wires.plan_to(lambda: mine, lambda: other, sibling)],
    ]
    for j in range(1, p.Z):
        sends[3].append(wires.plan(cut(held, lambda j=j: spot() + p.at("z", j) * q, q), lambda j=j: r3.at[pl.ds((j - 1) * q, q)], "z", j))
        sends[4].append(wires.plan(*(cut(mine, lambda: z * q, q),) * 2, "z", j))

    def add(dst, to, ref, start, size, parts):
        value = ref[spread(start, size), :].astype(F32)
        for part in parts:
            value = value + part().astype(F32)
        dst[spread(to, size), :] = value.astype(BF16)

    def step(t):
        if 1 <= t <= 5:
            wires.arrive(sends[t - 1])
        if t == 1:
            add(held, 0, src, c * 4 * h, 4 * h, [lambda: from_c[...]])
        if t == 2:
            add(held, first * 2 * h, held, first * 2 * h, 2 * h, [lambda: r1[...]])
        if t == 3:
            add(held, spot(), held, spot(), h, [lambda: r2[...]])
        if t == 4:
            add(mine, z * q, held, spot() + z * q, q, [lambda j=j: r3[(j - 1) * q : j * q, :] for j in range(1, p.Z)])
        if t < 5:
            wires.start(sends[t])
        if t == 5:

            @pl.when(c == 0)
            def _():
                wires.start(sends[5])

        if t == 6:
            wires.finish(skip=sends[5])

            @pl.when(c == 0)
            def _():
                wires.leave(sends[5])

            @pl.when(c == 1)
            def _():
                wires.arrive(sends[5])

    return [functools.partial(step, t) for t in range(7)]


class Solo:
    def __init__(self, p, half):
        self.half, self.rows, self.copies = half, 8 * half, 1 + 4 + 4 * (p.Z - 1)
        q = (p.Z - 1) * (half // p.Z)
        self.kinds = [8 * half, 8 * half] + [2 * half, half, q] * 2 + [2 * half]

    def scratch(self):
        return [pltpu.VMEM((k, 128), BF16) for k in self.kinds] + [pltpu.SemaphoreType.DMA((self.copies,))] * 2


def solo_steps(p, s, src, scratch):
    held, from_c, a1, a2, a3, b1, b2, b3, mine, send_sem, recv_sem = scratch
    wires = Wires(p, send_sem, recv_sem)
    h, q, z = s.half, s.half // p.Z, p.z
    cut = lambda ref, start, size: lambda: ref.at[spread(start(), size)]
    over = [wires.plan_to(lambda: src, lambda: from_c, lambda: p.device("c", 1))]
    sends = [[], [], [], []]
    ways = (("x", "y", p.x, p.y, 0, a1, a2, a3, 0), ("y", "x", p.y, p.x, 4 * h, b1, b2, b3, h))
    for one, two, first, second, base, r1, r2, r3, to in ways:
        sends[0].append(wires.plan(cut(held, lambda f=first, b=base: b + (1 - f) * 2 * h, 2 * h), lambda r=r1: r, one, 1))
        sends[1].append(wires.plan(cut(held, lambda f=first, e=second, b=base: b + (2 * f + 1 - e) * h, h), lambda r=r2: r, two, 1))
        for j in range(1, p.Z):
            part = lambda f=first, e=second, b=base, j=j: b + (2 * f + e) * h + p.at("z", j) * q
            sends[2].append(wires.plan(cut(held, part, q), lambda r=r3, j=j: r.at[pl.ds((j - 1) * q, q)], "z", j))
            sends[3].append(wires.plan(*(cut(mine, lambda t=to: t + z * q, q),) * 2, "z", j))

    def add(dst, to, ref, start, size, parts):
        value = ref[spread(start, size), :].astype(F32)
        for part in parts:
            value = value + part.astype(F32)
        dst[spread(to, size), :] = value.astype(BF16)

    def give():
        wires.start(over)

    def gave():
        wires.leave(over)

    def step(t):
        wires.arrive(over if t == 0 else sends[t - 1])
        if t == 0:
            held[...] = (src[...].astype(F32) + from_c[...].astype(F32)).astype(BF16)
        for one, two, first, second, base, r1, r2, r3, to in ways:
            spot = base + (2 * first + second) * h
            if t == 1:
                add(held, base + first * 2 * h, held, base + first * 2 * h, 2 * h, [r1[...]])
            if t == 2:
                add(held, spot, held, spot, h, [r2[...]])
            if t == 3:
                add(mine, to + z * q, held, spot + z * q, q, [r3[(j - 1) * q : j * q, :] for j in range(1, p.Z)])
        if t < 4:
            wires.start(sends[t])
        else:
            wires.finish(skip=over)

    return give, gave, [functools.partial(step, t) for t in range(5)]


def canon(odd, base):
    r = lax.broadcasted_iota(jnp.int32, (256, 128), 0)
    s = lax.broadcasted_iota(jnp.int32, (256, 128), 1)
    channel = jnp.where(odd, jnp.where(r < 128, r + 64, r - 128), r)
    return jnp.where(r < 192, channel - base, -1000), s


def paced(o, f1, f2):
    return ((5, o[2]), (7, f1[1]), (10, o[3]), (10, f2[1]), (13, f1[2]), (16, o[4]), (16, f2[2]), (19, f1[3]), (22, o[5]), (23, f2[3]))


def owner_kernel(p, shares, *refs):
    (len_ref, wt_ref, so_hbm, s1_hbm, s2_hbm, gv_ref, gmq_ref, wq_ref, wo_ref, w1_ref, w2_ref, vec_ref, vm1_ref, vm2_ref,
     x_hbm, qt_hbm, k_hbm, kt_hbm, v_hbm, ct_hbm, lse_ref, dct_hbm, res_hbm,
     gt_ref, mq_ref, mo_ref, m1_ref, m2_ref, nq_ref, no_ref, n1_ref, n2_ref, f_ref, s_ref, v_ref,
     so_ref, s1_ref, s2_ref, x_s, qt_s, k_s, kt_s, v_s, ct_s, dct_s, res_s, bias_s, dq_s, dk_s, dv_s, gq_s, gv2_s, sq_s, oo_s,
     yo_s, yf_s, yq_s, xo_s, xo_r, tmf_s, txf_s, tmq_s, txq_s, tv_s, rmf_s, rxf_s, rmq_s, rxq_s, rv_s,
     in_sem, src_sem, x_send, x_recv) = refs[: 35 + 38]
    rest = refs[35 + 38 :]
    p.locate()
    p.greet(corner=True)
    d, n = lax.axis_index("dp"), lax.axis_index("narrow")
    core0, core1 = p.c == 0, p.c == 1
    n_rows, seq = x_s.shape[:2]
    pairs = ((qt_hbm, qt_s), (k_hbm, k_s), (dct_hbm, dct_s), (v_hbm, v_s), (ct_hbm, ct_s), (kt_hbm, kt_s), (x_hbm, x_s), (res_hbm, res_s))

    def loads(row):
        return [pltpu.make_async_copy(src.at[row], dst.at[row], in_sem.at[row, i]) for i, (src, dst) in enumerate(pairs)]

    sources = [pltpu.make_async_copy(a, b, src_sem.at[i]) for i, (a, b) in enumerate(((so_hbm, so_ref), (s1_hbm, s1_ref), (s2_hbm, s2_ref)))]
    for copy in sources[:1] + loads(0) + sources[1:]:
        copy.start()
    for row in range(1, n_rows):
        for copy in loads(row):
            copy.start()
    o = sum_steps(p, shares[0], so_ref, oo_s, rest[:10])
    f1 = owned_steps(p, shares[1], s1_ref, rest[10:19])
    f2 = owned_steps(p, shares[2], s2_ref, rest[19:28])
    q_give, q_gave, q = solo_steps(p, shares[3], sq_s, rest[28:39])
    q_all = rest[36]
    f1_half, f1_other, f2_half, f2_other = rest[15], rest[16], rest[24], rest[25]
    p.meet(corner=True)
    sources[0].wait()
    o[0]()
    turns = [[] for _ in range(12 * n_rows)]
    for i, step in paced(o, f1, f2):
        turns[i * n_rows // 2].append(step)
    gq_s[...] = jnp.zeros_like(gq_s)
    gv2_s[...] = jnp.zeros_like(gv2_s)
    lane = lax.broadcasted_iota(jnp.int32, (192, 256), 1)

    def one_row(row, carry):
        same = ids(len_ref, row, (seq, seq), 0) == ids(len_ref, row, (seq, seq), 1)
        bias_s[...] = jnp.where(same, 0.0, -1e30)
        for copy in loads(row):
            copy.wait()

        @pl.when(row == 0)
        def _():
            for copy in sources[1:]:
                copy.wait()
            o[1]()
            f1[0]()
            f2[0]()

        def pair(j, carry):
            lo = pl.multiple_of(128 * j, 128)
            kp, vp = k_s[row, :, pl.ds(lo, 128)], v_s[row, :, pl.ds(lo, 128)]
            for e in range(2):
                at = pl.ds(pl.multiple_of(lo + 64 * e, 64), 64)
                qh, dc = qt_s[row, at, :], dct_s[row, at, :]
                none = jnp.zeros_like(qh)
                wide = lambda a: jnp.concatenate([none, a] if e else [a, none], axis=0)
                delta = jnp.sum(dc.astype(F32) * ct_s[row, at, :].astype(F32), axis=0, keepdims=True)
                s = nn(kp, wide(qh)) + bias_s[...]
                ex = jnp.exp(s - lse_ref[row, pl.ds(2 * j + e, 1), :])
                de = nn(vp, wide(dc))
                ds = (ex * (de - delta)).astype(BF16)
                dv_s[row, at, :] = nt(dc, ex.astype(BF16)).astype(BF16)
                dk_s[row, at, :] = nt(qh, ds).astype(BF16)
                dq_s[row, at, :] = (nn(kt_s[row, at, :], ds) * 0.125).astype(BF16)
                at_turn(row * 12 + 2 * j + e, turns)
            return carry

        lax.fori_loop(0, 6, pair, 0)
        for g in range(4):
            lo = window(g)
            r = slice(192 * g, 192 * g + 192)
            gq = nn(jnp.concatenate([dq_s[row, r, :], dk_s[row, r, :], dv_s[row, r, :]], axis=0), x_s[row, :, lo : lo + 256])
            keep = (lane < 192) if g % 2 == 0 else (lane >= 64)
            for c in range(3):
                gq_s[c, :, lo : lo + 256] += jnp.where(keep, gq[192 * c : 192 * c + 192], 0.0)
        ones = jnp.ones((16, seq), BF16)
        gv2_s[0:1, :] += nt(ones, dq_s[row])[0:1]
        gv2_s[1:2, :] += nt(ones, dv_s[row])[0:1]
        return carry

    lax.fori_loop(0, n_rows, one_row, 0)
    slim, tall = gmq_ref.shape[1:]
    half = shares[3].half
    up = hot((192, tall), 0, n * tall)
    values = []
    for c in range(3):
        held = jnp.zeros((tall, 768), F32)
        for g in range(4):
            held = held + tn((0.95 * gmq_ref[4 * c + g]).astype(BF16), hot((slim, 768), 192 * g + d * slim, 0))
        values.append(gq_s[c] + nn(up, held.astype(BF16)))
    gv = jnp.concatenate([gv_ref[0:4], gv2_s[0:2], gv_ref[6:12]], axis=0)
    lane = lax.broadcasted_iota(jnp.int32, (192, 128), 1)
    for g in range(4):
        lo = window(g)
        tiles = []
        edges = []
        for c in range(3):
            a, b = values[c][:, lo : lo + 128], values[c][:, lo + 128 : lo + 256]
            whole, edge = (b, pltpu.roll(a, 64, 1)) if g % 2 else (a, b)
            tiles.append(whole)
            edges.append(jnp.where(lane < 64, edge, 0.0))
        tiles.append(edges[0] + pltpu.roll(edges[1], 64, 1))
        tiles.append(edges[2][:96] + pltpu.roll(edges[2][96:], 64, 1))
        vec = [gv[0:8, 192 * g : 192 * g + 128]]
        vec.append(jnp.concatenate([gv[0:8, 192 * g + 128 : 192 * g + 192], jnp.zeros((8, 64), F32)], axis=1))
        vec += [gv[8 + g : 9 + g, 128 * j : 128 * j + 128] for j in range(6)]
        vec.append(jnp.zeros((2 * half - 864 - 22, 128), F32))
        flat = jnp.concatenate(tiles + vec, axis=0).astype(BF16)
        sq_s[g * half : g * half + half, :] = flat[:half]
        sq_s[(4 + turned(g)) * half : (5 + turned(g)) * half, :] = flat[half:]
    def blocks(a_ref, b_ref):
        return jnp.concatenate([r[192 * j : 192 * j + 192, :] for r in (a_ref, b_ref) for j in range(3)], axis=1)

    def grad_in(row):
        dx = []
        for g in range(4):
            r = slice(192 * g, 192 * g + 192)
            dx.append(nn(wt_ref[g], jnp.concatenate([dq_s[row, r, :], dk_s[row, r, :], dv_s[row, r, :]], axis=0)))
        gt_ref[row] = (res_s[row].astype(F32) + jnp.concatenate(dx, axis=0).T).astype(BF16)

    wires = Wires(p, x_send, x_recv)
    me = 2 * p.x + p.y
    odd = lax.rem(me, 2) == 1
    around = ((1, 0), (0, 1), (1, 1))

    def scatter(src, dst, cores=(1,)):
        return [
            wires.plan_to(
                lambda dx=dx, dy=dy: src.at[lax.rem(p.x + dx, 2), lax.rem(p.y + dy, 2)], lambda: dst.at[me], lambda dx=dx, dy=dy, c=c: p.other(dx, dy, c)
            )
            for dx, dy in around
            for c in cores
        ]

    early = [scatter(a, b) for a, b in ((tmf_s, rmf_s), (txf_s, rxf_s), (tmq_s, rmq_s), (tv_s, rv_s))]
    late = scatter(txq_s, rxq_s, (0, 1))
    late += [wires.plan_to(lambda: txq_s.at[p.x, p.y], lambda: rxq_s.at[me], lambda: p.device("c", 1))]
    late_on = {0: [late[0], late[2], late[4], late[6]], 1: [late[1], late[3], late[5]]}
    sibling = lambda: p.device("c", 1)
    pass_early = [wires.plan_to(lambda a=a: a, lambda a=a: a, sibling) for a in (rmf_s, rxf_s, rmq_s, rv_s)]
    pass_o = [wires.plan_to(lambda: xo_s, lambda: xo_r, sibling)]
    big = wo_ref.shape[2]
    sel_b = hot((big, 768), d * big, 0)
    wide, cols = w1_ref.shape[2], w1_ref.shape[1]

    def put_f(dst, pair):
        for x in range(2):
            sel = hot((cols, 192), (p.z * 2 + x) * cols, 0)
            part = jnp.concatenate([nn(sel, m) for m in pair], axis=0).astype(BF16)
            for y in range(2):
                dst[x, y] = part[:, 384 * y : 384 * y + 384]

    def put_q(dst, three):
        for x in range(2):
            part = jnp.zeros((192, 128), F32)
            for c, m in enumerate(three):
                at, s = canon(odd, (p.z * 2 + x) * slim)
                sel = jnp.logical_and(jnp.logical_and(at >= 0, at < slim), at + c * slim == s).astype(BF16)
                part = part + nn(m, sel)
            for y in range(2):
                dst[x, y] = part[96 * y : 96 * y + 96].astype(BF16)

    @pl.when(core0)
    def _():
        q_give()
        for step in (lambda: grad_in(0), o[6], f1[4], f2[4], lambda: grad_in(1), f1[5], o[7], f2[5], o[8], f1[6], f2[6]):
            step()
        yo_s[...] = ns_start([wide_rows(oo_s, 0, 4).astype(F32)])[0]

        def turn(t, carry):
            y = yo_s[...]
            yo_s[...] = ns_step([y], *ns_poly([y]))[0]
            return carry

        lax.fori_loop(0, NS_STEPS, turn, 0)
        xo_s[...] = nn(sel_b, yo_s[...].astype(BF16)).astype(BF16)
        wires.start(pass_o)
        q_gave()

    @pl.when(core1)
    def _():
        for step in (q[0], o[6], f1[4], f2[4], lambda: grad_in(0), q[1], lambda: grad_in(1), f1[5], o[7], f2[5], o[8], q[2], f1[6], f2[6]):
            step()
        for i, y in enumerate(ns_start([blocks(a, b).astype(F32) for a, b in ((f1_other, f1_half), (f2_other, f2_half))])):
            yf_s[i] = y

        def f_turn(t, carry):
            ys = [yf_s[i] for i in range(2)]
            for i, y in enumerate(ns_step(ys, *ns_poly(ys))):
                yf_s[i] = y
            return carry

        lax.fori_loop(0, 3, f_turn, 0)
        q[3]()
        lax.fori_loop(3, NS_STEPS, f_turn, 0)
        put_f(tmf_s, [blocks(f1_other, f1_half), blocks(f2_other, f2_half)])
        put_f(txf_s, [yf_s[i].astype(BF16) for i in range(2)])
        for a, b, copies in zip((tmf_s, txf_s), (rmf_s, rxf_s), early[:2]):
            wires.start(copies)
            b[me] = a[p.x, p.y]
        q[4]()
        tiles = [q_all[192 * j : 192 * j + 192, :].astype(F32) for j in range(4)]
        lane = lax.broadcasted_iota(jnp.int32, (192, 128), 1)
        last = q_all[768:864, :].astype(F32)
        last = jnp.concatenate([last, pltpu.roll(last, 64, 1)], axis=0)
        edges = [jnp.where(lane < 64, e, 0.0) for e in (tiles[3], pltpu.roll(tiles[3], 64, 1), last)]
        three = [jnp.concatenate([t, e], axis=1) for t, e in zip(tiles, edges)]
        for i, y in enumerate(ns_start(three)):
            yq_s[i] = y

        def turn(t, carry):
            ys = [yq_s[i] for i in range(3)]
            for i, y in enumerate(ns_step(ys, *ns_poly(ys))):
                yq_s[i] = y
            return carry

        lax.fori_loop(0, NS_STEPS, turn, 0)
        put_q(txq_s, [yq_s[i].astype(BF16) for i in range(3)])
        wires.start(late)
        rxq_s[me] = txq_s[p.x, p.y]
        put_q(tmq_s, [m.astype(BF16) for m in three])
        for x in range(2):
            for y in range(2):
                tv_s[x, y] = q_all[864:896, :]
        for a, b, copies in zip((tmq_s, tv_s), (rmq_s, rv_s), early[2:]):
            wires.start(copies)
            b[me] = a[p.x, p.y]
        for copies in early[:2]:
            wires.arrive(copies)
        wires.start(pass_early[:2])
        wires.arrive(pass_o)

    @pl.when(core0)
    def _():
        wires.arrive(pass_early[:2])

    def fresh(w, own, longest):
        return w - muon_rate * (0.2 * math.sqrt(longest) * own + muon_decay * w)

    sel_l = hot((wide, 768), n * wide, 0)
    sel_h = hot((wide, 384), p.c * wide, 0)
    sel_q = hot((tall, 96), p.c * tall, 0)
    mo_ref[0] = nt(sel_l, nn(sel_b, wide_rows(oo_s, 0, 4)).astype(BF16))
    no_ref[0] = fresh(wo_ref[0], nt(sel_l, jnp.where(core0, xo_s[...], xo_r[...])), 768)
    for g in range(4):
        for i, (w_ref, m_ref, n_ref) in enumerate(((w1_ref, m1_ref, n1_ref), (w2_ref, m2_ref, n2_ref))):
            at = slice(cols * i, cols * i + cols)
            m_ref[g] = nt(rmf_s[g, at, :], sel_h)
            n_ref[g] = fresh(w_ref[g], nt(rxf_s[g, at, :], sel_h), 768)

    @pl.when(core1)
    def _():
        for copies in early[2:]:
            wires.arrive(copies)
        wires.start(pass_early[2:])
        wires.arrive(late_on[1])

    @pl.when(core0)
    def _():
        wires.arrive(late_on[0])

    for g in range(4):
        own = nn(sel_q, rxq_s[g]).astype(BF16)
        for c in range(3):
            nq_ref[4 * c + g] = fresh(wq_ref[4 * c + g], nt(hot((slim, 128), c * slim, 0), own), 192)

    @pl.when(core0)
    def _():
        wires.arrive(pass_early[2:])

    for g in range(4):
        own = nn(sel_q, rmq_s[g]).astype(BF16)
        for c in range(3):
            mq_ref[4 * c + g] = nt(hot((slim, 128), c * slim, 0), own)
    parts = [rv_s[g].astype(F32) for g in range(4)]
    top = jnp.concatenate([t for v in parts for t in (v[0:8], v[8:16, :64])], axis=1)
    low = [jnp.concatenate([v[16 + j : 17 + j] for j in range(6)], axis=1) for v in parts]
    grad = jnp.concatenate([top] + low, axis=0)
    first = 0.9 * vm1_ref[...] + 0.1 * grad
    second = 0.999 * vm2_ref[...] + 0.001 * grad * grad
    f_ref[...] = first
    s_ref[...] = second
    v_ref[...] = vec_ref[...] - adam_rate * (first * (1.0 / (1.0 - 0.9**STEP))) / (jnp.sqrt(second * (1.0 / (1.0 - 0.999**STEP))) + 1e-08)

    @pl.when(core0)
    def _():
        wires.leave(pass_o)

    @pl.when(core1)
    def _():
        for copies in early + [late, pass_early]:
            wires.leave(copies)


def closing_owned(p, shares, lengths, wt, so, s1, s2, gv, mq, weights, vec, vm1, vm2, acts, ident):
    tokens = acts[0]
    n, seq, d = tokens.shape
    slim = mq.shape[1]
    shape = lambda a: jax.ShapeDtypeStruct(a.shape, F32)
    outs = [jax.ShapeDtypeStruct(tokens.shape, BF16)] + [shape(w) for w in weights] * 2 + [shape(vec)] * 3
    hbm = pl.BlockSpec(memory_space=pl.ANY)
    tm, mt = pltpu.VMEM((n, seq, d), BF16), pltpu.VMEM((n, d, seq), BF16)
    scratch = [pltpu.VMEM((4608, 128), BF16)] * 3
    scratch += [tm, mt, tm, mt, tm, mt, mt, pltpu.VMEM((n, seq, d), BF16), pltpu.VMEM((seq, seq), F32)]
    scratch += [mt] * 3 + [pltpu.VMEM((3, 192, 768), F32), pltpu.VMEM((8, 768), F32)]
    scratch += [pltpu.VMEM((shares[3].rows, 128), BF16), pltpu.VMEM((shares[0].rows, 128), BF16)]
    scratch += [pltpu.VMEM((768, 768), F32), pltpu.VMEM((2, 192, 768), F32), pltpu.VMEM((3, 192, 256), F32)]
    scratch += [pltpu.VMEM((4 * slim, 768), BF16)] * 2
    to_f, to_q, to_v = (2 * slim, 384), (96, 128), (32, 128)
    scratch += [pltpu.VMEM((2, 2) + k, BF16) for k in (to_f, to_f, to_q, to_q, to_v)]
    scratch += [pltpu.VMEM((4,) + k, BF16) for k in (to_f, to_f, to_q, to_q, to_v)]
    scratch += [pltpu.SemaphoreType.DMA((n, 8)), pltpu.SemaphoreType.DMA((3,)), pltpu.SemaphoreType.DMA((24,)), pltpu.SemaphoreType.DMA((24,))]
    scratch += shares[0].scratch(p)
    for s in shares[1:]:
        scratch += s.scratch()
    return pl.pallas_call(
        functools.partial(owner_kernel, p, shares),
        out_shape=outs,
        in_specs=[pl.BlockSpec(memory_space=pltpu.SMEM), VMEM] + [hbm] * 3 + [VMEM] * 9 + [hbm] * 6 + [VMEM] + [hbm] * 2,
        out_specs=[VMEM] * 12,
        scratch_shapes=scratch,
        compiler_params=pltpu.CompilerParams(collective_id=ident, has_side_effects=True, vmem_limit_bytes=62 * 2**20),
    )(lengths, wt, so, s1, s2, gv, mq, *weights, vec, vm1, vm2, *acts)


def hand_over_kernel(*refs):
    half = len(refs) // 2
    for src, dst in zip(refs[:half], refs[half:]):
        dst[...] = src[...]


def hand_over(values):
    return pl.pallas_call(
        hand_over_kernel,
        out_shape=[jax.ShapeDtypeStruct(a.shape, a.dtype) for a in values],
        in_specs=[VMEM] * len(values),
        out_specs=[VMEM] * len(values),
        compiler_params=pltpu.CompilerParams(vmem_limit_bytes=60 * 2**20),
    )(*values)


def local(tokens, doc_lengths, cotangent, qkv_weight, out_weight, ffn_in_weight, ffn_out_weight, vectors,
          qkv_moment, out_moment, ffn_in_moment, ffn_out_moment, vec_moment1, vec_moment2):
    p = Place(lax.axis_size("dp"), lax.axis_size("narrow"))
    flip = lambda a: a.transpose(0, 2, 1)
    wq, w1, w2, mq, m1, m2 = map(flip, (qkv_weight, ffn_in_weight, ffn_out_weight, qkv_moment, ffn_in_moment, ffn_out_moment))
    owned = p.X == 2 and p.Y == 2 and p.C == 2 and p.Z in (2, 4)
    if owned:
        shares = [Shares(p, 4608), Owned(p, 576), Owned(p, 576), Solo(p, 448)]
    else:
        shares = [Shares(p, r) for r in (4608, 4608, 4608, 3456 + 72)]
    qt, k, kt, v, ct, out_act, res, dct, lse, wt, so, s1, s2, gv = front(
        p, owned, shares[0].rows, doc_lengths, tokens, cotangent, wq, out_weight, w1, w2, vectors, out_moment, m1, m2, 0)
    acts = (tokens, qt, k, kt, v, ct, lse, dct, res)
    rest = (closing_owned if owned else closing)(
        p, shares, doc_lengths, wt, so, s1, s2, gv, mq, (wq, out_weight, w1, w2), vectors, vec_moment1, vec_moment2, acts, 1)
    out_act, gt, gq, go, g1, g2, nq, no, n1, n2, f, s, vn = hand_over([out_act] + list(rest))
    return (out_act, gt, flip(gq), go, flip(g1), flip(g2), flip(nq), no, flip(n1), flip(n2), f, s, vn)


def solution(mesh):
    rows = P(("dp", "narrow"), None, None)
    cut = P(None, "narrow", "dp")
    return jax.shard_map(
        local,
        mesh=mesh,
        in_specs=(rows, P(("dp", "narrow"), None), rows) + (cut,) * 4 + (P(),) + (cut,) * 4 + (P(), P()),
        out_specs=(rows, rows) + (cut,) * 8 + (P(),) * 3,
        check_vma=False,
    )
```

```python
import functools
import math

import jax
import jax.numpy as jnp
from jax import lax
from jax.experimental import pallas as pl
from jax.experimental.pallas import tpu as pltpu
from jax.sharding import PartitionSpec as P

F32, BF16 = jnp.float32, jnp.bfloat16
MESH = pl.DeviceIdType.MESH
NORM_EPS = 1e-05
NS_STEPS = 5
STEP = 5
ns_first = 3.4445
ns_second = -4.775
ns_third = 2.0315
muon_rate = 0.5
muon_decay = 0.01
adam_rate = 0.4
VMEM = pl.BlockSpec(memory_space=pltpu.VMEM)


def nn(a, b):
    return lax.dot_general(a, b, (((1,), (0,)), ((), ())), preferred_element_type=F32)


def nt(a, b):
    return lax.dot_general(a, b, (((1,), (1,)), ((), ())), preferred_element_type=F32)


def tn(a, b):
    return lax.dot_general(a, b, (((0,), (0,)), ((), ())), preferred_element_type=F32)


def window(g):
    return 128 * (3 * (g // 2) + g % 2)


def join(parts):
    out = []
    for p in range(2):
        a, b = parts[2 * p], parts[2 * p + 1]
        out += [a[:, :128], a[:, 128:] + b[:, :128], b[:, 128:]]
    return jnp.concatenate(out, axis=1)


def ids(len_ref, row, shape, dim):
    pos = lax.broadcasted_iota(jnp.int32, shape, dim)
    out = jnp.zeros(shape, jnp.int32)
    end = jnp.int32(0)
    for j in range(4):
        end = end + len_ref[row, j]
        out = out + (pos >= end).astype(jnp.int32)
    return out


def hot(shape, row_at, col_at):
    rows = lax.broadcasted_iota(jnp.int32, shape, 0) + row_at
    cols = lax.broadcasted_iota(jnp.int32, shape, 1) + col_at
    return (rows == cols).astype(BF16)


def put_blocks(dst, base, value):
    for j in range(value.shape[1] // 128):
        dst[base + 192 * j : base + 192 * j + 192, :] = value[:, 128 * j : 128 * j + 128].astype(BF16)


def add_blocks(dst, base, value):
    for j in range(value.shape[1] // 128):
        at = slice(base + 192 * j, base + 192 * j + 192)
        dst[at, :] = (dst[at, :].astype(F32) + value[:, 128 * j : 128 * j + 128]).astype(BF16)


def group_rows(owned, g):
    return (576 * g, 2304 + 576 * turned(g)) if owned else (1152 * g, 1152 * g + 576)


def wide_rows(ref, base, count):
    parts = []
    for q in range(count):
        at = base + 1152 * q
        parts.append(jnp.concatenate([ref[at + 192 * j : at + 192 * j + 192, :] for j in range(6)], axis=1))
    return parts[0] if count == 1 else jnp.concatenate(parts, axis=0)


def gelu_parts(v):
    t = pl.reciprocal(1.0 + (0.3275911 * 0.7071067811865476) * jnp.abs(v), approx=True)
    ex = jnp.exp2(v * v * (-0.5 * 1.4426950408889634))
    half = t * ex * (0.127414796 + t * (-0.142248368 + t * (0.7107068705 + t * (-0.7265760135 + t * 0.5307027145))))
    cdf = jnp.where(v >= 0, 1.0 - half, half)
    return v * cdf, cdf + (v * ex) * 0.3989422804014327


def norm(h):
    mu = jnp.mean(h, axis=-1, keepdims=True)
    c = h - mu
    inv = lax.rsqrt(jnp.mean(c * c, axis=-1, keepdims=True) + NORM_EPS)
    return c * inv, inv


def norm_back(up, n, inv, gain):
    w = up * gain
    return inv * (w - jnp.mean(w, axis=-1, keepdims=True) - n * jnp.mean(w * n, axis=-1, keepdims=True))


def col_sum(v):
    return jnp.sum(v, axis=0, keepdims=True)


def turned(g):
    return 2 * (g % 2) + g // 2


class Place:
    def __init__(self, dp, narrow):
        self.X = 2 if dp % 2 == 0 else 1
        self.C = 2 if narrow % 2 == 0 else 1
        self.Z, self.Y = dp // self.X, narrow // self.C

    def locate(self):
        d, n = lax.axis_index("dp"), lax.axis_index("narrow")
        self.z, self.x = d // self.X, lax.rem(d, self.X)
        self.y, self.c = n // self.C, lax.rem(n, self.C)

    def count(self):
        return self.Z + self.X + self.Y + self.C - 4

    def at(self, axis, j):
        return lax.rem(getattr(self, axis) + j, getattr(self, axis.upper()))

    def device(self, axis, j):
        where = {a: getattr(self, a) for a in "zxyc"}
        where[axis] = self.at(axis, j)
        return (where["z"] * self.X + where["x"], where["y"] * self.C + where["c"])

    def other(self, dx, dy, c):
        return (self.z * self.X + lax.rem(self.x + dx, self.X), lax.rem(self.y + dy, self.Y) * self.C + c)

    def barrier(self, corner=False):
        self.greet(corner)
        self.meet(corner)

    def greet(self, corner=False):
        sem = pltpu.get_barrier_semaphore()
        if corner:
            for c in range(self.C):
                pl.semaphore_signal(sem, inc=1, device_id=self.other(1, 1, c), device_id_type=MESH)
            for dx, dy in ((1, 0), (0, 1)):
                pl.semaphore_signal(sem, inc=1, device_id=self.other(dx, dy, 1 - self.c), device_id_type=MESH)
        for axis in "zxyc":
            for j in range(1, getattr(self, axis.upper())):
                pl.semaphore_signal(sem, inc=1, device_id=self.device(axis, j), device_id_type=MESH)

    def meet(self, corner=False):
        pl.semaphore_wait(pltpu.get_barrier_semaphore(), self.count() + 4 * int(corner))


class Wires:
    def __init__(self, place, send_sem, recv_sem):
        self.place, self.send_sem, self.recv_sem, self.makers = place, send_sem, recv_sem, []

    def plan(self, src, dst, axis, j):
        return self.plan_to(src, dst, lambda: self.place.device(axis, j))

    def plan_to(self, src, dst, device):
        k = len(self.makers)
        self.makers.append(
            lambda: pltpu.make_async_remote_copy(
                src_ref=src(),
                dst_ref=dst(),
                send_sem=self.send_sem.at[k],
                recv_sem=self.recv_sem.at[k],
                device_id=device(),
                device_id_type=MESH,
            )
        )
        return k

    def start(self, copies):
        for k in copies:
            self.makers[k]().start()

    def arrive(self, copies):
        for k in copies:
            self.makers[k]().wait_recv()

    def leave(self, copies):
        for k in copies:
            self.makers[k]().wait_send()

    def finish(self, skip=()):
        self.leave([k for k in range(len(self.makers)) if k not in skip])


def gather_copies(p):
    return (p.Z - 1) + p.Z * ((p.X - 1) + (p.Y - 1) + 2 * (p.X - 1) * (p.Y - 1) + (p.C - 1))


def gather_steps(p, wires, buf, half, corner=False):
    z, x, y, c = p.z, p.x, p.y, p.c
    rest = buf.shape[4] - half

    def same(at):
        return (lambda: buf.at[at()],) * 2

    along, first, second, last = {}, {}, {}, {}
    for j in range(1, p.Z):
        along[j] = wires.plan(*same(lambda: (z, c, x, y)), "z", j)
    for i in range(p.Z):
        from_z = lambda i=i: p.at("z", p.Z - i) if i else z
        mine = lambda f=from_z: (f(), c, x, y)
        first[i] = [wires.plan(*same(mine), "x", j) for j in range(1, p.X)] + [wires.plan(*same(mine), "y", j) for j in range(1, p.Y)]
        second[i] = []
        if corner:
            first[i].append(wires.plan_to(*same(mine), lambda: p.other(1, 1, c)))
        for j in range(1, p.X if not corner else 1):
            part = lambda f=from_z, j=j: (f(), c, p.at("x", p.X - j), y, pl.ds(0, half))
            second[i] += [wires.plan(*same(part), "y", q) for q in range(1, p.Y)]
        for j in range(1, p.Y if not corner else 1):
            part = lambda f=from_z, j=j: (f(), c, x, p.at("y", p.Y - j), pl.ds(half, rest))
            second[i] += [wires.plan(*same(part), "x", q) for q in range(1, p.X)]
        last[i] = [wires.plan(*same(lambda f=from_z: (f(), c)), "c", j) for j in range(1, p.C)]

    def own(i):
        if i:
            wires.arrive([along[i]])
        wires.start(first[i])

    def onward(i):
        wires.arrive(first[i])
        wires.start(second[i])

    def over(i):
        wires.arrive(first[i] if corner else second[i])
        wires.start(last[i])

    def done():
        for i in last:
            wires.arrive(last[i])

    of = lambda f: [functools.partial(f, i) for i in range(p.Z)]
    return lambda: wires.start(along.values()), of(own), [] if corner else of(onward), of(over), done


class Shares:
    def __init__(self, p, rows):
        cells = p.X * p.Y * p.Z
        unit = 16 * cells * p.C
        units = -(-rows // unit)
        self.a, self.b = 16 * ((units + 1) // 2), 16 * max(units // 2, 1)
        self.per_core = cells * (self.a + self.b)
        self.rows = p.C * self.per_core
        self.cells = cells
        self.copies = 2 * ((p.C - 1) + 2 * ((p.X - 1) + (p.Y - 1)) + 2 * (p.Z - 1))

    def scratch(self, p):
        a, b = self.a, self.b
        kinds = [
            (self.per_core,),
            (p.C - 1, self.per_core),
            (p.X - 1, p.Y * p.Z * a),
            (p.Y - 1, p.X * p.Z * b),
            (p.Y - 1, p.Z * a),
            (p.X - 1, p.Z * b),
            (p.Z - 1, a),
            (p.Z - 1, b),
        ]
        return [pltpu.VMEM(k + (128,), BF16) for k in kinds] + [pltpu.SemaphoreType.DMA((self.copies,))] * 2


def spread(start, size):
    return pl.ds(pl.multiple_of(start, 16), size)


def add_into(dst, at, parts):
    total = dst[at, :].astype(F32)
    for part in parts:
        total = total + part.astype(F32)
    dst[at, :] = total.astype(BF16)


def sum_steps(p, s, src, out, scratch):
    held, from_c, a1, b1, a2, b2, a3, b3, send_sem, recv_sem = scratch
    wires = Wires(p, send_sem, recv_sem)
    a, b, per = s.a, s.b, s.per_core
    ax, by = p.Y * p.Z * a, p.X * p.Z * b
    in_a = lambda x, y=0, z=0: ((x * p.Y + y) * p.Z + z) * a
    in_b = lambda y, x=0, z=0: s.cells * a + ((y * p.X + x) * p.Z + z) * b
    x, y, z, c = p.x, p.y, p.z, p.c
    base = c * per

    def cut(ref, start, size):
        return lambda: ref.at[spread(start(), size)]

    def both(start, size):
        return (cut(out, start, size),) * 2

    def slot(ref, j):
        return lambda: ref.at[j - 1]

    sends = [[] for _ in range(8)]
    for j in range(1, p.C):
        sends[0].append(wires.plan(cut(src, lambda j=j: p.at("c", j) * per, per), slot(from_c, j), "c", j))
        sends[7].append(wires.plan(*both(lambda: base, per), "c", j))
    for j in range(1, p.X):
        sends[1].append(wires.plan(cut(held, lambda j=j: in_a(p.at("x", j)), ax), slot(a1, j), "x", j))
        sends[2].append(wires.plan(cut(held, lambda j=j: in_b(y, p.at("x", j)), p.Z * b), slot(b2, j), "x", j))
        sends[5].append(wires.plan(*both(lambda: base + in_b(y, x), p.Z * b), "x", j))
        sends[6].append(wires.plan(*both(lambda: base + in_a(x), ax), "x", j))
    for j in range(1, p.Y):
        sends[1].append(wires.plan(cut(held, lambda j=j: in_b(p.at("y", j)), by), slot(b1, j), "y", j))
        sends[2].append(wires.plan(cut(held, lambda j=j: in_a(x, p.at("y", j)), p.Z * a), slot(a2, j), "y", j))
        sends[5].append(wires.plan(*both(lambda: base + in_a(x, y), p.Z * a), "y", j))
        sends[6].append(wires.plan(*both(lambda: base + in_b(y), by), "y", j))
    for j in range(1, p.Z):
        sends[3].append(wires.plan(cut(held, lambda j=j: in_a(x, y, p.at("z", j)), a), slot(a3, j), "z", j))
        sends[3].append(wires.plan(cut(held, lambda j=j: in_b(y, x, p.at("z", j)), b), slot(b3, j), "z", j))
        sends[4].append(wires.plan(*both(lambda: base + in_a(x, y, z), a), "z", j))
        sends[4].append(wires.plan(*both(lambda: base + in_b(y, x, z), b), "z", j))

    def total(ref, at, size, parts, count):
        value = ref[spread(at, size), :].astype(F32)
        for j in range(count):
            value = value + parts[j].astype(F32)
        return value.astype(BF16)

    def step(t):
        if t:
            wires.arrive(sends[t - 1])
        if t == 1:
            held[...] = total(src, base, per, from_c, p.C - 1)
        if t == 2:
            held[spread(in_a(x), ax), :] = total(held, in_a(x), ax, a1, p.X - 1)
            held[spread(in_b(y), by), :] = total(held, in_b(y), by, b1, p.Y - 1)
        if t == 3:
            held[spread(in_a(x, y), p.Z * a), :] = total(held, in_a(x, y), p.Z * a, a2, p.Y - 1)
            held[spread(in_b(y, x), p.Z * b), :] = total(held, in_b(y, x), p.Z * b, b2, p.X - 1)
        if t == 4:
            out[spread(base + in_a(x, y, z), a), :] = total(held, in_a(x, y, z), a, a3, p.Z - 1)
            out[spread(base + in_b(y, x, z), b), :] = total(held, in_b(y, x, z), b, b3, p.Z - 1)
        if t < 8:
            wires.start(sends[t])
        else:
            wires.finish()

    return [functools.partial(step, t) for t in range(9)]


def at_turn(turn, steps):
    for i, todo in enumerate(steps):
        if todo:

            @pl.when(turn == i)
            def _():
                for step in todo:
                    step()


def dealt(steps, turns):
    return [steps[len(steps) * i // turns : len(steps) * (i + 1) // turns] for i in range(turns)]


def fold(t, odd):
    rows, wide = t.shape
    if wide % 128 == 64:
        body = jnp.where(odd, t[:, 64:], t[:, : wide - 64])
        edge = jnp.where(odd, t[:, :64], t[:, wide - 64 :])
        a, b = edge[: rows // 2], edge[rows // 2 :]
        tiles = [body[:, 128 * j : 128 * j + 128] for j in range(wide // 128)]
        tiles.append(jnp.concatenate([jnp.where(odd, b, a), jnp.where(odd, a, b)], axis=1))
        return jnp.concatenate(tiles, axis=0)
    need = -(-wide // 128) * 128
    t = jnp.concatenate([t, jnp.zeros((rows, need - wide), t.dtype)], axis=1) if need > wide else t
    return jnp.concatenate([t[:, 128 * j : 128 * j + 128] for j in range(need // 128)], axis=0)


def fold_rows(rows, wide):
    return rows * (wide // 128) + rows // 2 if wide % 128 == 64 else rows * (-(-wide // 128))


def unfold(p, buf, base, rows, wide):
    out = []
    lane = lax.broadcasted_iota(jnp.int32, (rows // 2, 128), 1)
    size = fold_rows(rows, wide)
    for z in range(p.Z):
        for x in range(p.X):
            tiles = []
            for y in range(p.Y):
                got = [buf[z, c, x, y, base : base + size, :].astype(F32) for c in range(p.C)]
                if wide % 128 == 64:
                    k = wide // 128
                    even, odd = got
                    tiles += [even[rows * j : rows * j + rows] for j in range(k)]
                    e, o = even[rows * k :], odd[rows * k :]
                    top = jnp.where(lane < 64, e, o)
                    low = pltpu.roll(jnp.where(lane < 64, o, e), 64, 1)
                    tiles.append(jnp.concatenate([top, low], axis=0))
                    tiles += [odd[rows * j : rows * j + rows] for j in range(k)]
                else:
                    k = size // rows
                    for c in range(p.C):
                        t = jnp.concatenate([got[c][rows * j : rows * j + rows] for j in range(k)], axis=1).astype(BF16)
                        tiles.append(nn(t, hot((128 * k, 768), (y * p.C + c) * wide, 0)) if 128 * k == wide else nn(t, hot_cut((128 * k, 768), (y * p.C + c) * wide, wide)))
            if wide % 128 == 64:
                out.append(jnp.concatenate(tiles, axis=1))
            else:
                out.append(functools.reduce(lambda a, b: a + b, tiles))
    return out


def hot_cut(shape, at, limit):
    rows = lax.broadcasted_iota(jnp.int32, shape, 0)
    cols = lax.broadcasted_iota(jnp.int32, shape, 1)
    return jnp.logical_and(rows + at == cols, rows < limit).astype(BF16)


def front_kernel(p, owned, len_ref, x_ref, cot_ref, wq_ref, wo_ref, w1_ref, w2_ref, vec_ref, mo_ref, m1_ref, m2_ref,
                 qt_out, k_out, kt_out, v_out, ct_out, out_out, res_out, dct_out, lse_ref, wt_out, so_ref, s1_ref, s2_ref, gv_ref,
                 bufq, bufr, place_s, win_s, qt_s, k_s, kt_s, v_s, ct_s, vt_s, bias_s, vcol_s, w1_s, w2_s, wo_s, out_s, res_s, dct_s,
                 send_q, recv_q, send_r, recv_r, out_sem):
    p.locate()
    p.greet(corner=owned)
    n_rows, seq = x_ref.shape[:2]
    odd = lax.rem(lax.axis_index("narrow"), 2) == 1
    slim, tall = wq_ref.shape[1:]
    qrows = bufq.shape[4]
    for c in range(3):
        t = jnp.concatenate([wq_ref[4 * c + g] for g in range(4)], axis=0).T
        t = jnp.concatenate([t, jnp.zeros((tall, 128 - 4 * slim), F32)], axis=1)
        bufq[p.z, p.c, p.x, p.y, c * tall : c * tall + tall, :] = t.astype(BF16)
    if qrows > 3 * tall:
        bufq[p.z, p.c, p.x, p.y, 3 * tall :, :] = jnp.zeros((qrows - 3 * tall, 128), BF16)
    p.meet(corner=owned)
    wires_q, wires_r = Wires(p, send_q, recv_q), Wires(p, send_r, recv_r)
    q_z, q_own, q_on, q_over, q_done = gather_steps(p, wires_q, bufq, qrows // 32 * 16, corner=owned)
    q_z()
    q_own[0]()
    rows, wide = 4 * slim, 4 * tall
    size = fold_rows(rows, wide)
    big = wo_ref.shape[2]
    shards = [nt(hot((big, big), 0, 0), wo_ref[0].astype(BF16))]
    shards += [jnp.concatenate([r[g] for g in range(4)], axis=0) for r in (w1_ref, w2_ref)]
    folded = jnp.concatenate([fold(t, odd) for t in shards], axis=0)
    if bufr.shape[4] > 3 * size:
        folded = jnp.concatenate([folded, jnp.zeros((bufr.shape[4] - 3 * size, 128), F32)], axis=0)
    bufr[p.z, p.c, p.x, p.y] = folded.astype(BF16)
    d, n = lax.axis_index("dp"), lax.axis_index("narrow")
    sel_l = hot((wide, 768), n * wide, 0)
    placed = nt(hot((768, big), 0, d * big), (0.95 * mo_ref[0]).astype(BF16)).astype(BF16)
    value = nn(placed, sel_l)
    for q in range(4):
        put_blocks(so_ref, 1152 * q, value[192 * q : 192 * q + 192])
    for dst, m_ref in ((s1_ref, m1_ref), (s2_ref, m2_ref)):
        for g in range(4):
            value = nn(nn(hot((192, slim), 0, d * slim), (0.95 * m_ref[g]).astype(BF16)).astype(BF16), sel_l)
            for half, base in enumerate(group_rows(owned, g)):
                put_blocks(dst, base, value[:, 384 * half : 384 * half + 384])
    for dst in (so_ref, s1_ref, s2_ref):
        if dst.shape[0] > 4608:
            dst[4608:, :] = jnp.zeros((dst.shape[0] - 4608, 128), BF16)
    gv_ref[...] = jnp.zeros_like(gv_ref)
    dp = p.Z * p.X
    for pair in range(dp // 2):
        r = lax.broadcasted_iota(jnp.int32, (256, 1), 0)
        q = jnp.where(r < 128, r, r - 128)
        g = (q >= slim).astype(jnp.int32) + (q >= 2 * slim).astype(jnp.int32) + (q >= 3 * slim).astype(jnp.int32)
        col = 256 * g + jnp.where(jnp.logical_or(g == 1, g == 3), 64, 0) + jnp.where(r < 128, 2 * pair * slim, (2 * pair + 1) * slim) + q - g * slim
        col = jnp.where(q < 4 * slim, col, -1)
        place_s[pair] = (lax.broadcasted_iota(jnp.int32, (256, 1024), 1) == col).astype(BF16)
    win_s[...] = jnp.zeros_like(win_s)
    vcol_s[...] = vec_ref[0:8, :].T
    r_z, r_own, r_on, r_over, r_done = gather_steps(p, wires_r, bufr, bufr.shape[4] // 32 * 16)
    for t in range(1, p.Z + 2):
        for steps, at in ((q_own, t), (q_on, t - 1), (q_over, t - (1 if owned else 2))):
            if 0 <= at < len(steps):
                steps[at]()
        if t == p.Z - 2:
            r_z()
    r_own[0]()
    q_done()
    total = jnp.zeros((3 * 192, 1024), F32)
    for pair in range(dp // 2):
        tiles = []
        for d in (2 * pair, 2 * pair + 1):
            z, x = d // p.X, d % p.X
            got = [bufq[z, c, x, y].astype(F32) for y in range(p.Y) for c in range(p.C)]
            tiles.append(jnp.concatenate([b[c * tall : c * tall + tall] for c in range(3) for b in got], axis=0))
        total = total + nn(jnp.concatenate(tiles, axis=1).astype(BF16), place_s[pair])
    for g in range(4):
        off = 64 * (g % 2)
        stack = total[:, 256 * g : 256 * g + 256].astype(BF16)
        for c in range(3):
            win_s[c, g, off : off + 192, :] = stack[192 * c : 192 * c + 192]
        wt_out[g] = nt(hot((192, 256), off, 0), stack).astype(BF16)
    turns = [[] for _ in range(3 * n_rows)]
    for i, step in enumerate(r_on):
        turns[min(i, 3, len(turns) - 1)].append(step)
    for i, step in enumerate(r_over):
        turns[min(min(i, 3) // 2 + 3, len(turns) - 1)].append(step)
    turns[-1].append(r_done)

    for step in r_own[1:]:
        step()

    def out_copies(row, which):
        pairs = ((qt_s, qt_out), (k_s, k_out), (kt_s, kt_out), (v_s, v_out), (ct_s.at[row], ct_out), (out_s, out_out), (res_s, res_out), (dct_s, dct_out))
        return [pltpu.make_async_copy(pairs[i][0], pairs[i][1].at[row], out_sem.at[i]) for i in which]

    def reuse(row, which):
        @pl.when(row > 0)
        def _():
            for copy in out_copies(row - 1, which):
                copy.wait()

    def one_row(row, carry):
        same = ids(len_ref, row, (seq, seq), 0) == ids(len_ref, row, (seq, seq), 1)
        bias_s[...] = jnp.where(same, 0.0, -1e30)
        reuse(row, range(5))
        for g in range(4):
            lo = window(g)
            xw = x_ref[row, :, lo : lo + 256]
            off = 64 * (g % 2)
            r = slice(192 * g, 192 * g + 192)
            q = nt(win_s[0, g, off : off + 192, :], xw) + vcol_s[r, 4:5]
            qt_s[r, :] = q.astype(BF16) * BF16(0.125)
            kt_s[r, :] = nt(win_s[1, g, off : off + 192, :], xw).astype(BF16)
            v = nt(win_s[2, g, off : off + 192, :], xw) + vcol_s[r, 5:6]
            vt_s[r, :] = v.astype(BF16)
        wide_of = lambda c: join([nt(x_ref[row, :, window(g) : window(g) + 256], win_s[c, g]) for g in range(4)])
        k_s[...] = wide_of(1).astype(BF16)
        v_s[...] = (wide_of(2) + vec_ref[5:6, :]).astype(BF16)
        for copy in out_copies(row, range(4)):
            copy.start()

        def four(j, carry):
            heads = [(pl.multiple_of(256 * j + 128 * u, 128), e) for u in range(2) for e in range(2)]
            spots = [pl.ds(pl.multiple_of(lo + 64 * e, 64), 64) for lo, e in heads]
            scores = []
            for (lo, e), at in zip(heads, spots):
                qh = qt_s[at, :]
                none = jnp.zeros_like(qh)
                scores.append(nn(k_s[:, pl.ds(lo, 128)], jnp.concatenate([none, qh] if e else [qh, none], axis=0)))
            soft = []
            for s in scores:
                s = s + bias_s[...]
                m = jnp.max(s, axis=0, keepdims=True)
                ex = jnp.exp(s - m)
                soft.append((m, ex.astype(BF16), jnp.sum(ex, axis=0, keepdims=True)))
            for i, (at, (m, ex, tot)) in enumerate(zip(spots, soft)):
                ct_s[row, at, :] = (nn(vt_s[at, :], ex) * (1.0 / tot)).astype(BF16)
                lse_ref[row, pl.ds(4 * j + i, 1), :] = m + jnp.log(tot)
            at_turn(row * 3 + j, turns)
            return carry

        lax.fori_loop(0, 3, four, 0)
        out_copies(row, (4,))[0].start()
        return carry

    lax.fori_loop(0, n_rows, one_row, 0)
    wires_q.finish()
    wires_r.finish()
    whole = unfold(p, bufr, 0, rows, wide)
    wo_s[...] = jnp.concatenate(whole, axis=0).astype(BF16)
    for i, dst in enumerate((w1_s, w2_s)):
        whole = unfold(p, bufr, (i + 1) * size, rows, wide)
        for g in range(4):
            off = 64 * (g % 2)
            dst[g, off : off + 192, :] = jnp.concatenate([b[g * slim : g * slim + slim] for b in whole], axis=0).astype(BF16)
            dst[g, 192 - 192 * (g % 2) : 256 - 192 * (g % 2), :] = jnp.zeros((64, 768), BF16)
    vec = lambda i: vec_ref[i : i + 1, :]

    def feed_forward(row, carry):
        h1 = x_ref[row].astype(F32) + (nn(ct_s[row].T, wo_s[...]) + vec(6))
        n1, inv1 = norm(h1)
        first = n1 * vec(0) + vec(1)
        fl = first.astype(BF16)
        inner = lambda g: nn(fl[:, window(g) : window(g) + 256], w1_s[g]) + vec(8 + g)
        active, slope, branch = [], [], []
        ahead = inner(0)
        for g in range(4):
            now, ahead = ahead, (inner(g + 1) if g < 3 else None)
            a, sl = gelu_parts(now)
            active.append(a.astype(BF16))
            slope.append(sl)
            branch.append(nt(active[g], w2_s[g]))
        h2 = first + (join(branch) + vec(7))
        n2, inv2 = norm(h2)
        reuse(row, (5, 6, 7))
        out_s[...] = (n2 * vec(2) + vec(3)).astype(BF16)
        out_copies(row, (5,))[0].start()
        dy = cot_ref[row].astype(F32)
        dh2 = norm_back(dy, n2, inv2, vec(2))
        dbl = dh2.astype(BF16)
        dbt = dbl.T
        flt = fl.T
        ones = jnp.ones((16, seq), BF16)
        dfirst = []
        gb = []
        for g in range(4):
            da = nn(dbl[:, window(g) : window(g) + 256], w2_s[g])
            di = (da * slope[g]).astype(BF16)
            dfirst.append(nt(di, w1_s[g]))
            g2 = nn(dbt[192 * g : 192 * g + 192, :], active[g])
            ext = nn(jnp.concatenate([flt[192 * g : 192 * g + 192, :], ones], axis=0), di)
            for half, base in enumerate(group_rows(owned, g)):
                add_blocks(s2_ref, base, g2[:, 384 * half : 384 * half + 384])
                add_blocks(s1_ref, base, ext[:192, 384 * half : 384 * half + 384])
            gb.append(ext[192:193])
        df = dh2 + join(dfirst)
        dh1 = norm_back(df, n1, inv1, vec(0))
        dat = dh1.astype(BF16)
        res_s[...] = dat
        out_copies(row, (6,))[0].start()
        go = nn(ct_s[row], dat)
        for q in range(4):
            add_blocks(so_ref, 1152 * q, go[192 * q : 192 * q + 192])
        dct_s[...] = nt(wo_s[...], dat).astype(BF16)
        out_copies(row, (7,))[0].start()
        z = jnp.zeros((1, dy.shape[1]), F32)
        gv_ref[...] += jnp.concatenate(
            [col_sum(df * n1), col_sum(df), col_sum(dy * n2), col_sum(dy), z, z, col_sum(dat.astype(F32)), col_sum(dbl.astype(F32))] + gb, axis=0)
        return carry

    lax.fori_loop(0, n_rows, feed_forward, 0)
    for copy in out_copies(n_rows - 1, range(8)):
        copy.wait()


def front(p, owned, sum_rows, lengths, tokens, cot, wq, wo, w1, w2, vec, mo, m1, m2, ident):
    n, seq, d = tokens.shape
    slim, tall = wq.shape[1:]
    up = lambda r, m: -(-r // m) * m
    qrows = up(3 * tall, 32)
    rrows = up(3 * fold_rows(4 * slim, 4 * tall), 16)
    count = gather_copies(p)
    hbm = pl.BlockSpec(memory_space=pl.ANY)
    act = lambda a, b: jax.ShapeDtypeStruct((n, a, b), BF16)
    tm, mt = pltpu.VMEM((seq, d), BF16), pltpu.VMEM((d, seq), BF16)
    return pl.pallas_call(
        functools.partial(front_kernel, p, owned),
        out_shape=[act(d, seq), act(seq, d), act(d, seq), act(seq, d), act(d, seq), act(seq, d), act(seq, d), act(d, seq)]
        + [jax.ShapeDtypeStruct((n, 16, seq), F32), jax.ShapeDtypeStruct((4, 192, 576), BF16)]
        + [jax.ShapeDtypeStruct((sum_rows, 128), BF16)] * 3
        + [jax.ShapeDtypeStruct((12, 768), F32)],
        in_specs=[pl.BlockSpec(memory_space=pltpu.SMEM)] + [VMEM] * 10,
        out_specs=[hbm] * 8 + [VMEM] * 6,
        scratch_shapes=[
            pltpu.VMEM((p.Z, p.C, p.X, p.Y, qrows, 128), BF16),
            pltpu.VMEM((p.Z, p.C, p.X, p.Y, rrows, 128), BF16),
            pltpu.VMEM((p.Z * p.X // 2, 256, 1024), BF16),
            pltpu.VMEM((3, 4, 256, 256), BF16),
            mt, tm, mt, tm, pltpu.VMEM((n, d, seq), BF16),
            mt, pltpu.VMEM((seq, seq), F32), pltpu.VMEM((d, 8), F32),
            pltpu.VMEM((4, 256, 768), BF16), pltpu.VMEM((4, 256, 768), BF16), pltpu.VMEM((768, 768), BF16),
            tm, tm, mt,
            pltpu.SemaphoreType.DMA((count,)), pltpu.SemaphoreType.DMA((count,)),
            pltpu.SemaphoreType.DMA((count,)), pltpu.SemaphoreType.DMA((count,)),
            pltpu.SemaphoreType.DMA((8,)),
        ],
        compiler_params=pltpu.CompilerParams(collective_id=ident, has_side_effects=True, vmem_limit_bytes=62 * 2**20),
    )(lengths, tokens, cot, wq, wo, w1, w2, vec, mo, m1, m2)


def on_diagonal(n):
    return lax.broadcasted_iota(jnp.int32, (n, n), 0) == lax.broadcasted_iota(jnp.int32, (n, n), 1)


def ns_start(values):
    return [y * (1.0 / (jnp.sqrt(jnp.sum(y * y)) + 1e-07)) for y in values]


def ns_shift(t):
    return jnp.where(t >= 3, 0.8, jnp.where(t == 2, 0.5, 0.0)).astype(F32)


def ns_poly(values, m):
    diag = on_diagonal(values[0].shape[0])
    lows = [y.astype(BF16) for y in values]
    grams = [nt(l, l) for l in lows]
    rest = [jnp.where(diag, g - m, g) for g in grams]
    lowr = [r.astype(BF16) for r in rest]
    squares = [nn(r, r) for r in lowr]
    return [((ns_second + 2.0 * ns_third * m) * r + ns_third * s).astype(BF16) for r, s in zip(rest, squares)]


def ns_step(values, m, polys):
    moved = [nn(q, y.astype(BF16)) for q, y in zip(polys, values)]
    return [(ns_first + ns_second * m + ns_third * m * m) * y + t for y, t in zip(values, moved)]


def ns_sweep(values, t):
    m = ns_shift(t)
    return ns_step(values, m, ns_poly(values, m))


def close_kernel(p, shares, *refs):
    (len_ref, wt_ref, so_ref, s1_ref, s2_ref, gv_ref, gmq_ref, wq_ref, wo_ref, w1_ref, w2_ref, vec_ref, vm1_ref, vm2_ref,
     x_hbm, qt_hbm, k_hbm, kt_hbm, v_hbm, ct_hbm, lse_ref, dct_hbm, res_hbm,
     gt_ref, mq_ref, mo_ref, m1_ref, m2_ref, nq_ref, no_ref, n1_ref, n2_ref, f_ref, s_ref, v_ref,
     x_s, qt_s, k_s, kt_s, v_s, ct_s, dct_s, res_s, bias_s, dq_s, dk_s, dv_s, gq_s, gv2_s, sq_s, oo_s, o1_s, o2_s, oq_s,
     y_s, po_s, pf_s, xo_s, xf_s, xq_s, xo_r, xf_r, xq_r, in_sem, x_send, x_recv) = refs[: 35 + 31]
    rest = refs[35 + 31 :]
    p.locate()
    d, n = lax.axis_index("dp"), lax.axis_index("narrow")
    n_rows, seq = x_s.shape[:2]
    pairs = ((qt_hbm, qt_s), (k_hbm, k_s), (dct_hbm, dct_s), (v_hbm, v_s), (ct_hbm, ct_s), (kt_hbm, kt_s), (x_hbm, x_s), (res_hbm, res_s))

    def loads(row):
        return [pltpu.make_async_copy(src.at[row], dst.at[row], in_sem.at[row, i]) for i, (src, dst) in enumerate(pairs)]

    for row in range(n_rows):
        for copy in loads(row):
            copy.start()
    p.barrier()
    sums = [sum_steps(p, s, src, out, rest[10 * i : 10 * i + 10])
            for i, (s, src, out) in enumerate(zip(shares, (so_ref, s1_ref, s2_ref, sq_s), (oo_s, o1_s, o2_s, oq_s)))]
    o, f1, f2, q = sums
    for step in (o[0], f1[0], f2[0]):
        step()
    turns = dealt([o[1], f1[1], o[2], f2[1], o[3], f1[2], o[4], f2[2], o[5], f1[3], o[6], f2[3], o[7], f1[4], f2[4]], 6 * n_rows)
    gq_s[...] = jnp.zeros_like(gq_s)
    gv2_s[...] = jnp.zeros_like(gv2_s)
    lane = lax.broadcasted_iota(jnp.int32, (192, 256), 1)

    def one_row(row, carry):
        same = ids(len_ref, row, (seq, seq), 0) == ids(len_ref, row, (seq, seq), 1)
        bias_s[...] = jnp.where(same, 0.0, -1e30)
        for copy in loads(row):
            copy.wait()

        def pair(j, carry):
            lo = pl.multiple_of(128 * j, 128)
            kp, vp = k_s[row, :, pl.ds(lo, 128)], v_s[row, :, pl.ds(lo, 128)]
            for e in range(2):
                at = pl.ds(pl.multiple_of(lo + 64 * e, 64), 64)
                qh, dc = qt_s[row, at, :], dct_s[row, at, :]
                none = jnp.zeros_like(qh)
                wide = lambda a: jnp.concatenate([none, a] if e else [a, none], axis=0)
                delta = jnp.sum(dc.astype(F32) * ct_s[row, at, :].astype(F32), axis=0, keepdims=True)
                s = nn(kp, wide(qh)) + bias_s[...]
                ex = jnp.exp(s - lse_ref[row, pl.ds(2 * j + e, 1), :])
                de = nn(vp, wide(dc))
                ds = (ex * (de - delta)).astype(BF16)
                dv_s[at, :] = nt(dc, ex.astype(BF16)).astype(BF16)
                dk_s[at, :] = nt(qh, ds).astype(BF16)
                dq_s[at, :] = (nn(kt_s[row, at, :], ds) * 0.125).astype(BF16)
            at_turn(row * 6 + j, turns)
            return carry

        lax.fori_loop(0, 6, pair, 0)
        dx = []
        for g in range(4):
            lo = window(g)
            r = slice(192 * g, 192 * g + 192)
            cat = jnp.concatenate([dq_s[r, :], dk_s[r, :], dv_s[r, :]], axis=0)
            dx.append(nn(wt_ref[g], cat))
            gq = nn(cat, x_s[row, :, lo : lo + 256])
            keep = (lane < 192) if g % 2 == 0 else (lane >= 64)
            for c in range(3):
                gq_s[c, :, lo : lo + 256] += jnp.where(keep, gq[192 * c : 192 * c + 192], 0.0)
        gt_ref[row] = (res_s[row] + jnp.concatenate(dx, axis=0).T).astype(BF16)
        ones = jnp.ones((16, seq), BF16)
        gv2_s[0:1, :] += nt(ones, dq_s[...])[0:1]
        gv2_s[1:2, :] += nt(ones, dv_s[...])[0:1]
        return carry

    lax.fori_loop(0, n_rows, one_row, 0)
    slim, tall = gmq_ref.shape[1:]
    up = hot((192, tall), 0, n * tall)
    for c in range(3):
        held = jnp.zeros((tall, 768), F32)
        for g in range(4):
            held = held + tn((0.95 * gmq_ref[4 * c + g]).astype(BF16), hot((slim, 768), 192 * g + d * slim, 0))
        put_blocks(sq_s, 1152 * c, gq_s[c] + nn(up, held.astype(BF16)))
    gv = jnp.concatenate([gv_ref[0:4], gv2_s[0:2], gv_ref[6:12]], axis=0)
    tail = sq_s.shape[0] - 3456
    flat = jnp.concatenate([gv[:, 128 * j : 128 * j + 128] for j in range(6)] + [jnp.zeros((tail - 72, 128), F32)], axis=0)
    sq_s[3456:, :] = flat.astype(BF16)
    for step in (q[0], o[8], q[1]):
        step()
    wide, cols = w1_ref.shape[2], w1_ref.shape[1]
    sel_l = hot((wide, 768), n * wide, 0)
    sel_s = hot((cols, 192), d * cols, 0)
    big = wo_ref.shape[2]
    sel_b = hot((big, 768), d * big, 0)
    core0, core1 = p.c == 0, p.c == 1
    eight = lambda: [y_s[192 * i : 192 * i + 192, :] for i in range(8)]

    late = 3
    before = [[f1[5]], [f1[6]], [f1[7]], [q[5]], [q[7]]]
    between = [[q[2], f2[5]], [q[3], f2[6]], [q[4], f2[7], f1[8], f2[8]], [q[6]], [q[8]]]

    def sweep(t, carry):
        on0 = jnp.logical_and(core0, t < NS_STEPS)
        on1 = jnp.logical_and(core1, t >= late)

        @pl.when(jnp.logical_and(core0, t == 0))
        def _():
            y_s[0:768, :] = ns_start([wide_rows(oo_s, 0, 4).astype(F32)])[0]

        @pl.when(jnp.logical_and(core1, t == late))
        def _():
            for i, y in enumerate(ns_start([wide_rows(r, 1152 * g, 1).astype(F32) for r in (o1_s, o2_s) for g in range(4)])):
                y_s[192 * i : 192 * i + 192, :] = y

        @pl.when(on0)
        def _():
            po_s[...] = ns_poly([y_s[0:768, :]], ns_shift(t))[0]

        @pl.when(on1)
        def _():
            for i, poly in enumerate(ns_poly(eight(), ns_shift(t - late))):
                pf_s[i] = poly

        at_turn(t, before)

        @pl.when(on0)
        def _():
            y_s[0:768, :] = ns_step([y_s[0:768, :]], ns_shift(t), [po_s[...]])[0]

        @pl.when(on1)
        def _():
            for i, y in enumerate(ns_step(eight(), ns_shift(t - late), [pf_s[i] for i in range(8)])):
                y_s[192 * i : 192 * i + 192, :] = y

        at_turn(t, between)
        return carry

    lax.fori_loop(0, NS_STEPS + late, sweep, 0)
    wires = Wires(p, x_send, x_recv)
    mo_ref[0] = nt(sel_l, nn(sel_b, wide_rows(oo_s, 0, 4)).astype(BF16))
    for ref, m_ref in ((o1_s, m1_ref), (o2_s, m2_ref)):
        for g in range(4):
            m_ref[g] = nt(nn(sel_s, wide_rows(ref, 1152 * g, 1)).astype(BF16), sel_l)

    @pl.when(core0)
    def _():
        xo_s[...] = nn(sel_b, y_s[0:768, :].astype(BF16)).astype(BF16)

    @pl.when(core1)
    def _():
        for i in range(8):
            xf_s[cols * i : cols * i + cols, :] = nn(sel_s, y_s[192 * i : 192 * i + 192, :].astype(BF16)).astype(BF16)

    rows = [wide_rows(oq_s, 1152 * c, 1) for c in range(3)]
    spot = lambda g: hot_cut((256, 128), 0, 0)

    def square(parity):
        keep = (lane < 192) if parity == 0 else (lane >= 64)
        which = [(c, g) for c in range(3) for g in (parity, parity + 2)]
        ys = ns_start([jnp.where(keep, rows[c][:, window(g) : window(g) + 256].astype(F32), 0.0) for c, g in which])
        for i, y in enumerate(ys):
            y_s[192 * i : 192 * i + 192, :256] = y

        def turn(t, carry):
            ys = [y_s[192 * i : 192 * i + 192, :256] for i in range(6)]
            for i, y in enumerate(ns_sweep(ys, t)):
                y_s[192 * i : 192 * i + 192, :256] = y
            return carry

        lax.fori_loop(0, NS_STEPS, turn, 0)
        ys = [y_s[192 * i : 192 * i + 192, :256] for i in range(6)]
        for c in range(3):
            part = jnp.zeros((192, 128), F32)
            for (cc, g), y in zip(which, ys):
                if cc == c:
                    at = 64 * (g % 2) + d * slim
                    r = lax.broadcasted_iota(jnp.int32, (256, 128), 0) - at
                    q = lax.broadcasted_iota(jnp.int32, (256, 128), 1) - g * slim
                    sel = jnp.logical_and(r == q, jnp.logical_and(q >= 0, q < slim)).astype(BF16)
                    part = part + nn(y.astype(BF16), sel)
            xq_s[192 * c : 192 * c + 192, :] = part.astype(BF16)

    @pl.when(core0)
    def _():
        square(0)

    @pl.when(core1)
    def _():
        square(1)

    copies = [wires.plan(lambda a=a: a, lambda b=b: b, "c", 1) for a, b in ((xq_s, xq_r), (xo_s, xo_r), (xf_s, xf_r))]
    wires.start(copies)
    sel_o = hot((tall, 192), n * tall, 0)
    for c in range(3):
        mine = nn(sel_o, rows[c]).astype(BF16)
        for g in range(4):
            mq_ref[4 * c + g] = nt(hot((slim, 768), 192 * g + d * slim, 0), mine)
    vt = oq_s[3456 : 3456 + 80, :].astype(F32)
    grad = jnp.concatenate([vt[12 * j : 12 * j + 12] for j in range(6)], axis=1)
    first = 0.9 * vm1_ref[...] + 0.1 * grad
    second = 0.999 * vm2_ref[...] + 0.001 * grad * grad
    f_ref[...] = first
    s_ref[...] = second
    v_ref[...] = vec_ref[...] - adam_rate * (first * (1.0 / (1.0 - 0.9**STEP))) / (jnp.sqrt(second * (1.0 / (1.0 - 0.999**STEP))) + 1e-08)

    def fresh(w, own, longest):
        return w - muon_rate * (0.2 * math.sqrt(longest) * own + muon_decay * w)

    wires.arrive(copies)
    for c in range(3):
        both = (xq_s[192 * c : 192 * c + 192, :].astype(F32) + xq_r[192 * c : 192 * c + 192, :].astype(F32)).astype(BF16)
        mine = nn(sel_o, both).astype(BF16)
        for g in range(4):
            nq_ref[4 * c + g] = fresh(wq_ref[4 * c + g], nt(hot((slim, 128), g * slim, 0), mine), 192)
    xo = jnp.where(core0, xo_s[...], xo_r[...])
    no_ref[0] = fresh(wo_ref[0], nt(sel_l, xo), 768)
    for i, (w_ref, n_ref) in enumerate(((w1_ref, n1_ref), (w2_ref, n2_ref))):
        for g in range(4):
            at = slice(cols * (4 * i + g), cols * (4 * i + g) + cols)
            n_ref[g] = fresh(w_ref[g], nt(jnp.where(core1, xf_s[at, :], xf_r[at, :]), sel_l), 768)
    wires.finish()


def closing(p, shares, lengths, wt, so, s1, s2, gv, mq, weights, vec, vm1, vm2, acts, ident):
    tokens, lse = acts[0], acts[6]
    n, seq, d = tokens.shape
    slim = mq.shape[1]
    shape = lambda a: jax.ShapeDtypeStruct(a.shape, F32)
    outs = [jax.ShapeDtypeStruct(tokens.shape, BF16)] + [shape(w) for w in weights] * 2 + [shape(vec)] * 3
    hbm = pl.BlockSpec(memory_space=pl.ANY)
    tm, mt = pltpu.VMEM((n, seq, d), BF16), pltpu.VMEM((n, d, seq), BF16)
    flat = lambda r: pltpu.VMEM((r, 128), BF16)
    scratch = [tm, mt, tm, mt, tm, mt, mt, pltpu.VMEM((n, seq, d), BF16), pltpu.VMEM((seq, seq), F32)]
    scratch += [pltpu.VMEM((d, seq), BF16)] * 3 + [pltpu.VMEM((3, 192, 768), F32), pltpu.VMEM((8, 768), F32)]
    scratch += [flat(shares[3].rows)] + [flat(s.rows) for s in shares]
    scratch += [pltpu.VMEM((1536, 768), F32), pltpu.VMEM((768, 768), BF16), pltpu.VMEM((8, 192, 192), BF16)]
    scratch += [pltpu.VMEM((4 * slim, 768), BF16), pltpu.VMEM((8 * slim, 768), BF16), pltpu.VMEM((576, 128), BF16)] * 2
    scratch += [pltpu.SemaphoreType.DMA((n, 8)), pltpu.SemaphoreType.DMA((3,)), pltpu.SemaphoreType.DMA((3,))]
    for s in shares:
        scratch += s.scratch(p)
    return pl.pallas_call(
        functools.partial(close_kernel, p, shares),
        out_shape=outs,
        in_specs=[pl.BlockSpec(memory_space=pltpu.SMEM)] + [VMEM] * 13 + [hbm] * 6 + [VMEM] + [hbm] * 2,
        out_specs=[VMEM] * 12,
        scratch_shapes=scratch,
        compiler_params=pltpu.CompilerParams(collective_id=ident, has_side_effects=True, vmem_limit_bytes=62 * 2**20),
    )(lengths, wt, so, s1, s2, gv, mq, *weights, vec, vm1, vm2, *acts)


class Owned:
    def __init__(self, p, half):
        self.half, self.rows, self.copies = half, 8 * half, 4 + 2 * (p.Z - 1)
        self.kinds = [4 * half, 4 * half, 2 * half, half, (p.Z - 1) * (half // p.Z), half, half]

    def scratch(self):
        return [pltpu.VMEM((k, 128), BF16) for k in self.kinds] + [pltpu.SemaphoreType.DMA((self.copies,))] * 2


def owned_steps(p, s, src, scratch):
    held, from_c, r1, r2, r3, mine, other, send_sem, recv_sem = scratch
    wires = Wires(p, send_sem, recv_sem)
    h, q, z, c = s.half, s.half // p.Z, p.z, p.c
    first = jnp.where(c == 0, p.x, p.y)
    second = jnp.where(c == 0, p.y, p.x)
    cut = lambda ref, start, size: lambda: ref.at[spread(start(), size)]

    def partner(turn):
        along_x = c == turn
        x, y = jnp.where(along_x, 1 - p.x, p.x), jnp.where(along_x, p.y, 1 - p.y)
        return (z * p.X + x, y * p.C + c)

    sibling = lambda: p.device("c", 1)
    spot = lambda: (2 * first + second) * h
    sends = [
        [wires.plan_to(cut(src, lambda: (1 - c) * 4 * h, 4 * h), lambda: from_c, sibling)],
        [wires.plan_to(cut(held, lambda: (1 - first) * 2 * h, 2 * h), lambda: r1, lambda: partner(0))],
        [wires.plan_to(cut(held, lambda: (2 * first + 1 - second) * h, h), lambda: r2, lambda: partner(1))],
        [],
        [],
        [wires.plan_to(lambda: mine, lambda: other, sibling)],
    ]
    for j in range(1, p.Z):
        sends[3].append(wires.plan(cut(held, lambda j=j: spot() + p.at("z", j) * q, q), lambda j=j: r3.at[pl.ds((j - 1) * q, q)], "z", j))
        sends[4].append(wires.plan(*(cut(mine, lambda: z * q, q),) * 2, "z", j))

    def add(dst, to, ref, start, size, parts):
        value = ref[spread(start, size), :].astype(F32)
        for part in parts:
            value = value + part().astype(F32)
        dst[spread(to, size), :] = value.astype(BF16)

    def step(t):
        if 1 <= t <= 5:
            wires.arrive(sends[t - 1])
        if t == 1:
            add(held, 0, src, c * 4 * h, 4 * h, [lambda: from_c[...]])
        if t == 2:
            add(held, first * 2 * h, held, first * 2 * h, 2 * h, [lambda: r1[...]])
        if t == 3:
            add(held, spot(), held, spot(), h, [lambda: r2[...]])
        if t == 4:
            add(mine, z * q, held, spot() + z * q, q, [lambda j=j: r3[(j - 1) * q : j * q, :] for j in range(1, p.Z)])
        if t < 5:
            wires.start(sends[t])
        if t == 5:

            @pl.when(c == 0)
            def _():
                wires.start(sends[5])

        if t == 6:
            wires.finish(skip=sends[5])

            @pl.when(c == 0)
            def _():
                wires.leave(sends[5])

            @pl.when(c == 1)
            def _():
                wires.arrive(sends[5])

    return [functools.partial(step, t) for t in range(7)]


class Solo:
    def __init__(self, p, half):
        self.half, self.rows, self.copies = half, 8 * half, 1 + 4 + 4 * (p.Z - 1)
        q = (p.Z - 1) * (half // p.Z)
        self.kinds = [8 * half, 8 * half] + [2 * half, half, q] * 2 + [2 * half]

    def scratch(self):
        return [pltpu.VMEM((k, 128), BF16) for k in self.kinds] + [pltpu.SemaphoreType.DMA((self.copies,))] * 2


def solo_steps(p, s, src, scratch):
    held, from_c, a1, a2, a3, b1, b2, b3, mine, send_sem, recv_sem = scratch
    wires = Wires(p, send_sem, recv_sem)
    h, q, z = s.half, s.half // p.Z, p.z
    cut = lambda ref, start, size: lambda: ref.at[spread(start(), size)]
    over = [wires.plan_to(lambda: src, lambda: from_c, lambda: p.device("c", 1))]
    sends = [[], [], [], []]
    ways = (("x", "y", p.x, p.y, 0, a1, a2, a3, 0), ("y", "x", p.y, p.x, 4 * h, b1, b2, b3, h))
    for one, two, first, second, base, r1, r2, r3, to in ways:
        sends[0].append(wires.plan(cut(held, lambda f=first, b=base: b + (1 - f) * 2 * h, 2 * h), lambda r=r1: r, one, 1))
        sends[1].append(wires.plan(cut(held, lambda f=first, e=second, b=base: b + (2 * f + 1 - e) * h, h), lambda r=r2: r, two, 1))
        for j in range(1, p.Z):
            part = lambda f=first, e=second, b=base, j=j: b + (2 * f + e) * h + p.at("z", j) * q
            sends[2].append(wires.plan(cut(held, part, q), lambda r=r3, j=j: r.at[pl.ds((j - 1) * q, q)], "z", j))
            sends[3].append(wires.plan(*(cut(mine, lambda t=to: t + z * q, q),) * 2, "z", j))

    def add(dst, to, ref, start, size, parts):
        value = ref[spread(start, size), :].astype(F32)
        for part in parts:
            value = value + part.astype(F32)
        dst[spread(to, size), :] = value.astype(BF16)

    def give():
        wires.start(over)

    def gave():
        wires.leave(over)

    def step(t):
        wires.arrive(over if t == 0 else sends[t - 1])
        if t == 0:
            held[...] = (src[...].astype(F32) + from_c[...].astype(F32)).astype(BF16)
        for one, two, first, second, base, r1, r2, r3, to in ways:
            spot = base + (2 * first + second) * h
            if t == 1:
                add(held, base + first * 2 * h, held, base + first * 2 * h, 2 * h, [r1[...]])
            if t == 2:
                add(held, spot, held, spot, h, [r2[...]])
            if t == 3:
                add(mine, to + z * q, held, spot + z * q, q, [r3[(j - 1) * q : j * q, :] for j in range(1, p.Z)])
        if t < 4:
            wires.start(sends[t])
        else:
            wires.finish(skip=over)

    return give, gave, [functools.partial(step, t) for t in range(5)]


def canon(odd, base):
    r = lax.broadcasted_iota(jnp.int32, (256, 128), 0)
    s = lax.broadcasted_iota(jnp.int32, (256, 128), 1)
    channel = jnp.where(odd, jnp.where(r < 128, r + 64, r - 128), r)
    return jnp.where(r < 192, channel - base, -1000), s


def paced(o, f1, f2):
    return ((5, o[2]), (7, f1[1]), (10, o[3]), (10, f2[1]), (13, f1[2]), (16, o[4]), (16, f2[2]), (19, f1[3]), (22, o[5]), (23, f2[3]))


def owner_kernel(p, shares, *refs):
    (len_ref, wt_ref, so_hbm, s1_hbm, s2_hbm, gv_ref, gmq_ref, wq_ref, wo_ref, w1_ref, w2_ref, vec_ref, vm1_ref, vm2_ref,
     x_hbm, qt_hbm, k_hbm, kt_hbm, v_hbm, ct_hbm, lse_ref, dct_hbm, res_hbm,
     gt_ref, mq_ref, mo_ref, m1_ref, m2_ref, nq_ref, no_ref, n1_ref, n2_ref, f_ref, s_ref, v_ref,
     so_ref, s1_ref, s2_ref, x_s, qt_s, k_s, kt_s, v_s, ct_s, dct_s, res_s, bias_s, dq_s, dk_s, dv_s, gq_s, gv2_s, sq_s, oo_s,
     yo_s, yf_s, yq_s, xo_s, xo_r, tmf_s, txf_s, tmq_s, txq_s, tv_s, rmf_s, rxf_s, rmq_s, rxq_s, rv_s,
     in_sem, src_sem, x_send, x_recv) = refs[: 35 + 38]
    rest = refs[35 + 38 :]
    p.locate()
    p.greet(corner=True)
    d, n = lax.axis_index("dp"), lax.axis_index("narrow")
    core0, core1 = p.c == 0, p.c == 1
    n_rows, seq = x_s.shape[:2]
    pairs = ((qt_hbm, qt_s), (k_hbm, k_s), (dct_hbm, dct_s), (v_hbm, v_s), (ct_hbm, ct_s), (kt_hbm, kt_s), (x_hbm, x_s), (res_hbm, res_s))

    def loads(row):
        return [pltpu.make_async_copy(src.at[row], dst.at[row], in_sem.at[row, i]) for i, (src, dst) in enumerate(pairs)]

    sources = [pltpu.make_async_copy(a, b, src_sem.at[i]) for i, (a, b) in enumerate(((so_hbm, so_ref), (s1_hbm, s1_ref), (s2_hbm, s2_ref)))]
    for copy in sources[:1] + loads(0) + sources[1:]:
        copy.start()
    for row in range(1, n_rows):
        for copy in loads(row):
            copy.start()
    o = sum_steps(p, shares[0], so_ref, oo_s, rest[:10])
    f1 = owned_steps(p, shares[1], s1_ref, rest[10:19])
    f2 = owned_steps(p, shares[2], s2_ref, rest[19:28])
    q_give, q_gave, q = solo_steps(p, shares[3], sq_s, rest[28:39])
    q_all = rest[36]
    f1_half, f1_other, f2_half, f2_other = rest[15], rest[16], rest[24], rest[25]
    turns = [[] for _ in range(12 * n_rows)]
    for i, step in paced(o, f1, f2):
        turns[i * n_rows // 2].append(step)
    slim, tall = gmq_ref.shape[1:]
    up = hot((192, tall), 0, n * tall)
    for c in range(3):
        held = jnp.zeros((tall, 768), F32)
        for g in range(4):
            held = held + tn((0.95 * gmq_ref[4 * c + g]).astype(BF16), hot((slim, 768), 192 * g + d * slim, 0))
        gq_s[c] = nn(up, held.astype(BF16))
    gv2_s[...] = jnp.zeros_like(gv2_s)
    p.meet(corner=True)
    sources[0].wait()
    o[0]()
    lane = lax.broadcasted_iota(jnp.int32, (192, 256), 1)

    def one_row(row, carry):
        same = ids(len_ref, row, (seq, seq), 0) == ids(len_ref, row, (seq, seq), 1)
        bias_s[...] = jnp.where(same, 0.0, -1e30)
        for copy in loads(row):
            copy.wait()

        @pl.when(row == 0)
        def _():
            for copy in sources[1:]:
                copy.wait()
            o[1]()
            f1[0]()
            f2[0]()

        def pair(j, carry):
            lo = pl.multiple_of(128 * j, 128)
            kp, vp = k_s[row, :, pl.ds(lo, 128)], v_s[row, :, pl.ds(lo, 128)]
            for e in range(2):
                at = pl.ds(pl.multiple_of(lo + 64 * e, 64), 64)
                qh, dc = qt_s[row, at, :], dct_s[row, at, :]
                none = jnp.zeros_like(qh)
                wide = lambda a: jnp.concatenate([none, a] if e else [a, none], axis=0)
                delta = jnp.sum(dc.astype(F32) * ct_s[row, at, :].astype(F32), axis=0, keepdims=True)
                s = nn(kp, wide(qh)) + bias_s[...]
                ex = jnp.exp(s - lse_ref[row, pl.ds(2 * j + e, 1), :])
                de = nn(vp, wide(dc))
                ds = (ex * (de - delta)).astype(BF16)
                dv_s[row, at, :] = nt(dc, ex.astype(BF16)).astype(BF16)
                dk_s[row, at, :] = nt(qh, ds).astype(BF16)
                dq_s[row, at, :] = (nn(kt_s[row, at, :], ds) * 0.125).astype(BF16)
                at_turn(row * 12 + 2 * j + e, turns)
            return carry

        lax.fori_loop(0, 6, pair, 0)
        for g in range(4):
            lo = window(g)
            r = slice(192 * g, 192 * g + 192)
            gq = nn(jnp.concatenate([dq_s[row, r, :], dk_s[row, r, :], dv_s[row, r, :]], axis=0), x_s[row, :, lo : lo + 256])
            keep = (lane < 192) if g % 2 == 0 else (lane >= 64)
            for c in range(3):
                gq_s[c, :, lo : lo + 256] += jnp.where(keep, gq[192 * c : 192 * c + 192], 0.0)
        ones = jnp.ones((16, seq), BF16)
        gv2_s[0:1, :] += nt(ones, dq_s[row])[0:1]
        gv2_s[1:2, :] += nt(ones, dv_s[row])[0:1]
        return carry

    lax.fori_loop(0, n_rows, one_row, 0)
    half = shares[3].half
    values = [gq_s[c] for c in range(3)]
    gv = jnp.concatenate([gv_ref[0:4], gv2_s[0:2], gv_ref[6:12]], axis=0)
    lane = lax.broadcasted_iota(jnp.int32, (192, 128), 1)
    for g in range(4):
        lo = window(g)
        tiles = []
        edges = []
        for c in range(3):
            a, b = values[c][:, lo : lo + 128], values[c][:, lo + 128 : lo + 256]
            whole, edge = (b, pltpu.roll(a, 64, 1)) if g % 2 else (a, b)
            tiles.append(whole)
            edges.append(jnp.where(lane < 64, edge, 0.0))
        tiles.append(edges[0] + pltpu.roll(edges[1], 64, 1))
        tiles.append(edges[2][:96] + pltpu.roll(edges[2][96:], 64, 1))
        vec = [gv[0:8, 192 * g : 192 * g + 128]]
        vec.append(jnp.concatenate([gv[0:8, 192 * g + 128 : 192 * g + 192], jnp.zeros((8, 64), F32)], axis=1))
        vec += [gv[8 + g : 9 + g, 128 * j : 128 * j + 128] for j in range(6)]
        vec.append(jnp.zeros((2 * half - 864 - 22, 128), F32))
        flat = jnp.concatenate(tiles + vec, axis=0).astype(BF16)
        sq_s[g * half : g * half + half, :] = flat[:half]
        sq_s[(4 + turned(g)) * half : (5 + turned(g)) * half, :] = flat[half:]
    def blocks(a_ref, b_ref):
        return jnp.concatenate([r[192 * j : 192 * j + 192, :] for r in (a_ref, b_ref) for j in range(3)], axis=1)

    def grad_in(row):
        dx = []
        for g in range(4):
            r = slice(192 * g, 192 * g + 192)
            dx.append(nn(wt_ref[g], jnp.concatenate([dq_s[row, r, :], dk_s[row, r, :], dv_s[row, r, :]], axis=0)))
        gt_ref[row] = (res_s[row].astype(F32) + jnp.concatenate(dx, axis=0).T).astype(BF16)

    wires = Wires(p, x_send, x_recv)
    me = 2 * p.x + p.y
    odd = lax.rem(me, 2) == 1
    around = ((1, 0), (0, 1), (1, 1))

    def scatter(src, dst, cores=(1,)):
        return [
            wires.plan_to(
                lambda dx=dx, dy=dy: src.at[lax.rem(p.x + dx, 2), lax.rem(p.y + dy, 2)], lambda: dst.at[me], lambda dx=dx, dy=dy, c=c: p.other(dx, dy, c)
            )
            for dx, dy in around
            for c in cores
        ]

    early = [scatter(a, b) for a, b in ((tmf_s, rmf_s), (txf_s, rxf_s), (tmq_s, rmq_s), (tv_s, rv_s))]
    late = scatter(txq_s, rxq_s, (0, 1))
    late += [wires.plan_to(lambda: txq_s.at[p.x, p.y], lambda: rxq_s.at[me], lambda: p.device("c", 1))]
    late_on = {0: [late[0], late[2], late[4], late[6]], 1: [late[1], late[3], late[5]]}
    sibling = lambda: p.device("c", 1)
    pass_early = [wires.plan_to(lambda a=a: a, lambda a=a: a, sibling) for a in (rmf_s, rxf_s, rmq_s, rv_s)]
    pass_o = [wires.plan_to(lambda: xo_s, lambda: xo_r, sibling)]
    big = wo_ref.shape[2]
    sel_b = hot((big, 768), d * big, 0)
    wide, cols = w1_ref.shape[2], w1_ref.shape[1]

    def put_f(dst, pair):
        for x in range(2):
            sel = hot((cols, 192), (p.z * 2 + x) * cols, 0)
            part = jnp.concatenate([nn(sel, m) for m in pair], axis=0).astype(BF16)
            for y in range(2):
                dst[x, y] = part[:, 384 * y : 384 * y + 384]

    def put_q(dst, three):
        for x in range(2):
            part = jnp.zeros((192, 128), F32)
            for c, m in enumerate(three):
                at, s = canon(odd, (p.z * 2 + x) * slim)
                sel = jnp.logical_and(jnp.logical_and(at >= 0, at < slim), at + c * slim == s).astype(BF16)
                part = part + nn(m, sel)
            for y in range(2):
                dst[x, y] = part[96 * y : 96 * y + 96].astype(BF16)

    @pl.when(core0)
    def _():
        q_give()
        for step in (lambda: grad_in(0), o[6], f1[4], f2[4], lambda: grad_in(1), f1[5], o[7], f2[5], o[8], f1[6], f2[6]):
            step()
        yo_s[...] = ns_start([wide_rows(oo_s, 0, 4).astype(F32)])[0]

        def turn(t, carry):
            y = yo_s[...]
            yo_s[...] = ns_sweep([y], t)[0]
            return carry

        lax.fori_loop(0, NS_STEPS, turn, 0)
        xo_s[...] = nn(sel_b, yo_s[...].astype(BF16)).astype(BF16)
        wires.start(pass_o)
        q_gave()

    @pl.when(core1)
    def _():
        for step in (q[0], o[6], f1[4], f2[4], lambda: grad_in(0), q[1], lambda: grad_in(1), f1[5], o[7], f2[5], o[8], q[2], f1[6], f2[6]):
            step()
        for i, y in enumerate(ns_start([blocks(a, b).astype(F32) for a, b in ((f1_other, f1_half), (f2_other, f2_half))])):
            yf_s[i] = y

        def f_turn(t, carry):
            ys = [yf_s[i] for i in range(2)]
            for i, y in enumerate(ns_sweep(ys, t)):
                yf_s[i] = y
            return carry

        lax.fori_loop(0, 3, f_turn, 0)
        q[3]()
        lax.fori_loop(3, NS_STEPS, f_turn, 0)
        put_f(tmf_s, [blocks(f1_other, f1_half), blocks(f2_other, f2_half)])
        put_f(txf_s, [yf_s[i].astype(BF16) for i in range(2)])
        for a, b, copies in zip((tmf_s, txf_s), (rmf_s, rxf_s), early[:2]):
            wires.start(copies)
            b[me] = a[p.x, p.y]
        q[4]()
        tiles = [q_all[192 * j : 192 * j + 192, :].astype(F32) for j in range(4)]
        lane = lax.broadcasted_iota(jnp.int32, (192, 128), 1)
        last = q_all[768:864, :].astype(F32)
        last = jnp.concatenate([last, pltpu.roll(last, 64, 1)], axis=0)
        edges = [jnp.where(lane < 64, e, 0.0) for e in (tiles[3], pltpu.roll(tiles[3], 64, 1), last)]
        three = [jnp.concatenate([t, e], axis=1) for t, e in zip(tiles, edges)]
        for i, y in enumerate(ns_start(three)):
            yq_s[i] = y

        def turn(t, carry):
            ys = [yq_s[i] for i in range(3)]
            for i, y in enumerate(ns_sweep(ys, t)):
                yq_s[i] = y
            return carry

        lax.fori_loop(0, NS_STEPS, turn, 0)
        put_q(txq_s, [yq_s[i].astype(BF16) for i in range(3)])
        wires.start(late)
        rxq_s[me] = txq_s[p.x, p.y]
        put_q(tmq_s, [m.astype(BF16) for m in three])
        for x in range(2):
            for y in range(2):
                tv_s[x, y] = q_all[864:896, :]
        for a, b, copies in zip((tmq_s, tv_s), (rmq_s, rv_s), early[2:]):
            wires.start(copies)
            b[me] = a[p.x, p.y]
        for copies in early[:2]:
            wires.arrive(copies)
        wires.start(pass_early[:2])
        wires.arrive(pass_o)

    @pl.when(core0)
    def _():
        wires.arrive(pass_early[:2])

    def fresh(w, own, longest):
        return w - muon_rate * (0.2 * math.sqrt(longest) * own + muon_decay * w)

    sel_l = hot((wide, 768), n * wide, 0)
    sel_h = hot((wide, 384), p.c * wide, 0)
    sel_q = hot((tall, 96), p.c * tall, 0)
    mo_ref[0] = nt(sel_l, nn(sel_b, wide_rows(oo_s, 0, 4)).astype(BF16))
    no_ref[0] = fresh(wo_ref[0], nt(sel_l, jnp.where(core0, xo_s[...], xo_r[...])), 768)
    for g in range(4):
        for i, (w_ref, m_ref, n_ref) in enumerate(((w1_ref, m1_ref, n1_ref), (w2_ref, m2_ref, n2_ref))):
            at = slice(cols * i, cols * i + cols)
            m_ref[g] = nt(rmf_s[g, at, :], sel_h)
            n_ref[g] = fresh(w_ref[g], nt(rxf_s[g, at, :], sel_h), 768)

    @pl.when(core1)
    def _():
        for copies in early[2:]:
            wires.arrive(copies)
        wires.start(pass_early[2:])
        wires.arrive(late_on[1])

    @pl.when(core0)
    def _():
        wires.arrive(late_on[0])

    for g in range(4):
        own = nn(sel_q, rxq_s[g]).astype(BF16)
        for c in range(3):
            nq_ref[4 * c + g] = fresh(wq_ref[4 * c + g], nt(hot((slim, 128), c * slim, 0), own), 192)

    @pl.when(core0)
    def _():
        wires.arrive(pass_early[2:])

    for g in range(4):
        own = nn(sel_q, rmq_s[g]).astype(BF16)
        for c in range(3):
            mq_ref[4 * c + g] = nt(hot((slim, 128), c * slim, 0), own)
    parts = [rv_s[g].astype(F32) for g in range(4)]
    top = jnp.concatenate([t for v in parts for t in (v[0:8], v[8:16, :64])], axis=1)
    low = [jnp.concatenate([v[16 + j : 17 + j] for j in range(6)], axis=1) for v in parts]
    grad = jnp.concatenate([top] + low, axis=0)
    first = 0.9 * vm1_ref[...] + 0.1 * grad
    second = 0.999 * vm2_ref[...] + 0.001 * grad * grad
    f_ref[...] = first
    s_ref[...] = second
    v_ref[...] = vec_ref[...] - adam_rate * (first * (1.0 / (1.0 - 0.9**STEP))) / (jnp.sqrt(second * (1.0 / (1.0 - 0.999**STEP))) + 1e-08)

    @pl.when(core0)
    def _():
        wires.leave(pass_o)

    @pl.when(core1)
    def _():
        for copies in early + [late, pass_early]:
            wires.leave(copies)


def closing_owned(p, shares, lengths, wt, so, s1, s2, gv, mq, weights, vec, vm1, vm2, acts, ident):
    tokens = acts[0]
    n, seq, d = tokens.shape
    slim = mq.shape[1]
    shape = lambda a: jax.ShapeDtypeStruct(a.shape, F32)
    outs = [jax.ShapeDtypeStruct(tokens.shape, BF16)] + [shape(w) for w in weights] * 2 + [shape(vec)] * 3
    hbm = pl.BlockSpec(memory_space=pl.ANY)
    tm, mt = pltpu.VMEM((n, seq, d), BF16), pltpu.VMEM((n, d, seq), BF16)
    scratch = [pltpu.VMEM((4608, 128), BF16)] * 3
    scratch += [tm, mt, tm, mt, tm, mt, mt, pltpu.VMEM((n, seq, d), BF16), pltpu.VMEM((seq, seq), F32)]
    scratch += [mt] * 3 + [pltpu.VMEM((3, 192, 768), F32), pltpu.VMEM((8, 768), F32)]
    scratch += [pltpu.VMEM((shares[3].rows, 128), BF16), pltpu.VMEM((shares[0].rows, 128), BF16)]
    scratch += [pltpu.VMEM((768, 768), F32), pltpu.VMEM((2, 192, 768), F32), pltpu.VMEM((3, 192, 256), F32)]
    scratch += [pltpu.VMEM((4 * slim, 768), BF16)] * 2
    to_f, to_q, to_v = (2 * slim, 384), (96, 128), (32, 128)
    scratch += [pltpu.VMEM((2, 2) + k, BF16) for k in (to_f, to_f, to_q, to_q, to_v)]
    scratch += [pltpu.VMEM((4,) + k, BF16) for k in (to_f, to_f, to_q, to_q, to_v)]
    scratch += [pltpu.SemaphoreType.DMA((n, 8)), pltpu.SemaphoreType.DMA((3,)), pltpu.SemaphoreType.DMA((24,)), pltpu.SemaphoreType.DMA((24,))]
    scratch += shares[0].scratch(p)
    for s in shares[1:]:
        scratch += s.scratch()
    return pl.pallas_call(
        functools.partial(owner_kernel, p, shares),
        out_shape=outs,
        in_specs=[pl.BlockSpec(memory_space=pltpu.SMEM), VMEM] + [hbm] * 3 + [VMEM] * 9 + [hbm] * 6 + [VMEM] + [hbm] * 2,
        out_specs=[VMEM] * 12,
        scratch_shapes=scratch,
        compiler_params=pltpu.CompilerParams(collective_id=ident, has_side_effects=True, vmem_limit_bytes=62 * 2**20),
    )(lengths, wt, so, s1, s2, gv, mq, *weights, vec, vm1, vm2, *acts)


def hand_over_kernel(count, *refs):
    src, dst, held = refs[:count], refs[count : 2 * count], refs[2 * count : 3 * count]
    here, away = refs[3 * count :]
    loads = [pltpu.make_async_copy(src[i], held[i], here.at[i]) for i in range(count)]
    stores = [pltpu.make_async_copy(held[i], dst[i], away.at[i]) for i in range(count)]
    for load in loads:
        load.start()
    for load, store in zip(loads, stores):
        load.wait()
        store.start()
    for store in stores:
        store.wait()


def hand_over(values):
    hbm = pl.BlockSpec(memory_space=pl.ANY)
    count = len(values)
    return pl.pallas_call(
        functools.partial(hand_over_kernel, count),
        out_shape=[jax.ShapeDtypeStruct(a.shape, a.dtype) for a in values],
        in_specs=[hbm] * count,
        out_specs=[hbm] * count,
        scratch_shapes=[pltpu.VMEM(a.shape, a.dtype) for a in values] + [pltpu.SemaphoreType.DMA((count,))] * 2,
        compiler_params=pltpu.CompilerParams(vmem_limit_bytes=60 * 2**20),
    )(*values)


def local(tokens, doc_lengths, cotangent, qkv_weight, out_weight, ffn_in_weight, ffn_out_weight, vectors,
          qkv_moment, out_moment, ffn_in_moment, ffn_out_moment, vec_moment1, vec_moment2):
    p = Place(lax.axis_size("dp"), lax.axis_size("narrow"))
    flip = lambda a: a.transpose(0, 2, 1)
    wq, w1, w2, mq, m1, m2 = map(flip, (qkv_weight, ffn_in_weight, ffn_out_weight, qkv_moment, ffn_in_moment, ffn_out_moment))
    owned = p.X == 2 and p.Y == 2 and p.C == 2 and p.Z in (2, 4)
    if owned:
        shares = [Shares(p, 4608), Owned(p, 576), Owned(p, 576), Solo(p, 448)]
    else:
        shares = [Shares(p, r) for r in (4608, 4608, 4608, 3456 + 72)]
    qt, k, kt, v, ct, out_act, res, dct, lse, wt, so, s1, s2, gv = front(
        p, owned, shares[0].rows, doc_lengths, tokens, cotangent, wq, out_weight, w1, w2, vectors, out_moment, m1, m2, 0)
    acts = (tokens, qt, k, kt, v, ct, lse, dct, res)
    rest = (closing_owned if owned else closing)(
        p, shares, doc_lengths, wt, so, s1, s2, gv, mq, (wq, out_weight, w1, w2), vectors, vec_moment1, vec_moment2, acts, 1)
    out_act, gt, gq, go, g1, g2, nq, no, n1, n2, f, s, vn = hand_over([out_act] + list(rest))
    return (out_act, gt, flip(gq), go, flip(g1), flip(g2), flip(nq), no, flip(n1), flip(n2), f, s, vn)


def solution(mesh):
    rows = P(("dp", "narrow"), None, None)
    cut = P(None, "narrow", "dp")
    return jax.shard_map(
        local,
        mesh=mesh,
        in_specs=(rows, P(("dp", "narrow"), None), rows) + (cut,) * 4 + (P(),) + (cut,) * 4 + (P(), P()),
        out_specs=(rows, rows) + (cut,) * 8 + (P(),) * 3,
        check_vma=False,
    )
```

```python
import functools
import math

import jax
import jax.numpy as jnp
from jax import lax
from jax.experimental import pallas as pl
from jax.experimental.pallas import tpu as pltpu
from jax.sharding import PartitionSpec as P

F32, BF16 = jnp.float32, jnp.bfloat16
MESH = pl.DeviceIdType.MESH
NORM_EPS = 1e-05
NS_STEPS = 5
STEP = 5
ns_first = 3.4445
ns_second = -4.775
ns_third = 2.0315
muon_rate = 0.5
muon_decay = 0.01
adam_rate = 0.4
VMEM = pl.BlockSpec(memory_space=pltpu.VMEM)


def nn(a, b):
    return lax.dot_general(a, b, (((1,), (0,)), ((), ())), preferred_element_type=F32)


def nt(a, b):
    return lax.dot_general(a, b, (((1,), (1,)), ((), ())), preferred_element_type=F32)


def tn(a, b):
    return lax.dot_general(a, b, (((0,), (0,)), ((), ())), preferred_element_type=F32)


def window(g):
    return 128 * (3 * (g // 2) + g % 2)


def join(parts):
    out = []
    for p in range(2):
        a, b = parts[2 * p], parts[2 * p + 1]
        out += [a[:, :128], a[:, 128:] + b[:, :128], b[:, 128:]]
    return jnp.concatenate(out, axis=1)


def ids(len_ref, row, shape, dim):
    pos = lax.broadcasted_iota(jnp.int32, shape, dim)
    out = jnp.zeros(shape, jnp.int32)
    end = jnp.int32(0)
    for j in range(4):
        end = end + len_ref[row, j]
        out = out + (pos >= end).astype(jnp.int32)
    return out


def hot(shape, row_at, col_at):
    rows = lax.broadcasted_iota(jnp.int32, shape, 0) + row_at
    cols = lax.broadcasted_iota(jnp.int32, shape, 1) + col_at
    return (rows == cols).astype(BF16)


def put_blocks(dst, base, value):
    for j in range(value.shape[1] // 128):
        dst[base + 192 * j : base + 192 * j + 192, :] = value[:, 128 * j : 128 * j + 128].astype(BF16)


def add_blocks(dst, base, value):
    for j in range(value.shape[1] // 128):
        at = slice(base + 192 * j, base + 192 * j + 192)
        dst[at, :] = (dst[at, :].astype(F32) + value[:, 128 * j : 128 * j + 128]).astype(BF16)


def group_rows(owned, g):
    return (576 * g, 2304 + 576 * turned(g)) if owned else (1152 * g, 1152 * g + 576)


def wide_rows(ref, base, count):
    parts = []
    for q in range(count):
        at = base + 1152 * q
        parts.append(jnp.concatenate([ref[at + 192 * j : at + 192 * j + 192, :] for j in range(6)], axis=1))
    return parts[0] if count == 1 else jnp.concatenate(parts, axis=0)


def gelu_parts(v):
    t = pl.reciprocal(1.0 + (0.3275911 * 0.7071067811865476) * jnp.abs(v), approx=True)
    ex = jnp.exp2(v * v * (-0.5 * 1.4426950408889634))
    half = t * ex * (0.127414796 + t * (-0.142248368 + t * (0.7107068705 + t * (-0.7265760135 + t * 0.5307027145))))
    cdf = jnp.where(v >= 0, 1.0 - half, half)
    return v * cdf, cdf + (v * ex) * 0.3989422804014327


def norm(h):
    mu = jnp.mean(h, axis=-1, keepdims=True)
    c = h - mu
    inv = lax.rsqrt(jnp.mean(c * c, axis=-1, keepdims=True) + NORM_EPS)
    return c * inv, inv


def norm_back(up, n, inv, gain):
    w = up * gain
    return inv * (w - jnp.mean(w, axis=-1, keepdims=True) - n * jnp.mean(w * n, axis=-1, keepdims=True))


def col_sum(v):
    return jnp.sum(v, axis=0, keepdims=True)


def turned(g):
    return 2 * (g % 2) + g // 2


class Place:
    def __init__(self, dp, narrow):
        self.X = 2 if dp % 2 == 0 else 1
        self.C = 2 if narrow % 2 == 0 else 1
        self.Z, self.Y = dp // self.X, narrow // self.C

    def locate(self):
        d, n = lax.axis_index("dp"), lax.axis_index("narrow")
        self.z, self.x = d // self.X, lax.rem(d, self.X)
        self.y, self.c = n // self.C, lax.rem(n, self.C)

    def count(self):
        return self.Z + self.X + self.Y + self.C - 4

    def at(self, axis, j):
        return lax.rem(getattr(self, axis) + j, getattr(self, axis.upper()))

    def device(self, axis, j):
        where = {a: getattr(self, a) for a in "zxyc"}
        where[axis] = self.at(axis, j)
        return (where["z"] * self.X + where["x"], where["y"] * self.C + where["c"])

    def other(self, dx, dy, c):
        return (self.z * self.X + lax.rem(self.x + dx, self.X), lax.rem(self.y + dy, self.Y) * self.C + c)

    def barrier(self, corner=False):
        self.greet(corner)
        self.meet(corner)

    def greet(self, corner=False):
        sem = pltpu.get_barrier_semaphore()
        if corner:
            for c in range(self.C):
                pl.semaphore_signal(sem, inc=1, device_id=self.other(1, 1, c), device_id_type=MESH)
            for dx, dy in ((1, 0), (0, 1)):
                pl.semaphore_signal(sem, inc=1, device_id=self.other(dx, dy, 1 - self.c), device_id_type=MESH)
        for axis in "zxyc":
            for j in range(1, getattr(self, axis.upper())):
                pl.semaphore_signal(sem, inc=1, device_id=self.device(axis, j), device_id_type=MESH)

    def meet(self, corner=False):
        pl.semaphore_wait(pltpu.get_barrier_semaphore(), self.count() + 4 * int(corner))


class Wires:
    def __init__(self, place, send_sem, recv_sem):
        self.place, self.send_sem, self.recv_sem, self.makers = place, send_sem, recv_sem, []

    def plan(self, src, dst, axis, j):
        return self.plan_to(src, dst, lambda: self.place.device(axis, j))

    def plan_to(self, src, dst, device):
        k = len(self.makers)
        self.makers.append(
            lambda: pltpu.make_async_remote_copy(
                src_ref=src(),
                dst_ref=dst(),
                send_sem=self.send_sem.at[k],
                recv_sem=self.recv_sem.at[k],
                device_id=device(),
                device_id_type=MESH,
            )
        )
        return k

    def start(self, copies):
        for k in copies:
            self.makers[k]().start()

    def arrive(self, copies):
        for k in copies:
            self.makers[k]().wait_recv()

    def leave(self, copies):
        for k in copies:
            self.makers[k]().wait_send()

    def finish(self, skip=()):
        self.leave([k for k in range(len(self.makers)) if k not in skip])


def gather_copies(p):
    return (p.Z - 1) + p.Z * ((p.X - 1) + (p.Y - 1) + 2 * (p.X - 1) * (p.Y - 1) + (p.C - 1))


def gather_steps(p, wires, buf, half, corner=False):
    z, x, y, c = p.z, p.x, p.y, p.c
    rest = buf.shape[4] - half

    def same(at):
        return (lambda: buf.at[at()],) * 2

    along, first, second, last = {}, {}, {}, {}
    for j in range(1, p.Z):
        along[j] = wires.plan(*same(lambda: (z, c, x, y)), "z", j)
    for i in range(p.Z):
        from_z = lambda i=i: p.at("z", p.Z - i) if i else z
        mine = lambda f=from_z: (f(), c, x, y)
        first[i] = [wires.plan(*same(mine), "x", j) for j in range(1, p.X)] + [wires.plan(*same(mine), "y", j) for j in range(1, p.Y)]
        second[i] = []
        if corner:
            first[i].append(wires.plan_to(*same(mine), lambda: p.other(1, 1, c)))
        for j in range(1, p.X if not corner else 1):
            part = lambda f=from_z, j=j: (f(), c, p.at("x", p.X - j), y, pl.ds(0, half))
            second[i] += [wires.plan(*same(part), "y", q) for q in range(1, p.Y)]
        for j in range(1, p.Y if not corner else 1):
            part = lambda f=from_z, j=j: (f(), c, x, p.at("y", p.Y - j), pl.ds(half, rest))
            second[i] += [wires.plan(*same(part), "x", q) for q in range(1, p.X)]
        last[i] = [wires.plan(*same(lambda f=from_z: (f(), c)), "c", j) for j in range(1, p.C)]

    def own(i):
        if i:
            wires.arrive([along[i]])
        wires.start(first[i])

    def onward(i):
        wires.arrive(first[i])
        wires.start(second[i])

    def over(i):
        wires.arrive(first[i] if corner else second[i])
        wires.start(last[i])

    def done():
        for i in last:
            wires.arrive(last[i])

    of = lambda f: [functools.partial(f, i) for i in range(p.Z)]
    return lambda: wires.start(along.values()), of(own), [] if corner else of(onward), of(over), done


class Shares:
    def __init__(self, p, rows):
        cells = p.X * p.Y * p.Z
        unit = 16 * cells * p.C
        units = -(-rows // unit)
        self.a, self.b = 16 * ((units + 1) // 2), 16 * max(units // 2, 1)
        self.per_core = cells * (self.a + self.b)
        self.rows = p.C * self.per_core
        self.cells = cells
        self.copies = 2 * ((p.C - 1) + 2 * ((p.X - 1) + (p.Y - 1)) + 2 * (p.Z - 1))

    def scratch(self, p):
        a, b = self.a, self.b
        kinds = [
            (self.per_core,),
            (p.C - 1, self.per_core),
            (p.X - 1, p.Y * p.Z * a),
            (p.Y - 1, p.X * p.Z * b),
            (p.Y - 1, p.Z * a),
            (p.X - 1, p.Z * b),
            (p.Z - 1, a),
            (p.Z - 1, b),
        ]
        return [pltpu.VMEM(k + (128,), BF16) for k in kinds] + [pltpu.SemaphoreType.DMA((self.copies,))] * 2


def spread(start, size):
    return pl.ds(pl.multiple_of(start, 16), size)


def add_into(dst, at, parts):
    total = dst[at, :].astype(F32)
    for part in parts:
        total = total + part.astype(F32)
    dst[at, :] = total.astype(BF16)


def sum_steps(p, s, src, out, scratch):
    held, from_c, a1, b1, a2, b2, a3, b3, send_sem, recv_sem = scratch
    wires = Wires(p, send_sem, recv_sem)
    a, b, per = s.a, s.b, s.per_core
    ax, by = p.Y * p.Z * a, p.X * p.Z * b
    in_a = lambda x, y=0, z=0: ((x * p.Y + y) * p.Z + z) * a
    in_b = lambda y, x=0, z=0: s.cells * a + ((y * p.X + x) * p.Z + z) * b
    x, y, z, c = p.x, p.y, p.z, p.c
    base = c * per

    def cut(ref, start, size):
        return lambda: ref.at[spread(start(), size)]

    def both(start, size):
        return (cut(out, start, size),) * 2

    def slot(ref, j):
        return lambda: ref.at[j - 1]

    sends = [[] for _ in range(8)]
    for j in range(1, p.C):
        sends[0].append(wires.plan(cut(src, lambda j=j: p.at("c", j) * per, per), slot(from_c, j), "c", j))
        sends[7].append(wires.plan(*both(lambda: base, per), "c", j))
    for j in range(1, p.X):
        sends[1].append(wires.plan(cut(held, lambda j=j: in_a(p.at("x", j)), ax), slot(a1, j), "x", j))
        sends[2].append(wires.plan(cut(held, lambda j=j: in_b(y, p.at("x", j)), p.Z * b), slot(b2, j), "x", j))
        sends[5].append(wires.plan(*both(lambda: base + in_b(y, x), p.Z * b), "x", j))
        sends[6].append(wires.plan(*both(lambda: base + in_a(x), ax), "x", j))
    for j in range(1, p.Y):
        sends[1].append(wires.plan(cut(held, lambda j=j: in_b(p.at("y", j)), by), slot(b1, j), "y", j))
        sends[2].append(wires.plan(cut(held, lambda j=j: in_a(x, p.at("y", j)), p.Z * a), slot(a2, j), "y", j))
        sends[5].append(wires.plan(*both(lambda: base + in_a(x, y), p.Z * a), "y", j))
        sends[6].append(wires.plan(*both(lambda: base + in_b(y), by), "y", j))
    for j in range(1, p.Z):
        sends[3].append(wires.plan(cut(held, lambda j=j: in_a(x, y, p.at("z", j)), a), slot(a3, j), "z", j))
        sends[3].append(wires.plan(cut(held, lambda j=j: in_b(y, x, p.at("z", j)), b), slot(b3, j), "z", j))
        sends[4].append(wires.plan(*both(lambda: base + in_a(x, y, z), a), "z", j))
        sends[4].append(wires.plan(*both(lambda: base + in_b(y, x, z), b), "z", j))

    def total(ref, at, size, parts, count):
        value = ref[spread(at, size), :].astype(F32)
        for j in range(count):
            value = value + parts[j].astype(F32)
        return value.astype(BF16)

    def step(t):
        if t:
            wires.arrive(sends[t - 1])
        if t == 1:
            held[...] = total(src, base, per, from_c, p.C - 1)
        if t == 2:
            held[spread(in_a(x), ax), :] = total(held, in_a(x), ax, a1, p.X - 1)
            held[spread(in_b(y), by), :] = total(held, in_b(y), by, b1, p.Y - 1)
        if t == 3:
            held[spread(in_a(x, y), p.Z * a), :] = total(held, in_a(x, y), p.Z * a, a2, p.Y - 1)
            held[spread(in_b(y, x), p.Z * b), :] = total(held, in_b(y, x), p.Z * b, b2, p.X - 1)
        if t == 4:
            out[spread(base + in_a(x, y, z), a), :] = total(held, in_a(x, y, z), a, a3, p.Z - 1)
            out[spread(base + in_b(y, x, z), b), :] = total(held, in_b(y, x, z), b, b3, p.Z - 1)
        if t < 8:
            wires.start(sends[t])
        else:
            wires.finish()

    return [functools.partial(step, t) for t in range(9)]


def at_turn(turn, steps):
    for i, todo in enumerate(steps):
        if todo:

            @pl.when(turn == i)
            def _():
                for step in todo:
                    step()


def dealt(steps, turns):
    return [steps[len(steps) * i // turns : len(steps) * (i + 1) // turns] for i in range(turns)]


def fold(t, odd):
    rows, wide = t.shape
    if wide % 128 == 64:
        body = jnp.where(odd, t[:, 64:], t[:, : wide - 64])
        edge = jnp.where(odd, t[:, :64], t[:, wide - 64 :])
        a, b = edge[: rows // 2], edge[rows // 2 :]
        tiles = [body[:, 128 * j : 128 * j + 128] for j in range(wide // 128)]
        tiles.append(jnp.concatenate([jnp.where(odd, b, a), jnp.where(odd, a, b)], axis=1))
        return jnp.concatenate(tiles, axis=0)
    need = -(-wide // 128) * 128
    t = jnp.concatenate([t, jnp.zeros((rows, need - wide), t.dtype)], axis=1) if need > wide else t
    return jnp.concatenate([t[:, 128 * j : 128 * j + 128] for j in range(need // 128)], axis=0)


def fold_rows(rows, wide):
    return rows * (wide // 128) + rows // 2 if wide % 128 == 64 else rows * (-(-wide // 128))


def unfold(p, buf, base, rows, wide):
    out = []
    lane = lax.broadcasted_iota(jnp.int32, (rows // 2, 128), 1)
    size = fold_rows(rows, wide)
    for z in range(p.Z):
        for x in range(p.X):
            tiles = []
            for y in range(p.Y):
                got = [buf[z, c, x, y, base : base + size, :].astype(F32) for c in range(p.C)]
                if wide % 128 == 64:
                    k = wide // 128
                    even, odd = got
                    tiles += [even[rows * j : rows * j + rows] for j in range(k)]
                    e, o = even[rows * k :], odd[rows * k :]
                    top = jnp.where(lane < 64, e, o)
                    low = pltpu.roll(jnp.where(lane < 64, o, e), 64, 1)
                    tiles.append(jnp.concatenate([top, low], axis=0))
                    tiles += [odd[rows * j : rows * j + rows] for j in range(k)]
                else:
                    k = size // rows
                    for c in range(p.C):
                        t = jnp.concatenate([got[c][rows * j : rows * j + rows] for j in range(k)], axis=1).astype(BF16)
                        tiles.append(nn(t, hot((128 * k, 768), (y * p.C + c) * wide, 0)) if 128 * k == wide else nn(t, hot_cut((128 * k, 768), (y * p.C + c) * wide, wide)))
            if wide % 128 == 64:
                out.append(jnp.concatenate(tiles, axis=1))
            else:
                out.append(functools.reduce(lambda a, b: a + b, tiles))
    return out


def hot_cut(shape, at, limit):
    rows = lax.broadcasted_iota(jnp.int32, shape, 0)
    cols = lax.broadcasted_iota(jnp.int32, shape, 1)
    return jnp.logical_and(rows + at == cols, rows < limit).astype(BF16)


def front_kernel(p, owned, len_ref, x_ref, cot_ref, wq_ref, wo_ref, w1_ref, w2_ref, vec_ref, mo_ref, m1_ref, m2_ref,
                 qt_out, k_out, kt_out, v_out, ct_out, out_out, res_out, dct_out, lse_ref, wt_out, so_ref, s1_ref, s2_ref, gv_ref,
                 bufq, bufr, place_s, win_s, qt_s, k_s, kt_s, v_s, ct_s, vt_s, bias_s, vcol_s, w1_s, w2_s, wo_s, out_s, res_s, dct_s,
                 send_q, recv_q, send_r, recv_r, out_sem):
    p.locate()
    p.greet(corner=owned)
    n_rows, seq = x_ref.shape[:2]
    odd = lax.rem(lax.axis_index("narrow"), 2) == 1
    slim, tall = wq_ref.shape[1:]
    qrows = bufq.shape[4]
    for c in range(3):
        t = jnp.concatenate([wq_ref[4 * c + g] for g in range(4)], axis=0).T
        t = jnp.concatenate([t, jnp.zeros((tall, 128 - 4 * slim), F32)], axis=1)
        bufq[p.z, p.c, p.x, p.y, c * tall : c * tall + tall, :] = t.astype(BF16)
    if qrows > 3 * tall:
        bufq[p.z, p.c, p.x, p.y, 3 * tall :, :] = jnp.zeros((qrows - 3 * tall, 128), BF16)
    p.meet(corner=owned)
    wires_q, wires_r = Wires(p, send_q, recv_q), Wires(p, send_r, recv_r)
    q_z, q_own, q_on, q_over, q_done = gather_steps(p, wires_q, bufq, qrows // 32 * 16, corner=owned)
    q_z()
    q_own[0]()
    rows, wide = 4 * slim, 4 * tall
    size = fold_rows(rows, wide)
    big = wo_ref.shape[2]
    shards = [nt(hot((big, big), 0, 0), wo_ref[0].astype(BF16))]
    shards += [jnp.concatenate([r[g] for g in range(4)], axis=0) for r in (w1_ref, w2_ref)]
    folded = jnp.concatenate([fold(t, odd) for t in shards], axis=0)
    if bufr.shape[4] > 3 * size:
        folded = jnp.concatenate([folded, jnp.zeros((bufr.shape[4] - 3 * size, 128), F32)], axis=0)
    bufr[p.z, p.c, p.x, p.y] = folded.astype(BF16)
    d, n = lax.axis_index("dp"), lax.axis_index("narrow")
    sel_l = hot((wide, 768), n * wide, 0)
    placed = nt(hot((768, big), 0, d * big), (0.95 * mo_ref[0]).astype(BF16)).astype(BF16)
    value = nn(placed, sel_l)
    for q in range(4):
        put_blocks(so_ref, 1152 * q, value[192 * q : 192 * q + 192])
    for dst, m_ref in ((s1_ref, m1_ref), (s2_ref, m2_ref)):
        for g in range(4):
            value = nn(nn(hot((192, slim), 0, d * slim), (0.95 * m_ref[g]).astype(BF16)).astype(BF16), sel_l)
            for half, base in enumerate(group_rows(owned, g)):
                put_blocks(dst, base, value[:, 384 * half : 384 * half + 384])
    for dst in (so_ref, s1_ref, s2_ref):
        if dst.shape[0] > 4608:
            dst[4608:, :] = jnp.zeros((dst.shape[0] - 4608, 128), BF16)
    gv_ref[...] = jnp.zeros_like(gv_ref)
    dp = p.Z * p.X
    for pair in range(dp // 2):
        r = lax.broadcasted_iota(jnp.int32, (256, 1), 0)
        q = jnp.where(r < 128, r, r - 128)
        g = (q >= slim).astype(jnp.int32) + (q >= 2 * slim).astype(jnp.int32) + (q >= 3 * slim).astype(jnp.int32)
        col = 256 * g + jnp.where(jnp.logical_or(g == 1, g == 3), 64, 0) + jnp.where(r < 128, 2 * pair * slim, (2 * pair + 1) * slim) + q - g * slim
        col = jnp.where(q < 4 * slim, col, -1)
        place_s[pair] = (lax.broadcasted_iota(jnp.int32, (256, 1024), 1) == col).astype(BF16)
    win_s[...] = jnp.zeros_like(win_s)
    vcol_s[...] = vec_ref[0:8, :].T
    r_z, r_own, r_on, r_over, r_done = gather_steps(p, wires_r, bufr, bufr.shape[4] // 32 * 16)
    for t in range(1, p.Z + 2):
        for steps, at in ((q_own, t), (q_on, t - 1), (q_over, t - (1 if owned else 2))):
            if 0 <= at < len(steps):
                steps[at]()
        if t == p.Z - 3:
            r_z()
    r_own[0]()
    q_done()
    total = jnp.zeros((3 * 192, 1024), F32)
    for pair in range(dp // 2):
        tiles = []
        for d in (2 * pair, 2 * pair + 1):
            z, x = d // p.X, d % p.X
            got = [bufq[z, c, x, y].astype(F32) for y in range(p.Y) for c in range(p.C)]
            tiles.append(jnp.concatenate([b[c * tall : c * tall + tall] for c in range(3) for b in got], axis=0))
        total = total + nn(jnp.concatenate(tiles, axis=1).astype(BF16), place_s[pair])
    for g in range(4):
        off = 64 * (g % 2)
        stack = total[:, 256 * g : 256 * g + 256].astype(BF16)
        for c in range(3):
            win_s[c, g, off : off + 192, :] = stack[192 * c : 192 * c + 192]
        wt_out[g] = nt(hot((192, 256), off, 0), stack).astype(BF16)
    turns = [[] for _ in range(3 * n_rows)]
    for i, step in enumerate(r_on):
        turns[min(i, 3, len(turns) - 1)].append(step)
    for i, step in enumerate(r_over):
        turns[min(min(i, 3) // 2 + 3, len(turns) - 1)].append(step)
    turns[-1].append(r_done)

    for step in r_own[1:]:
        step()

    def out_copies(row, which):
        pairs = ((qt_s, qt_out), (k_s, k_out), (kt_s, kt_out), (v_s, v_out), (ct_s.at[row], ct_out), (out_s, out_out), (res_s, res_out), (dct_s, dct_out))
        return [pltpu.make_async_copy(pairs[i][0], pairs[i][1].at[row], out_sem.at[i]) for i in which]

    def reuse(row, which):
        @pl.when(row > 0)
        def _():
            for copy in out_copies(row - 1, which):
                copy.wait()

    def one_row(row, carry):
        same = ids(len_ref, row, (seq, seq), 0) == ids(len_ref, row, (seq, seq), 1)
        bias_s[...] = jnp.where(same, 0.0, -1e30)
        reuse(row, range(5))
        for g in range(4):
            lo = window(g)
            xw = x_ref[row, :, lo : lo + 256]
            off = 64 * (g % 2)
            r = slice(192 * g, 192 * g + 192)
            q = nt(win_s[0, g, off : off + 192, :], xw) + vcol_s[r, 4:5]
            qt_s[r, :] = q.astype(BF16) * BF16(0.125)
            kt_s[r, :] = nt(win_s[1, g, off : off + 192, :], xw).astype(BF16)
            v = nt(win_s[2, g, off : off + 192, :], xw) + vcol_s[r, 5:6]
            vt_s[r, :] = v.astype(BF16)
        wide_of = lambda c: join([nt(x_ref[row, :, window(g) : window(g) + 256], win_s[c, g]) for g in range(4)])
        k_s[...] = wide_of(1).astype(BF16)
        v_s[...] = (wide_of(2) + vec_ref[5:6, :]).astype(BF16)
        for copy in out_copies(row, range(4)):
            copy.start()

        def four(j, carry):
            heads = [(pl.multiple_of(256 * j + 128 * u, 128), e) for u in range(2) for e in range(2)]
            spots = [pl.ds(pl.multiple_of(lo + 64 * e, 64), 64) for lo, e in heads]
            scores = []
            for (lo, e), at in zip(heads, spots):
                qh = qt_s[at, :]
                none = jnp.zeros_like(qh)
                scores.append(nn(k_s[:, pl.ds(lo, 128)], jnp.concatenate([none, qh] if e else [qh, none], axis=0)))
            soft = []
            for s in scores:
                s = s + bias_s[...]
                m = jnp.max(s, axis=0, keepdims=True)
                ex = jnp.exp(s - m)
                soft.append((m, ex.astype(BF16), jnp.sum(ex, axis=0, keepdims=True)))
            for i, (at, (m, ex, tot)) in enumerate(zip(spots, soft)):
                ct_s[row, at, :] = (nn(vt_s[at, :], ex) * (1.0 / tot)).astype(BF16)
                lse_ref[row, pl.ds(4 * j + i, 1), :] = m + jnp.log(tot)
            at_turn(row * 3 + j, turns)
            return carry

        lax.fori_loop(0, 3, four, 0)
        out_copies(row, (4,))[0].start()
        return carry

    lax.fori_loop(0, n_rows, one_row, 0)
    wires_q.finish()
    wires_r.finish()
    whole = unfold(p, bufr, 0, rows, wide)
    wo_s[...] = jnp.concatenate(whole, axis=0).astype(BF16)
    for i, dst in enumerate((w1_s, w2_s)):
        whole = unfold(p, bufr, (i + 1) * size, rows, wide)
        for g in range(4):
            off = 64 * (g % 2)
            dst[g, off : off + 192, :] = jnp.concatenate([b[g * slim : g * slim + slim] for b in whole], axis=0).astype(BF16)
            dst[g, 192 - 192 * (g % 2) : 256 - 192 * (g % 2), :] = jnp.zeros((64, 768), BF16)
    vec = lambda i: vec_ref[i : i + 1, :]

    def feed_forward(row, carry):
        h1 = x_ref[row].astype(F32) + (nn(ct_s[row].T, wo_s[...]) + vec(6))
        n1, inv1 = norm(h1)
        first = n1 * vec(0) + vec(1)
        fl = first.astype(BF16)
        inner = lambda g: nn(fl[:, window(g) : window(g) + 256], w1_s[g]) + vec(8 + g)
        active, slope, branch = [], [], []
        ahead = inner(0)
        for g in range(4):
            now, ahead = ahead, (inner(g + 1) if g < 3 else None)
            a, sl = gelu_parts(now)
            active.append(a.astype(BF16))
            slope.append(sl)
            branch.append(nt(active[g], w2_s[g]))
        h2 = first + (join(branch) + vec(7))
        n2, inv2 = norm(h2)
        reuse(row, (5, 6, 7))
        out_s[...] = (n2 * vec(2) + vec(3)).astype(BF16)
        out_copies(row, (5,))[0].start()
        dy = cot_ref[row].astype(F32)
        dh2 = norm_back(dy, n2, inv2, vec(2))
        dbl = dh2.astype(BF16)
        dbt = dbl.T
        flt = fl.T
        ones = jnp.ones((16, seq), BF16)
        dfirst = []
        gb = []
        for g in range(4):
            da = nn(dbl[:, window(g) : window(g) + 256], w2_s[g])
            di = (da * slope[g]).astype(BF16)
            dfirst.append(nt(di, w1_s[g]))
            g2 = nn(dbt[192 * g : 192 * g + 192, :], active[g])
            ext = nn(jnp.concatenate([flt[192 * g : 192 * g + 192, :], ones], axis=0), di)
            for half, base in enumerate(group_rows(owned, g)):
                add_blocks(s2_ref, base, g2[:, 384 * half : 384 * half + 384])
                add_blocks(s1_ref, base, ext[:192, 384 * half : 384 * half + 384])
            gb.append(ext[192:193])
        df = dh2 + join(dfirst)
        dh1 = norm_back(df, n1, inv1, vec(0))
        dat = dh1.astype(BF16)
        res_s[...] = dat
        out_copies(row, (6,))[0].start()
        go = nn(ct_s[row], dat)
        for q in range(4):
            add_blocks(so_ref, 1152 * q, go[192 * q : 192 * q + 192])
        dct_s[...] = nt(wo_s[...], dat).astype(BF16)
        out_copies(row, (7,))[0].start()
        z = jnp.zeros((1, dy.shape[1]), F32)
        gv_ref[...] += jnp.concatenate(
            [col_sum(df * n1), col_sum(df), col_sum(dy * n2), col_sum(dy), z, z, col_sum(dat.astype(F32)), col_sum(dbl.astype(F32))] + gb, axis=0)
        return carry

    lax.fori_loop(0, n_rows, feed_forward, 0)
    for copy in out_copies(n_rows - 1, range(8)):
        copy.wait()


def front(p, owned, sum_rows, lengths, tokens, cot, wq, wo, w1, w2, vec, mo, m1, m2, ident):
    n, seq, d = tokens.shape
    slim, tall = wq.shape[1:]
    up = lambda r, m: -(-r // m) * m
    qrows = up(3 * tall, 32)
    rrows = up(3 * fold_rows(4 * slim, 4 * tall), 16)
    count = gather_copies(p)
    hbm = pl.BlockSpec(memory_space=pl.ANY)
    act = lambda a, b: jax.ShapeDtypeStruct((n, a, b), BF16)
    tm, mt = pltpu.VMEM((seq, d), BF16), pltpu.VMEM((d, seq), BF16)
    return pl.pallas_call(
        functools.partial(front_kernel, p, owned),
        out_shape=[act(d, seq), act(seq, d), act(d, seq), act(seq, d), act(d, seq), act(seq, d), act(seq, d), act(d, seq)]
        + [jax.ShapeDtypeStruct((n, 16, seq), F32), jax.ShapeDtypeStruct((4, 192, 576), BF16)]
        + [jax.ShapeDtypeStruct((sum_rows, 128), BF16)] * 3
        + [jax.ShapeDtypeStruct((12, 768), F32)],
        in_specs=[pl.BlockSpec(memory_space=pltpu.SMEM)] + [VMEM] * 10,
        out_specs=[hbm] * 8 + [VMEM] * 6,
        scratch_shapes=[
            pltpu.VMEM((p.Z, p.C, p.X, p.Y, qrows, 128), BF16),
            pltpu.VMEM((p.Z, p.C, p.X, p.Y, rrows, 128), BF16),
            pltpu.VMEM((p.Z * p.X // 2, 256, 1024), BF16),
            pltpu.VMEM((3, 4, 256, 256), BF16),
            mt, tm, mt, tm, pltpu.VMEM((n, d, seq), BF16),
            mt, pltpu.VMEM((seq, seq), F32), pltpu.VMEM((d, 8), F32),
            pltpu.VMEM((4, 256, 768), BF16), pltpu.VMEM((4, 256, 768), BF16), pltpu.VMEM((768, 768), BF16),
            tm, tm, mt,
            pltpu.SemaphoreType.DMA((count,)), pltpu.SemaphoreType.DMA((count,)),
            pltpu.SemaphoreType.DMA((count,)), pltpu.SemaphoreType.DMA((count,)),
            pltpu.SemaphoreType.DMA((8,)),
        ],
        compiler_params=pltpu.CompilerParams(collective_id=ident, has_side_effects=True, vmem_limit_bytes=62 * 2**20),
    )(lengths, tokens, cot, wq, wo, w1, w2, vec, mo, m1, m2)


def on_diagonal(n):
    return lax.broadcasted_iota(jnp.int32, (n, n), 0) == lax.broadcasted_iota(jnp.int32, (n, n), 1)


def ns_start(values):
    return [y * (1.0 / (jnp.sqrt(jnp.sum(y * y)) + 1e-07)) for y in values]


def less_diagonal(g, m):
    n = g.shape[0]
    if n % 128:
        return jnp.where(on_diagonal(n), g - m, g)
    unit = jnp.where(on_diagonal(128), m, 0.0)
    rows = []
    for i in range(n // 128):
        row = g[128 * i : 128 * i + 128, :]
        tiles = [row[:, 128 * j : 128 * j + 128] for j in range(n // 128)]
        tiles[i] = tiles[i] - unit
        rows.append(jnp.concatenate(tiles, axis=1))
    return jnp.concatenate(rows, axis=0)


def ns_shift(t):
    return jnp.where(t >= 3, 0.8, jnp.where(t == 2, 0.5, 0.0)).astype(F32)


def ns_poly(values, m):
    lows = [y.astype(BF16) for y in values]
    grams = [nt(l, l) for l in lows]
    rest = [less_diagonal(g, m) for g in grams]
    lowr = [r.astype(BF16) for r in rest]
    squares = [nn(r, r) for r in lowr]
    return [((ns_second + 2.0 * ns_third * m) * r + ns_third * s).astype(BF16) for r, s in zip(rest, squares)]


def ns_step(values, m, polys):
    moved = [nn(q, y.astype(BF16)) for q, y in zip(polys, values)]
    return [(ns_first + ns_second * m + ns_third * m * m) * y + t for y, t in zip(values, moved)]


def ns_sweep(values, t):
    m = ns_shift(t)
    return ns_step(values, m, ns_poly(values, m))


def close_kernel(p, shares, *refs):
    (len_ref, wt_ref, so_ref, s1_ref, s2_ref, gv_ref, gmq_ref, wq_ref, wo_ref, w1_ref, w2_ref, vec_ref, vm1_ref, vm2_ref,
     x_hbm, qt_hbm, k_hbm, kt_hbm, v_hbm, ct_hbm, lse_ref, dct_hbm, res_hbm,
     gt_ref, mq_ref, mo_ref, m1_ref, m2_ref, nq_ref, no_ref, n1_ref, n2_ref, f_ref, s_ref, v_ref,
     x_s, qt_s, k_s, kt_s, v_s, ct_s, dct_s, res_s, bias_s, dq_s, dk_s, dv_s, gq_s, gv2_s, sq_s, oo_s, o1_s, o2_s, oq_s,
     y_s, po_s, pf_s, xo_s, xf_s, xq_s, xo_r, xf_r, xq_r, in_sem, x_send, x_recv) = refs[: 35 + 31]
    rest = refs[35 + 31 :]
    p.locate()
    d, n = lax.axis_index("dp"), lax.axis_index("narrow")
    n_rows, seq = x_s.shape[:2]
    pairs = ((qt_hbm, qt_s), (k_hbm, k_s), (dct_hbm, dct_s), (v_hbm, v_s), (ct_hbm, ct_s), (kt_hbm, kt_s), (x_hbm, x_s), (res_hbm, res_s))

    def loads(row):
        return [pltpu.make_async_copy(src.at[row], dst.at[row], in_sem.at[row, i]) for i, (src, dst) in enumerate(pairs)]

    for row in range(n_rows):
        for copy in loads(row):
            copy.start()
    p.barrier()
    sums = [sum_steps(p, s, src, out, rest[10 * i : 10 * i + 10])
            for i, (s, src, out) in enumerate(zip(shares, (so_ref, s1_ref, s2_ref, sq_s), (oo_s, o1_s, o2_s, oq_s)))]
    o, f1, f2, q = sums
    for step in (o[0], f1[0], f2[0]):
        step()
    turns = dealt([o[1], f1[1], o[2], f2[1], o[3], f1[2], o[4], f2[2], o[5], f1[3], o[6], f2[3], o[7], f1[4], f2[4]], 6 * n_rows)
    gq_s[...] = jnp.zeros_like(gq_s)
    gv2_s[...] = jnp.zeros_like(gv2_s)
    lane = lax.broadcasted_iota(jnp.int32, (192, 256), 1)

    def one_row(row, carry):
        same = ids(len_ref, row, (seq, seq), 0) == ids(len_ref, row, (seq, seq), 1)
        bias_s[...] = jnp.where(same, 0.0, -1e30)
        for copy in loads(row):
            copy.wait()

        def pair(j, carry):
            lo = pl.multiple_of(128 * j, 128)
            kp, vp = k_s[row, :, pl.ds(lo, 128)], v_s[row, :, pl.ds(lo, 128)]
            for e in range(2):
                at = pl.ds(pl.multiple_of(lo + 64 * e, 64), 64)
                qh, dc = qt_s[row, at, :], dct_s[row, at, :]
                none = jnp.zeros_like(qh)
                wide = lambda a: jnp.concatenate([none, a] if e else [a, none], axis=0)
                delta = jnp.sum(dc.astype(F32) * ct_s[row, at, :].astype(F32), axis=0, keepdims=True)
                s = nn(kp, wide(qh)) + bias_s[...]
                ex = jnp.exp(s - lse_ref[row, pl.ds(2 * j + e, 1), :])
                de = nn(vp, wide(dc))
                ds = (ex * (de - delta)).astype(BF16)
                dv_s[at, :] = nt(dc, ex.astype(BF16)).astype(BF16)
                dk_s[at, :] = nt(qh, ds).astype(BF16)
                dq_s[at, :] = (nn(kt_s[row, at, :], ds) * 0.125).astype(BF16)
            at_turn(row * 6 + j, turns)
            return carry

        lax.fori_loop(0, 6, pair, 0)
        dx = []
        for g in range(4):
            lo = window(g)
            r = slice(192 * g, 192 * g + 192)
            cat = jnp.concatenate([dq_s[r, :], dk_s[r, :], dv_s[r, :]], axis=0)
            dx.append(nn(wt_ref[g], cat))
            gq = nn(cat, x_s[row, :, lo : lo + 256])
            keep = (lane < 192) if g % 2 == 0 else (lane >= 64)
            for c in range(3):
                gq_s[c, :, lo : lo + 256] += jnp.where(keep, gq[192 * c : 192 * c + 192], 0.0)
        gt_ref[row] = (res_s[row] + jnp.concatenate(dx, axis=0).T).astype(BF16)
        ones = jnp.ones((16, seq), BF16)
        gv2_s[0:1, :] += nt(ones, dq_s[...])[0:1]
        gv2_s[1:2, :] += nt(ones, dv_s[...])[0:1]
        return carry

    lax.fori_loop(0, n_rows, one_row, 0)
    slim, tall = gmq_ref.shape[1:]
    up = hot((192, tall), 0, n * tall)
    for c in range(3):
        held = jnp.zeros((tall, 768), F32)
        for g in range(4):
            held = held + tn((0.95 * gmq_ref[4 * c + g]).astype(BF16), hot((slim, 768), 192 * g + d * slim, 0))
        put_blocks(sq_s, 1152 * c, gq_s[c] + nn(up, held.astype(BF16)))
    gv = jnp.concatenate([gv_ref[0:4], gv2_s[0:2], gv_ref[6:12]], axis=0)
    tail = sq_s.shape[0] - 3456
    flat = jnp.concatenate([gv[:, 128 * j : 128 * j + 128] for j in range(6)] + [jnp.zeros((tail - 72, 128), F32)], axis=0)
    sq_s[3456:, :] = flat.astype(BF16)
    for step in (q[0], o[8], q[1]):
        step()
    wide, cols = w1_ref.shape[2], w1_ref.shape[1]
    sel_l = hot((wide, 768), n * wide, 0)
    sel_s = hot((cols, 192), d * cols, 0)
    big = wo_ref.shape[2]
    sel_b = hot((big, 768), d * big, 0)
    core0, core1 = p.c == 0, p.c == 1
    eight = lambda: [y_s[192 * i : 192 * i + 192, :] for i in range(8)]

    late = 3
    before = [[f1[5]], [f1[6]], [f1[7]], [q[5]], [q[7]]]
    between = [[q[2], f2[5]], [q[3], f2[6]], [q[4], f2[7], f1[8], f2[8]], [q[6]], [q[8]]]

    def sweep(t, carry):
        on0 = jnp.logical_and(core0, t < NS_STEPS)
        on1 = jnp.logical_and(core1, t >= late)

        @pl.when(jnp.logical_and(core0, t == 0))
        def _():
            y_s[0:768, :] = ns_start([wide_rows(oo_s, 0, 4).astype(F32)])[0]

        @pl.when(jnp.logical_and(core1, t == late))
        def _():
            for i, y in enumerate(ns_start([wide_rows(r, 1152 * g, 1).astype(F32) for r in (o1_s, o2_s) for g in range(4)])):
                y_s[192 * i : 192 * i + 192, :] = y

        @pl.when(on0)
        def _():
            po_s[...] = ns_poly([y_s[0:768, :]], ns_shift(t))[0]

        @pl.when(on1)
        def _():
            for i, poly in enumerate(ns_poly(eight(), ns_shift(t - late))):
                pf_s[i] = poly

        at_turn(t, before)

        @pl.when(on0)
        def _():
            y_s[0:768, :] = ns_step([y_s[0:768, :]], ns_shift(t), [po_s[...]])[0]

        @pl.when(on1)
        def _():
            for i, y in enumerate(ns_step(eight(), ns_shift(t - late), [pf_s[i] for i in range(8)])):
                y_s[192 * i : 192 * i + 192, :] = y

        at_turn(t, between)
        return carry

    lax.fori_loop(0, NS_STEPS + late, sweep, 0)
    wires = Wires(p, x_send, x_recv)
    mo_ref[0] = nt(sel_l, nn(sel_b, wide_rows(oo_s, 0, 4)).astype(BF16))
    for ref, m_ref in ((o1_s, m1_ref), (o2_s, m2_ref)):
        for g in range(4):
            m_ref[g] = nt(nn(sel_s, wide_rows(ref, 1152 * g, 1)).astype(BF16), sel_l)

    @pl.when(core0)
    def _():
        xo_s[...] = nn(sel_b, y_s[0:768, :].astype(BF16)).astype(BF16)

    @pl.when(core1)
    def _():
        for i in range(8):
            xf_s[cols * i : cols * i + cols, :] = nn(sel_s, y_s[192 * i : 192 * i + 192, :].astype(BF16)).astype(BF16)

    rows = [wide_rows(oq_s, 1152 * c, 1) for c in range(3)]
    spot = lambda g: hot_cut((256, 128), 0, 0)

    def square(parity):
        keep = (lane < 192) if parity == 0 else (lane >= 64)
        which = [(c, g) for c in range(3) for g in (parity, parity + 2)]
        ys = ns_start([jnp.where(keep, rows[c][:, window(g) : window(g) + 256].astype(F32), 0.0) for c, g in which])
        for i, y in enumerate(ys):
            y_s[192 * i : 192 * i + 192, :256] = y

        def turn(t, carry):
            ys = [y_s[192 * i : 192 * i + 192, :256] for i in range(6)]
            for i, y in enumerate(ns_sweep(ys, t)):
                y_s[192 * i : 192 * i + 192, :256] = y
            return carry

        lax.fori_loop(0, NS_STEPS, turn, 0)
        ys = [y_s[192 * i : 192 * i + 192, :256] for i in range(6)]
        for c in range(3):
            part = jnp.zeros((192, 128), F32)
            for (cc, g), y in zip(which, ys):
                if cc == c:
                    at = 64 * (g % 2) + d * slim
                    r = lax.broadcasted_iota(jnp.int32, (256, 128), 0) - at
                    q = lax.broadcasted_iota(jnp.int32, (256, 128), 1) - g * slim
                    sel = jnp.logical_and(r == q, jnp.logical_and(q >= 0, q < slim)).astype(BF16)
                    part = part + nn(y.astype(BF16), sel)
            xq_s[192 * c : 192 * c + 192, :] = part.astype(BF16)

    @pl.when(core0)
    def _():
        square(0)

    @pl.when(core1)
    def _():
        square(1)

    copies = [wires.plan(lambda a=a: a, lambda b=b: b, "c", 1) for a, b in ((xq_s, xq_r), (xo_s, xo_r), (xf_s, xf_r))]
    wires.start(copies)
    sel_o = hot((tall, 192), n * tall, 0)
    for c in range(3):
        mine = nn(sel_o, rows[c]).astype(BF16)
        for g in range(4):
            mq_ref[4 * c + g] = nt(hot((slim, 768), 192 * g + d * slim, 0), mine)
    vt = oq_s[3456 : 3456 + 80, :].astype(F32)
    grad = jnp.concatenate([vt[12 * j : 12 * j + 12] for j in range(6)], axis=1)
    first = 0.9 * vm1_ref[...] + 0.1 * grad
    second = 0.999 * vm2_ref[...] + 0.001 * grad * grad
    f_ref[...] = first
    s_ref[...] = second
    v_ref[...] = vec_ref[...] - adam_rate * (first * (1.0 / (1.0 - 0.9**STEP))) / (jnp.sqrt(second * (1.0 / (1.0 - 0.999**STEP))) + 1e-08)

    def fresh(w, own, longest):
        return w - muon_rate * (0.2 * math.sqrt(longest) * own + muon_decay * w)

    wires.arrive(copies)
    for c in range(3):
        both = (xq_s[192 * c : 192 * c + 192, :].astype(F32) + xq_r[192 * c : 192 * c + 192, :].astype(F32)).astype(BF16)
        mine = nn(sel_o, both).astype(BF16)
        for g in range(4):
            nq_ref[4 * c + g] = fresh(wq_ref[4 * c + g], nt(hot((slim, 128), g * slim, 0), mine), 192)
    xo = jnp.where(core0, xo_s[...], xo_r[...])
    no_ref[0] = fresh(wo_ref[0], nt(sel_l, xo), 768)
    for i, (w_ref, n_ref) in enumerate(((w1_ref, n1_ref), (w2_ref, n2_ref))):
        for g in range(4):
            at = slice(cols * (4 * i + g), cols * (4 * i + g) + cols)
            n_ref[g] = fresh(w_ref[g], nt(jnp.where(core1, xf_s[at, :], xf_r[at, :]), sel_l), 768)
    wires.finish()


def closing(p, shares, lengths, wt, so, s1, s2, gv, mq, weights, vec, vm1, vm2, acts, ident):
    tokens, lse = acts[0], acts[6]
    n, seq, d = tokens.shape
    slim = mq.shape[1]
    shape = lambda a: jax.ShapeDtypeStruct(a.shape, F32)
    outs = [jax.ShapeDtypeStruct(tokens.shape, BF16)] + [shape(w) for w in weights] * 2 + [shape(vec)] * 3
    hbm = pl.BlockSpec(memory_space=pl.ANY)
    tm, mt = pltpu.VMEM((n, seq, d), BF16), pltpu.VMEM((n, d, seq), BF16)
    flat = lambda r: pltpu.VMEM((r, 128), BF16)
    scratch = [tm, mt, tm, mt, tm, mt, mt, pltpu.VMEM((n, seq, d), BF16), pltpu.VMEM((seq, seq), F32)]
    scratch += [pltpu.VMEM((d, seq), BF16)] * 3 + [pltpu.VMEM((3, 192, 768), F32), pltpu.VMEM((8, 768), F32)]
    scratch += [flat(shares[3].rows)] + [flat(s.rows) for s in shares]
    scratch += [pltpu.VMEM((1536, 768), F32), pltpu.VMEM((768, 768), BF16), pltpu.VMEM((8, 192, 192), BF16)]
    scratch += [pltpu.VMEM((4 * slim, 768), BF16), pltpu.VMEM((8 * slim, 768), BF16), pltpu.VMEM((576, 128), BF16)] * 2
    scratch += [pltpu.SemaphoreType.DMA((n, 8)), pltpu.SemaphoreType.DMA((3,)), pltpu.SemaphoreType.DMA((3,))]
    for s in shares:
        scratch += s.scratch(p)
    return pl.pallas_call(
        functools.partial(close_kernel, p, shares),
        out_shape=outs,
        in_specs=[pl.BlockSpec(memory_space=pltpu.SMEM)] + [VMEM] * 13 + [hbm] * 6 + [VMEM] + [hbm] * 2,
        out_specs=[VMEM] * 12,
        scratch_shapes=scratch,
        compiler_params=pltpu.CompilerParams(collective_id=ident, has_side_effects=True, vmem_limit_bytes=62 * 2**20),
    )(lengths, wt, so, s1, s2, gv, mq, *weights, vec, vm1, vm2, *acts)


class Owned:
    def __init__(self, p, half):
        self.half, self.rows, self.copies = half, 8 * half, 4 + 2 * (p.Z - 1)
        self.kinds = [4 * half, 4 * half, 2 * half, half, (p.Z - 1) * (half // p.Z), half, half]

    def scratch(self):
        return [pltpu.VMEM((k, 128), BF16) for k in self.kinds] + [pltpu.SemaphoreType.DMA((self.copies,))] * 2


def owned_steps(p, s, src, scratch):
    held, from_c, r1, r2, r3, mine, other, send_sem, recv_sem = scratch
    wires = Wires(p, send_sem, recv_sem)
    h, q, z, c = s.half, s.half // p.Z, p.z, p.c
    first = jnp.where(c == 0, p.x, p.y)
    second = jnp.where(c == 0, p.y, p.x)
    cut = lambda ref, start, size: lambda: ref.at[spread(start(), size)]

    def partner(turn):
        along_x = c == turn
        x, y = jnp.where(along_x, 1 - p.x, p.x), jnp.where(along_x, p.y, 1 - p.y)
        return (z * p.X + x, y * p.C + c)

    sibling = lambda: p.device("c", 1)
    spot = lambda: (2 * first + second) * h
    sends = [
        [wires.plan_to(cut(src, lambda: (1 - c) * 4 * h, 4 * h), lambda: from_c, sibling)],
        [wires.plan_to(cut(held, lambda: (1 - first) * 2 * h, 2 * h), lambda: r1, lambda: partner(0))],
        [wires.plan_to(cut(held, lambda: (2 * first + 1 - second) * h, h), lambda: r2, lambda: partner(1))],
        [],
        [],
        [wires.plan_to(lambda: mine, lambda: other, sibling)],
    ]
    for j in range(1, p.Z):
        sends[3].append(wires.plan(cut(held, lambda j=j: spot() + p.at("z", j) * q, q), lambda j=j: r3.at[pl.ds((j - 1) * q, q)], "z", j))
        sends[4].append(wires.plan(*(cut(mine, lambda: z * q, q),) * 2, "z", j))

    def add(dst, to, ref, start, size, parts):
        value = ref[spread(start, size), :].astype(F32)
        for part in parts:
            value = value + part().astype(F32)
        dst[spread(to, size), :] = value.astype(BF16)

    def step(t):
        if 1 <= t <= 5:
            wires.arrive(sends[t - 1])
        if t == 1:
            add(held, 0, src, c * 4 * h, 4 * h, [lambda: from_c[...]])
        if t == 2:
            add(held, first * 2 * h, held, first * 2 * h, 2 * h, [lambda: r1[...]])
        if t == 3:
            add(held, spot(), held, spot(), h, [lambda: r2[...]])
        if t == 4:
            add(mine, z * q, held, spot() + z * q, q, [lambda j=j: r3[(j - 1) * q : j * q, :] for j in range(1, p.Z)])
        if t < 5:
            wires.start(sends[t])
        if t == 5:

            @pl.when(c == 0)
            def _():
                wires.start(sends[5])

        if t == 6:
            wires.finish(skip=sends[5])

            @pl.when(c == 0)
            def _():
                wires.leave(sends[5])

            @pl.when(c == 1)
            def _():
                wires.arrive(sends[5])

    return [functools.partial(step, t) for t in range(7)]


class Solo:
    def __init__(self, p, half):
        self.half, self.rows, self.copies = half, 8 * half, 1 + 4 + 4 * (p.Z - 1)
        q = (p.Z - 1) * (half // p.Z)
        self.kinds = [8 * half, 8 * half] + [2 * half, half, q] * 2 + [2 * half]

    def scratch(self):
        return [pltpu.VMEM((k, 128), BF16) for k in self.kinds] + [pltpu.SemaphoreType.DMA((self.copies,))] * 2


def solo_steps(p, s, src, scratch):
    held, from_c, a1, a2, a3, b1, b2, b3, mine, send_sem, recv_sem = scratch
    wires = Wires(p, send_sem, recv_sem)
    h, q, z = s.half, s.half // p.Z, p.z
    cut = lambda ref, start, size: lambda: ref.at[spread(start(), size)]
    over = [wires.plan_to(lambda: src, lambda: from_c, lambda: p.device("c", 1))]
    sends = [[], [], [], []]
    ways = (("x", "y", p.x, p.y, 0, a1, a2, a3, 0), ("y", "x", p.y, p.x, 4 * h, b1, b2, b3, h))
    for one, two, first, second, base, r1, r2, r3, to in ways:
        sends[0].append(wires.plan(cut(held, lambda f=first, b=base: b + (1 - f) * 2 * h, 2 * h), lambda r=r1: r, one, 1))
        sends[1].append(wires.plan(cut(held, lambda f=first, e=second, b=base: b + (2 * f + 1 - e) * h, h), lambda r=r2: r, two, 1))
        for j in range(1, p.Z):
            part = lambda f=first, e=second, b=base, j=j: b + (2 * f + e) * h + p.at("z", j) * q
            sends[2].append(wires.plan(cut(held, part, q), lambda r=r3, j=j: r.at[pl.ds((j - 1) * q, q)], "z", j))
            sends[3].append(wires.plan(*(cut(mine, lambda t=to: t + z * q, q),) * 2, "z", j))

    def add(dst, to, ref, start, size, parts):
        value = ref[spread(start, size), :].astype(F32)
        for part in parts:
            value = value + part.astype(F32)
        dst[spread(to, size), :] = value.astype(BF16)

    def give():
        wires.start(over)

    def gave():
        wires.leave(over)

    def step(t):
        wires.arrive(over if t == 0 else sends[t - 1])
        if t == 0:
            held[...] = (src[...].astype(F32) + from_c[...].astype(F32)).astype(BF16)
        for one, two, first, second, base, r1, r2, r3, to in ways:
            spot = base + (2 * first + second) * h
            if t == 1:
                add(held, base + first * 2 * h, held, base + first * 2 * h, 2 * h, [r1[...]])
            if t == 2:
                add(held, spot, held, spot, h, [r2[...]])
            if t == 3:
                add(mine, to + z * q, held, spot + z * q, q, [r3[(j - 1) * q : j * q, :] for j in range(1, p.Z)])
        if t < 4:
            wires.start(sends[t])
        else:
            wires.finish(skip=over)

    return give, gave, [functools.partial(step, t) for t in range(5)]


def canon(odd, base):
    r = lax.broadcasted_iota(jnp.int32, (256, 128), 0)
    s = lax.broadcasted_iota(jnp.int32, (256, 128), 1)
    channel = jnp.where(odd, jnp.where(r < 128, r + 64, r - 128), r)
    return jnp.where(r < 192, channel - base, -1000), s


def paced(o, f1, f2):
    return ((5, o[2]), (7, f1[1]), (10, o[3]), (10, f2[1]), (13, f1[2]), (16, o[4]), (16, f2[2]), (19, f1[3]), (22, o[5]), (23, f2[3]))


def owner_kernel(p, shares, *refs):
    (len_ref, wt_ref, so_hbm, s1_hbm, s2_hbm, gv_ref, gmq_ref, wq_ref, wo_ref, w1_ref, w2_ref, vec_ref, vm1_ref, vm2_ref,
     x_hbm, qt_hbm, k_hbm, kt_hbm, v_hbm, ct_hbm, lse_ref, dct_hbm, res_hbm,
     gt_ref, mq_ref, mo_ref, m1_ref, m2_ref, nq_ref, no_ref, n1_ref, n2_ref, f_ref, s_ref, v_ref,
     so_ref, s1_ref, s2_ref, x_s, qt_s, k_s, kt_s, v_s, ct_s, dct_s, res_s, bias_s, dq_s, dk_s, dv_s, gq_s, gv2_s, sq_s, oo_s,
     yo_s, yf_s, yq_s, xo_s, xo_r, tmf_s, txf_s, tmq_s, txq_s, tv_s, rmf_s, rxf_s, rmq_s, rxq_s, rv_s, sel_s,
     in_sem, src_sem, x_send, x_recv) = refs[: 35 + 39]
    rest = refs[35 + 39 :]
    p.locate()
    p.greet(corner=True)
    d, n = lax.axis_index("dp"), lax.axis_index("narrow")
    core0, core1 = p.c == 0, p.c == 1
    n_rows, seq = x_s.shape[:2]
    pairs = ((qt_hbm, qt_s), (k_hbm, k_s), (dct_hbm, dct_s), (v_hbm, v_s), (ct_hbm, ct_s), (kt_hbm, kt_s), (x_hbm, x_s), (res_hbm, res_s))

    def load(row, i):
        return pltpu.make_async_copy(pairs[i][0].at[row], pairs[i][1].at[row], in_sem.at[row, i])

    def loads(row, count=8):
        return [load(row, i) for i in range(count)]

    sources = [pltpu.make_async_copy(a, b, src_sem.at[i]) for i, (a, b) in enumerate(((so_hbm, so_ref), (s1_hbm, s1_ref), (s2_hbm, s2_ref)))]
    for copy in sources[:1] + loads(0) + sources[1:]:
        copy.start()
    for row in range(1, n_rows):
        for copy in loads(row):
            copy.start()
    o = sum_steps(p, shares[0], so_ref, oo_s, rest[:10])
    f1 = owned_steps(p, shares[1], s1_ref, rest[10:19])
    f2 = owned_steps(p, shares[2], s2_ref, rest[19:28])
    q_give, q_gave, q = solo_steps(p, shares[3], sq_s, rest[28:39])
    q_all = rest[36]
    f1_half, f1_other, f2_half, f2_other = rest[15], rest[16], rest[24], rest[25]
    turns = [[] for _ in range(12 * n_rows)]
    for i, step in paced(o, f1, f2):
        turns[i * n_rows // 2].append(step)
    slim, tall = gmq_ref.shape[1:]
    up = hot((192, tall), 0, n * tall)
    for c in range(3):
        held = jnp.zeros((tall, 768), F32)
        for g in range(4):
            held = held + tn((0.95 * gmq_ref[4 * c + g]).astype(BF16), hot((slim, 768), 192 * g + d * slim, 0))
        gq_s[c] = nn(up, held.astype(BF16))
    gv2_s[...] = jnp.zeros_like(gv2_s)
    for x in range(2):
        for c in range(3):
            at, lane_of = canon(p.y == 1, (p.z * 2 + x) * slim)
            sel_s[x, c] = jnp.logical_and(jnp.logical_and(at >= 0, at < slim), at + c * slim == lane_of).astype(BF16)
    p.meet(corner=True)
    sources[0].wait()
    o[0]()
    lane = lax.broadcasted_iota(jnp.int32, (192, 256), 1)

    def one_row(row, carry):
        same = ids(len_ref, row, (seq, seq), 0) == ids(len_ref, row, (seq, seq), 1)
        bias_s[...] = jnp.where(same, 0.0, -1e30)
        for copy in loads(row, 6):
            copy.wait()

        @pl.when(row == 0)
        def _():
            for copy in sources[1:]:
                copy.wait()
            o[1]()
            f1[0]()
            f2[0]()

        def pair(j, carry):
            lo = pl.multiple_of(128 * j, 128)
            kp, vp = k_s[row, :, pl.ds(lo, 128)], v_s[row, :, pl.ds(lo, 128)]
            for e in range(2):
                at = pl.ds(pl.multiple_of(lo + 64 * e, 64), 64)
                qh, dc = qt_s[row, at, :], dct_s[row, at, :]
                none = jnp.zeros_like(qh)
                wide = lambda a: jnp.concatenate([none, a] if e else [a, none], axis=0)
                delta = jnp.sum(dc.astype(F32) * ct_s[row, at, :].astype(F32), axis=0, keepdims=True)
                s = nn(kp, wide(qh)) + bias_s[...]
                ex = jnp.exp(s - lse_ref[row, pl.ds(2 * j + e, 1), :])
                de = nn(vp, wide(dc))
                ds = (ex * (de - delta)).astype(BF16)
                dv_s[row, at, :] = nt(dc, ex.astype(BF16)).astype(BF16)
                dk_s[row, at, :] = nt(qh, ds).astype(BF16)
                dq_s[row, at, :] = (nn(kt_s[row, at, :], ds) * 0.125).astype(BF16)
                at_turn(row * 12 + 2 * j + e, turns)
            return carry

        lax.fori_loop(0, 6, pair, 0)
        load(row, 6).wait()
        for g in range(4):
            lo = window(g)
            r = slice(192 * g, 192 * g + 192)
            gq = nn(jnp.concatenate([dq_s[row, r, :], dk_s[row, r, :], dv_s[row, r, :]], axis=0), x_s[row, :, lo : lo + 256])
            keep = (lane < 192) if g % 2 == 0 else (lane >= 64)
            for c in range(3):
                gq_s[c, :, lo : lo + 256] += jnp.where(keep, gq[192 * c : 192 * c + 192], 0.0)
        ones = jnp.ones((16, seq), BF16)
        gv2_s[0:1, :] += nt(ones, dq_s[row])[0:1]
        gv2_s[1:2, :] += nt(ones, dv_s[row])[0:1]
        return carry

    lax.fori_loop(0, n_rows, one_row, 0)
    half = shares[3].half
    values = [gq_s[c] for c in range(3)]
    gv = jnp.concatenate([gv_ref[0:4], gv2_s[0:2], gv_ref[6:12]], axis=0)
    lane = lax.broadcasted_iota(jnp.int32, (192, 128), 1)
    for g in range(4):
        lo = window(g)
        tiles = []
        edges = []
        for c in range(3):
            a, b = values[c][:, lo : lo + 128], values[c][:, lo + 128 : lo + 256]
            whole, edge = (b, pltpu.roll(a, 64, 1)) if g % 2 else (a, b)
            tiles.append(whole)
            edges.append(jnp.where(lane < 64, edge, 0.0))
        tiles.append(edges[0] + pltpu.roll(edges[1], 64, 1))
        tiles.append(edges[2][:96] + pltpu.roll(edges[2][96:], 64, 1))
        vec = [gv[0:8, 192 * g : 192 * g + 128]]
        vec.append(jnp.concatenate([gv[0:8, 192 * g + 128 : 192 * g + 192], jnp.zeros((8, 64), F32)], axis=1))
        vec += [gv[8 + g : 9 + g, 128 * j : 128 * j + 128] for j in range(6)]
        vec.append(jnp.zeros((2 * half - 864 - 22, 128), F32))
        flat = jnp.concatenate(tiles + vec, axis=0).astype(BF16)
        sq_s[g * half : g * half + half, :] = flat[:half]
        sq_s[(4 + turned(g)) * half : (5 + turned(g)) * half, :] = flat[half:]
    def blocks(a_ref, b_ref):
        return jnp.concatenate([r[192 * j : 192 * j + 192, :] for r in (a_ref, b_ref) for j in range(3)], axis=1)

    def grad_in(row):
        dx = []
        for g in range(4):
            r = slice(192 * g, 192 * g + 192)
            dx.append(nn(wt_ref[g], jnp.concatenate([dq_s[row, r, :], dk_s[row, r, :], dv_s[row, r, :]], axis=0)))
        load(row, 7).wait()
        gt_ref[row] = (res_s[row].astype(F32) + jnp.concatenate(dx, axis=0).T).astype(BF16)

    wires = Wires(p, x_send, x_recv)
    me = 2 * p.x + p.y
    around = ((1, 0), (0, 1), (1, 1))

    def scatter(src, dst, cores=(1,)):
        return [
            wires.plan_to(
                lambda dx=dx, dy=dy: src.at[lax.rem(p.x + dx, 2), lax.rem(p.y + dy, 2)], lambda: dst.at[me], lambda dx=dx, dy=dy, c=c: p.other(dx, dy, c)
            )
            for dx, dy in around
            for c in cores
        ]

    early = [scatter(a, b) for a, b in ((tmf_s, rmf_s), (txf_s, rxf_s), (tmq_s, rmq_s), (tv_s, rv_s))]
    late = scatter(txq_s, rxq_s, (0, 1))
    late += [wires.plan_to(lambda: txq_s.at[p.x, p.y], lambda: rxq_s.at[me], lambda: p.device("c", 1))]
    late_on = {0: [late[0], late[2], late[4], late[6]], 1: [late[1], late[3], late[5]]}
    sibling = lambda: p.device("c", 1)
    pass_early = [wires.plan_to(lambda a=a: a, lambda a=a: a, sibling) for a in (rmf_s, rxf_s, rmq_s, rv_s)]
    pass_o = [wires.plan_to(lambda: xo_s, lambda: xo_r, sibling)]
    big = wo_ref.shape[2]
    sel_b = hot((big, 768), d * big, 0)
    wide, cols = w1_ref.shape[2], w1_ref.shape[1]

    def put_f(dst, pair):
        for x in range(2):
            sel = hot((cols, 192), (p.z * 2 + x) * cols, 0)
            part = jnp.concatenate([nn(sel, m) for m in pair], axis=0).astype(BF16)
            for y in range(2):
                dst[x, y] = part[:, 384 * y : 384 * y + 384]

    def put_q(dst, three):
        for x in range(2):
            part = jnp.zeros((192, 128), F32)
            for c, m in enumerate(three):
                part = part + nn(m, sel_s[x, c])
            for y in range(2):
                dst[x, y] = part[96 * y : 96 * y + 96].astype(BF16)

    @pl.when(core0)
    def _():
        q_give()
        for step in (lambda: grad_in(0), o[6], f1[4], f2[4], lambda: grad_in(1), f1[5], o[7], f2[5], o[8], f1[6], f2[6]):
            step()
        yo_s[...] = ns_start([wide_rows(oo_s, 0, 4).astype(F32)])[0]

        def turn(t, carry):
            y = yo_s[...]
            yo_s[...] = ns_sweep([y], t)[0]
            return carry

        lax.fori_loop(0, NS_STEPS, turn, 0)
        xo_s[...] = nn(sel_b, yo_s[...].astype(BF16)).astype(BF16)
        wires.start(pass_o)
        q_gave()

    @pl.when(core1)
    def _():
        for step in (q[0], o[6], f1[4], f2[4], lambda: grad_in(0), q[1], lambda: grad_in(1), f1[5], o[7], f2[5], o[8], q[2], f1[6], f2[6]):
            step()
        for i, y in enumerate(ns_start([blocks(a, b).astype(F32) for a, b in ((f1_other, f1_half), (f2_other, f2_half))])):
            yf_s[i] = y

        def f_turn(t, carry):
            ys = [yf_s[i] for i in range(2)]
            for i, y in enumerate(ns_sweep(ys, t)):
                yf_s[i] = y
            return carry

        lax.fori_loop(0, 3, f_turn, 0)
        q[3]()
        lax.fori_loop(3, NS_STEPS, f_turn, 0)
        put_f(tmf_s, [blocks(f1_other, f1_half), blocks(f2_other, f2_half)])
        put_f(txf_s, [yf_s[i].astype(BF16) for i in range(2)])
        for a, b, copies in zip((tmf_s, txf_s), (rmf_s, rxf_s), early[:2]):
            wires.start(copies)
            b[me] = a[p.x, p.y]
        q[4]()
        tiles = [q_all[192 * j : 192 * j + 192, :].astype(F32) for j in range(4)]
        lane = lax.broadcasted_iota(jnp.int32, (192, 128), 1)
        last = q_all[768:864, :].astype(F32)
        last = jnp.concatenate([last, pltpu.roll(last, 64, 1)], axis=0)
        edges = [jnp.where(lane < 64, e, 0.0) for e in (tiles[3], pltpu.roll(tiles[3], 64, 1), last)]
        three = [jnp.concatenate([t, e], axis=1) for t, e in zip(tiles, edges)]
        for i, y in enumerate(ns_start(three)):
            yq_s[i] = y

        def turn(t, carry):
            ys = [yq_s[i] for i in range(3)]
            for i, y in enumerate(ns_sweep(ys, t)):
                yq_s[i] = y
            return carry

        lax.fori_loop(0, NS_STEPS, turn, 0)
        put_q(txq_s, [yq_s[i].astype(BF16) for i in range(3)])
        wires.start(late)
        rxq_s[me] = txq_s[p.x, p.y]
        put_q(tmq_s, [m.astype(BF16) for m in three])
        for x in range(2):
            for y in range(2):
                tv_s[x, y] = q_all[864:896, :]
        for a, b, copies in zip((tmq_s, tv_s), (rmq_s, rv_s), early[2:]):
            wires.start(copies)
            b[me] = a[p.x, p.y]
        for copies in early[:2]:
            wires.arrive(copies)
        wires.start(pass_early[:2])
        wires.arrive(pass_o)

    @pl.when(core0)
    def _():
        wires.arrive(pass_early[:2])

    def fresh(w, own, longest):
        return w - muon_rate * (0.2 * math.sqrt(longest) * own + muon_decay * w)

    sel_l = hot((wide, 768), n * wide, 0)
    sel_h = hot((wide, 384), p.c * wide, 0)
    sel_q = hot((tall, 96), p.c * tall, 0)
    mo_ref[0] = nt(sel_l, nn(sel_b, wide_rows(oo_s, 0, 4)).astype(BF16))
    no_ref[0] = fresh(wo_ref[0], nt(sel_l, jnp.where(core0, xo_s[...], xo_r[...])), 768)
    for g in range(4):
        for i, (w_ref, m_ref, n_ref) in enumerate(((w1_ref, m1_ref, n1_ref), (w2_ref, m2_ref, n2_ref))):
            at = slice(cols * i, cols * i + cols)
            m_ref[g] = nt(rmf_s[g, at, :], sel_h)
            n_ref[g] = fresh(w_ref[g], nt(rxf_s[g, at, :], sel_h), 768)

    @pl.when(core1)
    def _():
        for copies in early[2:]:
            wires.arrive(copies)
        wires.start(pass_early[2:])
        wires.arrive(late_on[1])

    @pl.when(core0)
    def _():
        wires.arrive(late_on[0])

    for g in range(4):
        own = nn(sel_q, rxq_s[g]).astype(BF16)
        for c in range(3):
            nq_ref[4 * c + g] = fresh(wq_ref[4 * c + g], nt(hot((slim, 128), c * slim, 0), own), 192)

    @pl.when(core0)
    def _():
        wires.arrive(pass_early[2:])

    for g in range(4):
        own = nn(sel_q, rmq_s[g]).astype(BF16)
        for c in range(3):
            mq_ref[4 * c + g] = nt(hot((slim, 128), c * slim, 0), own)
    parts = [rv_s[g].astype(F32) for g in range(4)]
    top = jnp.concatenate([t for v in parts for t in (v[0:8], v[8:16, :64])], axis=1)
    low = [jnp.concatenate([v[16 + j : 17 + j] for j in range(6)], axis=1) for v in parts]
    grad = jnp.concatenate([top] + low, axis=0)
    first = 0.9 * vm1_ref[...] + 0.1 * grad
    second = 0.999 * vm2_ref[...] + 0.001 * grad * grad
    f_ref[...] = first
    s_ref[...] = second
    v_ref[...] = vec_ref[...] - adam_rate * (first * (1.0 / (1.0 - 0.9**STEP))) / (jnp.sqrt(second * (1.0 / (1.0 - 0.999**STEP))) + 1e-08)

    @pl.when(core0)
    def _():
        wires.leave(pass_o)

    @pl.when(core1)
    def _():
        for copies in early + [late, pass_early]:
            wires.leave(copies)


def closing_owned(p, shares, lengths, wt, so, s1, s2, gv, mq, weights, vec, vm1, vm2, acts, ident):
    tokens = acts[0]
    n, seq, d = tokens.shape
    slim = mq.shape[1]
    shape = lambda a: jax.ShapeDtypeStruct(a.shape, F32)
    outs = [jax.ShapeDtypeStruct(tokens.shape, BF16)] + [shape(w) for w in weights] * 2 + [shape(vec)] * 3
    hbm = pl.BlockSpec(memory_space=pl.ANY)
    tm, mt = pltpu.VMEM((n, seq, d), BF16), pltpu.VMEM((n, d, seq), BF16)
    scratch = [pltpu.VMEM((4608, 128), BF16)] * 3
    scratch += [tm, mt, tm, mt, tm, mt, mt, pltpu.VMEM((n, seq, d), BF16), pltpu.VMEM((seq, seq), F32)]
    scratch += [mt] * 3 + [pltpu.VMEM((3, 192, 768), F32), pltpu.VMEM((8, 768), F32)]
    scratch += [pltpu.VMEM((shares[3].rows, 128), BF16), pltpu.VMEM((shares[0].rows, 128), BF16)]
    scratch += [pltpu.VMEM((768, 768), F32), pltpu.VMEM((2, 192, 768), F32), pltpu.VMEM((3, 192, 256), F32)]
    scratch += [pltpu.VMEM((4 * slim, 768), BF16)] * 2
    to_f, to_q, to_v = (2 * slim, 384), (96, 128), (32, 128)
    scratch += [pltpu.VMEM((2, 2) + k, BF16) for k in (to_f, to_f, to_q, to_q, to_v)]
    scratch += [pltpu.VMEM((4,) + k, BF16) for k in (to_f, to_f, to_q, to_q, to_v)]
    scratch += [pltpu.VMEM((2, 3, 256, 128), BF16)]
    scratch += [pltpu.SemaphoreType.DMA((n, 8)), pltpu.SemaphoreType.DMA((3,)), pltpu.SemaphoreType.DMA((24,)), pltpu.SemaphoreType.DMA((24,))]
    scratch += shares[0].scratch(p)
    for s in shares[1:]:
        scratch += s.scratch()
    return pl.pallas_call(
        functools.partial(owner_kernel, p, shares),
        out_shape=outs,
        in_specs=[pl.BlockSpec(memory_space=pltpu.SMEM), VMEM] + [hbm] * 3 + [VMEM] * 9 + [hbm] * 6 + [VMEM] + [hbm] * 2,
        out_specs=[VMEM] * 12,
        scratch_shapes=scratch,
        compiler_params=pltpu.CompilerParams(collective_id=ident, has_side_effects=True, vmem_limit_bytes=62 * 2**20),
    )(lengths, wt, so, s1, s2, gv, mq, *weights, vec, vm1, vm2, *acts)


def hand_over_kernel(count, *refs):
    src, dst, held = refs[:count], refs[count : 2 * count], refs[2 * count : 3 * count]
    here, away = refs[3 * count :]
    loads = [pltpu.make_async_copy(src[i], held[i], here.at[i]) for i in range(count)]
    stores = [pltpu.make_async_copy(held[i], dst[i], away.at[i]) for i in range(count)]
    for load in loads:
        load.start()
    for load, store in zip(loads, stores):
        load.wait()
        store.start()
    for store in stores:
        store.wait()


def hand_over(values):
    hbm = pl.BlockSpec(memory_space=pl.ANY)
    count = len(values)
    return pl.pallas_call(
        functools.partial(hand_over_kernel, count),
        out_shape=[jax.ShapeDtypeStruct(a.shape, a.dtype) for a in values],
        in_specs=[hbm] * count,
        out_specs=[hbm] * count,
        scratch_shapes=[pltpu.VMEM(a.shape, a.dtype) for a in values] + [pltpu.SemaphoreType.DMA((count,))] * 2,
        compiler_params=pltpu.CompilerParams(vmem_limit_bytes=60 * 2**20),
    )(*values)


def local(tokens, doc_lengths, cotangent, qkv_weight, out_weight, ffn_in_weight, ffn_out_weight, vectors,
          qkv_moment, out_moment, ffn_in_moment, ffn_out_moment, vec_moment1, vec_moment2):
    p = Place(lax.axis_size("dp"), lax.axis_size("narrow"))
    flip = lambda a: a.transpose(0, 2, 1)
    wq, w1, w2, mq, m1, m2 = map(flip, (qkv_weight, ffn_in_weight, ffn_out_weight, qkv_moment, ffn_in_moment, ffn_out_moment))
    owned = p.X == 2 and p.Y == 2 and p.C == 2 and p.Z in (2, 4)
    if owned:
        shares = [Shares(p, 4608), Owned(p, 576), Owned(p, 576), Solo(p, 448)]
    else:
        shares = [Shares(p, r) for r in (4608, 4608, 4608, 3456 + 72)]
    qt, k, kt, v, ct, out_act, res, dct, lse, wt, so, s1, s2, gv = front(
        p, owned, shares[0].rows, doc_lengths, tokens, cotangent, wq, out_weight, w1, w2, vectors, out_moment, m1, m2, 0)
    acts = (tokens, qt, k, kt, v, ct, lse, dct, res)
    rest = (closing_owned if owned else closing)(
        p, shares, doc_lengths, wt, so, s1, s2, gv, mq, (wq, out_weight, w1, w2), vectors, vec_moment1, vec_moment2, acts, 1)
    out_act, gt, gq, go, g1, g2, nq, no, n1, n2, f, s, vn = hand_over([out_act] + list(rest))
    return (out_act, gt, flip(gq), go, flip(g1), flip(g2), flip(nq), no, flip(n1), flip(n2), f, s, vn)


def solution(mesh):
    rows = P(("dp", "narrow"), None, None)
    cut = P(None, "narrow", "dp")
    return jax.shard_map(
        local,
        mesh=mesh,
        in_specs=(rows, P(("dp", "narrow"), None), rows) + (cut,) * 4 + (P(),) + (cut,) * 4 + (P(), P()),
        out_specs=(rows, rows) + (cut,) * 8 + (P(),) * 3,
        check_vma=False,
    )
```
